32 devices in a mesh: sec: 2 (over y), row: 4 (over x, core), col: 4 (over z).
Axes of the slice: x: 2, y: 2, z: 4, core: 2. Of those that a mesh axis runs over, the one named last changes fastest.
Arguments:
- sketch: float32 [32, 64, 2048], P(None, ('sec', 'row'), 'col'), parts along dimension 1, may hold values from -6 to 6
- weights: float32 [8, 64, 2048], P(None, ('sec', 'row'), 'col'), parts along dimension 1, may hold values from 0.05 to 1
Outputs:
- basis: float32 [32, 64, 2048], P(None, ('sec', 'row'), 'col'), parts along dimension 1
- factor: float32 [64, 32], P('sec'), parts along dimension 0
The draws below stay inside these ranges and needn't reach their ends.
There are 2 independent parts, one for each index of `sec`. The reference program is written for one: setup_inputs(seed, part) draws one part's arguments, and reference() takes and returns one part's arrays. A program takes and returns all parts, laid end to end along the dimension named above; each array names one. Nothing has to cross between parts.
All inputs are finite; a program needn't handle non-finite values.
Results may differ from the reference program's by a relative error of at most 0.0001.
Values sent between devices are 32-bit elements; how exact they have to be, the bound alone decides.
No kernel may reach another device: no remote copies, remote signals or barrier semaphores. Data moves between devices by JAX's collectives and lax.ppermute only.
A program may use at most 64 MiB of HBM per device.

```python
import math
import jax
import jax.numpy as jnp
from jax import lax

K = 32
ITERS = 2
H = 32
W = 2048


def steps_of(stream_key, extent, split, low, largest):
    gain, own = 1.0, jax.random.fold_in(stream_key, 6)
    for axis_at, parts in split:
        steps = jnp.exp(jax.random.uniform(jax.random.fold_in(own, axis_at), (parts,), jnp.float32, low / len(split), largest / len(split)))
        gain = gain * jnp.repeat(steps, extent[axis_at] // parts).reshape([-1 if axis == axis_at else 1 for axis in range(len(extent))])
    return gain


def scatter_about(stream_key, dims, width, bound, shards=(), kind=jnp.bfloat16):
    result = width * jax.random.normal(stream_key, dims, jnp.float32)
    if shards:
        result = result * steps_of(stream_key, dims, shards, -0.22, 0.18)
    return jnp.clip(result, -bound, bound).astype(kind)


def setup_inputs(seed: int = 0, part: int = 0) -> dict:
    key_of = jax.random.split(jax.random.key(seed), 3)
    part_splits = jax.random.split(jax.random.fold_in(key_of[2], part), 3)
    return {
        "sketch": scatter_about(part_splits[0], (K, H, W), 1.0, 6.0, ((1, 4), (2, 4)), jnp.float32),
        "weights": jnp.clip(jnp.exp(math.log(1.0) - 2.9957323 * jax.random.uniform(part_splits[1], (8, H, W), jnp.float32) ** steps_of(part_splits[1], (8, H, W), ((1, 4), (2, 4)), -0.2, 0.2)), 0.05, 1.0),
    }


NEIGHBOURS = ((-1, -1), (-1, 0), (-1, 1), (0, -1), (0, 1), (1, -1), (1, 0), (1, 1))

def operate(planes, weights):
    height = planes.shape[1]
    breadth = planes.shape[2]
    padded = jnp.pad(planes, ((0, 0), (1, 1), (1, 1)))
    summed = jnp.sum(weights, axis=0) * planes
    for position, offset in enumerate(NEIGHBOURS):
        shift_row = offset[0]
        shift_col = offset[1]
        summed = summed + weights[position] * padded[:, 1 + shift_row:1 + shift_row + height, 1 + shift_col:1 + shift_col + breadth]
    return summed

def reference(sketch, weights):
    sketch_field = sketch
    lower_tri = jnp.zeros((K, K), jnp.float32)
    for power_step in range(ITERS):
        blocks = sketch_field.reshape(K // 8, 8, H, W)
        image_vals = lax.map(lambda block: operate(block, weights), blocks).reshape(K, H * W)
        gram_full = jnp.dot(image_vals, image_vals.T, precision=lax.Precision.HIGHEST) / (H * W)
        lower_tri = jnp.linalg.cholesky(gram_full)
        solved = jax.scipy.linalg.solve_triangular(lower_tri, image_vals, lower=True)
        sketch_field = solved.reshape(K, H, W)
    return (sketch_field, lower_tri.T)
```

```python
import functools

import jax
import jax.numpy as jnp
from jax import lax
from jax.experimental import pallas as pl
from jax.experimental.pallas import tpu as pltpu
from jax.sharding import PartitionSpec as P

NEIGHBOURS = ((-1, -1), (-1, 0), (-1, 1), (0, -1), (0, 1), (1, -1), (1, 0), (1, 1))
LANES = 128
PITCH = 4
HIGHEST = lax.Precision.HIGHEST


def vmem(count):
    return [pl.BlockSpec(memory_space=pltpu.VMEM)] * count


def call(kernel, out_shapes, *operands, scratch=()):
    return pl.pallas_call(
        kernel,
        out_shape=out_shapes,
        in_specs=vmem(len(operands)),
        out_specs=vmem(len(out_shapes)),
        scratch_shapes=scratch,
        compiler_params=pltpu.CompilerParams(vmem_limit_bytes=40 * 1024 * 1024),
    )(*operands)


def f32(*shape):
    return jax.ShapeDtypeStruct(shape, jnp.float32)


def pack_rows_kernel(sketch, weights, first, last, by_row):
    planes, rows, _ = sketch.shape
    for row in range(rows):
        by_row[row] = sketch[:, row, :]
    for slot in range(2):
        first[slot * planes : (slot + 1) * planes] = by_row[slot]
        last[slot * planes : (slot + 1) * planes] = by_row[rows - 2 + slot]
    first[2 * planes :] = weights[:, 0, :]
    last[2 * planes :] = weights[:, rows - 1, :]


def pack_cols_kernel(by_row, weights, below, above, left, right):
    rows, planes, width = by_row.shape
    lane = lax.broadcasted_iota(jnp.int32, (1, LANES), 1)
    starts = (0, width - LANES)
    totals = [[None, None], [None, None]]
    for row in range(rows + 4):
        for side, start in enumerate(starts):
            window = pl.ds(start, LANES)
            if row < 2:
                piece = below[row * planes : (row + 1) * planes, window]
            elif row < rows + 2:
                piece = by_row[row - 2, :, window]
            else:
                at = row - rows - 2
                piece = above[at * planes : (at + 1) * planes, window]
            extra = None
            if row == 1:
                extra = below[2 * planes :, window]
            elif 2 <= row < rows + 2:
                extra = weights[:, row - 2, window]
            elif row == rows + 2:
                extra = above[2 * planes :, window]
            base = PITCH * row - 2 * side
            keep = (lane == base % LANES) | (lane == (base + 1) % LANES)
            for kind, value in enumerate((piece, extra)):
                if value is None:
                    continue
                moved = jnp.where(keep, pltpu.roll(value, (PITCH * row) % LANES, 1) if row else value, 0.0)
                old = totals[side][kind]
                totals[side][kind] = moved if old is None else old + moved
    for side, target in enumerate((left, right)):
        target[:planes] = totals[side][0]
        target[planes:] = totals[side][1]


def apply_operator(rows3, weight_rows):
    width = rows3[1].shape[1]
    degree = jnp.sum(weight_rows, axis=0, keepdims=True)
    total = degree * rows3[1]
    sides = {-1: None, 1: None}
    for position, (up, across) in enumerate(NEIGHBOURS):
        weight = weight_rows[position : position + 1]
        value = rows3[up + 1]
        if across == 0:
            total = total + weight * value
        else:
            shifted = pltpu.roll(weight_rows, across % width, 1)[position : position + 1]
            term = shifted * value
            sides[across] = term if sides[across] is None else sides[across] + term
    for across, value in sides.items():
        total = total + pltpu.roll(value, (-across) % width, 1)
    return total


def stencil_kernel(by_row, weights, below, above, from_left, from_right, second, grams, wide, wide_weights, middle):
    rows, planes, width = by_row.shape
    lane = lax.broadcasted_iota(jnp.int32, (1, LANES), 1)
    keep = (lane < 2) | (lane >= LANES - 2)
    sides = from_left[...] + from_right[...]
    for row in range(rows + 4):
        if row < 2:
            wide[row, :, :width] = below[row * planes : (row + 1) * planes]
        elif row < rows + 2:
            wide[row, :, :width] = by_row[row - 2]
        else:
            at = row - rows - 2
            wide[row, :, :width] = above[at * planes : (at + 1) * planes]
        moved = pltpu.roll(sides, (-PITCH * row) % LANES, 1) if row else sides
        moved = jnp.where(keep, moved, 0.0)
        wide[row, :, width:] = moved[:planes]
        if 1 <= row < rows + 3:
            if row == 1:
                wide_weights[0, :, :width] = below[2 * planes :]
            elif row < rows + 2:
                wide_weights[row - 1, :, :width] = weights[:, row - 2, :]
            else:
                wide_weights[row - 1, :, :width] = above[2 * planes :]
            wide_weights[row - 1, :, width:] = moved[planes:]
    for row in range(rows + 2):
        middle[row] = apply_operator([wide[row], wide[row + 1], wide[row + 2]], wide_weights[row])
    gram = [jnp.zeros((planes, planes), jnp.float32)] * 2
    for row in range(rows):
        image = apply_operator([middle[row], middle[row + 1], middle[row + 2]], wide_weights[row + 1])[:, :width]
        second[row] = image
        for at, value in enumerate((middle[row + 1][:, :width], image)):
            gram[at] = gram[at] + lax.dot_general(
                value, value, (((1,), (1,)), ((), ())), precision=HIGHEST, preferred_element_type=jnp.float32
            )
    grams[:, :planes] = gram[0]
    grams[:, planes:] = gram[1]


def finish_kernel(pixel_count, grams, second, basis, factor):
    planes = factor.shape[0]
    rows = second.shape[0]
    scaled = grams[...] / pixel_count
    at_row = lax.broadcasted_iota(jnp.int32, (planes, planes), 0)
    at_col = lax.broadcasted_iota(jnp.int32, (planes, planes), 1)
    unit = jnp.where(at_row == at_col, 1.0, 0.0)
    state = jnp.concatenate([scaled[:, :planes], unit, scaled[:, planes:], unit], axis=1)
    half = 2 * planes
    row_of = lax.broadcasted_iota(jnp.int32, state.shape, 0)
    low_half = lax.broadcasted_iota(jnp.int32, state.shape, 1) < half
    for step in range(planes):
        column = jnp.where(low_half, state[:, step : step + 1], state[:, half + step : half + step + 1])
        pivot = column[step : step + 1]
        pivot_row = state[step : step + 1]
        inverse_root = lax.rsqrt(pivot)
        unit_row = pivot_row * inverse_root
        state = jnp.where(
            row_of > step,
            state - (column * inverse_root) * unit_row,
            jnp.where(row_of == step, unit_row, state),
        )
    first_inverse = state[:, planes:half]
    product_upper = jnp.where(at_col >= at_row, state[:, half : half + planes], 0.0)
    product_inverse = state[:, half + planes :]
    upper = lax.dot_general(
        product_upper,
        first_inverse,
        (((1,), (1,)), ((), ())),
        precision=HIGHEST,
        preferred_element_type=jnp.float32,
    )
    factor[...] = jnp.where(at_col >= at_row, upper, 0.0)
    for row in range(rows):
        basis[:, row, :] = jnp.dot(
            product_inverse, second[row], precision=HIGHEST, preferred_element_type=jnp.float32
        )


def shifted(value, axis, step):
    count = lax.axis_size(axis)
    pairs = [(i, i + step) for i in range(count) if 0 <= i + step < count]
    return lax.ppermute(value, axis, pairs)


def sum_over(value, axis):
    count = lax.axis_size(axis)
    stride = 1
    while stride < count:
        left = count // stride
        radix = 4 if left % 4 == 0 else 2 if left % 2 == 0 else left
        parts = [value]
        for turn in range(1, radix):
            pairs = []
            for i in range(count):
                digit = (i // stride) % radix
                pairs.append((i, i + ((digit + turn) % radix - digit) * stride))
            parts.append(lax.ppermute(value, axis, pairs))
        value = functools.reduce(jnp.add, parts)
        stride *= radix
    return value


def on_device(sketch, weights):
    planes, rows, width = sketch.shape
    pixel_count = rows * width * lax.axis_size("row") * lax.axis_size("col")
    message = f32(2 * planes + 8, width)
    first, last, by_row = call(pack_rows_kernel, [message, message, f32(rows, planes, width)], sketch, weights)
    below = shifted(last, "row", 1)
    above = shifted(first, "row", -1)
    side = f32(planes + 8, LANES)
    left, right = call(pack_cols_kernel, [side, side], by_row, weights, below, above)
    from_left = shifted(right, "col", 1)
    from_right = shifted(left, "col", -1)
    second, grams = call(
        stencil_kernel,
        [f32(rows, planes, width), f32(planes, 2 * planes)],
        by_row,
        weights,
        below,
        above,
        from_left,
        from_right,
        scratch=[
            pltpu.VMEM((rows + 4, planes, width + LANES), jnp.float32),
            pltpu.VMEM((rows + 2, 8, width + LANES), jnp.float32),
            pltpu.VMEM((rows + 2, planes, width + LANES), jnp.float32),
        ],
    )
    grams = sum_over(sum_over(grams, "row"), "col")
    basis, factor = call(
        functools.partial(finish_kernel, float(pixel_count)),
        [f32(planes, rows, width), f32(planes, planes)],
        grams,
        second,
    )
    return basis, factor


def solution(mesh):
    return jax.shard_map(
        on_device,
        mesh=mesh,
        in_specs=(P(None, ("sec", "row"), "col"), P(None, ("sec", "row"), "col")),
        out_specs=(P(None, ("sec", "row"), "col"), P("sec", None)),
        check_vma=False,
    )
```

```python
import functools

import jax
import jax.numpy as jnp
from jax import lax
from jax.experimental import pallas as pl
from jax.experimental.pallas import tpu as pltpu
from jax.sharding import PartitionSpec as P

NEIGHBOURS = ((-1, -1), (-1, 0), (-1, 1), (0, -1), (0, 1), (1, -1), (1, 0), (1, 1))
LANES = 128
PITCH = 4
HIGHEST = lax.Precision.HIGHEST


def call(kernel, out_shapes, *operands, memory=pltpu.VMEM, scratch=()):
    return pl.pallas_call(
        kernel,
        out_shape=out_shapes,
        in_specs=[pl.BlockSpec(memory_space=memory)] * len(operands),
        out_specs=[pl.BlockSpec(memory_space=pltpu.VMEM)] * len(out_shapes),
        scratch_shapes=scratch,
        compiler_params=pltpu.CompilerParams(vmem_limit_bytes=40 * 1024 * 1024),
    )(*operands)


def f32(*shape):
    return jax.ShapeDtypeStruct(shape, jnp.float32)


def sides_of(axis):
    place = lax.axis_index(axis)
    return place % 2 == 0, place > 0, place < lax.axis_size(axis) - 1


def pack_kernel(sketch, weights, by_row, weights_by_row, *rest):
    row_messages, col_messages, corner_messages = rest[:2], rest[2:4], rest[4:8]
    tile, weight_tile, arrived = rest[8:]
    copies = [
        pltpu.make_async_copy(sketch, tile, arrived.at[0]),
        pltpu.make_async_copy(weights, weight_tile, arrived.at[1]),
    ]
    for copy in copies:
        copy.start()
    planes, rows, width = tile.shape
    even_row, _, _ = sides_of("row")
    even_col, _, _ = sides_of("col")
    copies[1].wait()
    for row in range(rows):
        weights_by_row[row] = weight_tile[:, row, :]
    copies[0].wait()
    for row in range(rows):
        by_row[row] = tile[:, row, :]
    for message, up in zip(row_messages, (even_row, jnp.logical_not(even_row))):
        start = jnp.where(up, rows - 2, 0)
        for slot in range(2):
            message[slot * planes : (slot + 1) * planes] = by_row[start + slot]
        message[2 * planes :] = weights_by_row[jnp.where(up, rows - 1, 0)]
    lane = lax.broadcasted_iota(jnp.int32, (1, LANES), 1)
    packed = []
    for side, start in enumerate((0, width - LANES)):
        window = pl.ds(start, LANES)
        total = None
        for row in range(rows):
            place = PITCH * (row + 2)
            base = place - 2 * side
            keep = (lane == base) | (lane == base + 1)
            value = jnp.concatenate([by_row[row, :, window], weights_by_row[row, :, window]], axis=0)
            value = jnp.where(keep, pltpu.roll(value, place, 1), 0.0)
            total = value if total is None else total + value
        packed.append(total)
    left, right = packed
    for col_at, up_col in enumerate((even_col, jnp.logical_not(even_col))):
        edge = jnp.where(up_col, right, left)
        col_messages[col_at][...] = edge
        first_lanes = lane < PITCH * 4 - 2
        last_lanes = (lane >= PITCH * rows - 2) & (lane < PITCH * (rows + 2) - 2)
        corner_first = pltpu.roll(jnp.where(first_lanes, edge, 0.0), PITCH * rows, 1)
        corner_last = pltpu.roll(jnp.where(last_lanes, edge, 0.0), LANES - PITCH * rows, 1)
        for row_at, up_row in enumerate((even_row, jnp.logical_not(even_row))):
            corner_messages[2 * row_at + col_at][...] = jnp.where(up_row, corner_last, corner_first)


def apply_operator(rows3, weight_rows):
    width = rows3[1].shape[1]
    degree = jnp.sum(weight_rows, axis=0, keepdims=True)
    total = degree * rows3[1]
    sides = {-1: None, 1: None}
    for position, (up, across) in enumerate(NEIGHBOURS):
        weight = weight_rows[position : position + 1]
        value = rows3[up + 1]
        if across == 0:
            total = total + weight * value
        else:
            shifted = pltpu.roll(weight_rows, across % width, 1)[position : position + 1]
            term = shifted * value
            sides[across] = term if sides[across] is None else sides[across] + term
    for across, value in sides.items():
        total = total + pltpu.roll(value, (-across) % width, 1)
    return total


def stencil_kernel(by_row, weights_by_row, *rest):
    row_messages, col_messages, corner_messages = rest[:2], rest[2:4], rest[4:8]
    second, grams, wide, wide_weights, middle = rest[8:]
    rows, planes, width = by_row.shape
    even_row, has_below, has_above = sides_of("row")
    even_col, has_left, has_right = sides_of("col")
    lane = lax.broadcasted_iota(jnp.int32, (1, LANES), 1)
    keep = (lane < 2) | (lane >= LANES - 2)
    partner_row = [jnp.where(even_row, has_above, has_below), jnp.where(even_row, has_below, has_above)]
    partner_col = [jnp.where(even_col, has_right, has_left), jnp.where(even_col, has_left, has_right)]
    sides = jnp.zeros(col_messages[0].shape, jnp.float32)
    for col_at in range(2):
        sides = sides + jnp.where(partner_col[col_at], col_messages[col_at][...], 0.0)
        for row_at in range(2):
            both = partner_col[col_at] & partner_row[row_at]
            sides = sides + jnp.where(both, corner_messages[2 * row_at + col_at][...], 0.0)
    for row_at, up in enumerate((even_row, jnp.logical_not(even_row))):
        start = jnp.where(up, rows + 2, 0)
        for slot in range(2):
            value = row_messages[row_at][slot * planes : (slot + 1) * planes]
            wide[start + slot, :, :width] = jnp.where(partner_row[row_at], value, 0.0)
        value = jnp.where(partner_row[row_at], row_messages[row_at][2 * planes :], 0.0)
        wide_weights[jnp.where(up, rows + 1, 0), :, :width] = value
    for row in range(rows):
        wide[row + 2, :, :width] = by_row[row]
        wide_weights[row + 1, :, :width] = weights_by_row[row]
    for row in range(rows + 4):
        moved = pltpu.roll(sides, (-PITCH * row) % LANES, 1) if row else sides
        moved = jnp.where(keep, moved, 0.0)
        wide[row, :, width:] = moved[:planes]
        if 1 <= row < rows + 3:
            wide_weights[row - 1, :, width:] = moved[planes:]
    for row in range(rows + 2):
        middle[row] = apply_operator([wide[row], wide[row + 1], wide[row + 2]], wide_weights[row])
    gram = [jnp.zeros((planes, planes), jnp.float32)] * 2
    for row in range(rows):
        image = apply_operator([middle[row], middle[row + 1], middle[row + 2]], wide_weights[row + 1])[:, :width]
        second[row] = image
        for at, value in enumerate((middle[row + 1][:, :width], image)):
            gram[at] = gram[at] + lax.dot_general(
                value, value, (((1,), (1,)), ((), ())), precision=HIGHEST, preferred_element_type=jnp.float32
            )
    grams[:, :planes] = gram[0]
    grams[:, planes:] = gram[1]


def finish_kernel(pixel_count, second, *rest):
    parts, (basis, factor) = [part[...] for part in rest[:-2]], rest[-2:]
    grams = tree_sum(parts)
    planes = factor.shape[0]
    rows = second.shape[0]
    scaled = grams / pixel_count
    at_row = lax.broadcasted_iota(jnp.int32, (planes, planes), 0)
    at_col = lax.broadcasted_iota(jnp.int32, (planes, planes), 1)
    unit = jnp.where(at_row == at_col, 1.0, 0.0)
    state = jnp.concatenate([scaled[:, :planes], unit, scaled[:, planes:], unit], axis=1)
    half = 2 * planes
    row_of = lax.broadcasted_iota(jnp.int32, state.shape, 0)
    low_half = lax.broadcasted_iota(jnp.int32, state.shape, 1) < half
    for step in range(planes):
        column = jnp.where(low_half, state[:, step : step + 1], state[:, half + step : half + step + 1])
        pivot = column[step : step + 1]
        pivot_row = state[step : step + 1]
        inverse_root = lax.rsqrt(pivot)
        unit_row = pivot_row * inverse_root
        state = jnp.where(
            row_of > step,
            state - (column * inverse_root) * unit_row,
            jnp.where(row_of == step, unit_row, state),
        )
    first_inverse = state[:, planes:half]
    product_upper = jnp.where(at_col >= at_row, state[:, half : half + planes], 0.0)
    product_inverse = state[:, half + planes :]
    upper = lax.dot_general(
        product_upper,
        first_inverse,
        (((1,), (1,)), ((), ())),
        precision=HIGHEST,
        preferred_element_type=jnp.float32,
    )
    factor[...] = jnp.where(at_col >= at_row, upper, 0.0)
    for row in range(rows):
        basis[:, row, :] = jnp.dot(
            product_inverse, second[row], precision=HIGHEST, preferred_element_type=jnp.float32
        )


def tree_sum(parts):
    while len(parts) > 1:
        parts = [parts[at] + parts[at + 1] for at in range(0, len(parts), 2)]
    return parts[0]


def swap(value, row_pairing, col_pairing):
    def partner(place, count, pairing):
        if pairing is None:
            return place
        other = place + 1 if place % 2 == pairing else place - 1
        return other if 0 <= other < count else place

    rows, cols = lax.axis_size("row"), lax.axis_size("col")
    pairs = [
        (row * cols + col, partner(row, rows, row_pairing) * cols + partner(col, cols, col_pairing))
        for row in range(rows)
        for col in range(cols)
    ]
    return lax.ppermute(value, ("row", "col"), pairs)


def exchanged(value, most=16):
    count = lax.axis_size("row") * lax.axis_size("col")
    stride = 1
    while True:
        radix = min(most, count // stride)
        parts = [value]
        for turn in range(1, radix):
            pairs = [(i, i ^ (turn * stride)) for i in range(count)]
            parts.append(lax.ppermute(value, ("row", "col"), pairs))
        stride *= radix
        if stride == count:
            return parts
        value = tree_sum(parts)


def on_device(sketch, weights):
    planes, rows, width = sketch.shape
    pixel_count = rows * width * lax.axis_size("row") * lax.axis_size("col")
    by_row, weights_by_row, *messages = call(
        pack_kernel,
        [f32(rows, planes, width), f32(rows, 8, width)]
        + [f32(2 * planes + 8, width)] * 2
        + [f32(planes + 8, LANES)] * 6,
        sketch,
        weights,
        memory=pl.ANY,
        scratch=[
            pltpu.VMEM(sketch.shape, jnp.float32),
            pltpu.VMEM(weights.shape, jnp.float32),
            pltpu.SemaphoreType.DMA((2,)),
        ],
    )
    pairings = [(0, None), (1, None), (None, 0), (None, 1), (0, 0), (0, 1), (1, 0), (1, 1)]
    received = [swap(message, *pairing) for message, pairing in zip(messages, pairings)]
    second, grams = call(
        stencil_kernel,
        [f32(rows, planes, width), f32(planes, 2 * planes)],
        by_row,
        weights_by_row,
        *received,
        scratch=[
            pltpu.VMEM((rows + 4, planes, width + LANES), jnp.float32),
            pltpu.VMEM((rows + 2, 8, width + LANES), jnp.float32),
            pltpu.VMEM((rows + 2, planes, width + LANES), jnp.float32),
        ],
    )
    basis, factor = call(
        functools.partial(finish_kernel, float(pixel_count)),
        [f32(planes, rows, width), f32(planes, planes)],
        second,
        *exchanged(grams),
    )
    return basis, factor


def solution(mesh):
    return jax.shard_map(
        on_device,
        mesh=mesh,
        in_specs=(P(None, ("sec", "row"), "col"), P(None, ("sec", "row"), "col")),
        out_specs=(P(None, ("sec", "row"), "col"), P("sec", None)),
        check_vma=False,
    )
```

```python
import functools

import jax
import jax.numpy as jnp
from jax import lax
from jax.experimental import pallas as pl
from jax.experimental.pallas import tpu as pltpu
from jax.sharding import PartitionSpec as P

NEIGHBOURS = ((-1, -1), (-1, 0), (-1, 1), (0, -1), (0, 1), (1, -1), (1, 0), (1, 1))
LANES = 128
PITCH = 4
HIGHEST = lax.Precision.HIGHEST


def call(kernel, out_shapes, *operands, memory=pltpu.VMEM, scratch=()):
    return pl.pallas_call(
        kernel,
        out_shape=out_shapes,
        in_specs=[pl.BlockSpec(memory_space=memory)] * len(operands),
        out_specs=[pl.BlockSpec(memory_space=pltpu.VMEM)] * len(out_shapes),
        scratch_shapes=scratch,
        compiler_params=pltpu.CompilerParams(vmem_limit_bytes=40 * 1024 * 1024),
    )(*operands)


def f32(*shape):
    return jax.ShapeDtypeStruct(shape, jnp.float32)


def sides_of(axis):
    place = lax.axis_index(axis)
    return place % 2 == 0, place > 0, place < lax.axis_size(axis) - 1


def pack_rows_kernel(sketch, weights, by_row, weights_by_row, *rest):
    row_messages = rest[:2]
    tile, weight_tile, arrived = rest[2:]
    copies = [
        pltpu.make_async_copy(sketch, tile, arrived.at[0]),
        pltpu.make_async_copy(weights, weight_tile, arrived.at[1]),
    ]
    for copy in copies:
        copy.start()
    planes, rows, _ = tile.shape
    even_row, _, _ = sides_of("row")
    copies[1].wait()
    for row in range(rows):
        weights_by_row[row] = weight_tile[:, row, :]
    copies[0].wait()
    for row in range(rows):
        by_row[row] = tile[:, row, :]
    for message, up in zip(row_messages, (even_row, jnp.logical_not(even_row))):
        start = jnp.where(up, rows - 2, 0)
        for slot in range(2):
            message[slot * planes : (slot + 1) * planes] = by_row[start + slot]
        message[2 * planes :] = weights_by_row[jnp.where(up, rows - 1, 0)]


def pack_cols_kernel(by_row, weights_by_row, first_message, second_message, *col_messages):
    rows, planes, width = by_row.shape
    even_row, has_below, has_above = sides_of("row")
    even_col, _, _ = sides_of("col")
    lane = lax.broadcasted_iota(jnp.int32, (1, LANES), 1)
    packed = []
    for side, start in enumerate((0, width - LANES)):
        window = pl.ds(start, LANES)
        one, other = first_message[:, window], second_message[:, window]
        below = jnp.where(has_below, jnp.where(even_row, other, one), 0.0)
        above = jnp.where(has_above, jnp.where(even_row, one, other), 0.0)
        total = None
        for row in range(rows + 4):
            place = PITCH * row
            base = place - 2 * side
            keep = (lane == base % LANES) | (lane == (base + 1) % LANES)
            if 2 <= row < rows + 2:
                value, weight = by_row[row - 2, :, window], weights_by_row[row - 2, :, window]
            else:
                halo, at = (below, row) if row < 2 else (above, row - rows - 2)
                value, weight = halo[at * planes : (at + 1) * planes], halo[2 * planes :]
            value = jnp.concatenate([value, weight], axis=0)
            value = jnp.where(keep, pltpu.roll(value, place, 1) if place else value, 0.0)
            total = value if total is None else total + value
        packed.append(total)
    left, right = packed
    for message, up in zip(col_messages, (even_col, jnp.logical_not(even_col))):
        message[...] = jnp.where(up, right, left)


def apply_operator(rows3, weight_rows):
    width = rows3[1].shape[1]
    degree = jnp.sum(weight_rows, axis=0, keepdims=True)
    total = degree * rows3[1]
    sides = {-1: None, 1: None}
    for position, (up, across) in enumerate(NEIGHBOURS):
        weight = weight_rows[position : position + 1]
        value = rows3[up + 1]
        if across == 0:
            total = total + weight * value
        else:
            shifted = pltpu.roll(weight_rows, across % width, 1)[position : position + 1]
            term = shifted * value
            sides[across] = term if sides[across] is None else sides[across] + term
    for across, value in sides.items():
        total = total + pltpu.roll(value, (-across) % width, 1)
    return total


def stencil_kernel(by_row, weights_by_row, *rest):
    row_messages, col_messages = rest[:2], rest[2:4]
    second, grams, wide, wide_weights, middle = rest[4:]
    rows, planes, width = by_row.shape
    even_row, has_below, has_above = sides_of("row")
    even_col, has_left, has_right = sides_of("col")
    lane = lax.broadcasted_iota(jnp.int32, (1, LANES), 1)
    keep = (lane < 2) | (lane >= LANES - 2)
    partner_row = [jnp.where(even_row, has_above, has_below), jnp.where(even_row, has_below, has_above)]
    partner_col = [jnp.where(even_col, has_right, has_left), jnp.where(even_col, has_left, has_right)]
    sides = jnp.zeros(col_messages[0].shape, jnp.float32)
    for col_at in range(2):
        sides = sides + jnp.where(partner_col[col_at], col_messages[col_at][...], 0.0)
    for row_at, up in enumerate((even_row, jnp.logical_not(even_row))):
        start = jnp.where(up, rows + 2, 0)
        for slot in range(2):
            value = row_messages[row_at][slot * planes : (slot + 1) * planes]
            wide[start + slot, :, :width] = jnp.where(partner_row[row_at], value, 0.0)
        value = jnp.where(partner_row[row_at], row_messages[row_at][2 * planes :], 0.0)
        wide_weights[jnp.where(up, rows + 1, 0), :, :width] = value
    for row in range(rows):
        wide[row + 2, :, :width] = by_row[row]
        wide_weights[row + 1, :, :width] = weights_by_row[row]
    for row in range(rows + 4):
        moved = pltpu.roll(sides, (-PITCH * row) % LANES, 1) if row else sides
        moved = jnp.where(keep, moved, 0.0)
        wide[row, :, width:] = moved[:planes]
        if 1 <= row < rows + 3:
            wide_weights[row - 1, :, width:] = moved[planes:]
    for row in range(rows + 2):
        middle[row] = apply_operator([wide[row], wide[row + 1], wide[row + 2]], wide_weights[row])
    gram = [jnp.zeros((planes, planes), jnp.float32)] * 2
    for row in range(rows):
        image = apply_operator([middle[row], middle[row + 1], middle[row + 2]], wide_weights[row + 1])[:, :width]
        second[row] = image
        for at, value in enumerate((middle[row + 1][:, :width], image)):
            gram[at] = gram[at] + lax.dot_general(
                value, value, (((1,), (1,)), ((), ())), precision=HIGHEST, preferred_element_type=jnp.float32
            )
    half = planes // 2
    block = jnp.concatenate([gram[0][:half], gram[1][:half], gram[0][half:], gram[1][half:]], axis=1)
    for target in range(grams.shape[0]):
        grams[target] = block


def finish_kernel(pixel_count, second, parts, basis, factor):
    planes = factor.shape[0]
    rows = second.shape[0]
    block = tree_sum([parts[at] for at in range(parts.shape[0])]) / pixel_count
    scaled = jnp.concatenate([block[:, : 2 * planes], block[:, 2 * planes :]], axis=0)
    at_row = lax.broadcasted_iota(jnp.int32, (planes, planes), 0)
    at_col = lax.broadcasted_iota(jnp.int32, (planes, planes), 1)
    unit = jnp.where(at_row == at_col, 1.0, 0.0)
    state = jnp.concatenate([scaled[:, :planes], unit, scaled[:, planes:], unit], axis=1)
    half = 2 * planes
    row_of = lax.broadcasted_iota(jnp.int32, state.shape, 0)
    low_half = lax.broadcasted_iota(jnp.int32, state.shape, 1) < half
    for step in range(planes):
        column = jnp.where(low_half, state[:, step : step + 1], state[:, half + step : half + step + 1])
        pivot = column[step : step + 1]
        pivot_row = state[step : step + 1]
        inverse_root = lax.rsqrt(pivot)
        unit_row = pivot_row * inverse_root
        state = jnp.where(
            row_of > step,
            state - (column * inverse_root) * unit_row,
            jnp.where(row_of == step, unit_row, state),
        )
    first_inverse = state[:, planes:half]
    product_upper = jnp.where(at_col >= at_row, state[:, half : half + planes], 0.0)
    product_inverse = state[:, half + planes :]
    upper = lax.dot_general(
        product_upper,
        first_inverse,
        (((1,), (1,)), ((), ())),
        precision=HIGHEST,
        preferred_element_type=jnp.float32,
    )
    factor[...] = jnp.where(at_col >= at_row, upper, 0.0)
    for row in range(rows):
        basis[:, row, :] = jnp.dot(
            product_inverse, second[row], precision=HIGHEST, preferred_element_type=jnp.float32
        )


def tree_sum(parts):
    while len(parts) > 1:
        parts = [sum(parts[at + 1 : at + 2], parts[at]) for at in range(0, len(parts), 2)]
    return parts[0]


def swap(value, axis, pairing):
    count = lax.axis_size(axis)
    pairs = []
    for place in range(count):
        other = place + 1 if place % 2 == pairing else place - 1
        pairs.append((place, other if 0 <= other < count else place))
    return lax.ppermute(value, axis, pairs)


def on_device(sketch, weights):
    planes, rows, width = sketch.shape
    group = lax.axis_size("row") * lax.axis_size("col")
    by_row, weights_by_row, *messages = call(
        pack_rows_kernel,
        [f32(rows, planes, width), f32(rows, 8, width)] + [f32(2 * planes + 8, width)] * 2,
        sketch,
        weights,
        memory=pltpu.HBM,
        scratch=[
            pltpu.VMEM(sketch.shape, jnp.float32),
            pltpu.VMEM(weights.shape, jnp.float32),
            pltpu.SemaphoreType.DMA((2,)),
        ],
    )
    from_rows = [swap(message, "row", pairing) for pairing, message in enumerate(messages)]
    messages = call(pack_cols_kernel, [f32(planes + 8, LANES)] * 2, by_row, weights_by_row, *from_rows)
    from_cols = [swap(message, "col", pairing) for pairing, message in enumerate(messages)]
    second, grams = call(
        stencil_kernel,
        [f32(rows, planes, width), f32(group, planes // 2, 4 * planes)],
        by_row,
        weights_by_row,
        *from_rows,
        *from_cols,
        scratch=[
            pltpu.VMEM((rows + 4, planes, width + LANES), jnp.float32),
            pltpu.VMEM((rows + 2, 8, width + LANES), jnp.float32),
            pltpu.VMEM((rows + 2, planes, width + LANES), jnp.float32),
        ],
    )
    parts = lax.all_to_all(grams, ("row", "col"), 0, 0, tiled=True)
    return call(
        functools.partial(finish_kernel, float(rows * width * group)),
        [f32(planes, rows, width), f32(planes, planes)],
        second,
        parts,
    )


def solution(mesh):
    return jax.shard_map(
        on_device,
        mesh=mesh,
        in_specs=(P(None, ("sec", "row"), "col"), P(None, ("sec", "row"), "col")),
        out_specs=(P(None, ("sec", "row"), "col"), P("sec", None)),
        check_vma=False,
    )
```

```python
import functools

import jax
import jax.numpy as jnp
from jax import lax
from jax.experimental import pallas as pl
from jax.experimental.pallas import tpu as pltpu
from jax.sharding import PartitionSpec as P

NEIGHBOURS = ((-1, -1), (-1, 0), (-1, 1), (0, -1), (0, 1), (1, -1), (1, 0), (1, 1))
LANES = 128
PITCH = 4
HIGHEST = lax.Precision.HIGHEST


def call(kernel, out_shapes, *operands, scratch=()):
    return pl.pallas_call(
        kernel,
        out_shape=out_shapes,
        in_specs=[pl.BlockSpec(memory_space=pltpu.VMEM)] * len(operands),
        out_specs=[pl.BlockSpec(memory_space=pltpu.VMEM)] * len(out_shapes),
        scratch_shapes=scratch,
        compiler_params=pltpu.CompilerParams(vmem_limit_bytes=40 * 1024 * 1024),
    )(*operands)


def f32(*shape):
    return jax.ShapeDtypeStruct(shape, jnp.float32)


def sides_of(axis):
    place = lax.axis_index(axis)
    return place % 2 == 0, place > 0, place < lax.axis_size(axis) - 1


def pack_rows_kernel(joined, by_row, weights_by_row, *row_messages):
    rows, planes, _ = by_row.shape
    even_row, _, _ = sides_of("row")
    for row in range(rows):
        weights_by_row[row] = joined[planes:, row, :]
        by_row[row] = joined[:planes, row, :]
    for message, up in zip(row_messages, (even_row, jnp.logical_not(even_row))):
        start = jnp.where(up, rows - 2, 0)
        for slot in range(2):
            message[slot * planes : (slot + 1) * planes] = by_row[start + slot]
        message[2 * planes :] = weights_by_row[jnp.where(up, rows - 1, 0)]


def pack_cols_kernel(by_row, weights_by_row, first_message, second_message, *col_messages):
    rows, planes, width = by_row.shape
    even_row, has_below, has_above = sides_of("row")
    even_col, _, _ = sides_of("col")
    lane = lax.broadcasted_iota(jnp.int32, (1, LANES), 1)
    packed = []
    for side, start in enumerate((0, width - LANES)):
        window = pl.ds(start, LANES)
        one, other = first_message[:, window], second_message[:, window]
        below = jnp.where(has_below, jnp.where(even_row, other, one), 0.0)
        above = jnp.where(has_above, jnp.where(even_row, one, other), 0.0)
        total = None
        for row in range(rows + 4):
            place = PITCH * row
            base = place - 2 * side
            keep = (lane == base % LANES) | (lane == (base + 1) % LANES)
            if 2 <= row < rows + 2:
                value, weight = by_row[row - 2, :, window], weights_by_row[row - 2, :, window]
            else:
                halo, at = (below, row) if row < 2 else (above, row - rows - 2)
                value, weight = halo[at * planes : (at + 1) * planes], halo[2 * planes :]
            value = jnp.concatenate([value, weight], axis=0)
            value = jnp.where(keep, pltpu.roll(value, place, 1) if place else value, 0.0)
            total = value if total is None else total + value
        packed.append(total)
    left, right = packed
    for message, up in zip(col_messages, (even_col, jnp.logical_not(even_col))):
        message[...] = jnp.where(up, right, left)


def apply_operator(rows3, weight_rows):
    width = rows3[1].shape[1]
    degree = jnp.sum(weight_rows, axis=0, keepdims=True)
    total = degree * rows3[1]
    sides = {-1: None, 1: None}
    for position, (up, across) in enumerate(NEIGHBOURS):
        weight = weight_rows[position : position + 1]
        value = rows3[up + 1]
        if across == 0:
            total = total + weight * value
        else:
            shifted = pltpu.roll(weight_rows, across % width, 1)[position : position + 1]
            term = shifted * value
            sides[across] = term if sides[across] is None else sides[across] + term
    for across, value in sides.items():
        total = total + pltpu.roll(value, (-across) % width, 1)
    return total


def stencil_kernel(by_row, weights_by_row, *rest):
    row_messages, col_messages = rest[:2], rest[2:4]
    second, grams, wide, wide_weights, middle = rest[4:]
    rows, planes, width = by_row.shape
    even_row, has_below, has_above = sides_of("row")
    even_col, has_left, has_right = sides_of("col")
    lane = lax.broadcasted_iota(jnp.int32, (1, LANES), 1)
    keep = (lane < 2) | (lane >= LANES - 2)
    partner_row = [jnp.where(even_row, has_above, has_below), jnp.where(even_row, has_below, has_above)]
    partner_col = [jnp.where(even_col, has_right, has_left), jnp.where(even_col, has_left, has_right)]
    sides = jnp.zeros(col_messages[0].shape, jnp.float32)
    for col_at in range(2):
        sides = sides + jnp.where(partner_col[col_at], col_messages[col_at][...], 0.0)
    for row_at, up in enumerate((even_row, jnp.logical_not(even_row))):
        start = jnp.where(up, rows + 2, 0)
        for slot in range(2):
            value = row_messages[row_at][slot * planes : (slot + 1) * planes]
            wide[start + slot, :, :width] = jnp.where(partner_row[row_at], value, 0.0)
        value = jnp.where(partner_row[row_at], row_messages[row_at][2 * planes :], 0.0)
        wide_weights[jnp.where(up, rows + 1, 0), :, :width] = value
    for row in range(rows):
        wide[row + 2, :, :width] = by_row[row]
        wide_weights[row + 1, :, :width] = weights_by_row[row]
    for row in range(rows + 4):
        moved = pltpu.roll(sides, (-PITCH * row) % LANES, 1) if row else sides
        moved = jnp.where(keep, moved, 0.0)
        wide[row, :, width:] = moved[:planes]
        if 1 <= row < rows + 3:
            wide_weights[row - 1, :, width:] = moved[planes:]
    for row in range(rows + 2):
        middle[row] = apply_operator([wide[row], wide[row + 1], wide[row + 2]], wide_weights[row])
    gram = [jnp.zeros((planes, planes), jnp.float32)] * 2
    for row in range(rows):
        image = apply_operator([middle[row], middle[row + 1], middle[row + 2]], wide_weights[row + 1])[:, :width]
        second[row] = image
        for at, value in enumerate((middle[row + 1][:, :width], image)):
            gram[at] = gram[at] + lax.dot_general(
                value, value, (((1,), (1,)), ((), ())), precision=HIGHEST, preferred_element_type=jnp.float32
            )
    half = planes // 2
    grams[...] = jnp.concatenate([gram[0][:half], gram[1][:half], gram[0][half:], gram[1][half:]], axis=1)


def finish_kernel(pixel_count, second, parts, basis, factor):
    planes = factor.shape[0]
    rows = second.shape[0]
    block = tree_sum([parts[at] for at in range(parts.shape[0])]) / pixel_count
    scaled = jnp.concatenate([block[:, : 2 * planes], block[:, 2 * planes :]], axis=0)
    at_row = lax.broadcasted_iota(jnp.int32, (planes, planes), 0)
    at_col = lax.broadcasted_iota(jnp.int32, (planes, planes), 1)
    unit = jnp.where(at_row == at_col, 1.0, 0.0)
    state = jnp.concatenate([scaled[:, :planes], unit, scaled[:, planes:], unit], axis=1)
    half = 2 * planes
    row_of = lax.broadcasted_iota(jnp.int32, state.shape, 0)
    low_half = lax.broadcasted_iota(jnp.int32, state.shape, 1) < half
    for step in range(planes):
        column = jnp.where(low_half, state[:, step : step + 1], state[:, half + step : half + step + 1])
        pivot = column[step : step + 1]
        pivot_row = state[step : step + 1]
        inverse_root = lax.rsqrt(pivot)
        unit_row = pivot_row * inverse_root
        state = jnp.where(
            row_of > step,
            state - (column * inverse_root) * unit_row,
            jnp.where(row_of == step, unit_row, state),
        )
    first_inverse = state[:, planes:half]
    product_upper = jnp.where(at_col >= at_row, state[:, half : half + planes], 0.0)
    product_inverse = state[:, half + planes :]
    upper = lax.dot_general(
        product_upper,
        first_inverse,
        (((1,), (1,)), ((), ())),
        precision=HIGHEST,
        preferred_element_type=jnp.float32,
    )
    factor[...] = jnp.where(at_col >= at_row, upper, 0.0)
    for row in range(rows):
        basis[:, row, :] = jnp.dot(
            product_inverse, second[row], precision=HIGHEST, preferred_element_type=jnp.float32
        )


def tree_sum(parts):
    while len(parts) > 1:
        parts = [sum(parts[at + 1 : at + 2], parts[at]) for at in range(0, len(parts), 2)]
    return parts[0]


def swap(value, axis, pairing):
    count = lax.axis_size(axis)
    pairs = []
    for place in range(count):
        other = place + 1 if place % 2 == pairing else place - 1
        pairs.append((place, other if 0 <= other < count else place))
    return lax.ppermute(value, axis, pairs)


def on_device(sketch, weights):
    planes, rows, width = sketch.shape
    group = lax.axis_size("row") * lax.axis_size("col")
    by_row, weights_by_row, *messages = call(
        pack_rows_kernel,
        [f32(rows, planes, width), f32(rows, 8, width)] + [f32(2 * planes + 8, width)] * 2,
        jnp.concatenate([sketch, weights], axis=0),
    )
    from_rows = [swap(messages[pairing], "row", pairing) for pairing in (1, 0)][::-1]
    messages = call(pack_cols_kernel, [f32(planes + 8, LANES)] * 2, by_row, weights_by_row, *from_rows)
    from_cols = [swap(message, "col", pairing) for pairing, message in enumerate(messages)]
    second, grams = call(
        stencil_kernel,
        [f32(rows, planes, width), f32(planes // 2, 4 * planes)],
        by_row,
        weights_by_row,
        *from_rows,
        *from_cols,
        scratch=[
            pltpu.VMEM((rows + 4, planes, width + LANES), jnp.float32),
            pltpu.VMEM((rows + 2, 8, width + LANES), jnp.float32),
            pltpu.VMEM((rows + 2, planes, width + LANES), jnp.float32),
        ],
    )
    parts = lax.all_gather(grams, ("row", "col"))
    return call(
        functools.partial(finish_kernel, float(rows * width * group)),
        [f32(planes, rows, width), f32(planes, planes)],
        second,
        parts,
    )


def solution(mesh):
    return jax.shard_map(
        on_device,
        mesh=mesh,
        in_specs=(P(None, ("sec", "row"), "col"), P(None, ("sec", "row"), "col")),
        out_specs=(P(None, ("sec", "row"), "col"), P("sec", None)),
        check_vma=False,
    )
```

```python
import functools

import jax
import jax.numpy as jnp
from jax import lax
from jax.experimental import pallas as pl
from jax.experimental.pallas import tpu as pltpu
from jax.sharding import PartitionSpec as P

NEIGHBOURS = ((-1, -1), (-1, 0), (-1, 1), (0, -1), (0, 1), (1, -1), (1, 0), (1, 1))
LANES = 128
PITCH = 4
HIGHEST = lax.Precision.HIGHEST


def call(kernel, out_shapes, *operands, scratch=()):
    return pl.pallas_call(
        kernel,
        out_shape=out_shapes,
        in_specs=[pl.BlockSpec(memory_space=pltpu.VMEM)] * len(operands),
        out_specs=[pl.BlockSpec(memory_space=pltpu.VMEM)] * len(out_shapes),
        scratch_shapes=scratch,
        compiler_params=pltpu.CompilerParams(vmem_limit_bytes=40 * 1024 * 1024),
    )(*operands)


def f32(*shape):
    return jax.ShapeDtypeStruct(shape, jnp.float32)


def sides_of(axis):
    place = lax.axis_index(axis)
    return place % 2 == 0, place > 0, place < lax.axis_size(axis) - 1


def pack_rows_kernel(joined, by_row, weights_by_row, *row_messages):
    rows, planes, _ = by_row.shape
    even_row, _, _ = sides_of("row")
    for row in range(rows):
        weights_by_row[row] = joined[planes:, row, :]
        by_row[row] = joined[:planes, row, :]
    for message, up in zip(row_messages, (even_row, jnp.logical_not(even_row))):
        start = jnp.where(up, rows - 2, 0)
        for slot in range(2):
            message[slot * planes : (slot + 1) * planes] = by_row[start + slot]
        message[2 * planes :] = weights_by_row[jnp.where(up, rows - 1, 0)]


def pack_cols_kernel(by_row, weights_by_row, first_message, second_message, *col_messages):
    rows, planes, width = by_row.shape
    even_row, has_below, has_above = sides_of("row")
    even_col, _, _ = sides_of("col")
    lane = lax.broadcasted_iota(jnp.int32, (1, LANES), 1)
    packed = []
    for side, start in enumerate((0, width - LANES)):
        window = pl.ds(start, LANES)
        one, other = first_message[:, window], second_message[:, window]
        below = jnp.where(has_below, jnp.where(even_row, other, one), 0.0)
        above = jnp.where(has_above, jnp.where(even_row, one, other), 0.0)
        total = None
        for row in range(rows + 4):
            place = PITCH * row
            base = place - 2 * side
            keep = (lane == base % LANES) | (lane == (base + 1) % LANES)
            if 2 <= row < rows + 2:
                value, weight = by_row[row - 2, :, window], weights_by_row[row - 2, :, window]
            else:
                halo, at = (below, row) if row < 2 else (above, row - rows - 2)
                value, weight = halo[at * planes : (at + 1) * planes], halo[2 * planes :]
            value = jnp.concatenate([value, weight], axis=0)
            value = jnp.where(keep, pltpu.roll(value, place, 1) if place else value, 0.0)
            total = value if total is None else total + value
        packed.append(total)
    left, right = packed
    for message, up in zip(col_messages, (even_col, jnp.logical_not(even_col))):
        message[...] = jnp.where(up, right, left)


def apply_operator(rows3, weight_rows):
    width = rows3[1].shape[1]
    degree = jnp.sum(weight_rows, axis=0, keepdims=True)
    total = degree * rows3[1]
    sides = {-1: None, 1: None}
    for position, (up, across) in enumerate(NEIGHBOURS):
        weight = weight_rows[position : position + 1]
        value = rows3[up + 1]
        if across == 0:
            total = total + weight * value
        else:
            shifted = pltpu.roll(weight_rows, across % width, 1)[position : position + 1]
            term = shifted * value
            sides[across] = term if sides[across] is None else sides[across] + term
    for across, value in sides.items():
        total = total + pltpu.roll(value, (-across) % width, 1)
    return total


def stencil_kernel(by_row, weights_by_row, *rest):
    row_messages, col_messages = rest[:2], rest[2:4]
    second, grams, wide, wide_weights, middle = rest[4:]
    rows, planes, width = by_row.shape
    even_row, has_below, has_above = sides_of("row")
    even_col, has_left, has_right = sides_of("col")
    lane = lax.broadcasted_iota(jnp.int32, (1, LANES), 1)
    keep = (lane < 2) | (lane >= LANES - 2)
    partner_row = [jnp.where(even_row, has_above, has_below), jnp.where(even_row, has_below, has_above)]
    partner_col = [jnp.where(even_col, has_right, has_left), jnp.where(even_col, has_left, has_right)]
    sides = jnp.zeros(col_messages[0].shape, jnp.float32)
    for col_at in range(2):
        sides = sides + jnp.where(partner_col[col_at], col_messages[col_at][...], 0.0)
    for row_at, up in enumerate((even_row, jnp.logical_not(even_row))):
        start = jnp.where(up, rows + 2, 0)
        for slot in range(2):
            value = row_messages[row_at][slot * planes : (slot + 1) * planes]
            wide[start + slot, :, :width] = jnp.where(partner_row[row_at], value, 0.0)
        value = jnp.where(partner_row[row_at], row_messages[row_at][2 * planes :], 0.0)
        wide_weights[jnp.where(up, rows + 1, 0), :, :width] = value
    for row in range(rows):
        wide[row + 2, :, :width] = by_row[row]
        wide_weights[row + 1, :, :width] = weights_by_row[row]
    for row in range(rows + 4):
        moved = pltpu.roll(sides, (-PITCH * row) % LANES, 1) if row else sides
        moved = jnp.where(keep, moved, 0.0)
        wide[row, :, width:] = moved[:planes]
        if 1 <= row < rows + 3:
            wide_weights[row - 1, :, width:] = moved[planes:]
    for row in range(rows + 2):
        middle[row] = apply_operator([wide[row], wide[row + 1], wide[row + 2]], wide_weights[row])
    gram = [jnp.zeros((planes, planes), jnp.float32)] * 2
    for row in range(rows):
        image = apply_operator([middle[row], middle[row + 1], middle[row + 2]], wide_weights[row + 1])[:, :width]
        second[row] = image
        for at, value in enumerate((middle[row + 1][:, :width], image)):
            gram[at] = gram[at] + lax.dot_general(
                value, value, (((1,), (1,)), ((), ())), precision=HIGHEST, preferred_element_type=jnp.float32
            )
    half = planes // 2
    block = jnp.concatenate([gram[0][:half], gram[1][:half], gram[0][half:], gram[1][half:]], axis=1)
    for target in range(grams.shape[0]):
        grams[target] = block


def finish_kernel(pixel_count, second, parts, basis, factor):
    planes = factor.shape[0]
    rows = second.shape[0]
    block = tree_sum([parts[at] for at in range(parts.shape[0])]) / pixel_count
    scaled = jnp.concatenate([block[:, : 2 * planes], block[:, 2 * planes :]], axis=0)
    at_row = lax.broadcasted_iota(jnp.int32, (planes, planes), 0)
    at_col = lax.broadcasted_iota(jnp.int32, (planes, planes), 1)
    unit = jnp.where(at_row == at_col, 1.0, 0.0)
    state = jnp.concatenate([scaled[:, :planes], unit, scaled[:, planes:], unit], axis=1)
    half = 2 * planes
    row_of = lax.broadcasted_iota(jnp.int32, state.shape, 0)
    low_half = lax.broadcasted_iota(jnp.int32, state.shape, 1) < half
    for step in range(planes):
        column = jnp.where(low_half, state[:, step : step + 1], state[:, half + step : half + step + 1])
        pivot = column[step : step + 1]
        pivot_row = state[step : step + 1]
        inverse_root = lax.rsqrt(pivot)
        unit_row = pivot_row * inverse_root
        state = jnp.where(
            row_of > step,
            state - (column * inverse_root) * unit_row,
            jnp.where(row_of == step, unit_row, state),
        )
    first_inverse = state[:, planes:half]
    product_upper = jnp.where(at_col >= at_row, state[:, half : half + planes], 0.0)
    product_inverse = state[:, half + planes :]
    upper = lax.dot_general(
        product_upper,
        first_inverse,
        (((1,), (1,)), ((), ())),
        precision=HIGHEST,
        preferred_element_type=jnp.float32,
    )
    factor[...] = jnp.where(at_col >= at_row, upper, 0.0)
    for row in range(rows):
        basis[:, row, :] = jnp.dot(
            product_inverse, second[row], precision=HIGHEST, preferred_element_type=jnp.float32
        )


def tree_sum(parts):
    while len(parts) > 1:
        parts = [sum(parts[at + 1 : at + 2], parts[at]) for at in range(0, len(parts), 2)]
    return parts[0]


def swap(value, axis, pairing):
    rows, cols = lax.axis_size("row"), lax.axis_size("col")
    pairs = []
    for row in range(rows):
        for col in range(cols):
            place, count = (row, rows) if axis == "row" else (col, cols)
            other = place + 1 if place % 2 == pairing else place - 1
            if not 0 <= other < count:
                partner = (row, col ^ 1) if axis == "row" else (row ^ 1, col)
            else:
                partner = (other, col) if axis == "row" else (row, other)
            pairs.append((row * cols + col, partner[0] * cols + partner[1]))
    return lax.ppermute(value, ("row", "col"), pairs)


def on_device(sketch, weights):
    planes, rows, width = sketch.shape
    group = lax.axis_size("row") * lax.axis_size("col")
    by_row, weights_by_row, *messages = call(
        pack_rows_kernel,
        [f32(rows, planes, width), f32(rows, 8, width)] + [f32(2 * planes + 8, width)] * 2,
        jnp.concatenate([sketch, weights], axis=0),
    )
    from_rows = [swap(messages[pairing], "row", pairing) for pairing in (1, 0)][::-1]
    messages = call(pack_cols_kernel, [f32(planes + 8, LANES)] * 2, by_row, weights_by_row, *from_rows)
    from_cols = [swap(message, "col", pairing) for pairing, message in enumerate(messages)]
    second, grams = call(
        stencil_kernel,
        [f32(rows, planes, width), f32(group, planes // 2, 4 * planes)],
        by_row,
        weights_by_row,
        *from_rows,
        *from_cols,
        scratch=[
            pltpu.VMEM((rows + 4, planes, width + LANES), jnp.float32),
            pltpu.VMEM((rows + 2, 8, width + LANES), jnp.float32),
            pltpu.VMEM((rows + 2, planes, width + LANES), jnp.float32),
        ],
    )
    parts = lax.all_to_all(grams, ("row", "col"), 0, 0, tiled=True)
    return call(
        functools.partial(finish_kernel, float(rows * width * group)),
        [f32(planes, rows, width), f32(planes, planes)],
        second,
        parts,
    )


def solution(mesh):
    return jax.shard_map(
        on_device,
        mesh=mesh,
        in_specs=(P(None, ("sec", "row"), "col"), P(None, ("sec", "row"), "col")),
        out_specs=(P(None, ("sec", "row"), "col"), P("sec", None)),
        check_vma=False,
    )
```

```python
import functools

import jax
import jax.numpy as jnp
from jax import lax
from jax.experimental import pallas as pl
from jax.experimental.pallas import tpu as pltpu
from jax.sharding import PartitionSpec as P

NEIGHBOURS = ((-1, -1), (-1, 0), (-1, 1), (0, -1), (0, 1), (1, -1), (1, 0), (1, 1))
LANES = 128
PITCH = 4
HIGHEST = lax.Precision.HIGHEST


def call(kernel, out_shapes, *operands, scratch=()):
    return pl.pallas_call(
        kernel,
        out_shape=out_shapes,
        in_specs=[pl.BlockSpec(memory_space=pltpu.VMEM)] * len(operands),
        out_specs=[pl.BlockSpec(memory_space=pltpu.VMEM)] * len(out_shapes),
        scratch_shapes=scratch,
        compiler_params=pltpu.CompilerParams(vmem_limit_bytes=40 * 1024 * 1024),
    )(*operands)


def f32(*shape):
    return jax.ShapeDtypeStruct(shape, jnp.float32)


def sides_of(axis):
    place = lax.axis_index(axis)
    return place % 2 == 0, place > 0, place < lax.axis_size(axis) - 1


def pack_rows_kernel(joined, by_row, weights_by_row, *row_messages):
    rows, planes, _ = by_row.shape
    even_row, _, _ = sides_of("row")
    for row in range(rows):
        weights_by_row[row] = joined[planes:, row, :]
        by_row[row] = joined[:planes, row, :]
    for message, up in zip(row_messages, (even_row, jnp.logical_not(even_row))):
        start = jnp.where(up, rows - 2, 0)
        for slot in range(2):
            message[slot * planes : (slot + 1) * planes] = by_row[start + slot]
        message[2 * planes :] = weights_by_row[jnp.where(up, rows - 1, 0)]


def pack_cols_kernel(by_row, weights_by_row, first_message, second_message, *col_messages):
    rows, planes, width = by_row.shape
    even_row, has_below, has_above = sides_of("row")
    even_col, _, _ = sides_of("col")
    lane = lax.broadcasted_iota(jnp.int32, (1, LANES), 1)
    packed = []
    for side, start in enumerate((0, width - LANES)):
        window = pl.ds(start, LANES)
        one, other = first_message[:, window], second_message[:, window]
        below = jnp.where(has_below, jnp.where(even_row, other, one), 0.0)
        above = jnp.where(has_above, jnp.where(even_row, one, other), 0.0)
        total = None
        for row in range(rows + 4):
            place = PITCH * row
            base = place - 2 * side
            keep = (lane == base % LANES) | (lane == (base + 1) % LANES)
            if 2 <= row < rows + 2:
                value, weight = by_row[row - 2, :, window], weights_by_row[row - 2, :, window]
            else:
                halo, at = (below, row) if row < 2 else (above, row - rows - 2)
                value, weight = halo[at * planes : (at + 1) * planes], halo[2 * planes :]
            value = jnp.concatenate([value, weight], axis=0)
            value = jnp.where(keep, pltpu.roll(value, place, 1) if place else value, 0.0)
            total = value if total is None else total + value
        packed.append(total)
    left, right = packed
    for message, up in zip(col_messages, (even_col, jnp.logical_not(even_col))):
        message[...] = jnp.where(up, right, left)


def apply_operator(rows3, weight_rows):
    width = rows3[1].shape[1]
    degree = jnp.sum(weight_rows, axis=0, keepdims=True)
    total = degree * rows3[1]
    sides = {-1: None, 1: None}
    for position, (up, across) in enumerate(NEIGHBOURS):
        weight = weight_rows[position : position + 1]
        value = rows3[up + 1]
        if across == 0:
            total = total + weight * value
        else:
            shifted = pltpu.roll(weight_rows, across % width, 1)[position : position + 1]
            term = shifted * value
            sides[across] = term if sides[across] is None else sides[across] + term
    for across, value in sides.items():
        total = total + pltpu.roll(value, (-across) % width, 1)
    return total


def stencil_kernel(by_row, weights_by_row, *rest):
    row_messages, col_messages = rest[:2], rest[2:4]
    second, grams, wide, wide_weights, middle = rest[4:]
    rows, planes, width = by_row.shape
    even_row, has_below, has_above = sides_of("row")
    even_col, has_left, has_right = sides_of("col")
    lane = lax.broadcasted_iota(jnp.int32, (1, LANES), 1)
    keep = (lane < 2) | (lane >= LANES - 2)
    partner_row = [jnp.where(even_row, has_above, has_below), jnp.where(even_row, has_below, has_above)]
    partner_col = [jnp.where(even_col, has_right, has_left), jnp.where(even_col, has_left, has_right)]
    sides = jnp.zeros(col_messages[0].shape, jnp.float32)
    for col_at in range(2):
        sides = sides + jnp.where(partner_col[col_at], col_messages[col_at][...], 0.0)
    for row_at, up in enumerate((even_row, jnp.logical_not(even_row))):
        start = jnp.where(up, rows + 2, 0)
        for slot in range(2):
            value = row_messages[row_at][slot * planes : (slot + 1) * planes]
            wide[start + slot, :, :width] = jnp.where(partner_row[row_at], value, 0.0)
        value = jnp.where(partner_row[row_at], row_messages[row_at][2 * planes :], 0.0)
        wide_weights[jnp.where(up, rows + 1, 0), :, :width] = value
    for row in range(rows):
        wide[row + 2, :, :width] = by_row[row]
        wide_weights[row + 1, :, :width] = weights_by_row[row]
    for row in range(rows + 4):
        moved = pltpu.roll(sides, (-PITCH * row) % LANES, 1) if row else sides
        moved = jnp.where(keep, moved, 0.0)
        wide[row, :, width:] = moved[:planes]
        if 1 <= row < rows + 3:
            wide_weights[row - 1, :, width:] = moved[planes:]
    for row in range(rows + 2):
        middle[row] = apply_operator([wide[row], wide[row + 1], wide[row + 2]], wide_weights[row])
    gram = [jnp.zeros((planes, planes), jnp.float32)] * 2
    for row in range(rows):
        image = apply_operator([middle[row], middle[row + 1], middle[row + 2]], wide_weights[row + 1])[:, :width]
        second[row] = image
        for at, value in enumerate((middle[row + 1][:, :width], image)):
            gram[at] = gram[at] + lax.dot_general(
                value, value, (((1,), (1,)), ((), ())), precision=HIGHEST, preferred_element_type=jnp.float32
            )
    half = planes // 2
    grams[...] = jnp.concatenate([gram[0][:half], gram[1][:half], gram[0][half:], gram[1][half:]], axis=1)


def finish_kernel(pixel_count, second, parts, basis, factor):
    planes = factor.shape[0]
    rows = second.shape[0]
    block = tree_sum([parts[at] for at in range(parts.shape[0])]) / pixel_count
    scaled = jnp.concatenate([block[:, : 2 * planes], block[:, 2 * planes :]], axis=0)
    at_row = lax.broadcasted_iota(jnp.int32, (planes, planes), 0)
    at_col = lax.broadcasted_iota(jnp.int32, (planes, planes), 1)
    unit = jnp.where(at_row == at_col, 1.0, 0.0)
    state = jnp.concatenate([scaled[:, :planes], unit, scaled[:, planes:], unit], axis=1)
    half = 2 * planes
    row_of = lax.broadcasted_iota(jnp.int32, state.shape, 0)
    low_half = lax.broadcasted_iota(jnp.int32, state.shape, 1) < half
    for step in range(planes):
        column = jnp.where(low_half, state[:, step : step + 1], state[:, half + step : half + step + 1])
        pivot = column[step : step + 1]
        pivot_row = state[step : step + 1]
        inverse_root = lax.rsqrt(pivot)
        unit_row = pivot_row * inverse_root
        state = jnp.where(
            row_of > step,
            state - (column * inverse_root) * unit_row,
            jnp.where(row_of == step, unit_row, state),
        )
    first_inverse = state[:, planes:half]
    product_upper = jnp.where(at_col >= at_row, state[:, half : half + planes], 0.0)
    product_inverse = state[:, half + planes :]
    upper = lax.dot_general(
        product_upper,
        first_inverse,
        (((1,), (1,)), ((), ())),
        precision=HIGHEST,
        preferred_element_type=jnp.float32,
    )
    factor[...] = jnp.where(at_col >= at_row, upper, 0.0)
    for row in range(rows):
        basis[:, row, :] = jnp.dot(
            product_inverse, second[row], precision=HIGHEST, preferred_element_type=jnp.float32
        )


def tree_sum(parts):
    while len(parts) > 1:
        parts = [sum(parts[at + 1 : at + 2], parts[at]) for at in range(0, len(parts), 2)]
    return parts[0]


def swap(value, axis, pairing):
    rows, cols = lax.axis_size("row"), lax.axis_size("col")
    pairs = []
    for row in range(rows):
        for col in range(cols):
            place, count = (row, rows) if axis == "row" else (col, cols)
            other = place + 1 if place % 2 == pairing else place - 1
            if not 0 <= other < count:
                partner = (row, col ^ 1) if axis == "row" else (row ^ 1, col)
            else:
                partner = (other, col) if axis == "row" else (row, other)
            pairs.append((row * cols + col, partner[0] * cols + partner[1]))
    return lax.ppermute(value, ("row", "col"), pairs)


def on_device(sketch, weights):
    planes, rows, width = sketch.shape
    group = lax.axis_size("row") * lax.axis_size("col")
    by_row, weights_by_row, *messages = call(
        pack_rows_kernel,
        [f32(rows, planes, width), f32(rows, 8, width)] + [f32(2 * planes + 8, width)] * 2,
        jnp.concatenate([sketch, weights], axis=0),
    )
    from_rows = [swap(messages[pairing], "row", pairing) for pairing in (1, 0)][::-1]
    messages = call(pack_cols_kernel, [f32(planes + 8, LANES)] * 2, by_row, weights_by_row, *from_rows)
    from_cols = [swap(message, "col", pairing) for pairing, message in enumerate(messages)]
    second, grams = call(
        stencil_kernel,
        [f32(rows, planes, width), f32(planes // 2, 4 * planes)],
        by_row,
        weights_by_row,
        *from_rows,
        *from_cols,
        scratch=[
            pltpu.VMEM((rows + 4, planes, width + LANES), jnp.float32),
            pltpu.VMEM((rows + 2, 8, width + LANES), jnp.float32),
            pltpu.VMEM((rows + 2, planes, width + LANES), jnp.float32),
        ],
    )
    grams = grams + swap(grams, "row", 0)
    rows_of, cols_of = lax.axis_size("row"), lax.axis_size("col")
    groups = [[row * cols_of + col for row in range(start, rows_of, 2) for col in range(cols_of)] for start in (0, 1)]
    copies = jnp.broadcast_to(grams, (group // 2, *grams.shape))
    parts = lax.all_to_all(copies, ("row", "col"), 0, 0, axis_index_groups=groups, tiled=True)
    return call(
        functools.partial(finish_kernel, float(rows * width * group)),
        [f32(planes, rows, width), f32(planes, planes)],
        second,
        parts,
    )


def solution(mesh):
    return jax.shard_map(
        on_device,
        mesh=mesh,
        in_specs=(P(None, ("sec", "row"), "col"), P(None, ("sec", "row"), "col")),
        out_specs=(P(None, ("sec", "row"), "col"), P("sec", None)),
        check_vma=False,
    )
```

```python
import functools

import jax
import jax.numpy as jnp
from jax import lax
from jax.experimental import pallas as pl
from jax.experimental.pallas import tpu as pltpu
from jax.sharding import PartitionSpec as P

NEIGHBOURS = ((-1, -1), (-1, 0), (-1, 1), (0, -1), (0, 1), (1, -1), (1, 0), (1, 1))
LANES = 128
PITCH = 8
HIGHEST = lax.Precision.HIGHEST


def call(kernel, out_shapes, *operands, scratch=()):
    return pl.pallas_call(
        kernel,
        out_shape=out_shapes,
        in_specs=[pl.BlockSpec(memory_space=pltpu.VMEM)] * len(operands),
        out_specs=[pl.BlockSpec(memory_space=pltpu.VMEM)] * len(out_shapes),
        scratch_shapes=scratch,
        compiler_params=pltpu.CompilerParams(vmem_limit_bytes=40 * 1024 * 1024),
    )(*operands)


def f32(*shape):
    return jax.ShapeDtypeStruct(shape, jnp.float32)


def sides_of(axis):
    place = lax.axis_index(axis)
    return place % 2 == 0, place > 0, place < lax.axis_size(axis) - 1


def pack_rows_kernel(joined, by_row, weights_by_row, *row_messages):
    rows, planes, _ = by_row.shape
    even_row, _, _ = sides_of("row")
    for row in range(rows):
        weights_by_row[row] = joined[planes:, row, :]
        by_row[row] = joined[:planes, row, :]
    for message, up in zip(row_messages, (even_row, jnp.logical_not(even_row))):
        start = jnp.where(up, rows - 2, 0)
        for slot in range(2):
            message[slot * planes : (slot + 1) * planes] = by_row[start + slot]
        message[2 * planes :] = weights_by_row[jnp.where(up, rows - 1, 0)]


def row_parts(by_row, weights_by_row, first_message, second_message, window):
    rows, planes, _ = by_row.shape
    even_row, has_below, has_above = sides_of("row")
    one, other = first_message[:, window], second_message[:, window]
    below = jnp.where(has_below, jnp.where(even_row, other, one), 0.0)
    above = jnp.where(has_above, jnp.where(even_row, one, other), 0.0)
    values = [below[:planes], below[planes : 2 * planes]]
    values += [by_row[row, :, window] for row in range(rows)]
    values += [above[:planes], above[planes : 2 * planes]]
    weights = [below[2 * planes :]]
    weights += [weights_by_row[row, :, window] for row in range(rows)]
    weights += [above[2 * planes :]]
    return values, weights


def strips_kernel(by_row, weights_by_row, first_message, second_message, left, right, *col_messages):
    planes, width = by_row.shape[1:]
    even_col, _, _ = sides_of("col")
    lane = lax.broadcasted_iota(jnp.int32, (1, LANES), 1)
    own = PITCH - 2
    for target, start, low, at in ((left, 0, 2, 0), (right, width - LANES, 0, LANES - own)):
        values, weights = row_parts(by_row, weights_by_row, first_message, second_message, pl.ds(start, LANES))
        for part, some, skip in ((slice(None, planes), values, 0), (slice(planes, None), weights, 1)):
            total = None
            for row, value in enumerate(some):
                place = PITCH * (row + skip) + low
                moved = pltpu.roll(value, (place - at) % LANES, 1)
                moved = jnp.where((lane >= place) & (lane < place + own), moved, 0.0)
                total = moved if total is None else total + moved
            target[part] = total
    spot = lane % PITCH
    to_left = jnp.where(spot >= PITCH - 2, pltpu.roll(left[...], PITCH - 4, 1), 0.0)
    to_right = jnp.where(spot < 2, pltpu.roll(right[...], LANES - (PITCH - 4), 1), 0.0)
    for message, up in zip(col_messages, (even_col, jnp.logical_not(even_col))):
        message[...] = jnp.where(up, to_right, to_left)


def apply_operator(rows3, weight_rows):
    width = rows3[1].shape[1]
    degree = jnp.sum(weight_rows, axis=0, keepdims=True)
    total = degree * rows3[1]
    sides = {-1: None, 1: None}
    for position, (up, across) in enumerate(NEIGHBOURS):
        weight = weight_rows[position : position + 1]
        value = rows3[up + 1]
        if across == 0:
            total = total + weight * value
        else:
            shifted = pltpu.roll(weight_rows, across % width, 1)[position : position + 1]
            term = shifted * value
            sides[across] = term if sides[across] is None else sides[across] + term
    for across, value in sides.items():
        total = total + pltpu.roll(value, (-across) % width, 1)
    return total


def gram_of(value, other):
    return lax.dot_general(
        value, other, (((1,), (1,)), ((), ())), precision=HIGHEST, preferred_element_type=jnp.float32
    )


def split(value):
    high = value.astype(jnp.bfloat16)
    rest = value - high.astype(jnp.float32)
    middle = rest.astype(jnp.bfloat16)
    low = (rest - middle.astype(jnp.float32)).astype(jnp.bfloat16)
    return high, middle, low


def early_kernel(by_row, weights_by_row, first_message, second_message, second, grams, middle):
    rows, planes, width = by_row.shape
    values, weights = row_parts(by_row, weights_by_row, first_message, second_message, slice(None))
    col = lax.broadcasted_iota(jnp.int32, (1, width), 1)
    inner = (col >= 2) & (col < width - 2)
    for row in range(rows + 2):
        middle[row] = apply_operator(values[row : row + 3], weights[row])
    gram = [jnp.zeros((planes, planes), jnp.float32)] * 2
    for row in range(rows):
        image = apply_operator([middle[row], middle[row + 1], middle[row + 2]], weights[row + 1])
        for at, part in enumerate(split(image)):
            second[row, at * planes : (at + 1) * planes] = part
        for at, value in enumerate((middle[row + 1], image)):
            gram[at] = gram[at] + gram_of(jnp.where(inner, value, 0.0), value)
    grams[:, :planes] = gram[0]
    grams[:, planes:] = gram[1]


def apply_on_strip(values, weights):
    total = jnp.sum(weights, axis=0, keepdims=True) * values
    for position, (up, across) in enumerate(NEIGHBOURS):
        moved = pltpu.roll(values, (-PITCH * up - across) % LANES, 1)
        total = total + weights[position : position + 1] * moved
    return total


def late_kernel(rows, left, right, first_message, second_message, early_grams, grams, edges):
    planes = early_grams.shape[0]
    even_col, has_left, has_right = sides_of("col")
    one, other = first_message[...], second_message[...]
    lane = lax.broadcasted_iota(jnp.int32, (1, LANES), 1)
    spot, row = lane % PITCH, lane // PITCH
    gram = [early_grams[:, :planes], early_grams[:, planes:]]
    for side, (strip, present, halo) in enumerate(
        ((left, has_left, jnp.where(even_col, other, one)), (right, has_right, jnp.where(even_col, one, other)))
    ):
        whole = strip[...] + jnp.where(present, halo, 0.0)
        values, weights = whole[:planes], whole[planes:]
        low = 2 if side == 0 else PITCH - 4
        outer = (spot >= low) & (spot < low + 2) & (row >= 2) & (row < rows + 2)
        for at in range(2):
            values = apply_on_strip(values, weights)
            gram[at] = gram[at] + gram_of(jnp.where(outer, values, 0.0), values)
        edges[:, side * LANES : (side + 1) * LANES] = values
    half = planes // 2
    block = jnp.concatenate([gram[0][:half], gram[1][:half], gram[0][half:], gram[1][half:]], axis=1)
    for target in range(grams.shape[0]):
        grams[target] = block


def eliminate(block, planes):
    lane = lax.broadcasted_iota(jnp.int32, (8, LANES), 1)
    sub = lax.broadcasted_iota(jnp.int32, (8, LANES), 0)
    first_half = lane < 2 * planes
    groups = planes // 8
    sources = [(block[8 * (g % (groups // 2)) :][:8], 2 * planes * (g // (groups // 2))) for g in range(groups)]
    state = []
    for g, (source, base) in enumerate(sources):
        unit = jnp.where(sub + 8 * g == lane % (2 * planes) - planes, 1.0, 0.0)
        first = pltpu.roll(source, LANES - base, 1) if base else source
        later = pltpu.roll(source, (planes - base) % LANES, 1)
        state.append(
            jnp.where(lane < planes, first, jnp.where((lane >= 2 * planes) & (lane < 3 * planes), later, unit))
        )
    columns = []
    for j in range(planes):
        columns.append(
            {
                g: jnp.where(
                    first_half,
                    jnp.broadcast_to(sources[g][0][:, sources[g][1] + j :][:, :1], (8, LANES)),
                    jnp.broadcast_to(sources[g][0][:, sources[g][1] + planes + j :][:, :1], (8, LANES)),
                )
                for g in range(j // 8, groups)
            }
        )
    scale = [jnp.ones((8, LANES), jnp.float32)] * groups
    for step in range(planes):
        own, at = step // 8, step % 8
        column = columns[step]
        root = lax.rsqrt(jnp.broadcast_to(column[own][at : at + 1], (8, LANES)))
        inverse = root * root
        scale[own] = jnp.where(sub == at, root, scale[own])
        factors = {g: value * inverse for g, value in column.items()}
        factors[own] = jnp.where(sub > at, factors[own], 0.0)
        for j in range(step + 1, planes):
            entry = jnp.broadcast_to(column[j // 8][j % 8 : j % 8 + 1], (8, LANES))
            for g in columns[j]:
                columns[j][g] = columns[j][g] - factors[g] * entry
        pivot_row = jnp.broadcast_to(state[own][at : at + 1], (8, LANES))
        for g in range(own, groups):
            state[g] = state[g] - factors[g] * pivot_row
    return jnp.concatenate([state[g] * scale[g] for g in range(groups)], axis=0)


def finish_kernel(pixel_count, second, edges, parts, basis, factor):
    planes = factor.shape[0]
    rows, _, width = second.shape
    block = tree_sum([parts[at] for at in range(parts.shape[0])]) / pixel_count
    state = eliminate(block, planes)
    at_row = lax.broadcasted_iota(jnp.int32, (planes, planes), 0)
    at_col = lax.broadcasted_iota(jnp.int32, (planes, planes), 1)
    first_inverse = state[:, planes : 2 * planes]
    product_upper = jnp.where(at_col >= at_row, state[:, 2 * planes : 3 * planes], 0.0)
    product_inverse = jnp.where(at_col <= at_row, state[:, 3 * planes :], 0.0)
    factor[...] = jnp.where(at_col >= at_row, gram_of(product_upper, first_inverse), 0.0)
    high, middle, low = split(product_inverse)
    left_side = jnp.concatenate([high, high, middle, high, low, middle], axis=1)

    def solved(high, middle, low):
        right_side = jnp.concatenate([high, middle, high, low, high, middle], axis=0)
        return jnp.dot(left_side, right_side, preferred_element_type=jnp.float32)

    lane = lax.broadcasted_iota(jnp.int32, (1, LANES), 1)
    outer = solved(*split(edges[...]))
    for row in range(rows):
        value = solved(*(second[row, at * planes : (at + 1) * planes] for at in range(3)))
        place = PITCH * (row + 2)
        low_end = pltpu.roll(outer[:, :LANES], LANES - (place + 2), 1)
        high_end = pltpu.roll(outer[:, LANES:], (LANES - 2 - (place + PITCH - 4)) % LANES, 1)
        basis[:, row, :LANES] = jnp.where(lane < 2, low_end, value[:, :LANES])
        basis[:, row, LANES : width - LANES] = value[:, LANES : width - LANES]
        basis[:, row, width - LANES :] = jnp.where(lane >= LANES - 2, high_end, value[:, width - LANES :])


def tree_sum(parts):
    while len(parts) > 1:
        parts = [sum(parts[at + 1 : at + 2], parts[at]) for at in range(0, len(parts), 2)]
    return parts[0]


def swap(value, axis, pairing):
    rows, cols = lax.axis_size("row"), lax.axis_size("col")
    pairs = []
    for row in range(rows):
        for col in range(cols):
            place, count = (row, rows) if axis == "row" else (col, cols)
            other = place + 1 if place % 2 == pairing else place - 1
            if not 0 <= other < count:
                partner = (row, col ^ 1) if axis == "row" else (row ^ 1, col)
            else:
                partner = (other, col) if axis == "row" else (row, other)
            pairs.append((row * cols + col, partner[0] * cols + partner[1]))
    return lax.ppermute(value, ("row", "col"), pairs)


def on_device(sketch, weights):
    planes, rows, width = sketch.shape
    group = lax.axis_size("row") * lax.axis_size("col")
    by_row, weights_by_row, *messages = call(
        pack_rows_kernel,
        [f32(rows, planes, width), f32(rows, 8, width)] + [f32(2 * planes + 8, width)] * 2,
        jnp.concatenate([sketch, weights], axis=0),
    )
    from_rows = [swap(messages[pairing], "row", pairing) for pairing in (1, 0)][::-1]
    left, right, *messages = call(strips_kernel, [f32(planes + 8, LANES)] * 4, by_row, weights_by_row, *from_rows)
    from_cols = [swap(message, "col", pairing) for pairing, message in enumerate(messages)]
    second, early_grams = call(
        early_kernel,
        [jax.ShapeDtypeStruct((rows, 3 * planes, width), jnp.bfloat16), f32(planes, 2 * planes)],
        by_row,
        weights_by_row,
        *from_rows,
        scratch=[pltpu.VMEM((rows + 2, planes, width), jnp.float32)],
    )
    grams, edges = call(
        functools.partial(late_kernel, rows),
        [f32(group, planes // 2, 4 * planes), f32(planes, 2 * LANES)],
        left,
        right,
        *from_cols,
        early_grams,
    )
    parts = lax.all_to_all(grams, ("row", "col"), 0, 0, tiled=True)
    return call(
        functools.partial(finish_kernel, float(rows * width * group)),
        [f32(planes, rows, width), f32(planes, planes)],
        second,
        edges,
        parts,
    )


def solution(mesh):
    return jax.shard_map(
        on_device,
        mesh=mesh,
        in_specs=(P(None, ("sec", "row"), "col"), P(None, ("sec", "row"), "col")),
        out_specs=(P(None, ("sec", "row"), "col"), P("sec", None)),
        check_vma=False,
    )
```

```python
import functools

import jax
import jax.numpy as jnp
from jax import lax
from jax.experimental import pallas as pl
from jax.experimental.pallas import tpu as pltpu
from jax.sharding import PartitionSpec as P

NEIGHBOURS = ((-1, -1), (-1, 0), (-1, 1), (0, -1), (0, 1), (1, -1), (1, 0), (1, 1))
LANES = 128
PITCH = 8
HIGHEST = lax.Precision.HIGHEST


def call(kernel, out_shapes, *operands, scratch=()):
    return pl.pallas_call(
        kernel,
        out_shape=out_shapes,
        in_specs=[pl.BlockSpec(memory_space=pltpu.VMEM)] * len(operands),
        out_specs=[pl.BlockSpec(memory_space=pltpu.VMEM)] * len(out_shapes),
        scratch_shapes=scratch,
        compiler_params=pltpu.CompilerParams(vmem_limit_bytes=40 * 1024 * 1024),
    )(*operands)


def f32(*shape):
    return jax.ShapeDtypeStruct(shape, jnp.float32)


def sides_of(axis):
    place = lax.axis_index(axis)
    return place % 2 == 0, place > 0, place < lax.axis_size(axis) - 1


def pack_rows_kernel(joined, by_row, weights_by_row, *row_messages):
    rows, planes, _ = by_row.shape
    even_row, _, _ = sides_of("row")
    for row in range(rows):
        weights_by_row[row] = joined[planes:, row, :]
        by_row[row] = joined[:planes, row, :]
    for message, up in zip(row_messages, (even_row, jnp.logical_not(even_row))):
        start = jnp.where(up, rows - 2, 0)
        for slot in range(2):
            message[slot * planes : (slot + 1) * planes] = by_row[start + slot]
        message[2 * planes :] = weights_by_row[jnp.where(up, rows - 1, 0)]


def row_parts(by_row, weights_by_row, first_message, second_message, window):
    rows, planes, _ = by_row.shape
    even_row, has_below, has_above = sides_of("row")
    one, other = first_message[:, window], second_message[:, window]
    below = jnp.where(has_below, jnp.where(even_row, other, one), 0.0)
    above = jnp.where(has_above, jnp.where(even_row, one, other), 0.0)
    values = [below[:planes], below[planes : 2 * planes]]
    values += [by_row[row, :, window] for row in range(rows)]
    values += [above[:planes], above[planes : 2 * planes]]
    weights = [below[2 * planes :]]
    weights += [weights_by_row[row, :, window] for row in range(rows)]
    weights += [above[2 * planes :]]
    return values, weights


def strips_kernel(by_row, weights_by_row, first_message, second_message, left, right, *col_messages):
    planes, width = by_row.shape[1:]
    even_col, _, _ = sides_of("col")
    lane = lax.broadcasted_iota(jnp.int32, (1, LANES), 1)
    own = PITCH - 2
    for target, start, low, at in ((left, 0, 2, 0), (right, width - LANES, 0, LANES - own)):
        values, weights = row_parts(by_row, weights_by_row, first_message, second_message, pl.ds(start, LANES))
        for part, some, skip in ((slice(None, planes), values, 0), (slice(planes, None), weights, 1)):
            total = None
            for row, value in enumerate(some):
                place = PITCH * (row + skip) + low
                moved = pltpu.roll(value, (place - at) % LANES, 1)
                moved = jnp.where((lane >= place) & (lane < place + own), moved, 0.0)
                total = moved if total is None else total + moved
            target[part] = total
    to_left, to_right = folded(left[...], 2), folded(right[...], own - 2)
    for message, up in zip(col_messages, (even_col, jnp.logical_not(even_col))):
        message[...] = jnp.where(up, to_right, to_left)


def folded(strip, spot):
    lane = lax.broadcasted_iota(jnp.int32, (1, LANES), 1)
    groups = strip.shape[0] // 8
    pieces = []
    for group in range(groups):
        target = 2 * group if group < groups - 1 else 0
        moved = rolled(strip[8 * group : 8 * (group + 1)], target - spot)
        pieces.append(jnp.where((lane % PITCH) // 2 == target // 2, moved, 0.0))
    return jnp.concatenate([functools.reduce(jnp.add, pieces[:-1]), pieces[-1]], axis=0)


def unfolded(message, spot, planes):
    lane = lax.broadcasted_iota(jnp.int32, (1, LANES), 1)
    pieces = [rolled(message[:8], spot - 2 * group) for group in range(planes // 8)] + [rolled(message[8:], spot)]
    return jnp.where((lane % PITCH) // 2 == spot // 2, jnp.concatenate(pieces, axis=0), 0.0)


def rolled(value, shift):
    return pltpu.roll(value, shift % LANES, 1) if shift % LANES else value


def apply_operator(rows3, weight_rows):
    width = rows3[1].shape[1]
    degree = jnp.sum(weight_rows, axis=0, keepdims=True)
    total = degree * rows3[1]
    sides = {-1: None, 1: None}
    for position, (up, across) in enumerate(NEIGHBOURS):
        weight = weight_rows[position : position + 1]
        value = rows3[up + 1]
        if across == 0:
            total = total + weight * value
        else:
            shifted = pltpu.roll(weight_rows, across % width, 1)[position : position + 1]
            term = shifted * value
            sides[across] = term if sides[across] is None else sides[across] + term
    for across, value in sides.items():
        total = total + pltpu.roll(value, (-across) % width, 1)
    return total


def gram_of(value, other):
    return lax.dot_general(
        value, other, (((1,), (1,)), ((), ())), precision=HIGHEST, preferred_element_type=jnp.float32
    )


def split(value):
    high = value.astype(jnp.bfloat16)
    rest = value - high.astype(jnp.float32)
    middle = rest.astype(jnp.bfloat16)
    low = (rest - middle.astype(jnp.float32)).astype(jnp.bfloat16)
    return high, middle, low


def early_kernel(by_row, weights_by_row, first_message, second_message, second, grams, middle):
    rows, planes, width = by_row.shape
    values, weights = row_parts(by_row, weights_by_row, first_message, second_message, slice(None))
    col = lax.broadcasted_iota(jnp.int32, (1, width), 1)
    inner = (col >= 2) & (col < width - 2)
    for row in range(rows + 2):
        middle[row] = apply_operator(values[row : row + 3], weights[row])
    gram = [jnp.zeros((planes, planes), jnp.float32)] * 2
    for row in range(rows):
        image = apply_operator([middle[row], middle[row + 1], middle[row + 2]], weights[row + 1])
        for at, part in enumerate(split(image)):
            second[row, at * planes : (at + 1) * planes] = part
        for at, value in enumerate((middle[row + 1], image)):
            gram[at] = gram[at] + gram_of(jnp.where(inner, value, 0.0), value)
    grams[:, :planes] = gram[0]
    grams[:, planes:] = gram[1]


def apply_on_strip(values, weights):
    total = jnp.sum(weights, axis=0, keepdims=True) * values
    for position, (up, across) in enumerate(NEIGHBOURS):
        moved = pltpu.roll(values, (-PITCH * up - across) % LANES, 1)
        total = total + weights[position : position + 1] * moved
    return total


def late_kernel(rows, left, right, first_message, second_message, early_grams, grams, edges):
    planes = early_grams.shape[0]
    even_col, has_left, has_right = sides_of("col")
    one, other = first_message[...], second_message[...]
    lane = lax.broadcasted_iota(jnp.int32, (1, LANES), 1)
    spot, row = lane % PITCH, lane // PITCH
    gram = [early_grams[:, :planes], early_grams[:, planes:]]
    for side, (strip, present, halo) in enumerate(
        ((left, has_left, jnp.where(even_col, other, one)), (right, has_right, jnp.where(even_col, one, other)))
    ):
        whole = strip[...] + jnp.where(present, unfolded(halo, side * (PITCH - 2), planes), 0.0)
        values, weights = whole[:planes], whole[planes:]
        low = 2 if side == 0 else PITCH - 4
        outer = (spot >= low) & (spot < low + 2) & (row >= 2) & (row < rows + 2)
        for at in range(2):
            values = apply_on_strip(values, weights)
            gram[at] = gram[at] + gram_of(jnp.where(outer, values, 0.0), values)
        edges[:, side * LANES : (side + 1) * LANES] = values
    at_row = lax.broadcasted_iota(jnp.int32, (planes, planes), 0)
    at_col = lax.broadcasted_iota(jnp.int32, (planes, planes), 1)
    mixed = jnp.where(at_row >= at_col, gram[0], gram[1])
    diagonal = jnp.sum(jnp.where(at_row == at_col, gram[1], 0.0), axis=0, keepdims=True)
    block = jnp.concatenate([mixed[8 * g : 8 * (g + 1)] for g in range(planes // 8)], axis=1)
    last = jnp.concatenate([diagonal] * (LANES // planes), axis=1)
    for target in range(grams.shape[0]):
        for at in range(8):
            grams[target, :, at * LANES : (at + 1) * LANES] = block[at : at + 1]
        grams[target, :, 8 * LANES :] = last


def eliminate(grams, planes):
    lane = lax.broadcasted_iota(jnp.int32, (8, LANES), 1)
    sub = lax.broadcasted_iota(jnp.int32, (8, LANES), 0)
    first_half = lane < 2 * planes
    groups = planes // 8
    sources = [[gram[8 * g : 8 * (g + 1)] for g in range(groups)] for gram in grams]
    state = []
    for g in range(groups):
        unit = jnp.where(sub + 8 * g == lane % (2 * planes) - planes, 1.0, 0.0)
        unit = unit[:, planes : 2 * planes]
        state.append(jnp.concatenate([sources[0][g], unit, sources[1][g], unit], axis=1))
    columns = []
    for j in range(planes):
        columns.append(
            {
                g: jnp.where(
                    first_half,
                    jnp.broadcast_to(sources[0][g][:, j : j + 1], (8, LANES)),
                    jnp.broadcast_to(sources[1][g][:, j : j + 1], (8, LANES)),
                )
                for g in range(j // 8, groups)
            }
        )
    scale = [jnp.ones((8, LANES), jnp.float32)] * groups
    for step in range(planes):
        own, at = step // 8, step % 8
        column = columns[step]
        root = lax.rsqrt(jnp.broadcast_to(column[own][at : at + 1], (8, LANES)))
        inverse = root * root
        scale[own] = jnp.where(sub == at, root, scale[own])
        factors = {g: value * inverse for g, value in column.items()}
        factors[own] = jnp.where(sub > at, factors[own], 0.0)
        for j in range(step + 1, planes):
            entry = jnp.broadcast_to(column[j // 8][j % 8 : j % 8 + 1], (8, LANES))
            for g in columns[j]:
                columns[j][g] = columns[j][g] - factors[g] * entry
        pivot_row = jnp.broadcast_to(state[own][at : at + 1], (8, LANES))
        for g in range(own, groups):
            state[g] = state[g] - factors[g] * pivot_row
    return jnp.concatenate([state[g] * scale[g] for g in range(groups)], axis=0)


def finish_kernel(pixel_count, second, edges, parts, basis, factor):
    planes = factor.shape[0]
    rows, _, width = second.shape
    at_row = lax.broadcasted_iota(jnp.int32, (planes, planes), 0)
    at_col = lax.broadcasted_iota(jnp.int32, (planes, planes), 1)
    block = tree_sum([parts[at] for at in range(parts.shape[0])]) / pixel_count
    block = [block[:, at * LANES : (at + 1) * LANES] for at in range(9)]
    mixed, diagonal = jnp.concatenate(block[:8], axis=0), block[8][:, :planes]
    mixed = jnp.concatenate([mixed[:, at * planes : (at + 1) * planes] for at in range(LANES // planes)], axis=0)
    flipped = mixed.T
    first = jnp.where(at_row >= at_col, mixed, flipped)
    second_gram = jnp.where(at_row < at_col, mixed, jnp.where(at_row > at_col, flipped, diagonal))
    state = eliminate([first, second_gram], planes)
    first_inverse = state[:, planes : 2 * planes]
    product_upper = jnp.where(at_col >= at_row, state[:, 2 * planes : 3 * planes], 0.0)
    product_inverse = jnp.where(at_col <= at_row, state[:, 3 * planes :], 0.0)
    factor[...] = jnp.where(at_col >= at_row, gram_of(product_upper, first_inverse), 0.0)
    high, middle, low = split(product_inverse)
    left_side = jnp.concatenate([high, high, middle, high, low, middle], axis=1)

    def solved(high, middle, low):
        right_side = jnp.concatenate([high, middle, high, low, high, middle], axis=0)
        return jnp.dot(left_side, right_side, preferred_element_type=jnp.float32)

    lane = lax.broadcasted_iota(jnp.int32, (1, LANES), 1)
    outer = solved(*split(edges[...]))
    for row in range(rows):
        value = solved(*(second[row, at * planes : (at + 1) * planes] for at in range(3)))
        place = PITCH * (row + 2)
        low_end = pltpu.roll(outer[:, :LANES], LANES - (place + 2), 1)
        high_end = pltpu.roll(outer[:, LANES:], (LANES - 2 - (place + PITCH - 4)) % LANES, 1)
        basis[:, row, :LANES] = jnp.where(lane < 2, low_end, value[:, :LANES])
        basis[:, row, LANES : width - LANES] = value[:, LANES : width - LANES]
        basis[:, row, width - LANES :] = jnp.where(lane >= LANES - 2, high_end, value[:, width - LANES :])


def tree_sum(parts):
    while len(parts) > 1:
        parts = [sum(parts[at + 1 : at + 2], parts[at]) for at in range(0, len(parts), 2)]
    return parts[0]


def swap(value, axis, pairing):
    rows, cols = lax.axis_size("row"), lax.axis_size("col")
    pairs = []
    for row in range(rows):
        for col in range(cols):
            place, count = (row, rows) if axis == "row" else (col, cols)
            other = place + 1 if place % 2 == pairing else place - 1
            if not 0 <= other < count:
                partner = (row, col ^ 1) if axis == "row" else (row ^ 1, col)
            else:
                partner = (other, col) if axis == "row" else (row, other)
            pairs.append((row * cols + col, partner[0] * cols + partner[1]))
    return lax.ppermute(value, ("row", "col"), pairs)


def on_device(sketch, weights):
    planes, rows, width = sketch.shape
    group = lax.axis_size("row") * lax.axis_size("col")
    by_row, weights_by_row, *messages = call(
        pack_rows_kernel,
        [f32(rows, planes, width), f32(rows, 8, width)] + [f32(2 * planes + 8, width)] * 2,
        jnp.concatenate([sketch, weights], axis=0),
    )
    from_rows = [swap(messages[pairing], "row", pairing) for pairing in (1, 0)][::-1]
    left, right, *messages = call(strips_kernel, [f32(planes + 8, LANES)] * 2 + [f32(16, LANES)] * 2, by_row, weights_by_row, *from_rows)
    from_cols = [swap(message, "col", pairing) for pairing, message in enumerate(messages)]
    second, early_grams = call(
        early_kernel,
        [jax.ShapeDtypeStruct((rows, 3 * planes, width), jnp.bfloat16), f32(planes, 2 * planes)],
        by_row,
        weights_by_row,
        *from_rows,
        scratch=[pltpu.VMEM((rows + 2, planes, width), jnp.float32)],
    )
    grams, edges = call(
        functools.partial(late_kernel, rows),
        [f32(group, 1, 9 * LANES), f32(planes, 2 * LANES)],
        left,
        right,
        *from_cols,
        early_grams,
    )
    parts = lax.all_to_all(grams, ("row", "col"), 0, 0, tiled=True)
    return call(
        functools.partial(finish_kernel, float(rows * width * group)),
        [f32(planes, rows, width), f32(planes, planes)],
        second,
        edges,
        parts,
    )


def solution(mesh):
    return jax.shard_map(
        on_device,
        mesh=mesh,
        in_specs=(P(None, ("sec", "row"), "col"), P(None, ("sec", "row"), "col")),
        out_specs=(P(None, ("sec", "row"), "col"), P("sec", None)),
        check_vma=False,
    )
```

```python
import functools
import itertools

import jax
import jax.numpy as jnp
from jax import lax
from jax.experimental import pallas as pl
from jax.experimental.pallas import tpu as pltpu
from jax.sharding import PartitionSpec as P

NEIGHBOURS = ((-1, -1), (-1, 0), (-1, 1), (0, -1), (0, 1), (1, -1), (1, 0), (1, 1))
LANES = 128
PITCH = 8
HIGHEST = lax.Precision.HIGHEST


def call(kernel, out_shapes, *operands, scratch=(), cost=None):
    return pl.pallas_call(
        kernel,
        out_shape=out_shapes,
        in_specs=[pl.BlockSpec(memory_space=pltpu.VMEM)] * len(operands),
        out_specs=[pl.BlockSpec(memory_space=pltpu.VMEM)] * len(out_shapes),
        scratch_shapes=scratch,
        cost_estimate=cost,
        compiler_params=pltpu.CompilerParams(vmem_limit_bytes=40 * 1024 * 1024),
    )(*operands)


def f32(*shape):
    return jax.ShapeDtypeStruct(shape, jnp.float32)


def sides_of(axis):
    place = lax.axis_index(axis)
    return place % 2 == 1, place > 0, place < lax.axis_size(axis) - 1


def pack_rows_kernel(joined, by_row, weights_by_row, left, right, *messages):
    corner_messages, bulk_messages = messages[:2], messages[2:]
    rows, planes, width = by_row.shape
    odd_row, _, _ = sides_of("row")
    lane = lax.broadcasted_iota(jnp.int32, (1, LANES), 1)
    own = PITCH - 2
    for target, start, low, at in ((left, 0, 2, 0), (right, width - LANES, 0, LANES - own)):
        total = None
        for row in range(rows):
            place = PITCH * (row + 2) + low
            moved = rolled(joined[:, row, start : start + LANES], place - at)
            moved = jnp.where((lane >= place) & (lane < place + own), moved, 0.0)
            total = moved if total is None else total + moved
        target[...] = total
    pair = 2 * PITCH
    for message, up in zip(corner_messages, (odd_row, jnp.logical_not(odd_row))):
        pieces = []
        for group in range(planes // 8 + 1):
            piece = None
            for side, strip in enumerate((left, right)):
                target = (2 * group + side) * pair if group < planes // 8 else side * pair
                value = strip[8 * group : 8 * (group + 1)]
                moved = jnp.where(up, rolled(value, target - PITCH * rows), rolled(value, target - 2 * PITCH))
                moved = jnp.where(lane // pair == target // pair, moved, 0.0)
                piece = moved if piece is None else piece + moved
            pieces.append(piece)
        message[:8] = functools.reduce(jnp.add, pieces[:-1])
        message[8:] = pieces[-1]
    for row in range(rows):
        weights_by_row[row] = joined[planes:, row, :]
        by_row[row] = joined[:planes, row, :]
    for message, up in zip(bulk_messages, (odd_row, jnp.logical_not(odd_row))):
        start = jnp.where(up, rows - 2, 0)
        for slot in range(2):
            message[slot * planes : (slot + 1) * planes] = by_row[start + slot]
        message[2 * planes :] = weights_by_row[jnp.where(up, rows - 1, 0)]


def row_parts(by_row, weights_by_row, first_message, second_message):
    rows, planes, _ = by_row.shape
    odd_row, has_below, has_above = sides_of("row")
    one, other = first_message[...], second_message[...]
    below = jnp.where(has_below, jnp.where(odd_row, other, one), 0.0)
    above = jnp.where(has_above, jnp.where(odd_row, one, other), 0.0)
    values = [below[:planes], below[planes : 2 * planes]]
    values += [by_row[row] for row in range(rows)]
    values += [above[:planes], above[planes : 2 * planes]]
    weights = [below[2 * planes :]]
    weights += [weights_by_row[row] for row in range(rows)]
    weights += [above[2 * planes :]]
    return values, weights


def strips_kernel(rows, own_left, own_right, first_message, second_message, left, right, *col_messages):
    planes = own_left.shape[0] - 8
    odd_row, has_below, has_above = sides_of("row")
    odd_col, _, _ = sides_of("col")
    one, other = first_message[...], second_message[...]
    lane = lax.broadcasted_iota(jnp.int32, (1, LANES), 1)
    pair = 2 * PITCH
    halos = (
        (jnp.where(has_below, jnp.where(odd_row, other, one), 0.0), 0),
        (jnp.where(has_above, jnp.where(odd_row, one, other), 0.0), PITCH * (rows + 2)),
    )
    for side, (strip, target) in enumerate(((own_left, left), (own_right, right))):
        total = strip[...]
        for halo, place in halos:
            pieces = [rolled(halo[:8], place - (2 * group + side) * pair) for group in range(planes // 8)]
            pieces.append(rolled(halo[8:], place - side * pair))
            total = total + jnp.where(lane // pair == place // pair, jnp.concatenate(pieces, axis=0), 0.0)
        target[...] = total
    to_left, to_right = folded(left[...], 2), folded(right[...], PITCH - 4)
    for message, up in zip(col_messages, (odd_col, jnp.logical_not(odd_col))):
        message[...] = jnp.where(up, to_right, to_left)


def folded(strip, spot):
    lane = lax.broadcasted_iota(jnp.int32, (1, LANES), 1)
    groups = strip.shape[0] // 8
    pieces = []
    for group in range(groups):
        target = 2 * group if group < groups - 1 else 0
        moved = rolled(strip[8 * group : 8 * (group + 1)], target - spot)
        pieces.append(jnp.where((lane % PITCH) // 2 == target // 2, moved, 0.0))
    return jnp.concatenate([functools.reduce(jnp.add, pieces[:-1]), pieces[-1]], axis=0)


def unfolded(message, spot, planes):
    lane = lax.broadcasted_iota(jnp.int32, (1, LANES), 1)
    pieces = [rolled(message[:8], spot - 2 * group) for group in range(planes // 8)] + [rolled(message[8:], spot)]
    return jnp.where((lane % PITCH) // 2 == spot // 2, jnp.concatenate(pieces, axis=0), 0.0)


def rolled(value, shift):
    return pltpu.roll(value, shift % LANES, 1) if shift % LANES else value


def apply_operator(rows3, weight_rows):
    width = rows3[1].shape[1]
    degree = jnp.sum(weight_rows, axis=0, keepdims=True)
    total = degree * rows3[1]
    sides = {-1: None, 1: None}
    for position, (up, across) in enumerate(NEIGHBOURS):
        weight = weight_rows[position : position + 1]
        value = rows3[up + 1]
        if across == 0:
            total = total + weight * value
        else:
            shifted = pltpu.roll(weight_rows, across % width, 1)[position : position + 1]
            term = shifted * value
            sides[across] = term if sides[across] is None else sides[across] + term
    for across, value in sides.items():
        total = total + pltpu.roll(value, (-across) % width, 1)
    return total


def gram_of(value, other):
    return lax.dot_general(
        value, other, (((1,), (1,)), ((), ())), precision=HIGHEST, preferred_element_type=jnp.float32
    )


def split(value):
    high = value.astype(jnp.bfloat16)
    rest = value - high.astype(jnp.float32)
    middle = rest.astype(jnp.bfloat16)
    low = (rest - middle.astype(jnp.float32)).astype(jnp.bfloat16)
    return high, middle, low


def early_kernel(by_row, weights_by_row, first_message, second_message, second, grams, middle):
    rows, planes, width = by_row.shape
    values, weights = row_parts(by_row, weights_by_row, first_message, second_message)
    col = lax.broadcasted_iota(jnp.int32, (1, width), 1)
    inner = (col >= 2) & (col < width - 2)
    for row in range(rows + 2):
        middle[row] = apply_operator(values[row : row + 3], weights[row])
    gram = [jnp.zeros((planes, planes), jnp.float32)] * 2
    for row in range(rows):
        image = apply_operator([middle[row], middle[row + 1], middle[row + 2]], weights[row + 1])
        for at, part in enumerate(split(image)):
            second[row, at * planes : (at + 1) * planes] = part
        for at, value in enumerate((middle[row + 1], image)):
            gram[at] = gram[at] + gram_of(jnp.where(inner, value, 0.0), value)
    grams[:, :planes] = gram[0]
    grams[:, planes:] = gram[1]


def apply_on_strip(values, weights):
    total = jnp.sum(weights, axis=0, keepdims=True) * values
    for position, (up, across) in enumerate(NEIGHBOURS):
        moved = pltpu.roll(values, (-PITCH * up - across) % LANES, 1)
        total = total + weights[position : position + 1] * moved
    return total


def late_kernel(rows, left, right, first_message, second_message, early_grams, grams, edges):
    planes = early_grams.shape[0]
    odd_col, has_left, has_right = sides_of("col")
    one, other = first_message[...], second_message[...]
    lane = lax.broadcasted_iota(jnp.int32, (1, LANES), 1)
    spot, row = lane % PITCH, lane // PITCH
    gram = [early_grams[:, :planes], early_grams[:, planes:]]
    for side, (strip, present, halo) in enumerate(
        ((left, has_left, jnp.where(odd_col, other, one)), (right, has_right, jnp.where(odd_col, one, other)))
    ):
        whole = strip[...] + jnp.where(present, unfolded(halo, side * (PITCH - 2), planes), 0.0)
        values, weights = whole[:planes], whole[planes:]
        low = 2 if side == 0 else PITCH - 4
        outer = (spot >= low) & (spot < low + 2) & (row >= 2) & (row < rows + 2)
        for at in range(2):
            values = apply_on_strip(values, weights)
            gram[at] = gram[at] + gram_of(jnp.where(outer, values, 0.0), values)
        edges[:, side * LANES : (side + 1) * LANES] = values
    at_row = lax.broadcasted_iota(jnp.int32, (planes, planes), 0)
    at_col = lax.broadcasted_iota(jnp.int32, (planes, planes), 1)
    mixed = jnp.where(at_row >= at_col, gram[0], gram[1])
    diagonal = jnp.sum(jnp.where(at_row == at_col, gram[1], 0.0), axis=0, keepdims=True)
    block = jnp.concatenate([mixed[8 * g : 8 * (g + 1)] for g in range(planes // 8)], axis=1)
    last = jnp.concatenate([diagonal] * (LANES // planes), axis=1)
    for target in range(grams.shape[0]):
        for at in range(8):
            grams[target, :, at * LANES : (at + 1) * LANES] = block[at : at + 1]
        grams[target, :, 8 * LANES :] = last


def eliminate(grams, planes):
    lane = lax.broadcasted_iota(jnp.int32, (8, LANES), 1)
    sub = lax.broadcasted_iota(jnp.int32, (8, LANES), 0)
    first_half = lane < 2 * planes
    groups = planes // 8
    sources = [[gram[8 * g : 8 * (g + 1)] for g in range(groups)] for gram in grams]
    state = []
    for g in range(groups):
        unit = jnp.where(sub + 8 * g == lane % (2 * planes) - planes, 1.0, 0.0)
        unit = unit[:, planes : 2 * planes]
        state.append(jnp.concatenate([sources[0][g], unit, sources[1][g], unit], axis=1))
    columns = []
    for j in range(planes):
        columns.append(
            {
                g: jnp.where(
                    first_half,
                    jnp.broadcast_to(sources[0][g][:, j : j + 1], (8, LANES)),
                    jnp.broadcast_to(sources[1][g][:, j : j + 1], (8, LANES)),
                )
                for g in range(j // 8, groups)
            }
        )
    scale = [jnp.ones((8, LANES), jnp.float32)] * groups
    for step in range(planes):
        own, at = step // 8, step % 8
        column = columns[step]
        root = lax.rsqrt(jnp.broadcast_to(column[own][at : at + 1], (8, LANES)))
        inverse = root * root
        scale[own] = jnp.where(sub == at, root, scale[own])
        factors = {g: value * inverse for g, value in column.items()}
        factors[own] = jnp.where(sub > at, factors[own], 0.0)
        for j in range(step + 1, planes):
            entry = jnp.broadcast_to(column[j // 8][j % 8 : j % 8 + 1], (8, LANES))
            for g in columns[j]:
                columns[j][g] = columns[j][g] - factors[g] * entry
        pivot_row = jnp.broadcast_to(state[own][at : at + 1], (8, LANES))
        for g in range(own, groups):
            state[g] = state[g] - factors[g] * pivot_row
    return jnp.concatenate([state[g] * scale[g] for g in range(groups)], axis=0)


def finish_kernel(pixel_count, second, edges, parts, basis, factor):
    planes = factor.shape[0]
    rows, _, width = second.shape
    at_row = lax.broadcasted_iota(jnp.int32, (planes, planes), 0)
    at_col = lax.broadcasted_iota(jnp.int32, (planes, planes), 1)
    block = tree_sum([parts[at] for at in range(parts.shape[0])]) / pixel_count
    block = [block[:, at * LANES : (at + 1) * LANES] for at in range(9)]
    mixed, diagonal = jnp.concatenate(block[:8], axis=0), block[8][:, :planes]
    mixed = jnp.concatenate([mixed[:, at * planes : (at + 1) * planes] for at in range(LANES // planes)], axis=0)
    flipped = mixed.T
    first = jnp.where(at_row >= at_col, mixed, flipped)
    second_gram = jnp.where(at_row < at_col, mixed, jnp.where(at_row > at_col, flipped, diagonal))
    state = eliminate([first, second_gram], planes)
    first_inverse = state[:, planes : 2 * planes]
    product_upper = jnp.where(at_col >= at_row, state[:, 2 * planes : 3 * planes], 0.0)
    product_inverse = jnp.where(at_col <= at_row, state[:, 3 * planes :], 0.0)
    factor[...] = jnp.where(at_col >= at_row, gram_of(product_upper, first_inverse), 0.0)
    high, middle, low = split(product_inverse)
    left_side = jnp.concatenate([high, high, middle, high, low, middle], axis=1)

    def solved(high, middle, low):
        right_side = jnp.concatenate([high, middle, high, low, high, middle], axis=0)
        return jnp.dot(left_side, right_side, preferred_element_type=jnp.float32)

    lane = lax.broadcasted_iota(jnp.int32, (1, LANES), 1)
    outer = solved(*split(edges[...]))
    for row in range(rows):
        value = solved(*(second[row, at * planes : (at + 1) * planes] for at in range(3)))
        place = PITCH * (row + 2)
        low_end = pltpu.roll(outer[:, :LANES], LANES - (place + 2), 1)
        high_end = pltpu.roll(outer[:, LANES:], (LANES - 2 - (place + PITCH - 4)) % LANES, 1)
        basis[:, row, :LANES] = jnp.where(lane < 2, low_end, value[:, :LANES])
        basis[:, row, LANES : width - LANES] = value[:, LANES : width - LANES]
        basis[:, row, width - LANES :] = jnp.where(lane >= LANES - 2, high_end, value[:, width - LANES :])


def tree_sum(parts):
    while len(parts) > 1:
        parts = [sum(parts[at + 1 : at + 2], parts[at]) for at in range(0, len(parts), 2)]
    return parts[0]


def swap(value, axis, pairing):
    names = ("sec", "row", "col")
    shape = [lax.axis_size(name) for name in names]
    at = names.index(axis)

    def number(place):
        return (place[0] * shape[1] + place[1]) * shape[2] + place[2]

    pairs = []
    for place in itertools.product(*(range(extent) for extent in shape)):
        partner = list(place)
        partner[at] += 1 if place[at] % 2 != pairing else -1
        if not 0 <= partner[at] < shape[at]:
            partner[at] = place[at]
            partner[at - 1] ^= 1
        pairs.append((number(place), number(partner)))
    return lax.ppermute(value, names, pairs)


def on_device(sketch, weights):
    planes, rows, width = sketch.shape
    group = lax.axis_size("row") * lax.axis_size("col")
    side = f32(planes + 8, LANES)
    by_row, weights_by_row, left, right, *messages = call(
        pack_rows_kernel,
        [f32(rows, planes, width), f32(rows, 8, width), side, side]
        + [f32(16, LANES)] * 2
        + [f32(2 * planes + 8, width)] * 2,
        jnp.concatenate([sketch, weights], axis=0),
    )
    corners = [swap(message, "row", pairing) for pairing, message in enumerate(messages[:2])]
    from_rows = [swap(message, "row", pairing) for pairing, message in enumerate(messages[2:])]
    left, right, *messages = call(
        functools.partial(strips_kernel, rows), [side, side] + [f32(16, LANES)] * 2, left, right, *corners, cost=pl.CostEstimate(flops=2000000000, bytes_accessed=4000000, transcendentals=0)
    )
    from_cols = [swap(message, "col", pairing) for pairing, message in enumerate(messages)]
    second, early_grams = call(
        early_kernel,
        [jax.ShapeDtypeStruct((rows, 3 * planes, width), jnp.bfloat16), f32(planes, 2 * planes)],
        by_row,
        weights_by_row,
        *from_rows,
        scratch=[pltpu.VMEM((rows + 2, planes, width), jnp.float32)],
    )
    grams, edges = call(
        functools.partial(late_kernel, rows),
        [f32(group, 1, 9 * LANES), f32(planes, 2 * LANES)],
        left,
        right,
        *from_cols,
        early_grams,
    )
    parts = lax.all_to_all(grams, ("row", "col"), 0, 0, tiled=True)
    return call(
        functools.partial(finish_kernel, float(rows * width * group)),
        [f32(planes, rows, width), f32(planes, planes)],
        second,
        edges,
        parts,
    )


def solution(mesh):
    return jax.shard_map(
        on_device,
        mesh=mesh,
        in_specs=(P(None, ("sec", "row"), "col"), P(None, ("sec", "row"), "col")),
        out_specs=(P(None, ("sec", "row"), "col"), P("sec", None)),
        check_vma=False,
    )
```

```python
import functools
import itertools

import jax
import jax.numpy as jnp
from jax import lax
from jax.experimental import pallas as pl
from jax.experimental.pallas import tpu as pltpu
from jax.sharding import PartitionSpec as P

NEIGHBOURS = ((-1, -1), (-1, 0), (-1, 1), (0, -1), (0, 1), (1, -1), (1, 0), (1, 1))
LANES = 128
PITCH = 8
HIGHEST = lax.Precision.HIGHEST


def call(kernel, out_shapes, *operands, memory=pltpu.VMEM, scratch=(), cost=None):
    return pl.pallas_call(
        kernel,
        out_shape=out_shapes,
        in_specs=[pl.BlockSpec(memory_space=memory)] * len(operands),
        out_specs=[pl.BlockSpec(memory_space=pltpu.VMEM)] * len(out_shapes),
        scratch_shapes=scratch,
        cost_estimate=cost,
        compiler_params=pltpu.CompilerParams(vmem_limit_bytes=40 * 1024 * 1024),
    )(*operands)


def f32(*shape):
    return jax.ShapeDtypeStruct(shape, jnp.float32)


def sides_of(axis):
    place = lax.axis_index(axis)
    return place % 2 == 1, place > 0, place < lax.axis_size(axis) - 1


def pack_rows_kernel(sketch, weights, by_row, weights_by_row, left, right, *rest):
    corner_messages, bulk_messages = rest[:2], rest[2:4]
    tile, weight_tile, arrived = rest[4:]
    copies = [
        pltpu.make_async_copy(sketch, tile, arrived.at[0]),
        pltpu.make_async_copy(weights, weight_tile, arrived.at[1]),
    ]
    for copy in copies:
        copy.start()
    for copy in copies:
        copy.wait()
    rows, planes, width = by_row.shape
    odd_row, _, _ = sides_of("row")
    lane = lax.broadcasted_iota(jnp.int32, (1, LANES), 1)
    own = PITCH - 2
    for target, start, low, at in ((left, 0, 2, 0), (right, width - LANES, 0, LANES - own)):
        total = None
        for row in range(rows):
            place = PITCH * (row + 2) + low
            window = slice(start, start + LANES)
            value = jnp.concatenate([tile[:, row, window], weight_tile[:, row, window]], axis=0)
            moved = rolled(value, place - at)
            moved = jnp.where((lane >= place) & (lane < place + own), moved, 0.0)
            total = moved if total is None else total + moved
        target[...] = total
    pair = 2 * PITCH
    for message, up in zip(corner_messages, (odd_row, jnp.logical_not(odd_row))):
        pieces = []
        for group in range(planes // 8 + 1):
            piece = None
            for side, strip in enumerate((left, right)):
                target = (2 * group + side) * pair if group < planes // 8 else side * pair
                value = strip[8 * group : 8 * (group + 1)]
                moved = jnp.where(up, rolled(value, target - PITCH * rows), rolled(value, target - 2 * PITCH))
                moved = jnp.where(lane // pair == target // pair, moved, 0.0)
                piece = moved if piece is None else piece + moved
            pieces.append(piece)
        message[:8] = functools.reduce(jnp.add, pieces[:-1])
        message[8:] = pieces[-1]
    for row in range(rows):
        weights_by_row[row] = weight_tile[:, row, :]
        by_row[row] = tile[:, row, :]
    for message, up in zip(bulk_messages, (odd_row, jnp.logical_not(odd_row))):
        start = jnp.where(up, rows - 2, 0)
        for slot in range(2):
            message[slot * planes : (slot + 1) * planes] = by_row[start + slot]
        message[2 * planes :] = weights_by_row[jnp.where(up, rows - 1, 0)]


def strips_kernel(rows, own_left, own_right, first_message, second_message, left, right, *col_messages):
    planes = own_left.shape[0] - 8
    odd_row, has_below, has_above = sides_of("row")
    odd_col, _, _ = sides_of("col")
    one, other = first_message[...], second_message[...]
    lane = lax.broadcasted_iota(jnp.int32, (1, LANES), 1)
    pair = 2 * PITCH
    halos = (
        (jnp.where(has_below, jnp.where(odd_row, other, one), 0.0), 0),
        (jnp.where(has_above, jnp.where(odd_row, one, other), 0.0), PITCH * (rows + 2)),
    )
    for side, (strip, target) in enumerate(((own_left, left), (own_right, right))):
        total = strip[...]
        for halo, place in halos:
            pieces = [rolled(halo[:8], place - (2 * group + side) * pair) for group in range(planes // 8)]
            pieces.append(rolled(halo[8:], place - side * pair))
            total = total + jnp.where(lane // pair == place // pair, jnp.concatenate(pieces, axis=0), 0.0)
        target[...] = total
    to_left, to_right = folded(left[...], 2), folded(right[...], PITCH - 4)
    for message, up in zip(col_messages, (odd_col, jnp.logical_not(odd_col))):
        message[...] = jnp.where(up, to_right, to_left)


def folded(strip, spot):
    lane = lax.broadcasted_iota(jnp.int32, (1, LANES), 1)
    groups = strip.shape[0] // 8
    pieces = []
    for group in range(groups):
        target = 2 * group if group < groups - 1 else 0
        moved = rolled(strip[8 * group : 8 * (group + 1)], target - spot)
        pieces.append(jnp.where((lane % PITCH) // 2 == target // 2, moved, 0.0))
    return jnp.concatenate([functools.reduce(jnp.add, pieces[:-1]), pieces[-1]], axis=0)


def unfolded(message, spot, planes):
    lane = lax.broadcasted_iota(jnp.int32, (1, LANES), 1)
    pieces = [rolled(message[:8], spot - 2 * group) for group in range(planes // 8)] + [rolled(message[8:], spot)]
    return jnp.where((lane % PITCH) // 2 == spot // 2, jnp.concatenate(pieces, axis=0), 0.0)


def rolled(value, shift):
    return pltpu.roll(value, shift % LANES, 1) if shift % LANES else value


def apply_operator(rows3, weight_rows):
    width = rows3[1].shape[1]
    degree = jnp.sum(weight_rows, axis=0, keepdims=True)
    total = degree * rows3[1]
    sides = {-1: None, 1: None}
    for position, (up, across) in enumerate(NEIGHBOURS):
        weight = weight_rows[position : position + 1]
        value = rows3[up + 1]
        if across == 0:
            total = total + weight * value
        else:
            shifted = pltpu.roll(weight_rows, across % width, 1)[position : position + 1]
            term = shifted * value
            sides[across] = term if sides[across] is None else sides[across] + term
    for across, value in sides.items():
        total = total + pltpu.roll(value, (-across) % width, 1)
    return total


def gram_of(value, other):
    return lax.dot_general(
        value, other, (((1,), (1,)), ((), ())), precision=HIGHEST, preferred_element_type=jnp.float32
    )


def split(value):
    high = value.astype(jnp.bfloat16)
    rest = value - high.astype(jnp.float32)
    middle = rest.astype(jnp.bfloat16)
    low = (rest - middle.astype(jnp.float32)).astype(jnp.bfloat16)
    return high, middle, low


def images_of(planes, width, middle, weights, wanted, second, gram):
    for at, row in enumerate(wanted):
        image = apply_operator([middle(row - 1), middle(row), middle(row + 1)], weights(row))
        for place, part in enumerate(split(image)):
            second[at, place * planes : (place + 1) * planes] = part
        gram = gram + gram_of(inner_only(image), image)
    return gram


def inner_only(value):
    width = value.shape[1]
    col = lax.broadcasted_iota(jnp.int32, (1, width), 1)
    return jnp.where((col >= 2) & (col < width - 2), value, 0.0)


def inner_rows_kernel(by_row, weights_by_row, middle, second, grams):
    rows, planes, width = by_row.shape
    first = jnp.zeros((planes, planes), jnp.float32)
    for row in range(1, rows - 1):
        image = apply_operator([by_row[row - 1], by_row[row], by_row[row + 1]], weights_by_row[row])
        middle[row - 1] = image
        first = first + gram_of(inner_only(image), image)
    grams[:, :planes] = first
    grams[:, planes:] = images_of(
        planes,
        width,
        lambda row: middle[row - 1],
        lambda row: weights_by_row[row],
        range(2, rows - 2),
        second,
        jnp.zeros((planes, planes), jnp.float32),
    )


def outer_rows_kernel(
    by_row, weights_by_row, first_message, second_message, middle, inner_grams, second, grams, outer
):
    rows, planes, width = by_row.shape
    odd_row, has_below, has_above = sides_of("row")
    one, other = first_message[...], second_message[...]
    below = jnp.where(has_below, jnp.where(odd_row, other, one), 0.0)
    above = jnp.where(has_above, jnp.where(odd_row, one, other), 0.0)

    def field(row):
        if 0 <= row < rows:
            return by_row[row]
        at = (row + 2 if row < 0 else row - rows) * planes
        return (below if row < 0 else above)[at : at + planes]

    def weights(row):
        if 0 <= row < rows:
            return weights_by_row[row]
        return (below if row < 0 else above)[2 * planes :]

    first = inner_grams[:, :planes]
    places = (-1, 0, rows - 1, rows)
    for at, row in enumerate(places):
        image = apply_operator([field(row - 1), field(row), field(row + 1)], weights(row))
        outer[at] = image
        if 0 <= row < rows:
            first = first + gram_of(inner_only(image), image)
    grams[:, :planes] = first
    grams[:, planes:] = images_of(
        planes,
        width,
        lambda row: outer[places.index(row)] if row in places else middle[row - 1],
        weights,
        (0, 1, rows - 2, rows - 1),
        second,
        inner_grams[:, planes:],
    )


def apply_on_strip(values, weights):
    total = jnp.sum(weights, axis=0, keepdims=True) * values
    for position, (up, across) in enumerate(NEIGHBOURS):
        moved = pltpu.roll(values, (-PITCH * up - across) % LANES, 1)
        total = total + weights[position : position + 1] * moved
    return total


def late_kernel(rows, left, right, first_message, second_message, early_grams, grams, edges):
    planes = early_grams.shape[0]
    odd_col, has_left, has_right = sides_of("col")
    one, other = first_message[...], second_message[...]
    lane = lax.broadcasted_iota(jnp.int32, (1, LANES), 1)
    spot, row = lane % PITCH, lane // PITCH
    gram = [early_grams[:, :planes], early_grams[:, planes:]]
    for side, (strip, present, halo) in enumerate(
        ((left, has_left, jnp.where(odd_col, other, one)), (right, has_right, jnp.where(odd_col, one, other)))
    ):
        whole = strip[...] + jnp.where(present, unfolded(halo, side * (PITCH - 2), planes), 0.0)
        values, weights = whole[:planes], whole[planes:]
        low = 2 if side == 0 else PITCH - 4
        outer = (spot >= low) & (spot < low + 2) & (row >= 2) & (row < rows + 2)
        for at in range(2):
            values = apply_on_strip(values, weights)
            gram[at] = gram[at] + gram_of(jnp.where(outer, values, 0.0), values)
        edges[:, side * LANES : (side + 1) * LANES] = values
    at_row = lax.broadcasted_iota(jnp.int32, (planes, planes), 0)
    at_col = lax.broadcasted_iota(jnp.int32, (planes, planes), 1)
    mixed = jnp.where(at_row >= at_col, gram[0], gram[1])
    diagonal = jnp.sum(jnp.where(at_row == at_col, gram[1], 0.0), axis=0, keepdims=True)
    block = jnp.concatenate([mixed[8 * g : 8 * (g + 1)] for g in range(planes // 8)], axis=1)
    last = jnp.concatenate([diagonal] * (LANES // planes), axis=1)
    for target in range(grams.shape[0]):
        for at in range(8):
            grams[target, :, at * LANES : (at + 1) * LANES] = block[at : at + 1]
        grams[target, :, 8 * LANES :] = last


def eliminate(grams, planes):
    lane = lax.broadcasted_iota(jnp.int32, (8, LANES), 1)
    sub = lax.broadcasted_iota(jnp.int32, (8, LANES), 0)
    first_half = lane < 2 * planes
    groups = planes // 8
    sources = [[gram[8 * g : 8 * (g + 1)] for g in range(groups)] for gram in grams]
    state = []
    for g in range(groups):
        unit = jnp.where(sub + 8 * g == lane % (2 * planes) - planes, 1.0, 0.0)
        unit = unit[:, planes : 2 * planes]
        state.append(jnp.concatenate([sources[0][g], unit, sources[1][g], unit], axis=1))
    columns = []
    for j in range(planes):
        columns.append(
            {
                g: jnp.where(
                    first_half,
                    jnp.broadcast_to(sources[0][g][:, j : j + 1], (8, LANES)),
                    jnp.broadcast_to(sources[1][g][:, j : j + 1], (8, LANES)),
                )
                for g in range(j // 8, groups)
            }
        )
    scale = [jnp.ones((8, LANES), jnp.float32)] * groups
    for step in range(planes):
        own, at = step // 8, step % 8
        column = columns[step]
        root = lax.rsqrt(jnp.broadcast_to(column[own][at : at + 1], (8, LANES)))
        inverse = root * root
        scale[own] = jnp.where(sub == at, root, scale[own])
        factors = {g: value * inverse for g, value in column.items()}
        factors[own] = jnp.where(sub > at, factors[own], 0.0)
        for j in range(step + 1, planes):
            entry = jnp.broadcast_to(column[j // 8][j % 8 : j % 8 + 1], (8, LANES))
            for g in columns[j]:
                columns[j][g] = columns[j][g] - factors[g] * entry
        pivot_row = jnp.broadcast_to(state[own][at : at + 1], (8, LANES))
        for g in range(own, groups):
            state[g] = state[g] - factors[g] * pivot_row
    return jnp.concatenate([state[g] * scale[g] for g in range(groups)], axis=0)


def finish_kernel(pixel_count, inner_second, outer_second, edges, parts, basis, factor):
    planes = factor.shape[0]
    _, rows, width = basis.shape
    at_row = lax.broadcasted_iota(jnp.int32, (planes, planes), 0)
    at_col = lax.broadcasted_iota(jnp.int32, (planes, planes), 1)
    block = tree_sum([parts[at] for at in range(parts.shape[0])]) / pixel_count
    block = [block[:, at * LANES : (at + 1) * LANES] for at in range(9)]
    mixed, diagonal = jnp.concatenate(block[:8], axis=0), block[8][:, :planes]
    mixed = jnp.concatenate([mixed[:, at * planes : (at + 1) * planes] for at in range(LANES // planes)], axis=0)
    flipped = mixed.T
    first = jnp.where(at_row >= at_col, mixed, flipped)
    second_gram = jnp.where(at_row < at_col, mixed, jnp.where(at_row > at_col, flipped, diagonal))
    state = eliminate([first, second_gram], planes)
    first_inverse = state[:, planes : 2 * planes]
    product_upper = jnp.where(at_col >= at_row, state[:, 2 * planes : 3 * planes], 0.0)
    product_inverse = jnp.where(at_col <= at_row, state[:, 3 * planes :], 0.0)
    factor[...] = jnp.where(at_col >= at_row, gram_of(product_upper, first_inverse), 0.0)
    high, middle, low = split(product_inverse)
    left_side = jnp.concatenate([high, high, middle, high, low, middle], axis=1)

    def solved(high, middle, low):
        right_side = jnp.concatenate([high, middle, high, low, high, middle], axis=0)
        return jnp.dot(left_side, right_side, preferred_element_type=jnp.float32)

    lane = lax.broadcasted_iota(jnp.int32, (1, LANES), 1)
    outer = solved(*split(edges[...]))
    for row in range(rows):
        if 2 <= row < rows - 2:
            held, spot = inner_second, row - 2
        else:
            held, spot = outer_second, row if row < 2 else row - rows + 4
        value = solved(*(held[spot, at * planes : (at + 1) * planes] for at in range(3)))
        place = PITCH * (row + 2)
        low_end = pltpu.roll(outer[:, :LANES], LANES - (place + 2), 1)
        high_end = pltpu.roll(outer[:, LANES:], (LANES - 2 - (place + PITCH - 4)) % LANES, 1)
        basis[:, row, :LANES] = jnp.where(lane < 2, low_end, value[:, :LANES])
        basis[:, row, LANES : width - LANES] = value[:, LANES : width - LANES]
        basis[:, row, width - LANES :] = jnp.where(lane >= LANES - 2, high_end, value[:, width - LANES :])


def tree_sum(parts):
    while len(parts) > 1:
        parts = [sum(parts[at + 1 : at + 2], parts[at]) for at in range(0, len(parts), 2)]
    return parts[0]


def swap(value, axis, pairing):
    names = ("sec", "row", "col")
    shape = [lax.axis_size(name) for name in names]
    at = names.index(axis)

    def number(place):
        return (place[0] * shape[1] + place[1]) * shape[2] + place[2]

    pairs = []
    for place in itertools.product(*(range(extent) for extent in shape)):
        partner = list(place)
        partner[at] += 1 if place[at] % 2 != pairing else -1
        if not 0 <= partner[at] < shape[at]:
            partner[at] = place[at]
            partner[at - 1] ^= 1
        pairs.append((number(place), number(partner)))
    return lax.ppermute(value, names, pairs)


def on_device(sketch, weights):
    planes, rows, width = sketch.shape
    group = lax.axis_size("row") * lax.axis_size("col")
    side = f32(planes + 8, LANES)
    by_row, weights_by_row, left, right, *messages = call(
        pack_rows_kernel,
        [f32(rows, planes, width), f32(rows, 8, width), side, side]
        + [f32(16, LANES)] * 2
        + [f32(2 * planes + 8, width)] * 2,
        pltpu.with_memory_space_constraint(sketch, pltpu.HBM),
        pltpu.with_memory_space_constraint(weights, pltpu.HBM),
        memory=pltpu.HBM,
        scratch=[
            pltpu.VMEM(sketch.shape, jnp.float32),
            pltpu.VMEM(weights.shape, jnp.float32),
            pltpu.SemaphoreType.DMA((2,)),
        ],
    )
    corners = [swap(message, "row", pairing) for pairing, message in enumerate(messages[:2])]
    from_rows = [swap(message, "row", pairing) for pairing, message in enumerate(messages[2:])]
    left, right, *messages = call(
        functools.partial(strips_kernel, rows), [side, side] + [f32(16, LANES)] * 2, left, right, *corners, cost=pl.CostEstimate(flops=2000000000, bytes_accessed=4000000, transcendentals=0)
    )
    from_cols = [swap(message, "col", pairing) for pairing, message in enumerate(messages)]
    parts_of = functools.partial(jax.ShapeDtypeStruct, dtype=jnp.bfloat16)
    sums = f32(planes, 2 * planes)
    middle, inner_second, inner_grams = call(
        inner_rows_kernel,
        [f32(rows - 2, planes, width), parts_of((rows - 4, 3 * planes, width)), sums],
        by_row,
        weights_by_row,
    )
    outer_second, early_grams = call(
        outer_rows_kernel,
        [parts_of((4, 3 * planes, width)), sums],
        by_row,
        weights_by_row,
        *from_rows,
        middle,
        inner_grams,
        scratch=[pltpu.VMEM((4, planes, width), jnp.float32)],
    )
    grams, edges = call(
        functools.partial(late_kernel, rows),
        [f32(group, 1, 9 * LANES), f32(planes, 2 * LANES)],
        left,
        right,
        *from_cols,
        early_grams,
    )
    parts = lax.all_to_all(grams, ("row", "col"), 0, 0, tiled=True)
    return call(
        functools.partial(finish_kernel, float(rows * width * group)),
        [f32(planes, rows, width), f32(planes, planes)],
        inner_second,
        outer_second,
        edges,
        parts,
    )


def solution(mesh):
    return jax.shard_map(
        on_device,
        mesh=mesh,
        in_specs=(P(None, ("sec", "row"), "col"), P(None, ("sec", "row"), "col")),
        out_specs=(P(None, ("sec", "row"), "col"), P("sec", None)),
        check_vma=False,
    )
```

```python
import functools
import itertools

import jax
import jax.numpy as jnp
from jax import lax
from jax.experimental import pallas as pl
from jax.experimental.pallas import tpu as pltpu
from jax.sharding import PartitionSpec as P

NEIGHBOURS = ((-1, -1), (-1, 0), (-1, 1), (0, -1), (0, 1), (1, -1), (1, 0), (1, 1))
LANES = 128
PITCH = 8
PIECE = 4
HIGHEST = lax.Precision.HIGHEST


def call(kernel, out_shapes, *operands, memory=pltpu.VMEM, out_memory=pltpu.VMEM, scratch=(), cost=None):
    return pl.pallas_call(
        kernel,
        out_shape=out_shapes,
        in_specs=[pl.BlockSpec(memory_space=memory)] * len(operands),
        out_specs=[pl.BlockSpec(memory_space=out_memory)] * len(out_shapes),
        scratch_shapes=scratch,
        cost_estimate=cost,
        compiler_params=pltpu.CompilerParams(vmem_limit_bytes=40 * 1024 * 1024),
    )(*operands)


def f32(*shape):
    return jax.ShapeDtypeStruct(shape, jnp.float32)


def sides_of(axis):
    place = lax.axis_index(axis)
    return place % 2 == 1, place > 0, place < lax.axis_size(axis) - 1


def in_pieces(pairs, semaphores):
    copies = []
    for source, target in pairs:
        for start in range(0, source.shape[0], PIECE):
            planes = pl.ds(start, PIECE)
            copies.append(pltpu.make_async_copy(source.at[planes], target.at[planes], semaphores.at[len(copies)]))
    return copies


def pack_rows_kernel(sketch, weights, by_row, weights_by_row, left, right, *rest):
    corner_messages, bulk_messages = rest[:2], rest[2:4]
    tile, weight_tile, arrived = rest[4:]
    copies = in_pieces([(sketch, tile), (weights, weight_tile)], arrived)
    for copy in copies:
        copy.start()
    for copy in copies:
        copy.wait()
    rows, planes, width = by_row.shape
    odd_row, _, _ = sides_of("row")
    lane = lax.broadcasted_iota(jnp.int32, (1, LANES), 1)
    own = PITCH - 2
    for target, start, low, at in ((left, 0, 2, 0), (right, width - LANES, 0, LANES - own)):
        total = None
        for row in range(rows):
            place = PITCH * (row + 2) + low
            window = slice(start, start + LANES)
            value = jnp.concatenate([tile[:, row, window], weight_tile[:, row, window]], axis=0)
            moved = rolled(value, place - at)
            moved = jnp.where((lane >= place) & (lane < place + own), moved, 0.0)
            total = moved if total is None else total + moved
        target[...] = total
    pair = 2 * PITCH
    for message, up in zip(corner_messages, (odd_row, jnp.logical_not(odd_row))):
        pieces = []
        for group in range(planes // 8 + 1):
            piece = None
            for side, strip in enumerate((left, right)):
                target = (2 * group + side) * pair if group < planes // 8 else side * pair
                value = strip[8 * group : 8 * (group + 1)]
                moved = jnp.where(up, rolled(value, target - PITCH * rows), rolled(value, target - 2 * PITCH))
                moved = jnp.where(lane // pair == target // pair, moved, 0.0)
                piece = moved if piece is None else piece + moved
            pieces.append(piece)
        message[:8] = functools.reduce(jnp.add, pieces[:-1])
        message[8:] = pieces[-1]
    for row in range(rows):
        weights_by_row[row] = weight_tile[:, row, :]
        by_row[row] = tile[:, row, :]
    for message, up in zip(bulk_messages, (odd_row, jnp.logical_not(odd_row))):
        start = jnp.where(up, rows - 2, 0)
        for slot in range(2):
            message[slot * planes : (slot + 1) * planes] = by_row[start + slot]
        message[2 * planes :] = weights_by_row[jnp.where(up, rows - 1, 0)]


def strips_kernel(rows, own_left, own_right, first_message, second_message, left, right, *col_messages):
    planes = own_left.shape[0] - 8
    odd_row, has_below, has_above = sides_of("row")
    odd_col, _, _ = sides_of("col")
    one, other = first_message[...], second_message[...]
    lane = lax.broadcasted_iota(jnp.int32, (1, LANES), 1)
    pair = 2 * PITCH
    halos = (
        (jnp.where(has_below, jnp.where(odd_row, other, one), 0.0), 0),
        (jnp.where(has_above, jnp.where(odd_row, one, other), 0.0), PITCH * (rows + 2)),
    )
    for side, (strip, target) in enumerate(((own_left, left), (own_right, right))):
        total = strip[...]
        for halo, place in halos:
            pieces = [rolled(halo[:8], place - (2 * group + side) * pair) for group in range(planes // 8)]
            pieces.append(rolled(halo[8:], place - side * pair))
            total = total + jnp.where(lane // pair == place // pair, jnp.concatenate(pieces, axis=0), 0.0)
        target[...] = total
    to_left, to_right = folded(left[...], 2), folded(right[...], PITCH - 4)
    for message, up in zip(col_messages, (odd_col, jnp.logical_not(odd_col))):
        message[...] = jnp.where(up, to_right, to_left)


def folded(strip, spot):
    lane = lax.broadcasted_iota(jnp.int32, (1, LANES), 1)
    groups = strip.shape[0] // 8
    pieces = []
    for group in range(groups):
        target = 2 * group if group < groups - 1 else 0
        moved = rolled(strip[8 * group : 8 * (group + 1)], target - spot)
        pieces.append(jnp.where((lane % PITCH) // 2 == target // 2, moved, 0.0))
    return jnp.concatenate([functools.reduce(jnp.add, pieces[:-1]), pieces[-1]], axis=0)


def unfolded(message, spot, planes):
    lane = lax.broadcasted_iota(jnp.int32, (1, LANES), 1)
    pieces = [rolled(message[:8], spot - 2 * group) for group in range(planes // 8)] + [rolled(message[8:], spot)]
    return jnp.where((lane % PITCH) // 2 == spot // 2, jnp.concatenate(pieces, axis=0), 0.0)


def rolled(value, shift):
    return pltpu.roll(value, shift % LANES, 1) if shift % LANES else value


def apply_operator(rows3, weight_rows):
    width = rows3[1].shape[1]
    degree = jnp.sum(weight_rows, axis=0, keepdims=True)
    total = degree * rows3[1]
    sides = {-1: None, 1: None}
    for position, (up, across) in enumerate(NEIGHBOURS):
        weight = weight_rows[position : position + 1]
        value = rows3[up + 1]
        if across == 0:
            total = total + weight * value
        else:
            shifted = pltpu.roll(weight_rows, across % width, 1)[position : position + 1]
            term = shifted * value
            sides[across] = term if sides[across] is None else sides[across] + term
    for across, value in sides.items():
        total = total + pltpu.roll(value, (-across) % width, 1)
    return total


def gram_of(value, other):
    return lax.dot_general(
        value, other, (((1,), (1,)), ((), ())), precision=HIGHEST, preferred_element_type=jnp.float32
    )


def split(value):
    high = value.astype(jnp.bfloat16)
    rest = value - high.astype(jnp.float32)
    middle = rest.astype(jnp.bfloat16)
    low = (rest - middle.astype(jnp.float32)).astype(jnp.bfloat16)
    return high, middle, low


def images_of(planes, width, middle, weights, wanted, second, gram):
    for at, row in enumerate(wanted):
        image = apply_operator([middle(row - 1), middle(row), middle(row + 1)], weights(row))
        for place, part in enumerate(split(image)):
            second[at, place * planes : (place + 1) * planes] = part
        gram = gram + gram_of(inner_only(image), image)
    return gram


def inner_only(value):
    width = value.shape[1]
    col = lax.broadcasted_iota(jnp.int32, (1, width), 1)
    return jnp.where((col >= 2) & (col < width - 2), value, 0.0)


def inner_rows_kernel(by_row, weights_by_row, middle, second, grams):
    rows, planes, width = by_row.shape
    first = jnp.zeros((planes, planes), jnp.float32)
    for row in range(1, rows - 1):
        image = apply_operator([by_row[row - 1], by_row[row], by_row[row + 1]], weights_by_row[row])
        middle[row - 1] = image
        first = first + gram_of(inner_only(image), image)
    grams[:, :planes] = first
    grams[:, planes:] = images_of(
        planes,
        width,
        lambda row: middle[row - 1],
        lambda row: weights_by_row[row],
        range(2, rows - 2),
        second,
        jnp.zeros((planes, planes), jnp.float32),
    )


def outer_rows_kernel(
    by_row, weights_by_row, first_message, second_message, middle, inner_grams, second, grams, outer
):
    rows, planes, width = by_row.shape
    odd_row, has_below, has_above = sides_of("row")
    one, other = first_message[...], second_message[...]
    below = jnp.where(has_below, jnp.where(odd_row, other, one), 0.0)
    above = jnp.where(has_above, jnp.where(odd_row, one, other), 0.0)

    def field(row):
        if 0 <= row < rows:
            return by_row[row]
        at = (row + 2 if row < 0 else row - rows) * planes
        return (below if row < 0 else above)[at : at + planes]

    def weights(row):
        if 0 <= row < rows:
            return weights_by_row[row]
        return (below if row < 0 else above)[2 * planes :]

    first = inner_grams[:, :planes]
    places = (-1, 0, rows - 1, rows)
    for at, row in enumerate(places):
        image = apply_operator([field(row - 1), field(row), field(row + 1)], weights(row))
        outer[at] = image
        if 0 <= row < rows:
            first = first + gram_of(inner_only(image), image)
    grams[:, :planes] = first
    grams[:, planes:] = images_of(
        planes,
        width,
        lambda row: outer[places.index(row)] if row in places else middle[row - 1],
        weights,
        (0, 1, rows - 2, rows - 1),
        second,
        inner_grams[:, planes:],
    )


def apply_on_strip(values, weights):
    total = jnp.sum(weights, axis=0, keepdims=True) * values
    for position, (up, across) in enumerate(NEIGHBOURS):
        moved = pltpu.roll(values, (-PITCH * up - across) % LANES, 1)
        total = total + weights[position : position + 1] * moved
    return total


def late_kernel(rows, left, right, first_message, second_message, early_grams, grams, edges):
    planes = early_grams.shape[0]
    odd_col, has_left, has_right = sides_of("col")
    one, other = first_message[...], second_message[...]
    lane = lax.broadcasted_iota(jnp.int32, (1, LANES), 1)
    spot, row = lane % PITCH, lane // PITCH
    strips, masks = [], []
    for side, (strip, present, halo) in enumerate(
        ((left, has_left, jnp.where(odd_col, other, one)), (right, has_right, jnp.where(odd_col, one, other)))
    ):
        strips.append(strip[...] + jnp.where(present, unfolded(halo, side * (PITCH - 2), planes), 0.0))
        low = 2 if side == 0 else PITCH - 4
        masks.append((spot >= low) & (spot < low + 2) & (row >= 2) & (row < rows + 2))
    values = [strip[:planes] for strip in strips]
    gram = []
    for at in range(2):
        values = [apply_on_strip(value, strip[planes:]) for value, strip in zip(values, strips)]
        kept = jnp.concatenate([jnp.where(mask, value, 0.0) for mask, value in zip(masks, values)], axis=1)
        both = jnp.concatenate(values, axis=1)
        gram.append(early_grams[:, at * planes : (at + 1) * planes] + gram_of(kept, both))
    edges[...] = both
    at_row = lax.broadcasted_iota(jnp.int32, (planes, planes), 0)
    at_col = lax.broadcasted_iota(jnp.int32, (planes, planes), 1)
    mixed = jnp.where(at_row >= at_col, gram[0], gram[1])
    diagonal = jnp.sum(jnp.where(at_row == at_col, gram[1], 0.0), axis=0, keepdims=True)
    block = jnp.concatenate([mixed[8 * g : 8 * (g + 1)] for g in range(planes // 8)], axis=1)
    last = jnp.concatenate([diagonal] * (LANES // planes), axis=1)
    for target in range(grams.shape[0]):
        for at in range(8):
            grams[target, :, at * LANES : (at + 1) * LANES] = block[at : at + 1]
        grams[target, :, 8 * LANES :] = last


def eliminate(grams, planes):
    lane = lax.broadcasted_iota(jnp.int32, (8, LANES), 1)
    sub = lax.broadcasted_iota(jnp.int32, (8, LANES), 0)
    first_half = lane < 2 * planes
    groups = planes // 8
    sources = [[gram[8 * g : 8 * (g + 1)] for g in range(groups)] for gram in grams]
    state = []
    for g in range(groups):
        unit = jnp.where(sub + 8 * g == lane % (2 * planes) - planes, 1.0, 0.0)
        unit = unit[:, planes : 2 * planes]
        state.append(jnp.concatenate([sources[0][g], unit, sources[1][g], unit], axis=1))
    columns = []
    for j in range(planes):
        columns.append(
            {
                g: jnp.where(
                    first_half,
                    jnp.broadcast_to(sources[0][g][:, j : j + 1], (8, LANES)),
                    jnp.broadcast_to(sources[1][g][:, j : j + 1], (8, LANES)),
                )
                for g in range(j // 8, groups)
            }
        )
    scale = [jnp.ones((8, LANES), jnp.float32)] * groups
    for step in range(planes):
        own, at = step // 8, step % 8
        column = columns[step]
        root = lax.rsqrt(jnp.broadcast_to(column[own][at : at + 1], (8, LANES)))
        inverse = root * root
        scale[own] = jnp.where(sub == at, root, scale[own])
        factors = {g: value * inverse for g, value in column.items()}
        factors[own] = jnp.where(sub > at, factors[own], 0.0)
        for j in range(step + 1, planes):
            entry = jnp.broadcast_to(column[j // 8][j % 8 : j % 8 + 1], (8, LANES))
            for g in columns[j]:
                columns[j][g] = columns[j][g] - factors[g] * entry
        pivot_row = jnp.broadcast_to(state[own][at : at + 1], (8, LANES))
        for g in range(own, groups):
            state[g] = state[g] - factors[g] * pivot_row
    return jnp.concatenate([state[g] * scale[g] for g in range(groups)], axis=0)


def finish_kernel(
    pixel_count, inner_second, outer_second, edges, parts, basis_out, factor_out, basis, factor, written
):
    planes, rows, width = basis.shape
    at_row = lax.broadcasted_iota(jnp.int32, (planes, planes), 0)
    at_col = lax.broadcasted_iota(jnp.int32, (planes, planes), 1)
    block = tree_sum([parts[at] for at in range(parts.shape[0])]) / pixel_count
    block = [block[:, at * LANES : (at + 1) * LANES] for at in range(9)]
    mixed, diagonal = jnp.concatenate(block[:8], axis=0), block[8][:, :planes]
    mixed = jnp.concatenate([mixed[:, at * planes : (at + 1) * planes] for at in range(LANES // planes)], axis=0)
    flipped = mixed.T
    first = jnp.where(at_row >= at_col, mixed, flipped)
    second_gram = jnp.where(at_row < at_col, mixed, jnp.where(at_row > at_col, flipped, diagonal))
    state = eliminate([first, second_gram], planes)
    first_inverse = state[:, planes : 2 * planes]
    product_upper = jnp.where(at_col >= at_row, state[:, 2 * planes : 3 * planes], 0.0)
    product_inverse = jnp.where(at_col <= at_row, state[:, 3 * planes :], 0.0)
    factor[...] = jnp.where(at_col >= at_row, gram_of(product_upper, first_inverse), 0.0)
    copies = [pltpu.make_async_copy(factor, factor_out, written.at[0])]
    copies[0].start()
    high, middle, low = split(product_inverse)
    left_side = jnp.concatenate([high, high, middle, high, low, middle], axis=1)

    def solved(high, middle, low):
        right_side = jnp.concatenate([high, middle, high, low, high, middle], axis=0)
        return jnp.dot(left_side, right_side, preferred_element_type=jnp.float32)

    lane = lax.broadcasted_iota(jnp.int32, (1, LANES), 1)
    outer = solved(*split(edges[...]))
    half = width // 2
    for side in range(2):
        window = pl.ds(side * half, half)
        for row in range(rows):
            if 2 <= row < rows - 2:
                held, spot = inner_second, row - 2
            else:
                held, spot = outer_second, row if row < 2 else row - rows + 4
            value = solved(*(held[spot, at * planes : (at + 1) * planes, window] for at in range(3)))
            place = PITCH * (row + 2)
            if side == 0:
                ends = rolled(outer[:, :LANES], -(place + 2))
                basis[:, row, :LANES] = jnp.where(lane < 2, ends, value[:, :LANES])
                basis[:, row, LANES:half] = value[:, LANES:]
            else:
                ends = rolled(outer[:, LANES:], LANES - 2 - (place + PITCH - 4))
                basis[:, row, half : width - LANES] = value[:, : half - LANES]
                basis[:, row, width - LANES :] = jnp.where(lane >= LANES - 2, ends, value[:, half - LANES :])
        for start in range(0, planes, 2 * PIECE):
            some = pl.ds(start, 2 * PIECE)
            copies.append(
                pltpu.make_async_copy(
                    basis.at[some, :, window], basis_out.at[some, :, window], written.at[len(copies)]
                )
            )
            copies[-1].start()
    for copy in copies:
        copy.wait()


def tree_sum(parts):
    while len(parts) > 1:
        parts = [sum(parts[at + 1 : at + 2], parts[at]) for at in range(0, len(parts), 2)]
    return parts[0]


def swap(value, axis, pairing):
    names = ("sec", "row", "col")
    shape = [lax.axis_size(name) for name in names]
    at = names.index(axis)

    def number(place):
        return (place[0] * shape[1] + place[1]) * shape[2] + place[2]

    pairs = []
    for place in itertools.product(*(range(extent) for extent in shape)):
        partner = list(place)
        partner[at] += 1 if place[at] % 2 != pairing else -1
        if not 0 <= partner[at] < shape[at]:
            partner[at] = place[at]
            partner[at - 1] ^= 1
        pairs.append((number(place), number(partner)))
    return lax.ppermute(value, names, pairs)


def on_device(sketch, weights):
    planes, rows, width = sketch.shape
    group = lax.axis_size("row") * lax.axis_size("col")
    side = f32(planes + 8, LANES)
    by_row, weights_by_row, left, right, *messages = call(
        pack_rows_kernel,
        [f32(rows, planes, width), f32(rows, 8, width), side, side]
        + [f32(16, LANES)] * 2
        + [f32(2 * planes + 8, width)] * 2,
        pltpu.with_memory_space_constraint(sketch, pltpu.HBM),
        pltpu.with_memory_space_constraint(weights, pltpu.HBM),
        memory=pltpu.HBM,
        scratch=[
            pltpu.VMEM(sketch.shape, jnp.float32),
            pltpu.VMEM(weights.shape, jnp.float32),
            pltpu.SemaphoreType.DMA(((planes + 8) // PIECE,)),
        ],
    )
    corners = [swap(message, "row", pairing) for pairing, message in enumerate(messages[:2])]
    from_rows = [swap(message, "row", pairing) for pairing, message in enumerate(messages[2:])]
    left, right, *messages = call(
        functools.partial(strips_kernel, rows), [side, side] + [f32(16, LANES)] * 2, left, right, *corners, cost=pl.CostEstimate(flops=2000000000, bytes_accessed=4000000, transcendentals=0)
    )
    from_cols = [swap(message, "col", pairing) for pairing, message in enumerate(messages)]
    parts_of = functools.partial(jax.ShapeDtypeStruct, dtype=jnp.bfloat16)
    sums = f32(planes, 2 * planes)
    middle, inner_second, inner_grams = call(
        inner_rows_kernel,
        [f32(rows - 2, planes, width), parts_of((rows - 4, 3 * planes, width)), sums],
        by_row,
        weights_by_row,
    )
    outer_second, early_grams = call(
        outer_rows_kernel,
        [parts_of((4, 3 * planes, width)), sums],
        by_row,
        weights_by_row,
        *from_rows,
        middle,
        inner_grams,
        scratch=[pltpu.VMEM((4, planes, width), jnp.float32)],
    )
    grams, edges = call(
        functools.partial(late_kernel, rows),
        [f32(group, 1, 9 * LANES), f32(planes, 2 * LANES)],
        left,
        right,
        *from_cols,
        early_grams,
    )
    parts = lax.all_to_all(grams, ("row", "col"), 0, 0, tiled=True)
    return call(
        functools.partial(finish_kernel, float(rows * width * group)),
        [f32(planes, rows, width), f32(planes, planes)],
        inner_second,
        outer_second,
        edges,
        parts,
        out_memory=pl.ANY,
        scratch=[
            pltpu.VMEM(sketch.shape, jnp.float32),
            pltpu.VMEM((planes, planes), jnp.float32),
            pltpu.SemaphoreType.DMA((planes // PIECE + 1,)),
        ],
    )


def solution(mesh):
    return jax.shard_map(
        on_device,
        mesh=mesh,
        in_specs=(P(None, ("sec", "row"), "col"), P(None, ("sec", "row"), "col")),
        out_specs=(P(None, ("sec", "row"), "col"), P("sec", None)),
        check_vma=False,
    )
```

```python
import functools
import itertools

import jax
import jax.numpy as jnp
from jax import lax
from jax.experimental import pallas as pl
from jax.experimental.pallas import tpu as pltpu
from jax.sharding import PartitionSpec as P

NEIGHBOURS = ((-1, -1), (-1, 0), (-1, 1), (0, -1), (0, 1), (1, -1), (1, 0), (1, 1))
LANES = 128
PITCH = 8
HIGHEST = lax.Precision.HIGHEST


def call(kernel, out_shapes, *operands, memory=pltpu.VMEM, scratch=(), cost=None):
    return pl.pallas_call(
        kernel,
        out_shape=out_shapes,
        in_specs=[pl.BlockSpec(memory_space=memory)] * len(operands),
        out_specs=[pl.BlockSpec(memory_space=pltpu.VMEM)] * len(out_shapes),
        scratch_shapes=scratch,
        cost_estimate=cost,
        compiler_params=pltpu.CompilerParams(vmem_limit_bytes=40 * 1024 * 1024),
    )(*operands)


def f32(*shape):
    return jax.ShapeDtypeStruct(shape, jnp.float32)


def sides_of(axis):
    place = lax.axis_index(axis)
    return place % 2 == 1, place > 0, place < lax.axis_size(axis) - 1


def pack_rows_kernel(sketch, weights, by_row, weights_by_row, left, right, *rest):
    corner_messages, bulk_messages = rest[:2], rest[2:4]
    tile, weight_tile, arrived = rest[4:]
    copies = [
        pltpu.make_async_copy(sketch, tile, arrived.at[0]),
        pltpu.make_async_copy(weights, weight_tile, arrived.at[1]),
    ]
    for copy in copies:
        copy.start()
    for copy in copies:
        copy.wait()
    rows, planes, width = by_row.shape
    odd_row, _, _ = sides_of("row")
    lane = lax.broadcasted_iota(jnp.int32, (1, LANES), 1)
    own = PITCH - 2
    for target, start, low, at in ((left, 0, 2, 0), (right, width - LANES, 0, LANES - own)):
        total = None
        for row in range(rows):
            place = PITCH * (row + 2) + low
            window = slice(start, start + LANES)
            value = jnp.concatenate([tile[:, row, window], weight_tile[:, row, window]], axis=0)
            moved = rolled(value, place - at)
            moved = jnp.where((lane >= place) & (lane < place + own), moved, 0.0)
            total = moved if total is None else total + moved
        target[...] = total
    pair = 2 * PITCH
    for message, up in zip(corner_messages, (odd_row, jnp.logical_not(odd_row))):
        pieces = []
        for group in range(planes // 8 + 1):
            piece = None
            for side, strip in enumerate((left, right)):
                target = (2 * group + side) * pair if group < planes // 8 else side * pair
                value = strip[8 * group : 8 * (group + 1)]
                moved = jnp.where(up, rolled(value, target - PITCH * rows), rolled(value, target - 2 * PITCH))
                moved = jnp.where(lane // pair == target // pair, moved, 0.0)
                piece = moved if piece is None else piece + moved
            pieces.append(piece)
        message[:8] = functools.reduce(jnp.add, pieces[:-1])
        message[8:] = pieces[-1]
    for row in range(rows):
        weights_by_row[row] = weight_tile[:, row, :]
        by_row[row] = tile[:, row, :]
    for message, up in zip(bulk_messages, (odd_row, jnp.logical_not(odd_row))):
        start = jnp.where(up, rows - 2, 0)
        for slot in range(2):
            message[slot * planes : (slot + 1) * planes] = by_row[start + slot]
        message[2 * planes :] = weights_by_row[jnp.where(up, rows - 1, 0)]


def strips_kernel(rows, own_left, own_right, first_message, second_message, left, right, *col_messages):
    planes = own_left.shape[0] - 8
    odd_row, has_below, has_above = sides_of("row")
    odd_col, _, _ = sides_of("col")
    one, other = first_message[...], second_message[...]
    lane = lax.broadcasted_iota(jnp.int32, (1, LANES), 1)
    pair = 2 * PITCH
    halos = (
        (jnp.where(has_below, jnp.where(odd_row, other, one), 0.0), 0),
        (jnp.where(has_above, jnp.where(odd_row, one, other), 0.0), PITCH * (rows + 2)),
    )
    for side, (strip, target) in enumerate(((own_left, left), (own_right, right))):
        total = strip[...]
        for halo, place in halos:
            pieces = [rolled(halo[:8], place - (2 * group + side) * pair) for group in range(planes // 8)]
            pieces.append(rolled(halo[8:], place - side * pair))
            total = total + jnp.where(lane // pair == place // pair, jnp.concatenate(pieces, axis=0), 0.0)
        target[...] = total
    to_left, to_right = folded(left[...], 2), folded(right[...], PITCH - 4)
    for message, up in zip(col_messages, (odd_col, jnp.logical_not(odd_col))):
        message[...] = jnp.where(up, to_right, to_left)


def folded(strip, spot):
    lane = lax.broadcasted_iota(jnp.int32, (1, LANES), 1)
    groups = strip.shape[0] // 8
    pieces = []
    for group in range(groups):
        target = 2 * group if group < groups - 1 else 0
        moved = rolled(strip[8 * group : 8 * (group + 1)], target - spot)
        pieces.append(jnp.where((lane % PITCH) // 2 == target // 2, moved, 0.0))
    return jnp.concatenate([functools.reduce(jnp.add, pieces[:-1]), pieces[-1]], axis=0)


def unfolded(message, spot, planes):
    lane = lax.broadcasted_iota(jnp.int32, (1, LANES), 1)
    pieces = [rolled(message[:8], spot - 2 * group) for group in range(planes // 8)] + [rolled(message[8:], spot)]
    return jnp.where((lane % PITCH) // 2 == spot // 2, jnp.concatenate(pieces, axis=0), 0.0)


def rolled(value, shift):
    return pltpu.roll(value, shift % LANES, 1) if shift % LANES else value


def apply_operator(rows3, weight_rows):
    width = rows3[1].shape[1]
    total = jnp.sum(weight_rows, axis=0, keepdims=True) * rows3[1]
    for across in (0, -1, 1):
        moved = pltpu.roll(weight_rows, across % width, 1) if across else weight_rows
        terms = [
            moved[position : position + 1] * rows3[up + 1]
            for position, (up, side) in enumerate(NEIGHBOURS)
            if side == across
        ]
        part = functools.reduce(jnp.add, terms)
        total = total + (pltpu.roll(part, -across % width, 1) if across else part)
    return total


def gram_of(value, other):
    return lax.dot_general(
        value, other, (((1,), (1,)), ((), ())), precision=HIGHEST, preferred_element_type=jnp.float32
    )


def split(value):
    high = value.astype(jnp.bfloat16)
    rest = value - high.astype(jnp.float32)
    middle = rest.astype(jnp.bfloat16)
    low = (rest - middle.astype(jnp.float32)).astype(jnp.bfloat16)
    return high, middle, low


def inner_parts(image):
    width = image.shape[1]
    lane = lax.broadcasted_iota(jnp.int32, (1, LANES), 1)
    kept = [
        jnp.where(lane >= 2, image[:, :LANES], 0.0),
        image[:, LANES : width - LANES],
        jnp.where(lane < LANES - 2, image[:, width - LANES :], 0.0),
    ]
    return jnp.concatenate(split(jnp.concatenate(kept, axis=1)), axis=0)


def products_of(parts):
    return lax.dot_general(parts, parts, (((1,), (1,)), ((), ())), preferred_element_type=jnp.float32)


def images_of(middle, weights, wanted, second, products):
    for at, row in enumerate(wanted):
        parts = inner_parts(apply_operator([middle(row - 1), middle(row), middle(row + 1)], weights(row)))
        second[at] = parts
        products = products + products_of(parts)
    return products


def inner_rows_kernel(by_row, weights_by_row, middle, second, first_products, second_products):
    rows = by_row.shape[0]
    products = jnp.zeros(first_products.shape, jnp.float32)
    for row in range(1, rows - 1):
        image = apply_operator([by_row[row - 1], by_row[row], by_row[row + 1]], weights_by_row[row])
        middle[row - 1] = image
        products = products + products_of(inner_parts(image))
    first_products[...] = products
    second_products[...] = images_of(
        lambda row: middle[row - 1],
        lambda row: weights_by_row[row],
        range(2, rows - 2),
        second,
        jnp.zeros(second_products.shape, jnp.float32),
    )


def outer_rows_kernel(
    by_row,
    weights_by_row,
    first_message,
    second_message,
    middle,
    first_products,
    second_products,
    second,
    grams,
    outer,
):
    rows, planes, _ = by_row.shape
    odd_row, has_below, has_above = sides_of("row")
    one, other = first_message[...], second_message[...]
    below = jnp.where(has_below, jnp.where(odd_row, other, one), 0.0)
    above = jnp.where(has_above, jnp.where(odd_row, one, other), 0.0)

    def field(row):
        if 0 <= row < rows:
            return by_row[row]
        at = (row + 2 if row < 0 else row - rows) * planes
        return (below if row < 0 else above)[at : at + planes]

    def weights(row):
        if 0 <= row < rows:
            return weights_by_row[row]
        return (below if row < 0 else above)[2 * planes :]

    products = first_products[...]
    places = (-1, 0, rows - 1, rows)
    for at, row in enumerate(places):
        image = apply_operator([field(row - 1), field(row), field(row + 1)], weights(row))
        outer[at] = image
        if 0 <= row < rows:
            products = products + products_of(inner_parts(image))
    both = [products]
    both.append(
        images_of(
            lambda row: outer[places.index(row)] if row in places else middle[row - 1],
            weights,
            (0, 1, rows - 2, rows - 1),
            second,
            second_products[...],
        )
    )
    for at, products in enumerate(both):
        some = products[:planes] + products[planes : 2 * planes] + products[2 * planes :]
        total = some[:, :planes] + some[:, planes : 2 * planes] + some[:, 2 * planes :]
        grams[:, at * planes : (at + 1) * planes] = total


def apply_on_strip(values, weights):
    total = jnp.sum(weights, axis=0, keepdims=True) * values
    for position, (up, across) in enumerate(NEIGHBOURS):
        moved = pltpu.roll(values, (-PITCH * up - across) % LANES, 1)
        total = total + weights[position : position + 1] * moved
    return total


def late_kernel(rows, left, right, first_message, second_message, early_grams, grams, edges):
    planes = early_grams.shape[0]
    odd_col, has_left, has_right = sides_of("col")
    one, other = first_message[...], second_message[...]
    lane = lax.broadcasted_iota(jnp.int32, (1, LANES), 1)
    spot, row = lane % PITCH, lane // PITCH
    strips, masks = [], []
    for side, (strip, present, halo) in enumerate(
        ((left, has_left, jnp.where(odd_col, other, one)), (right, has_right, jnp.where(odd_col, one, other)))
    ):
        strips.append(strip[...] + jnp.where(present, unfolded(halo, side * (PITCH - 2), planes), 0.0))
        low = 2 if side == 0 else PITCH - 4
        masks.append((spot >= low) & (spot < low + 2) & (row >= 2) & (row < rows + 2))
    values = [strip[:planes] for strip in strips]
    gram = []
    for at in range(2):
        values = [apply_on_strip(value, strip[planes:]) for value, strip in zip(values, strips)]
        kept = jnp.concatenate([jnp.where(mask, value, 0.0) for mask, value in zip(masks, values)], axis=1)
        both = jnp.concatenate(values, axis=1)
        gram.append(early_grams[:, at * planes : (at + 1) * planes] + gram_of(kept, both))
    edges[...] = both
    at_row = lax.broadcasted_iota(jnp.int32, (planes, planes), 0)
    at_col = lax.broadcasted_iota(jnp.int32, (planes, planes), 1)
    mixed = jnp.where(at_row >= at_col, gram[0], gram[1])
    diagonal = jnp.sum(jnp.where(at_row == at_col, gram[1], 0.0), axis=0, keepdims=True)
    block = jnp.concatenate([mixed[8 * g : 8 * (g + 1)] for g in range(planes // 8)], axis=1)
    last = jnp.concatenate([diagonal] * (LANES // planes), axis=1)
    for target in range(grams.shape[0]):
        for at in range(8):
            grams[target, :, at * LANES : (at + 1) * LANES] = block[at : at + 1]
        grams[target, :, 8 * LANES :] = last


def eliminate(grams, planes):
    lane = lax.broadcasted_iota(jnp.int32, (8, LANES), 1)
    sub = lax.broadcasted_iota(jnp.int32, (8, LANES), 0)
    first_half = lane < 2 * planes
    groups = planes // 8
    sources = [[gram[8 * g : 8 * (g + 1)] for g in range(groups)] for gram in grams]
    state = []
    for g in range(groups):
        unit = jnp.where(sub + 8 * g == lane % (2 * planes) - planes, 1.0, 0.0)
        unit = unit[:, planes : 2 * planes]
        state.append(jnp.concatenate([sources[0][g], unit, sources[1][g], unit], axis=1))
    columns = []
    for j in range(planes):
        columns.append(
            {
                g: jnp.where(
                    first_half,
                    jnp.broadcast_to(sources[0][g][:, j : j + 1], (8, LANES)),
                    jnp.broadcast_to(sources[1][g][:, j : j + 1], (8, LANES)),
                )
                for g in range(j // 8, groups)
            }
        )
    scale = [jnp.ones((8, LANES), jnp.float32)] * groups
    for step in range(planes):
        own, at = step // 8, step % 8
        column = columns[step]
        root = lax.rsqrt(jnp.broadcast_to(column[own][at : at + 1], (8, LANES)))
        inverse = root * root
        scale[own] = jnp.where(sub == at, root, scale[own])
        factors = {g: value * inverse for g, value in column.items()}
        factors[own] = jnp.where(sub > at, factors[own], 0.0)
        for j in range(step + 1, planes):
            entry = jnp.broadcast_to(column[j // 8][j % 8 : j % 8 + 1], (8, LANES))
            for g in columns[j]:
                columns[j][g] = columns[j][g] - factors[g] * entry
        pivot_row = jnp.broadcast_to(state[own][at : at + 1], (8, LANES))
        for g in range(own, groups):
            state[g] = state[g] - factors[g] * pivot_row
    return jnp.concatenate([state[g] * scale[g] for g in range(groups)], axis=0)


def finish_kernel(pixel_count, inner_second, outer_second, edges, parts, basis, factor):
    planes = factor.shape[0]
    _, rows, width = basis.shape
    at_row = lax.broadcasted_iota(jnp.int32, (planes, planes), 0)
    at_col = lax.broadcasted_iota(jnp.int32, (planes, planes), 1)
    block = tree_sum([parts[at] for at in range(parts.shape[0])]) / pixel_count
    block = [block[:, at * LANES : (at + 1) * LANES] for at in range(9)]
    mixed, diagonal = jnp.concatenate(block[:8], axis=0), block[8][:, :planes]
    mixed = jnp.concatenate([mixed[:, at * planes : (at + 1) * planes] for at in range(LANES // planes)], axis=0)
    flipped = mixed.T
    first = jnp.where(at_row >= at_col, mixed, flipped)
    second_gram = jnp.where(at_row < at_col, mixed, jnp.where(at_row > at_col, flipped, diagonal))
    state = eliminate([first, second_gram], planes)
    first_inverse = state[:, planes : 2 * planes]
    product_upper = jnp.where(at_col >= at_row, state[:, 2 * planes : 3 * planes], 0.0)
    product_inverse = jnp.where(at_col <= at_row, state[:, 3 * planes :], 0.0)
    factor[...] = jnp.where(at_col >= at_row, gram_of(product_upper, first_inverse), 0.0)
    high, middle, low = split(product_inverse)
    left_side = jnp.concatenate([high, high, middle, high, low, middle], axis=1)

    def solved(high, middle, low):
        right_side = jnp.concatenate([high, middle, high, low, high, middle], axis=0)
        return jnp.dot(left_side, right_side, preferred_element_type=jnp.float32)

    lane = lax.broadcasted_iota(jnp.int32, (1, LANES), 1)
    outer = solved(*split(edges[...]))
    for row in range(rows):
        if 2 <= row < rows - 2:
            held, spot = inner_second, row - 2
        else:
            held, spot = outer_second, row if row < 2 else row - rows + 4
        value = solved(*(held[spot, at * planes : (at + 1) * planes] for at in range(3)))
        place = PITCH * (row + 2)
        low_end = pltpu.roll(outer[:, :LANES], LANES - (place + 2), 1)
        high_end = pltpu.roll(outer[:, LANES:], (LANES - 2 - (place + PITCH - 4)) % LANES, 1)
        basis[:, row, :LANES] = jnp.where(lane < 2, low_end, value[:, :LANES])
        basis[:, row, LANES : width - LANES] = value[:, LANES : width - LANES]
        basis[:, row, width - LANES :] = jnp.where(lane >= LANES - 2, high_end, value[:, width - LANES :])


def tree_sum(parts):
    while len(parts) > 1:
        parts = [sum(parts[at + 1 : at + 2], parts[at]) for at in range(0, len(parts), 2)]
    return parts[0]


def swap(value, axis, pairing):
    names = ("sec", "row", "col")
    shape = [lax.axis_size(name) for name in names]
    at = names.index(axis)

    def number(place):
        return (place[0] * shape[1] + place[1]) * shape[2] + place[2]

    pairs = []
    for place in itertools.product(*(range(extent) for extent in shape)):
        partner = list(place)
        partner[at] += 1 if place[at] % 2 != pairing else -1
        if not 0 <= partner[at] < shape[at]:
            partner[at] = place[at]
            partner[at - 1] ^= 1
        pairs.append((number(place), number(partner)))
    return lax.ppermute(value, names, pairs)


def on_device(sketch, weights):
    planes, rows, width = sketch.shape
    group = lax.axis_size("row") * lax.axis_size("col")
    side = f32(planes + 8, LANES)
    by_row, weights_by_row, left, right, *messages = call(
        pack_rows_kernel,
        [f32(rows, planes, width), f32(rows, 8, width), side, side]
        + [f32(16, LANES)] * 2
        + [f32(2 * planes + 8, width)] * 2,
        pltpu.with_memory_space_constraint(sketch, pltpu.HBM),
        pltpu.with_memory_space_constraint(weights, pltpu.HBM),
        memory=pltpu.HBM,
        scratch=[
            pltpu.VMEM(sketch.shape, jnp.float32),
            pltpu.VMEM(weights.shape, jnp.float32),
            pltpu.SemaphoreType.DMA((2,)),
        ],
    )
    corners = [swap(message, "row", pairing) for pairing, message in enumerate(messages[:2])]
    from_rows = [swap(message, "row", pairing) for pairing, message in enumerate(messages[2:])]
    left, right, *messages = call(
        functools.partial(strips_kernel, rows), [side, side] + [f32(16, LANES)] * 2, left, right, *corners, cost=pl.CostEstimate(flops=2000000000, bytes_accessed=4000000, transcendentals=0)
    )
    from_cols = [swap(message, "col", pairing) for pairing, message in enumerate(messages)]
    parts_of = functools.partial(jax.ShapeDtypeStruct, dtype=jnp.bfloat16)
    products = f32(3 * planes, 3 * planes)
    middle, inner_second, *inner_products = call(
        inner_rows_kernel,
        [f32(rows - 2, planes, width), parts_of((rows - 4, 3 * planes, width)), products, products],
        by_row,
        weights_by_row,
    )
    outer_second, early_grams = call(
        outer_rows_kernel,
        [parts_of((4, 3 * planes, width)), f32(planes, 2 * planes)],
        by_row,
        weights_by_row,
        *from_rows,
        middle,
        *inner_products,
        scratch=[pltpu.VMEM((4, planes, width), jnp.float32)],
    )
    grams, edges = call(
        functools.partial(late_kernel, rows),
        [f32(group, 1, 9 * LANES), f32(planes, 2 * LANES)],
        left,
        right,
        *from_cols,
        early_grams,
    )
    parts = lax.all_to_all(grams, ("row", "col"), 0, 0, tiled=True)
    return call(
        functools.partial(finish_kernel, float(rows * width * group)),
        [f32(planes, rows, width), f32(planes, planes)],
        inner_second,
        outer_second,
        edges,
        parts,
    )


def solution(mesh):
    return jax.shard_map(
        on_device,
        mesh=mesh,
        in_specs=(P(None, ("sec", "row"), "col"), P(None, ("sec", "row"), "col")),
        out_specs=(P(None, ("sec", "row"), "col"), P("sec", None)),
        check_vma=False,
    )
```

```python
import functools
import itertools

import jax
import jax.numpy as jnp
from jax import lax
from jax.experimental import pallas as pl
from jax.experimental.pallas import tpu as pltpu
from jax.sharding import PartitionSpec as P

NEIGHBOURS = ((-1, -1), (-1, 0), (-1, 1), (0, -1), (0, 1), (1, -1), (1, 0), (1, 1))
LANES = 128
PITCH = 8
HIGHEST = lax.Precision.HIGHEST


def call(kernel, out_shapes, *operands, memory=pltpu.VMEM, scratch=(), cost=None):
    return pl.pallas_call(
        kernel,
        out_shape=out_shapes,
        in_specs=[pl.BlockSpec(memory_space=memory)] * len(operands),
        out_specs=[pl.BlockSpec(memory_space=pltpu.VMEM)] * len(out_shapes),
        scratch_shapes=scratch,
        cost_estimate=cost,
        compiler_params=pltpu.CompilerParams(vmem_limit_bytes=40 * 1024 * 1024),
    )(*operands)


def f32(*shape):
    return jax.ShapeDtypeStruct(shape, jnp.float32)


def sides_of(axis):
    place = lax.axis_index(axis)
    return place % 2 == 1, place > 0, place < lax.axis_size(axis) - 1


def edge_columns(first, last, place):
    lane = lax.broadcasted_iota(jnp.int32, (1, LANES), 1)
    own = PITCH - 2
    left = jnp.where((lane >= place + 2) & (lane < place + PITCH), rolled(first, place + 2), 0.0)
    right = jnp.where((lane >= place) & (lane < place + own), rolled(last, place - (LANES - own)), 0.0)
    return left, right


def pack_rows_kernel(sketch, weights, by_row, weights_by_row, left, right, *rest):
    bulk_messages, diagonal_messages = rest[:2], rest[2:4]
    tile, weight_tile, arrived = rest[4:]
    copies = [
        pltpu.make_async_copy(sketch, tile, arrived.at[0]),
        pltpu.make_async_copy(weights, weight_tile, arrived.at[1]),
    ]
    for copy in copies:
        copy.start()
    for copy in copies:
        copy.wait()
    rows, planes, width = by_row.shape
    odd_row, _, _ = sides_of("row")
    odd_col, _, _ = sides_of("col")
    lane = lax.broadcasted_iota(jnp.int32, (1, LANES), 1)
    for row in range(rows):
        weights_by_row[row] = weight_tile[:, row, :]
        by_row[row] = tile[:, row, :]
    for message, up in zip(bulk_messages, (odd_row, jnp.logical_not(odd_row))):
        start = jnp.where(up, rows - 2, 0)
        for slot in range(2):
            message[slot * planes : (slot + 1) * planes] = by_row[start + slot]
        message[2 * planes : 2 * planes + 8] = weights_by_row[jnp.where(up, rows - 1, 0)]
    strips = [None, None]
    for row in range(rows):
        first = jnp.concatenate([by_row[row, :, :LANES], weights_by_row[row, :, :LANES]], axis=0)
        last = jnp.concatenate([by_row[row, :, width - LANES :], weights_by_row[row, :, width - LANES :]], axis=0)
        parts = edge_columns(first, last, PITCH * (row + 2))
        strips = [part if strip is None else strip + part for strip, part in zip(strips, parts)]
    left[...], right[...] = strips
    pair = 2 * PITCH
    up = jnp.logical_not(odd_row)
    pieces = []
    for group in range(planes // 8 + 1):
        piece = None
        for side, strip in enumerate(strips):
            target = (2 * group + side) * pair if group < planes // 8 else side * pair
            value = strip[8 * group : 8 * (group + 1)]
            moved = jnp.where(up, rolled(value, target - PITCH * rows), rolled(value, target - 2 * PITCH))
            moved = jnp.where(lane // pair == target // pair, moved, 0.0)
            piece = moved if piece is None else piece + moved
        pieces.append(piece)
    extra = bulk_messages[1].at[2 * planes + 8 :]
    extra[:, :LANES] = functools.reduce(jnp.add, pieces[:-1])
    extra[:, LANES : 2 * LANES] = pieces[-1]
    extra[:, 2 * LANES :] = jnp.zeros((8, width - 2 * LANES), jnp.float32)
    to_left, to_right = folded(strips[0], 2), folded(strips[1], PITCH - 4)
    for message, up in zip(diagonal_messages, (odd_col, jnp.logical_not(odd_col))):
        edge = jnp.where(up, to_right, to_left)
        below = jnp.where(lane < pair, rolled(edge, -PITCH * rows), 0.0)
        start = PITCH * (rows + 2)
        above = jnp.where((lane >= start) & (lane < start + pair), rolled(edge, PITCH * rows), 0.0)
        message[...] = jnp.where(odd_row, below, above)


def strips_kernel(rows, own_left, own_right, bulk_message, left, right, *col_messages):
    planes = own_left.shape[0] - 8
    odd_row, has_below, has_above = sides_of("row")
    odd_col, _, _ = sides_of("col")
    extra = bulk_message[2 * planes + 8 :, : 2 * LANES]
    lane = lax.broadcasted_iota(jnp.int32, (1, LANES), 1)
    pair = 2 * PITCH
    halos = ((odd_row & has_below, 0), (jnp.logical_not(odd_row) & has_above, PITCH * (rows + 2)))
    for side, (strip, target) in enumerate(((own_left, left), (own_right, right))):
        total = strip[...]
        for present, place in halos:
            pieces = [rolled(extra[:, :LANES], place - (2 * group + side) * pair) for group in range(planes // 8)]
            pieces.append(rolled(extra[:, LANES:], place - side * pair))
            halo = jnp.where(lane // pair == place // pair, jnp.concatenate(pieces, axis=0), 0.0)
            total = total + jnp.where(present, halo, 0.0)
        target[...] = total
    to_left, to_right = folded(left[...], 2), folded(right[...], PITCH - 4)
    for message, up in zip(col_messages, (odd_col, jnp.logical_not(odd_col))):
        message[...] = jnp.where(up, to_right, to_left)


def folded(strip, spot):
    lane = lax.broadcasted_iota(jnp.int32, (1, LANES), 1)
    groups = strip.shape[0] // 8
    pieces = []
    for group in range(groups):
        target = 2 * group if group < groups - 1 else 0
        moved = rolled(strip[8 * group : 8 * (group + 1)], target - spot)
        pieces.append(jnp.where((lane % PITCH) // 2 == target // 2, moved, 0.0))
    return jnp.concatenate([functools.reduce(jnp.add, pieces[:-1]), pieces[-1]], axis=0)


def unfolded(message, spot, planes):
    lane = lax.broadcasted_iota(jnp.int32, (1, LANES), 1)
    pieces = [rolled(message[:8], spot - 2 * group) for group in range(planes // 8)] + [rolled(message[8:], spot)]
    return jnp.where((lane % PITCH) // 2 == spot // 2, jnp.concatenate(pieces, axis=0), 0.0)


def rolled(value, shift):
    return pltpu.roll(value, shift % LANES, 1) if shift % LANES else value


def apply_operator(rows3, weight_rows):
    width = rows3[1].shape[1]
    total = jnp.sum(weight_rows, axis=0, keepdims=True) * rows3[1]
    for across in (0, -1, 1):
        moved = pltpu.roll(weight_rows, across % width, 1) if across else weight_rows
        terms = [
            moved[position : position + 1] * rows3[up + 1]
            for position, (up, side) in enumerate(NEIGHBOURS)
            if side == across
        ]
        part = functools.reduce(jnp.add, terms)
        total = total + (pltpu.roll(part, -across % width, 1) if across else part)
    return total


def gram_of(value, other):
    return lax.dot_general(
        value, other, (((1,), (1,)), ((), ())), precision=HIGHEST, preferred_element_type=jnp.float32
    )


def split(value):
    high = value.astype(jnp.bfloat16)
    rest = value - high.astype(jnp.float32)
    middle = rest.astype(jnp.bfloat16)
    low = (rest - middle.astype(jnp.float32)).astype(jnp.bfloat16)
    return high, middle, low


def inner_parts(image):
    width = image.shape[1]
    lane = lax.broadcasted_iota(jnp.int32, (1, LANES), 1)
    kept = [
        jnp.where(lane >= 2, image[:, :LANES], 0.0),
        image[:, LANES : width - LANES],
        jnp.where(lane < LANES - 2, image[:, width - LANES :], 0.0),
    ]
    return jnp.concatenate(split(jnp.concatenate(kept, axis=1)), axis=0)


def products_of(parts):
    return lax.dot_general(parts, parts, (((1,), (1,)), ((), ())), preferred_element_type=jnp.float32)


def images_of(middle, weights, wanted, second, products):
    for at, row in enumerate(wanted):
        parts = inner_parts(apply_operator([middle(row - 1), middle(row), middle(row + 1)], weights(row)))
        second[at] = parts
        products = products + products_of(parts)
    return products


def inner_rows_kernel(by_row, weights_by_row, middle, second, first_products, second_products):
    rows = by_row.shape[0]
    products = jnp.zeros(first_products.shape, jnp.float32)
    for row in range(1, rows - 1):
        image = apply_operator([by_row[row - 1], by_row[row], by_row[row + 1]], weights_by_row[row])
        middle[row - 1] = image
        products = products + products_of(inner_parts(image))
    first_products[...] = products
    second_products[...] = images_of(
        lambda row: middle[row - 1],
        lambda row: weights_by_row[row],
        range(2, rows - 2),
        second,
        jnp.zeros(second_products.shape, jnp.float32),
    )


def outer_rows_kernel(
    by_row,
    weights_by_row,
    first_message,
    second_message,
    middle,
    first_products,
    second_products,
    second,
    grams,
    left_halo,
    right_halo,
    outer,
):
    rows, planes, width = by_row.shape
    odd_row, has_below, has_above = sides_of("row")
    one, other = first_message[...], second_message[: 2 * planes + 8]
    below = jnp.where(has_below, jnp.where(odd_row, other, one), 0.0)
    above = jnp.where(has_above, jnp.where(odd_row, one, other), 0.0)
    halos = [None, None]
    for side, (halo, present) in enumerate(
        ((below, jnp.logical_not(odd_row)), (above, odd_row))
    ):
        for slot in range(2):
            index = slot if side == 0 else rows + 2 + slot
            blank = jnp.zeros((8, width), jnp.float32)
            weight = halo[2 * planes :] if slot != side else blank
            row_values = jnp.concatenate([halo[slot * planes : (slot + 1) * planes], weight], axis=0)
            parts = edge_columns(row_values[:, :LANES], row_values[:, width - LANES :], PITCH * index)
            parts = [jnp.where(present, part, 0.0) for part in parts]
            halos = [part if total is None else total + part for total, part in zip(halos, parts)]
    left_halo[...], right_halo[...] = halos

    def field(row):
        if 0 <= row < rows:
            return by_row[row]
        at = (row + 2 if row < 0 else row - rows) * planes
        return (below if row < 0 else above)[at : at + planes]

    def weights(row):
        if 0 <= row < rows:
            return weights_by_row[row]
        return (below if row < 0 else above)[2 * planes :]

    products = first_products[...]
    places = (-1, 0, rows - 1, rows)
    for at, row in enumerate(places):
        image = apply_operator([field(row - 1), field(row), field(row + 1)], weights(row))
        outer[at] = image
        if 0 <= row < rows:
            products = products + products_of(inner_parts(image))
    both = [products]
    both.append(
        images_of(
            lambda row: outer[places.index(row)] if row in places else middle[row - 1],
            weights,
            (0, 1, rows - 2, rows - 1),
            second,
            second_products[...],
        )
    )
    for at, products in enumerate(both):
        some = products[:planes] + products[planes : 2 * planes] + products[2 * planes :]
        total = some[:, :planes] + some[:, planes : 2 * planes] + some[:, 2 * planes :]
        grams[:, at * planes : (at + 1) * planes] = total


def apply_on_strip(values, weights):
    total = jnp.sum(weights, axis=0, keepdims=True) * values
    for position, (up, across) in enumerate(NEIGHBOURS):
        moved = pltpu.roll(values, (-PITCH * up - across) % LANES, 1)
        total = total + weights[position : position + 1] * moved
    return total


def late_kernel(rows, left, right, left_halo, right_halo, *rest):
    diagonal_messages, col_messages, (early_grams, grams, edges) = rest[:2], rest[2:4], rest[4:]
    planes = early_grams.shape[0]
    odd_row, has_below, has_above = sides_of("row")
    odd_col, has_left, has_right = sides_of("col")
    beyond = jnp.where(odd_row, has_above, has_below)
    one, other = (
        col[...] + jnp.where(beyond, diagonal[...], 0.0)
        for col, diagonal in zip(col_messages, diagonal_messages)
    )
    lane = lax.broadcasted_iota(jnp.int32, (1, LANES), 1)
    spot, row = lane % PITCH, lane // PITCH
    strips, masks = [], []
    for side, (strip, present, halo) in enumerate(
        (
            (left[...] + left_halo[...], has_left, jnp.where(odd_col, other, one)),
            (right[...] + right_halo[...], has_right, jnp.where(odd_col, one, other)),
        )
    ):
        strips.append(strip + jnp.where(present, unfolded(halo, side * (PITCH - 2), planes), 0.0))
        low = 2 if side == 0 else PITCH - 4
        masks.append((spot >= low) & (spot < low + 2) & (row >= 2) & (row < rows + 2))
    values = [strip[:planes] for strip in strips]
    gram = []
    for at in range(2):
        values = [apply_on_strip(value, strip[planes:]) for value, strip in zip(values, strips)]
        kept = jnp.concatenate([jnp.where(mask, value, 0.0) for mask, value in zip(masks, values)], axis=1)
        both = jnp.concatenate(values, axis=1)
        gram.append(early_grams[:, at * planes : (at + 1) * planes] + gram_of(kept, both))
    edges[...] = both
    at_row = lax.broadcasted_iota(jnp.int32, (planes, planes), 0)
    at_col = lax.broadcasted_iota(jnp.int32, (planes, planes), 1)
    mixed = jnp.where(at_row >= at_col, gram[0], gram[1])
    diagonal = jnp.sum(jnp.where(at_row == at_col, gram[1], 0.0), axis=0, keepdims=True)
    block = jnp.concatenate([mixed[8 * g : 8 * (g + 1)] for g in range(planes // 8)], axis=1)
    last = jnp.concatenate([diagonal] * (LANES // planes), axis=1)
    for target in range(grams.shape[0]):
        for at in range(8):
            grams[target, :, at * LANES : (at + 1) * LANES] = block[at : at + 1]
        grams[target, :, 8 * LANES :] = last


def eliminate(grams, planes):
    lane = lax.broadcasted_iota(jnp.int32, (8, LANES), 1)
    sub = lax.broadcasted_iota(jnp.int32, (8, LANES), 0)
    first_half = lane < 2 * planes
    groups = planes // 8
    sources = [[gram[8 * g : 8 * (g + 1)] for g in range(groups)] for gram in grams]
    state = []
    for g in range(groups):
        unit = jnp.where(sub + 8 * g == lane % (2 * planes) - planes, 1.0, 0.0)
        unit = unit[:, planes : 2 * planes]
        state.append(jnp.concatenate([sources[0][g], unit, sources[1][g], unit], axis=1))
    columns = []
    for j in range(planes):
        columns.append(
            {
                g: jnp.where(
                    first_half,
                    jnp.broadcast_to(sources[0][g][:, j : j + 1], (8, LANES)),
                    jnp.broadcast_to(sources[1][g][:, j : j + 1], (8, LANES)),
                )
                for g in range(j // 8, groups)
            }
        )
    scale = [jnp.ones((8, LANES), jnp.float32)] * groups
    for step in range(planes):
        own, at = step // 8, step % 8
        column = columns[step]
        root = lax.rsqrt(jnp.broadcast_to(column[own][at : at + 1], (8, LANES)))
        inverse = root * root
        scale[own] = jnp.where(sub == at, root, scale[own])
        factors = {g: value * inverse for g, value in column.items()}
        factors[own] = jnp.where(sub > at, factors[own], 0.0)
        for j in range(step + 1, planes):
            entry = jnp.broadcast_to(column[j // 8][j % 8 : j % 8 + 1], (8, LANES))
            for g in columns[j]:
                columns[j][g] = columns[j][g] - factors[g] * entry
        pivot_row = jnp.broadcast_to(state[own][at : at + 1], (8, LANES))
        for g in range(own, groups):
            state[g] = state[g] - factors[g] * pivot_row
    return jnp.concatenate([state[g] * scale[g] for g in range(groups)], axis=0)


def finish_kernel(pixel_count, inner_second, outer_second, edges, parts, basis, factor):
    planes = factor.shape[0]
    _, rows, width = basis.shape
    at_row = lax.broadcasted_iota(jnp.int32, (planes, planes), 0)
    at_col = lax.broadcasted_iota(jnp.int32, (planes, planes), 1)
    block = tree_sum([parts[at] for at in range(parts.shape[0])]) / pixel_count
    block = [block[:, at * LANES : (at + 1) * LANES] for at in range(9)]
    mixed, diagonal = jnp.concatenate(block[:8], axis=0), block[8][:, :planes]
    mixed = jnp.concatenate([mixed[:, at * planes : (at + 1) * planes] for at in range(LANES // planes)], axis=0)
    flipped = mixed.T
    first = jnp.where(at_row >= at_col, mixed, flipped)
    second_gram = jnp.where(at_row < at_col, mixed, jnp.where(at_row > at_col, flipped, diagonal))
    state = eliminate([first, second_gram], planes)
    first_inverse = state[:, planes : 2 * planes]
    product_upper = jnp.where(at_col >= at_row, state[:, 2 * planes : 3 * planes], 0.0)
    product_inverse = jnp.where(at_col <= at_row, state[:, 3 * planes :], 0.0)
    factor[...] = jnp.where(at_col >= at_row, gram_of(product_upper, first_inverse), 0.0)
    high, middle, low = split(product_inverse)
    left_side = jnp.concatenate([high, high, middle, high, low, middle], axis=1)

    def solved(high, middle, low):
        right_side = jnp.concatenate([high, middle, high, low, high, middle], axis=0)
        return jnp.dot(left_side, right_side, preferred_element_type=jnp.float32)

    lane = lax.broadcasted_iota(jnp.int32, (1, LANES), 1)
    outer = solved(*split(edges[...]))
    for row in range(rows):
        if 2 <= row < rows - 2:
            held, spot = inner_second, row - 2
        else:
            held, spot = outer_second, row if row < 2 else row - rows + 4
        value = solved(*(held[spot, at * planes : (at + 1) * planes] for at in range(3)))
        place = PITCH * (row + 2)
        low_end = pltpu.roll(outer[:, :LANES], LANES - (place + 2), 1)
        high_end = pltpu.roll(outer[:, LANES:], (LANES - 2 - (place + PITCH - 4)) % LANES, 1)
        basis[:, row, :LANES] = jnp.where(lane < 2, low_end, value[:, :LANES])
        basis[:, row, LANES : width - LANES] = value[:, LANES : width - LANES]
        basis[:, row, width - LANES :] = jnp.where(lane >= LANES - 2, high_end, value[:, width - LANES :])


def tree_sum(parts):
    while len(parts) > 1:
        parts = [sum(parts[at + 1 : at + 2], parts[at]) for at in range(0, len(parts), 2)]
    return parts[0]


def swap(value, row_pairing=None, col_pairing=None):
    names = ("sec", "row", "col")
    shape = [lax.axis_size(name) for name in names]

    def partner(at, place, pairing):
        other = place if pairing is None else place + 1 if place % 2 != pairing else place - 1
        return other if 0 <= other < shape[at] else None

    pairs = []
    for sec, row, col in itertools.product(*(range(extent) for extent in shape)):
        other_row, other_col = partner(1, row, row_pairing), partner(2, col, col_pairing)
        if other_col is None:
            target = (sec, row ^ 1, col)
        elif other_row is None:
            target = (sec ^ 1, row, col)
        else:
            target = (sec, other_row, other_col)
        pairs.append(tuple((a * shape[1] + b) * shape[2] + c for a, b, c in ((sec, row, col), target)))
    return lax.ppermute(value, names, pairs)


def on_device(sketch, weights):
    planes, rows, width = sketch.shape
    group = lax.axis_size("row") * lax.axis_size("col")
    side = f32(planes + 8, LANES)
    by_row, weights_by_row, left, right, *messages = call(
        pack_rows_kernel,
        [f32(rows, planes, width), f32(rows, 8, width), side, side]
        + [f32(2 * planes + 8, width), f32(2 * planes + 16, width)]
        + [f32(16, LANES)] * 2,
        pltpu.with_memory_space_constraint(sketch, pltpu.HBM),
        pltpu.with_memory_space_constraint(weights, pltpu.HBM),
        memory=pltpu.HBM,
        scratch=[
            pltpu.VMEM(sketch.shape, jnp.float32),
            pltpu.VMEM(weights.shape, jnp.float32),
            pltpu.SemaphoreType.DMA((2,)),
        ],
    )
    from_rows = [swap(messages[at], row_pairing=at) for at in range(2)]
    from_diagonals = [swap(messages[2 + at], row_pairing=0, col_pairing=at) for at in range(2)]
    left, right, *messages = call(
        functools.partial(strips_kernel, rows), [side, side] + [f32(16, LANES)] * 2, left, right, from_rows[1]
    )
    from_cols = [swap(messages[at], col_pairing=at) for at in range(2)]
    parts_of = functools.partial(jax.ShapeDtypeStruct, dtype=jnp.bfloat16)
    products = f32(3 * planes, 3 * planes)
    middle, inner_second, *inner_products = call(
        inner_rows_kernel,
        [f32(rows - 2, planes, width), parts_of((rows - 4, 3 * planes, width)), products, products],
        by_row,
        weights_by_row,
    )
    outer_second, early_grams, *halos = call(
        outer_rows_kernel,
        [parts_of((4, 3 * planes, width)), f32(planes, 2 * planes), side, side],
        by_row,
        weights_by_row,
        *from_rows,
        middle,
        *inner_products,
        scratch=[pltpu.VMEM((4, planes, width), jnp.float32)],
    )
    grams, edges = call(
        functools.partial(late_kernel, rows),
        [f32(group, 1, 9 * LANES), f32(planes, 2 * LANES)],
        left,
        right,
        *halos,
        *from_diagonals,
        *from_cols,
        early_grams,
    )
    parts = lax.all_to_all(grams, ("row", "col"), 0, 0, tiled=True)
    return call(
        functools.partial(finish_kernel, float(rows * width * group)),
        [f32(planes, rows, width), f32(planes, planes)],
        inner_second,
        outer_second,
        edges,
        parts,
    )


def solution(mesh):
    return jax.shard_map(
        on_device,
        mesh=mesh,
        in_specs=(P(None, ("sec", "row"), "col"), P(None, ("sec", "row"), "col")),
        out_specs=(P(None, ("sec", "row"), "col"), P("sec", None)),
        check_vma=False,
    )
```

```python
import functools
import itertools

import jax
import jax.numpy as jnp
from jax import lax
from jax.experimental import pallas as pl
from jax.experimental.pallas import tpu as pltpu
from jax.sharding import PartitionSpec as P

NEIGHBOURS = ((-1, -1), (-1, 0), (-1, 1), (0, -1), (0, 1), (1, -1), (1, 0), (1, 1))
LANES = 128
PITCH = 8
HIGHEST = lax.Precision.HIGHEST


def call(kernel, out_shapes, *operands, memory=pltpu.VMEM, out_memory=pltpu.VMEM, scratch=(), cost=None):
    return pl.pallas_call(
        kernel,
        out_shape=out_shapes,
        in_specs=[pl.BlockSpec(memory_space=memory)] * len(operands),
        out_specs=[pl.BlockSpec(memory_space=out_memory)] * len(out_shapes),
        scratch_shapes=scratch,
        cost_estimate=cost,
        compiler_params=pltpu.CompilerParams(vmem_limit_bytes=40 * 1024 * 1024),
    )(*operands)


def f32(*shape):
    return jax.ShapeDtypeStruct(shape, jnp.float32)


def sides_of(axis):
    place = lax.axis_index(axis)
    return place % 2 == 1, place > 0, place < lax.axis_size(axis) - 1


def edge_columns(first, last, place):
    lane = lax.broadcasted_iota(jnp.int32, (1, LANES), 1)
    own = PITCH - 2
    left = jnp.where((lane >= place + 2) & (lane < place + PITCH), rolled(first, place + 2), 0.0)
    right = jnp.where((lane >= place) & (lane < place + own), rolled(last, place - (LANES - own)), 0.0)
    return left, right


def pack_rows_kernel(sketch, weights, tile, weight_tile, left, right, *rest):
    bulk_messages, diagonal_messages, arrived = rest[:2], rest[2:4], rest[4]
    copies = [
        pltpu.make_async_copy(sketch, tile, arrived.at[0]),
        pltpu.make_async_copy(weights, weight_tile, arrived.at[1]),
    ]
    for copy in copies:
        copy.start()
    for copy in copies:
        copy.wait()
    planes, rows, width = tile.shape
    odd_row, _, _ = sides_of("row")
    odd_col, _, _ = sides_of("col")
    lane = lax.broadcasted_iota(jnp.int32, (1, LANES), 1)
    for slot in range(2):
        low, high = tile[:, slot, :], tile[:, rows - 2 + slot, :]
        for message, up in zip(bulk_messages, (odd_row, jnp.logical_not(odd_row))):
            message[slot * planes : (slot + 1) * planes] = jnp.where(up, high, low)
    low, high = weight_tile[:, 0, :], weight_tile[:, rows - 1, :]
    for message, up in zip(bulk_messages, (odd_row, jnp.logical_not(odd_row))):
        message[2 * planes : 2 * planes + 8] = jnp.where(up, high, low)
    strips = [None, None]
    for row in range(rows):
        first = jnp.concatenate([tile[:, row, :LANES], weight_tile[:, row, :LANES]], axis=0)
        last = jnp.concatenate([tile[:, row, width - LANES :], weight_tile[:, row, width - LANES :]], axis=0)
        parts = edge_columns(first, last, PITCH * (row + 2))
        strips = [part if strip is None else strip + part for strip, part in zip(strips, parts)]
    left[...], right[...] = strips
    pair = 2 * PITCH
    up = jnp.logical_not(odd_row)
    pieces = []
    for group in range(planes // 8 + 1):
        piece = None
        for side, strip in enumerate(strips):
            target = (2 * group + side) * pair if group < planes // 8 else side * pair
            value = strip[8 * group : 8 * (group + 1)]
            moved = jnp.where(up, rolled(value, target - PITCH * rows), rolled(value, target - 2 * PITCH))
            moved = jnp.where(lane // pair == target // pair, moved, 0.0)
            piece = moved if piece is None else piece + moved
        pieces.append(piece)
    extra = bulk_messages[1].at[2 * planes + 8 :]
    extra[:, :LANES] = functools.reduce(jnp.add, pieces[:-1])
    extra[:, LANES : 2 * LANES] = pieces[-1]
    extra[:, 2 * LANES :] = jnp.zeros((8, width - 2 * LANES), jnp.float32)
    to_left, to_right = folded(strips[0], 2), folded(strips[1], PITCH - 4)
    for message, up in zip(diagonal_messages, (odd_col, jnp.logical_not(odd_col))):
        edge = jnp.where(up, to_right, to_left)
        below = jnp.where(lane < pair, rolled(edge, -PITCH * rows), 0.0)
        start = PITCH * (rows + 2)
        above = jnp.where((lane >= start) & (lane < start + pair), rolled(edge, PITCH * rows), 0.0)
        message[...] = jnp.where(odd_row, below, above)


def strips_kernel(rows, own_left, own_right, bulk_message, left, right, *col_messages):
    planes = own_left.shape[0] - 8
    odd_row, has_below, has_above = sides_of("row")
    odd_col, _, _ = sides_of("col")
    extra = bulk_message[2 * planes + 8 :, : 2 * LANES]
    lane = lax.broadcasted_iota(jnp.int32, (1, LANES), 1)
    pair = 2 * PITCH
    halos = ((odd_row & has_below, 0), (jnp.logical_not(odd_row) & has_above, PITCH * (rows + 2)))
    for side, (strip, target) in enumerate(((own_left, left), (own_right, right))):
        total = strip[...]
        for present, place in halos:
            pieces = [rolled(extra[:, :LANES], place - (2 * group + side) * pair) for group in range(planes // 8)]
            pieces.append(rolled(extra[:, LANES:], place - side * pair))
            halo = jnp.where(lane // pair == place // pair, jnp.concatenate(pieces, axis=0), 0.0)
            total = total + jnp.where(present, halo, 0.0)
        target[...] = total
    to_left, to_right = folded(left[...], 2), folded(right[...], PITCH - 4)
    for message, up in zip(col_messages, (odd_col, jnp.logical_not(odd_col))):
        message[...] = jnp.where(up, to_right, to_left)


def folded(strip, spot):
    lane = lax.broadcasted_iota(jnp.int32, (1, LANES), 1)
    groups = strip.shape[0] // 8
    pieces = []
    for group in range(groups):
        target = 2 * group if group < groups - 1 else 0
        moved = rolled(strip[8 * group : 8 * (group + 1)], target - spot)
        pieces.append(jnp.where((lane % PITCH) // 2 == target // 2, moved, 0.0))
    return jnp.concatenate([functools.reduce(jnp.add, pieces[:-1]), pieces[-1]], axis=0)


def unfolded(message, spot, planes):
    lane = lax.broadcasted_iota(jnp.int32, (1, LANES), 1)
    pieces = [rolled(message[:8], spot - 2 * group) for group in range(planes // 8)] + [rolled(message[8:], spot)]
    return jnp.where((lane % PITCH) // 2 == spot // 2, jnp.concatenate(pieces, axis=0), 0.0)


def rolled(value, shift):
    return pltpu.roll(value, shift % LANES, 1) if shift % LANES else value


def apply_operator(rows3, weight_rows):
    width = rows3[1].shape[1]
    total = jnp.sum(weight_rows, axis=0, keepdims=True) * rows3[1]
    for across in (0, -1, 1):
        moved = pltpu.roll(weight_rows, across % width, 1) if across else weight_rows
        terms = [
            moved[position : position + 1] * rows3[up + 1]
            for position, (up, side) in enumerate(NEIGHBOURS)
            if side == across
        ]
        part = functools.reduce(jnp.add, terms)
        total = total + (pltpu.roll(part, -across % width, 1) if across else part)
    return total


def gram_of(value, other):
    return lax.dot_general(
        value, other, (((1,), (1,)), ((), ())), precision=HIGHEST, preferred_element_type=jnp.float32
    )


def split(value):
    high = value.astype(jnp.bfloat16)
    rest = value - high.astype(jnp.float32)
    middle = rest.astype(jnp.bfloat16)
    low = (rest - middle.astype(jnp.float32)).astype(jnp.bfloat16)
    return high, middle, low


def inner_parts(image):
    width = image.shape[1]
    lane = lax.broadcasted_iota(jnp.int32, (1, LANES), 1)
    kept = [
        jnp.where(lane >= 2, image[:, :LANES], 0.0),
        image[:, LANES : width - LANES],
        jnp.where(lane < LANES - 2, image[:, width - LANES :], 0.0),
    ]
    return jnp.concatenate(split(jnp.concatenate(kept, axis=1)), axis=0)


def products_of(parts):
    return lax.dot_general(parts, parts, (((1,), (1,)), ((), ())), preferred_element_type=jnp.float32)


def sum_of(products):
    planes = products.shape[0] // 3
    some = products[:planes] + products[planes : 2 * planes] + products[2 * planes :]
    return some[:, :planes] + some[:, planes : 2 * planes] + some[:, 2 * planes :]


def images_of(middle, weights, wanted, second, products):
    for at, row in enumerate(wanted):
        parts = inner_parts(apply_operator([middle(row - 1), middle(row), middle(row + 1)], weights(row)))
        second[at] = parts
        products = products + products_of(parts)
    return products


def inner_rows_kernel(
    tile, weight_tile, by_row, weights_by_row, middle, second, first_products, second_products
):
    rows = by_row.shape[0]
    for row in range(rows):
        weights_by_row[row] = weight_tile[:, row, :]
        by_row[row] = tile[:, row, :]
    products = jnp.zeros(first_products.shape, jnp.float32)
    for row in range(1, rows - 1):
        image = apply_operator([by_row[row - 1], by_row[row], by_row[row + 1]], weights_by_row[row])
        middle[row - 1] = image
        products = products + products_of(inner_parts(image))
    first_products[...] = products
    second_products[...] = images_of(
        lambda row: middle[row - 1],
        lambda row: weights_by_row[row],
        range(2, rows - 2),
        second,
        jnp.zeros(second_products.shape, jnp.float32),
    )


def outer_rows_kernel(
    by_row,
    weights_by_row,
    first_message,
    second_message,
    middle,
    first_products,
    second_products,
    second,
    grams,
    left_halo,
    right_halo,
    outer,
):
    rows, planes, width = by_row.shape
    odd_row, has_below, has_above = sides_of("row")
    one, other = first_message[...], second_message[: 2 * planes + 8]
    below = jnp.where(has_below, jnp.where(odd_row, other, one), 0.0)
    above = jnp.where(has_above, jnp.where(odd_row, one, other), 0.0)
    halos = [None, None]
    for side, (halo, present) in enumerate(
        ((below, jnp.logical_not(odd_row)), (above, odd_row))
    ):
        for slot in range(2):
            index = slot if side == 0 else rows + 2 + slot
            blank = jnp.zeros((8, width), jnp.float32)
            weight = halo[2 * planes :] if slot != side else blank
            row_values = jnp.concatenate([halo[slot * planes : (slot + 1) * planes], weight], axis=0)
            parts = edge_columns(row_values[:, :LANES], row_values[:, width - LANES :], PITCH * index)
            parts = [jnp.where(present, part, 0.0) for part in parts]
            halos = [part if total is None else total + part for total, part in zip(halos, parts)]
    left_halo[...], right_halo[...] = halos

    def field(row):
        if 0 <= row < rows:
            return by_row[row]
        at = (row + 2 if row < 0 else row - rows) * planes
        return (below if row < 0 else above)[at : at + planes]

    def weights(row):
        if 0 <= row < rows:
            return weights_by_row[row]
        return (below if row < 0 else above)[2 * planes :]

    products = first_products[...]
    places = (-1, 0, rows - 1, rows)
    for at, row in enumerate(places):
        image = apply_operator([field(row - 1), field(row), field(row + 1)], weights(row))
        outer[at] = image
        if 0 <= row < rows:
            products = products + products_of(inner_parts(image))
    both = [products]
    both.append(
        images_of(
            lambda row: outer[places.index(row)] if row in places else middle[row - 1],
            weights,
            (0, 1, rows - 2, rows - 1),
            second,
            second_products[...],
        )
    )
    for at, products in enumerate(both):
        grams[:, at * planes : (at + 1) * planes] = sum_of(products)


def apply_on_strip(values, weights):
    near = {up: rolled(values, -PITCH * up) for up in (-1, 0, 1)}
    total = jnp.sum(weights, axis=0, keepdims=True) * values
    for across in (0, -1, 1):
        moved = rolled(weights, across)
        terms = [
            moved[position : position + 1] * near[up]
            for position, (up, side) in enumerate(NEIGHBOURS)
            if side == across
        ]
        total = total + rolled(functools.reduce(jnp.add, terms), -across)
    return total


def late_kernel(rows, left, right, left_halo, right_halo, *rest):
    diagonal_messages, col_messages, (early_grams, grams, edges) = rest[:2], rest[2:4], rest[4:]
    planes = early_grams.shape[0]
    odd_row, has_below, has_above = sides_of("row")
    odd_col, has_left, has_right = sides_of("col")
    beyond = jnp.where(odd_row, has_above, has_below)
    one, other = (
        col[...] + jnp.where(beyond, diagonal[...], 0.0)
        for col, diagonal in zip(col_messages, diagonal_messages)
    )
    lane = lax.broadcasted_iota(jnp.int32, (1, LANES), 1)
    spot, row = lane % PITCH, lane // PITCH
    strips, masks = [], []
    for side, (strip, present, halo) in enumerate(
        (
            (left[...] + left_halo[...], has_left, jnp.where(odd_col, other, one)),
            (right[...] + right_halo[...], has_right, jnp.where(odd_col, one, other)),
        )
    ):
        strips.append(strip + jnp.where(present, unfolded(halo, side * (PITCH - 2), planes), 0.0))
        low = 2 if side == 0 else PITCH - 4
        masks.append((spot >= low) & (spot < low + 2) & (row >= 2) & (row < rows + 2))
    values = [strip[:planes] for strip in strips]
    gram = []
    for at in range(2):
        values = [apply_on_strip(value, strip[planes:]) for value, strip in zip(values, strips)]
        kept = jnp.concatenate([jnp.where(mask, value, 0.0) for mask, value in zip(masks, values)], axis=1)
        both = jnp.concatenate(values, axis=1)
        products = products_of(jnp.concatenate(split(kept), axis=0))
        gram.append(early_grams[:, at * planes : (at + 1) * planes] + sum_of(products))
    edges[...] = both
    at_row = lax.broadcasted_iota(jnp.int32, (planes, planes), 0)
    at_col = lax.broadcasted_iota(jnp.int32, (planes, planes), 1)
    mixed = jnp.where(at_row >= at_col, gram[0], gram[1])
    diagonal = jnp.sum(jnp.where(at_row == at_col, gram[1], 0.0), axis=0, keepdims=True)
    block = jnp.concatenate([mixed[8 * g : 8 * (g + 1)] for g in range(planes // 8)], axis=1)
    last = jnp.concatenate([diagonal] * (LANES // planes), axis=1)
    for target in range(grams.shape[0]):
        for at in range(8):
            grams[target, :, at * LANES : (at + 1) * LANES] = block[at : at + 1]
        grams[target, :, 8 * LANES :] = last


def eliminate(grams, planes, half_way):
    lane = lax.broadcasted_iota(jnp.int32, (8, LANES), 1)
    sub = lax.broadcasted_iota(jnp.int32, (8, LANES), 0)
    first_half = lane < 2 * planes
    groups = planes // 8
    sources = [[gram[8 * g : 8 * (g + 1)] for g in range(groups)] for gram in grams]
    state = []
    for g in range(groups):
        unit = jnp.where(sub + 8 * g == lane % (2 * planes) - planes, 1.0, 0.0)
        unit = unit[:, planes : 2 * planes]
        state.append(jnp.concatenate([sources[0][g], unit, sources[1][g], unit], axis=1))
    columns = []
    for j in range(planes):
        columns.append(
            {
                g: jnp.where(
                    first_half,
                    jnp.broadcast_to(sources[0][g][:, j : j + 1], (8, LANES)),
                    jnp.broadcast_to(sources[1][g][:, j : j + 1], (8, LANES)),
                )
                for g in range(j // 8, groups)
            }
        )
    scale = [jnp.ones((8, LANES), jnp.float32)] * groups
    for step in range(planes):
        own, at = step // 8, step % 8
        column = columns[step]
        root = lax.rsqrt(jnp.broadcast_to(column[own][at : at + 1], (8, LANES)))
        inverse = root * root
        scale[own] = jnp.where(sub == at, root, scale[own])
        left = {g: jnp.where(sub > at, value, 0.0) if g == own else value for g, value in column.items()}
        factors = {g: value * inverse for g, value in left.items()}
        for j in range(step + 1, planes):
            entry = jnp.broadcast_to(column[j // 8][j % 8 : j % 8 + 1], (8, LANES))
            for g in columns[j]:
                change = (left[g] * entry) * inverse if j == step + 1 else factors[g] * entry
                columns[j][g] = columns[j][g] - change
        pivot_row = jnp.broadcast_to(state[own][at : at + 1], (8, LANES))
        for g in range(own, groups):
            state[g] = state[g] - factors[g] * pivot_row
        if step + 1 == planes // 2:
            half_way(jnp.concatenate([state[g] * scale[g] for g in range(groups // 2)], axis=0))
    return jnp.concatenate([state[g] * scale[g] for g in range(groups)], axis=0)


def finish_kernel(
    pixel_count, inner_second, outer_second, edges, parts, basis_out, factor_out, basis, factor, written
):
    planes, rows, width = basis.shape
    half = planes // 2
    at_row = lax.broadcasted_iota(jnp.int32, (planes, planes), 0)
    at_col = lax.broadcasted_iota(jnp.int32, (planes, planes), 1)
    lane = lax.broadcasted_iota(jnp.int32, (1, LANES), 1)
    outer_parts = split(edges[...])
    copies = []

    def solve(inverse, start):
        stop = start + inverse.shape[0]
        high, middle, low = split(inverse)
        left_side = jnp.concatenate([high, high, middle, high, low, middle], axis=1)

        def solved(high, middle, low):
            right_side = jnp.concatenate([high, middle, high, low, high, middle], axis=0)
            return jnp.dot(left_side, right_side, preferred_element_type=jnp.float32)

        outer = solved(*(part[:stop] for part in outer_parts))
        for row in range(rows):
            if 2 <= row < rows - 2:
                held, spot = inner_second, row - 2
            else:
                held, spot = outer_second, row if row < 2 else row - rows + 4
            value = solved(*(held[spot, at * planes : at * planes + stop] for at in range(3)))
            place = PITCH * (row + 2)
            first = rolled(outer[:, :LANES], -(place + 2))
            last = rolled(outer[:, LANES:], LANES - 2 - (place + PITCH - 4))
            basis[start:stop, row, :LANES] = jnp.where(lane < 2, first, value[:, :LANES])
            basis[start:stop, row, LANES : width - LANES] = value[:, LANES : width - LANES]
            basis[start:stop, row, width - LANES :] = jnp.where(
                lane >= LANES - 2, last, value[:, width - LANES :]
            )
        some = pl.ds(start, stop - start)
        copies.append(pltpu.make_async_copy(basis.at[some], basis_out.at[some], written.at[len(copies)]))
        copies[-1].start()

    block = tree_sum([parts[at] for at in range(parts.shape[0])]) / pixel_count
    block = [block[:, at * LANES : (at + 1) * LANES] for at in range(9)]
    mixed, diagonal = jnp.concatenate(block[:8], axis=0), block[8][:, :planes]
    mixed = jnp.concatenate([mixed[:, at * planes : (at + 1) * planes] for at in range(LANES // planes)], axis=0)
    flipped = mixed.T
    first = jnp.where(at_row >= at_col, mixed, flipped)
    second = jnp.where(at_row < at_col, mixed, jnp.where(at_row > at_col, flipped, diagonal))
    low_half = (at_col <= at_row)[:half, :half]
    state = eliminate(
        [first, second],
        planes,
        lambda state: solve(jnp.where(low_half, state[:, 3 * planes : 3 * planes + half], 0.0), 0),
    )
    first_inverse = state[:, planes : 2 * planes]
    product_upper = jnp.where(at_col >= at_row, state[:, 2 * planes : 3 * planes], 0.0)
    solve(jnp.where(at_col <= at_row, state[:, 3 * planes :], 0.0)[half:], half)
    factor[...] = jnp.where(at_col >= at_row, gram_of(product_upper, first_inverse), 0.0)
    copies.append(pltpu.make_async_copy(factor, factor_out, written.at[2]))
    copies[-1].start()
    for copy in copies:
        copy.wait()


def tree_sum(parts):
    while len(parts) > 1:
        parts = [sum(parts[at + 1 : at + 2], parts[at]) for at in range(0, len(parts), 2)]
    return parts[0]


def swap(value, row_pairing=None, col_pairing=None):
    names = ("sec", "row", "col")
    shape = [lax.axis_size(name) for name in names]

    def partner(at, place, pairing):
        other = place if pairing is None else place + 1 if place % 2 != pairing else place - 1
        return other if 0 <= other < shape[at] else None

    pairs = []
    for sec, row, col in itertools.product(*(range(extent) for extent in shape)):
        other_row, other_col = partner(1, row, row_pairing), partner(2, col, col_pairing)
        if other_col is None:
            target = (sec, row ^ 1, col)
        elif other_row is None:
            target = (sec ^ 1, row, col)
        else:
            target = (sec, other_row, other_col)
        pairs.append(tuple((a * shape[1] + b) * shape[2] + c for a, b, c in ((sec, row, col), target)))
    return lax.ppermute(value, names, pairs)


def on_device(sketch, weights):
    planes, rows, width = sketch.shape
    group = lax.axis_size("row") * lax.axis_size("col")
    side = f32(planes + 8, LANES)
    tile, weight_tile, left, right, *messages = call(
        pack_rows_kernel,
        [f32(*sketch.shape), f32(*weights.shape), side, side]
        + [f32(2 * planes + 8, width), f32(2 * planes + 16, width)]
        + [f32(16, LANES)] * 2,
        pltpu.with_memory_space_constraint(sketch, pltpu.HBM),
        pltpu.with_memory_space_constraint(weights, pltpu.HBM),
        memory=pltpu.HBM,
        scratch=[pltpu.SemaphoreType.DMA((2,))],
    )
    from_rows = [swap(messages[at], row_pairing=at) for at in range(2)]
    from_diagonals = [swap(messages[2 + at], row_pairing=0, col_pairing=at) for at in range(2)]
    left, right, *messages = call(
        functools.partial(strips_kernel, rows), [side, side] + [f32(16, LANES)] * 2, left, right, from_rows[1]
    )
    from_cols = [swap(messages[at], col_pairing=at) for at in range(2)]
    parts_of = functools.partial(jax.ShapeDtypeStruct, dtype=jnp.bfloat16)
    products = f32(3 * planes, 3 * planes)
    by_row, weights_by_row, middle, inner_second, *inner_products = call(
        inner_rows_kernel,
        [f32(rows, planes, width), f32(rows, 8, width), f32(rows - 2, planes, width)]
        + [parts_of((rows - 4, 3 * planes, width)), products, products],
        tile,
        weight_tile,
    )
    outer_second, early_grams, *halos = call(
        outer_rows_kernel,
        [parts_of((4, 3 * planes, width)), f32(planes, 2 * planes), side, side],
        by_row,
        weights_by_row,
        *from_rows,
        middle,
        *inner_products,
        scratch=[pltpu.VMEM((4, planes, width), jnp.float32)],
    )
    grams, edges = call(
        functools.partial(late_kernel, rows),
        [f32(group, 1, 9 * LANES), f32(planes, 2 * LANES)],
        left,
        right,
        *halos,
        *from_diagonals,
        *from_cols,
        early_grams,
    )
    parts = lax.all_to_all(grams, ("row", "col"), 0, 0, tiled=True)
    return call(
        functools.partial(finish_kernel, float(rows * width * group)),
        [f32(planes, rows, width), f32(planes, planes)],
        inner_second,
        outer_second,
        edges,
        parts,
        out_memory=pl.ANY,
        scratch=[
            pltpu.VMEM(sketch.shape, jnp.float32),
            pltpu.VMEM((planes, planes), jnp.float32),
            pltpu.SemaphoreType.DMA((3,)),
        ],
    )


def solution(mesh):
    return jax.shard_map(
        on_device,
        mesh=mesh,
        in_specs=(P(None, ("sec", "row"), "col"), P(None, ("sec", "row"), "col")),
        out_specs=(P(None, ("sec", "row"), "col"), P("sec", None)),
        check_vma=False,
    )
```

```python
import functools
import itertools

import jax
import jax.numpy as jnp
from jax import lax
from jax.experimental import pallas as pl
from jax.experimental.pallas import tpu as pltpu
from jax.sharding import PartitionSpec as P

NEIGHBOURS = ((-1, -1), (-1, 0), (-1, 1), (0, -1), (0, 1), (1, -1), (1, 0), (1, 1))
LANES = 128
PITCH = 8
HIGHEST = lax.Precision.HIGHEST


def call(kernel, out_shapes, *operands, memory=pltpu.VMEM, out_memory=pltpu.VMEM, scratch=(), cost=None):
    return pl.pallas_call(
        kernel,
        out_shape=out_shapes,
        in_specs=[pl.BlockSpec(memory_space=memory)] * len(operands),
        out_specs=[pl.BlockSpec(memory_space=out_memory)] * len(out_shapes),
        scratch_shapes=scratch,
        cost_estimate=cost,
        compiler_params=pltpu.CompilerParams(vmem_limit_bytes=40 * 1024 * 1024),
    )(*operands)


def f32(*shape):
    return jax.ShapeDtypeStruct(shape, jnp.float32)


def sides_of(axis):
    place = lax.axis_index(axis)
    return place % 2 == 1, place > 0, place < lax.axis_size(axis) - 1


def edge_columns(first, last, place):
    lane = lax.broadcasted_iota(jnp.int32, (1, LANES), 1)
    own = PITCH - 2
    left = jnp.where((lane >= place + 2) & (lane < place + PITCH), rolled(first, place + 2), 0.0)
    right = jnp.where((lane >= place) & (lane < place + own), rolled(last, place - (LANES - own)), 0.0)
    return left, right


def pack_rows_kernel(sketch, weights, by_row, weights_by_row, left, right, *rest):
    bulk_messages, diagonal_messages = rest[:2], rest[2:4]
    tile, weight_tile, arrived = rest[4:]
    copies = [
        pltpu.make_async_copy(sketch, tile, arrived.at[0]),
        pltpu.make_async_copy(weights, weight_tile, arrived.at[1]),
    ]
    for copy in copies:
        copy.start()
    for copy in copies:
        copy.wait()
    rows, planes, width = by_row.shape
    odd_row, _, _ = sides_of("row")
    odd_col, _, _ = sides_of("col")
    lane = lax.broadcasted_iota(jnp.int32, (1, LANES), 1)
    for row in range(rows):
        weights_by_row[row] = weight_tile[:, row, :]
        by_row[row] = tile[:, row, :]
    for message, up in zip(bulk_messages, (odd_row, jnp.logical_not(odd_row))):
        start = jnp.where(up, rows - 2, 0)
        for slot in range(2):
            message[slot * planes : (slot + 1) * planes] = by_row[start + slot]
        message[2 * planes : 2 * planes + 8] = weights_by_row[jnp.where(up, rows - 1, 0)]
    strips = [None, None]
    for row in range(rows):
        first = jnp.concatenate([by_row[row, :, :LANES], weights_by_row[row, :, :LANES]], axis=0)
        last = jnp.concatenate([by_row[row, :, width - LANES :], weights_by_row[row, :, width - LANES :]], axis=0)
        parts = edge_columns(first, last, PITCH * (row + 2))
        strips = [part if strip is None else strip + part for strip, part in zip(strips, parts)]
    left[...], right[...] = strips
    pair = 2 * PITCH
    up = jnp.logical_not(odd_row)
    pieces = []
    for group in range(planes // 8 + 1):
        piece = None
        for side, strip in enumerate(strips):
            target = (2 * group + side) * pair if group < planes // 8 else side * pair
            value = strip[8 * group : 8 * (group + 1)]
            moved = jnp.where(up, rolled(value, target - PITCH * rows), rolled(value, target - 2 * PITCH))
            moved = jnp.where(lane // pair == target // pair, moved, 0.0)
            piece = moved if piece is None else piece + moved
        pieces.append(piece)
    extra = bulk_messages[1].at[2 * planes + 8 :]
    extra[:, :LANES] = functools.reduce(jnp.add, pieces[:-1])
    extra[:, LANES : 2 * LANES] = pieces[-1]
    extra[:, 2 * LANES :] = jnp.zeros((8, width - 2 * LANES), jnp.float32)
    to_left, to_right = folded(strips[0], 2), folded(strips[1], PITCH - 4)
    for message, up in zip(diagonal_messages, (odd_col, jnp.logical_not(odd_col))):
        edge = jnp.where(up, to_right, to_left)
        below = jnp.where(lane < pair, rolled(edge, -PITCH * rows), 0.0)
        start = PITCH * (rows + 2)
        above = jnp.where((lane >= start) & (lane < start + pair), rolled(edge, PITCH * rows), 0.0)
        message[...] = jnp.where(odd_row, below, above)


def strips_kernel(rows, own_left, own_right, bulk_message, left, right, *col_messages):
    planes = own_left.shape[0] - 8
    odd_row, has_below, has_above = sides_of("row")
    odd_col, _, _ = sides_of("col")
    extra = bulk_message[2 * planes + 8 :, : 2 * LANES]
    lane = lax.broadcasted_iota(jnp.int32, (1, LANES), 1)
    pair = 2 * PITCH
    halos = ((odd_row & has_below, 0), (jnp.logical_not(odd_row) & has_above, PITCH * (rows + 2)))
    for side, (strip, target) in enumerate(((own_left, left), (own_right, right))):
        total = strip[...]
        for present, place in halos:
            pieces = [rolled(extra[:, :LANES], place - (2 * group + side) * pair) for group in range(planes // 8)]
            pieces.append(rolled(extra[:, LANES:], place - side * pair))
            halo = jnp.where(lane // pair == place // pair, jnp.concatenate(pieces, axis=0), 0.0)
            total = total + jnp.where(present, halo, 0.0)
        target[...] = total
    to_left, to_right = folded(left[...], 2), folded(right[...], PITCH - 4)
    for message, up in zip(col_messages, (odd_col, jnp.logical_not(odd_col))):
        message[...] = jnp.where(up, to_right, to_left)


def folded(strip, spot):
    lane = lax.broadcasted_iota(jnp.int32, (1, LANES), 1)
    groups = strip.shape[0] // 8
    pieces = []
    for group in range(groups):
        target = 2 * group if group < groups - 1 else 0
        moved = rolled(strip[8 * group : 8 * (group + 1)], target - spot)
        pieces.append(jnp.where((lane % PITCH) // 2 == target // 2, moved, 0.0))
    return jnp.concatenate([functools.reduce(jnp.add, pieces[:-1]), pieces[-1]], axis=0)


def unfolded(message, spot, planes):
    lane = lax.broadcasted_iota(jnp.int32, (1, LANES), 1)
    pieces = [rolled(message[:8], spot - 2 * group) for group in range(planes // 8)] + [rolled(message[8:], spot)]
    return jnp.where((lane % PITCH) // 2 == spot // 2, jnp.concatenate(pieces, axis=0), 0.0)


def rolled(value, shift):
    return pltpu.roll(value, shift % LANES, 1) if shift % LANES else value


def apply_operator(rows3, weight_rows):
    width = rows3[1].shape[1]
    total = jnp.sum(weight_rows, axis=0, keepdims=True) * rows3[1]
    for across in (0, -1, 1):
        moved = pltpu.roll(weight_rows, across % width, 1) if across else weight_rows
        terms = [
            moved[position : position + 1] * rows3[up + 1]
            for position, (up, side) in enumerate(NEIGHBOURS)
            if side == across
        ]
        part = functools.reduce(jnp.add, terms)
        total = total + (pltpu.roll(part, -across % width, 1) if across else part)
    return total


def gram_of(value, other):
    return lax.dot_general(
        value, other, (((1,), (1,)), ((), ())), precision=HIGHEST, preferred_element_type=jnp.float32
    )


def split(value):
    high = value.astype(jnp.bfloat16)
    rest = value - high.astype(jnp.float32)
    middle = rest.astype(jnp.bfloat16)
    low = (rest - middle.astype(jnp.float32)).astype(jnp.bfloat16)
    return high, middle, low


def inner_parts(image):
    width = image.shape[1]
    lane = lax.broadcasted_iota(jnp.int32, (1, LANES), 1)
    kept = [
        jnp.where(lane >= 2, image[:, :LANES], 0.0),
        image[:, LANES : width - LANES],
        jnp.where(lane < LANES - 2, image[:, width - LANES :], 0.0),
    ]
    return jnp.concatenate(split(jnp.concatenate(kept, axis=1)), axis=0)


def products_of(parts):
    return lax.dot_general(parts, parts, (((1,), (1,)), ((), ())), preferred_element_type=jnp.float32)


def images_of(middle, weights, wanted, second, products):
    for at, row in enumerate(wanted):
        parts = inner_parts(apply_operator([middle(row - 1), middle(row), middle(row + 1)], weights(row)))
        second[at] = parts
        products = products + products_of(parts)
    return products


def inner_rows_kernel(by_row, weights_by_row, middle, second, first_products, second_products):
    rows = by_row.shape[0]
    products = jnp.zeros(first_products.shape, jnp.float32)
    for row in range(1, rows - 1):
        image = apply_operator([by_row[row - 1], by_row[row], by_row[row + 1]], weights_by_row[row])
        middle[row - 1] = image
        products = products + products_of(inner_parts(image))
    first_products[...] = products
    second_products[...] = images_of(
        lambda row: middle[row - 1],
        lambda row: weights_by_row[row],
        range(2, rows - 2),
        second,
        jnp.zeros(second_products.shape, jnp.float32),
    )


def outer_rows_kernel(
    by_row,
    weights_by_row,
    first_message,
    second_message,
    middle,
    first_products,
    second_products,
    second,
    grams,
    left_halo,
    right_halo,
    outer,
):
    rows, planes, width = by_row.shape
    odd_row, has_below, has_above = sides_of("row")
    one, other = first_message[...], second_message[: 2 * planes + 8]
    below = jnp.where(has_below, jnp.where(odd_row, other, one), 0.0)
    above = jnp.where(has_above, jnp.where(odd_row, one, other), 0.0)
    halos = [None, None]
    for side, (halo, present) in enumerate(
        ((below, jnp.logical_not(odd_row)), (above, odd_row))
    ):
        for slot in range(2):
            index = slot if side == 0 else rows + 2 + slot
            blank = jnp.zeros((8, width), jnp.float32)
            weight = halo[2 * planes :] if slot != side else blank
            row_values = jnp.concatenate([halo[slot * planes : (slot + 1) * planes], weight], axis=0)
            parts = edge_columns(row_values[:, :LANES], row_values[:, width - LANES :], PITCH * index)
            parts = [jnp.where(present, part, 0.0) for part in parts]
            halos = [part if total is None else total + part for total, part in zip(halos, parts)]
    left_halo[...], right_halo[...] = halos

    def field(row):
        if 0 <= row < rows:
            return by_row[row]
        at = (row + 2 if row < 0 else row - rows) * planes
        return (below if row < 0 else above)[at : at + planes]

    def weights(row):
        if 0 <= row < rows:
            return weights_by_row[row]
        return (below if row < 0 else above)[2 * planes :]

    products = first_products[...]
    places = (-1, 0, rows - 1, rows)
    for at, row in enumerate(places):
        image = apply_operator([field(row - 1), field(row), field(row + 1)], weights(row))
        outer[at] = image
        if 0 <= row < rows:
            products = products + products_of(inner_parts(image))
    both = [products]
    both.append(
        images_of(
            lambda row: outer[places.index(row)] if row in places else middle[row - 1],
            weights,
            (0, 1, rows - 2, rows - 1),
            second,
            second_products[...],
        )
    )
    for at, products in enumerate(both):
        some = products[:planes] + products[planes : 2 * planes] + products[2 * planes :]
        total = some[:, :planes] + some[:, planes : 2 * planes] + some[:, 2 * planes :]
        grams[:, at * planes : (at + 1) * planes] = total


def apply_on_strip(values, weights):
    total = jnp.sum(weights, axis=0, keepdims=True) * values
    for position, (up, across) in enumerate(NEIGHBOURS):
        moved = pltpu.roll(values, (-PITCH * up - across) % LANES, 1)
        total = total + weights[position : position + 1] * moved
    return total


def late_kernel(rows, left, right, left_halo, right_halo, *rest):
    diagonal_messages, col_messages, (early_grams, grams, edges) = rest[:2], rest[2:4], rest[4:]
    planes = early_grams.shape[0]
    odd_row, has_below, has_above = sides_of("row")
    odd_col, has_left, has_right = sides_of("col")
    beyond = jnp.where(odd_row, has_above, has_below)
    one, other = (
        col[...] + jnp.where(beyond, diagonal[...], 0.0)
        for col, diagonal in zip(col_messages, diagonal_messages)
    )
    lane = lax.broadcasted_iota(jnp.int32, (1, LANES), 1)
    spot, row = lane % PITCH, lane // PITCH
    strips, masks = [], []
    for side, (strip, present, halo) in enumerate(
        (
            (left[...] + left_halo[...], has_left, jnp.where(odd_col, other, one)),
            (right[...] + right_halo[...], has_right, jnp.where(odd_col, one, other)),
        )
    ):
        strips.append(strip + jnp.where(present, unfolded(halo, side * (PITCH - 2), planes), 0.0))
        low = 2 if side == 0 else PITCH - 4
        masks.append((spot >= low) & (spot < low + 2) & (row >= 2) & (row < rows + 2))
    values = [strip[:planes] for strip in strips]
    gram = []
    for at in range(2):
        values = [apply_on_strip(value, strip[planes:]) for value, strip in zip(values, strips)]
        kept = jnp.concatenate([jnp.where(mask, value, 0.0) for mask, value in zip(masks, values)], axis=1)
        both = jnp.concatenate(values, axis=1)
        gram.append(early_grams[:, at * planes : (at + 1) * planes] + gram_of(kept, both))
    edges[...] = both
    at_row = lax.broadcasted_iota(jnp.int32, (planes, planes), 0)
    at_col = lax.broadcasted_iota(jnp.int32, (planes, planes), 1)
    mixed = jnp.where(at_row >= at_col, gram[0], gram[1])
    diagonal = jnp.sum(jnp.where(at_row == at_col, gram[1], 0.0), axis=0, keepdims=True)
    block = jnp.concatenate([mixed[8 * g : 8 * (g + 1)] for g in range(planes // 8)], axis=1)
    last = jnp.concatenate([diagonal] * (LANES // planes), axis=1)
    for target in range(grams.shape[0]):
        for at in range(8):
            grams[target, :, at * LANES : (at + 1) * LANES] = block[at : at + 1]
        grams[target, :, 8 * LANES :] = last


def eliminate(grams, planes, half_way):
    lane = lax.broadcasted_iota(jnp.int32, (8, LANES), 1)
    sub = lax.broadcasted_iota(jnp.int32, (8, LANES), 0)
    first_half = lane < 2 * planes
    groups = planes // 8
    sources = [[gram[8 * g : 8 * (g + 1)] for g in range(groups)] for gram in grams]
    state = []
    for g in range(groups):
        unit = jnp.where(sub + 8 * g == lane % (2 * planes) - planes, 1.0, 0.0)
        unit = unit[:, planes : 2 * planes]
        state.append(jnp.concatenate([sources[0][g], unit, sources[1][g], unit], axis=1))
    columns = []
    for j in range(planes):
        columns.append(
            {
                g: jnp.where(
                    first_half,
                    jnp.broadcast_to(sources[0][g][:, j : j + 1], (8, LANES)),
                    jnp.broadcast_to(sources[1][g][:, j : j + 1], (8, LANES)),
                )
                for g in range(j // 8, groups)
            }
        )
    scale = [jnp.ones((8, LANES), jnp.float32)] * groups
    for step in range(planes):
        own, at = step // 8, step % 8
        column = columns[step]
        root = lax.rsqrt(jnp.broadcast_to(column[own][at : at + 1], (8, LANES)))
        inverse = root * root
        scale[own] = jnp.where(sub == at, root, scale[own])
        left = {g: jnp.where(sub > at, value, 0.0) if g == own else value for g, value in column.items()}
        factors = {g: value * inverse for g, value in left.items()}
        for j in range(step + 1, planes):
            entry = jnp.broadcast_to(column[j // 8][j % 8 : j % 8 + 1], (8, LANES))
            for g in columns[j]:
                change = (left[g] * entry) * inverse if j == step + 1 else factors[g] * entry
                columns[j][g] = columns[j][g] - change
        pivot_row = jnp.broadcast_to(state[own][at : at + 1], (8, LANES))
        for g in range(own, groups):
            state[g] = state[g] - factors[g] * pivot_row
        if step + 1 == planes // 2:
            half_way(jnp.concatenate([state[g] * scale[g] for g in range(groups // 2)], axis=0))
    return jnp.concatenate([state[g] * scale[g] for g in range(groups)], axis=0)


def finish_kernel(
    pixel_count, inner_second, outer_second, edges, parts, basis_out, factor_out, basis, factor, written
):
    planes, rows, width = basis.shape
    half = planes // 2
    at_row = lax.broadcasted_iota(jnp.int32, (planes, planes), 0)
    at_col = lax.broadcasted_iota(jnp.int32, (planes, planes), 1)
    lane = lax.broadcasted_iota(jnp.int32, (1, LANES), 1)
    outer_parts = split(edges[...])
    copies = []

    def solve(inverse, start):
        stop = start + inverse.shape[0]
        high, middle, low = split(inverse)
        left_side = jnp.concatenate([high, high, middle, high, low, middle], axis=1)

        def solved(high, middle, low):
            right_side = jnp.concatenate([high, middle, high, low, high, middle], axis=0)
            return jnp.dot(left_side, right_side, preferred_element_type=jnp.float32)

        outer = solved(*(part[:stop] for part in outer_parts))
        for row in range(rows):
            if 2 <= row < rows - 2:
                held, spot = inner_second, row - 2
            else:
                held, spot = outer_second, row if row < 2 else row - rows + 4
            value = solved(*(held[spot, at * planes : at * planes + stop] for at in range(3)))
            place = PITCH * (row + 2)
            first = rolled(outer[:, :LANES], -(place + 2))
            last = rolled(outer[:, LANES:], LANES - 2 - (place + PITCH - 4))
            basis[start:stop, row, :LANES] = jnp.where(lane < 2, first, value[:, :LANES])
            basis[start:stop, row, LANES : width - LANES] = value[:, LANES : width - LANES]
            basis[start:stop, row, width - LANES :] = jnp.where(
                lane >= LANES - 2, last, value[:, width - LANES :]
            )
        some = pl.ds(start, stop - start)
        copies.append(pltpu.make_async_copy(basis.at[some], basis_out.at[some], written.at[len(copies)]))
        copies[-1].start()

    block = tree_sum([parts[at] for at in range(parts.shape[0])]) / pixel_count
    block = [block[:, at * LANES : (at + 1) * LANES] for at in range(9)]
    mixed, diagonal = jnp.concatenate(block[:8], axis=0), block[8][:, :planes]
    mixed = jnp.concatenate([mixed[:, at * planes : (at + 1) * planes] for at in range(LANES // planes)], axis=0)
    flipped = mixed.T
    first = jnp.where(at_row >= at_col, mixed, flipped)
    second = jnp.where(at_row < at_col, mixed, jnp.where(at_row > at_col, flipped, diagonal))
    low_half = (at_col <= at_row)[:half, :half]
    state = eliminate(
        [first, second],
        planes,
        lambda state: solve(jnp.where(low_half, state[:, 3 * planes : 3 * planes + half], 0.0), 0),
    )
    first_inverse = state[:, planes : 2 * planes]
    product_upper = jnp.where(at_col >= at_row, state[:, 2 * planes : 3 * planes], 0.0)
    solve(jnp.where(at_col <= at_row, state[:, 3 * planes :], 0.0)[half:], half)
    factor[...] = jnp.where(at_col >= at_row, gram_of(product_upper, first_inverse), 0.0)
    copies.append(pltpu.make_async_copy(factor, factor_out, written.at[2]))
    copies[-1].start()
    for copy in copies:
        copy.wait()


def tree_sum(parts):
    while len(parts) > 1:
        parts = [sum(parts[at + 1 : at + 2], parts[at]) for at in range(0, len(parts), 2)]
    return parts[0]


def swap(value, row_pairing=None, col_pairing=None):
    names = ("sec", "row", "col")
    shape = [lax.axis_size(name) for name in names]

    def partner(at, place, pairing):
        other = place if pairing is None else place + 1 if place % 2 != pairing else place - 1
        return other if 0 <= other < shape[at] else None

    pairs = []
    for sec, row, col in itertools.product(*(range(extent) for extent in shape)):
        other_row, other_col = partner(1, row, row_pairing), partner(2, col, col_pairing)
        if other_col is None:
            target = (sec, row ^ 1, col)
        elif other_row is None:
            target = (sec ^ 1, row, col)
        else:
            target = (sec, other_row, other_col)
        pairs.append(tuple((a * shape[1] + b) * shape[2] + c for a, b, c in ((sec, row, col), target)))
    return lax.ppermute(value, names, pairs)


def on_device(sketch, weights):
    planes, rows, width = sketch.shape
    group = lax.axis_size("row") * lax.axis_size("col")
    side = f32(planes + 8, LANES)
    by_row, weights_by_row, left, right, *messages = call(
        pack_rows_kernel,
        [f32(rows, planes, width), f32(rows, 8, width), side, side]
        + [f32(2 * planes + 8, width), f32(2 * planes + 16, width)]
        + [f32(16, LANES)] * 2,
        pltpu.with_memory_space_constraint(sketch, pltpu.HBM),
        pltpu.with_memory_space_constraint(weights, pltpu.HBM),
        memory=pltpu.HBM,
        scratch=[
            pltpu.VMEM(sketch.shape, jnp.float32),
            pltpu.VMEM(weights.shape, jnp.float32),
            pltpu.SemaphoreType.DMA((2,)),
        ],
    )
    from_rows = [swap(messages[at], row_pairing=at) for at in range(2)]
    from_diagonals = [swap(messages[2 + at], row_pairing=0, col_pairing=at) for at in range(2)]
    left, right, *messages = call(
        functools.partial(strips_kernel, rows), [side, side] + [f32(16, LANES)] * 2, left, right, from_rows[1]
    )
    from_cols = [swap(messages[at], col_pairing=at) for at in range(2)]
    parts_of = functools.partial(jax.ShapeDtypeStruct, dtype=jnp.bfloat16)
    products = f32(3 * planes, 3 * planes)
    middle, inner_second, *inner_products = call(
        inner_rows_kernel,
        [f32(rows - 2, planes, width), parts_of((rows - 4, 3 * planes, width)), products, products],
        by_row,
        weights_by_row,
    )
    outer_second, early_grams, *halos = call(
        outer_rows_kernel,
        [parts_of((4, 3 * planes, width)), f32(planes, 2 * planes), side, side],
        by_row,
        weights_by_row,
        *from_rows,
        middle,
        *inner_products,
        scratch=[pltpu.VMEM((4, planes, width), jnp.float32)],
    )
    grams, edges = call(
        functools.partial(late_kernel, rows),
        [f32(group, 1, 9 * LANES), f32(planes, 2 * LANES)],
        left,
        right,
        *halos,
        *from_diagonals,
        *from_cols,
        early_grams,
    )
    parts = lax.all_to_all(grams, ("row", "col"), 0, 0, tiled=True)
    return call(
        functools.partial(finish_kernel, float(rows * width * group)),
        [f32(planes, rows, width), f32(planes, planes)],
        inner_second,
        outer_second,
        edges,
        parts,
        out_memory=pl.ANY,
        scratch=[
            pltpu.VMEM(sketch.shape, jnp.float32),
            pltpu.VMEM((planes, planes), jnp.float32),
            pltpu.SemaphoreType.DMA((3,)),
        ],
    )


def solution(mesh):
    return jax.shard_map(
        on_device,
        mesh=mesh,
        in_specs=(P(None, ("sec", "row"), "col"), P(None, ("sec", "row"), "col")),
        out_specs=(P(None, ("sec", "row"), "col"), P("sec", None)),
        check_vma=False,
    )
```

```python
import functools
import itertools

import jax
import jax.numpy as jnp
from jax import lax
from jax.experimental import pallas as pl
from jax.experimental.pallas import tpu as pltpu
from jax.sharding import PartitionSpec as P

NEIGHBOURS = ((-1, -1), (-1, 0), (-1, 1), (0, -1), (0, 1), (1, -1), (1, 0), (1, 1))
LANES = 128
PITCH = 8
HIGHEST = lax.Precision.HIGHEST


def call(kernel, out_shapes, *operands, memory=pltpu.VMEM, out_memory=pltpu.VMEM, scratch=(), cost=None):
    return pl.pallas_call(
        kernel,
        out_shape=out_shapes,
        in_specs=[pl.BlockSpec(memory_space=memory)] * len(operands),
        out_specs=[pl.BlockSpec(memory_space=out_memory)] * len(out_shapes),
        scratch_shapes=scratch,
        cost_estimate=cost,
        compiler_params=pltpu.CompilerParams(vmem_limit_bytes=40 * 1024 * 1024),
    )(*operands)


def f32(*shape):
    return jax.ShapeDtypeStruct(shape, jnp.float32)


def sides_of(axis):
    place = lax.axis_index(axis)
    return place % 2 == 1, place > 0, place < lax.axis_size(axis) - 1


def edge_columns(first, last, place):
    lane = lax.broadcasted_iota(jnp.int32, (1, LANES), 1)
    own = PITCH - 2
    left = jnp.where((lane >= place + 2) & (lane < place + PITCH), pltpu.roll(first, place + 2, 1), 0.0)
    right = jnp.where((lane >= place) & (lane < place + own), pltpu.roll(last, place + own, 1), 0.0)
    return left, right


def pack_rows_kernel(sketch, weights, by_row, weights_by_row, left, right, *rest):
    bulk_messages, diagonal_messages = rest[:2], rest[2:4]
    tile, weight_tile, arrived = rest[4:]
    copies = [
        pltpu.make_async_copy(sketch, tile, arrived.at[0]),
        pltpu.make_async_copy(weights, weight_tile, arrived.at[1]),
    ]
    for copy in copies:
        copy.start()
    for copy in copies:
        copy.wait()
    rows, planes, width = by_row.shape
    odd_row, _, _ = sides_of("row")
    odd_col, _, _ = sides_of("col")
    lane = lax.broadcasted_iota(jnp.int32, (1, LANES), 1)
    for row in range(rows):
        weights_by_row[row] = weight_tile[:, row, :]
        by_row[row] = tile[:, row, :]
    for message, up in zip(bulk_messages, (odd_row, jnp.logical_not(odd_row))):
        start = jnp.where(up, rows - 2, 0)
        for slot in range(2):
            message[slot * planes : (slot + 1) * planes] = by_row[start + slot]
        message[2 * planes : 2 * planes + 8] = weights_by_row[jnp.where(up, rows - 1, 0)]
    strips = [None, None]
    for row in range(rows):
        first = jnp.concatenate([by_row[row, :, :LANES], weights_by_row[row, :, :LANES]], axis=0)
        last = jnp.concatenate([by_row[row, :, width - LANES :], weights_by_row[row, :, width - LANES :]], axis=0)
        parts = edge_columns(first, last, PITCH * (row + 2))
        strips = [part if strip is None else strip + part for strip, part in zip(strips, parts)]
    left[...], right[...] = strips
    bulk_messages[0][2 * planes + 8 :] = jnp.zeros((8, width), jnp.float32)
    pair = 2 * PITCH
    to_left, to_right = folded(strips[0], 2), folded(strips[1], PITCH - 4)
    for message, up in zip(diagonal_messages, (odd_col, jnp.logical_not(odd_col))):
        edge = jnp.where(up, to_right, to_left)
        below = jnp.where(lane < pair, rolled(edge, -PITCH * rows), 0.0)
        start = PITCH * (rows + 2)
        above = jnp.where((lane >= start) & (lane < start + pair), rolled(edge, PITCH * rows), 0.0)
        message[...] = jnp.where(odd_row, below, above)


def strips_kernel(rows, own_left, own_right, bulk_message, left, right, *col_messages):
    planes = own_left.shape[0] - 8
    odd_row, has_below, has_above = sides_of("row")
    odd_col, _, _ = sides_of("col")
    width = bulk_message.shape[1]
    totals = [own_left[...], own_right[...]]
    present = jnp.where(odd_row, has_below, has_above)
    for slot in range(2):
        place = PITCH * (slot + jnp.where(odd_row, 0, rows + 2))
        halo = [bulk_message[slot * planes : (slot + 1) * planes], bulk_message[2 * planes :]]
        first = jnp.concatenate([part[:, :LANES] for part in halo], axis=0)
        last = jnp.concatenate([part[:, width - LANES :] for part in halo], axis=0)
        parts = edge_columns(first, last, place)
        totals = [total + jnp.where(present, part, 0.0) for total, part in zip(totals, parts)]
    left[...], right[...] = totals
    to_left, to_right = folded(left[...], 2), folded(right[...], PITCH - 4)
    for message, up in zip(col_messages, (odd_col, jnp.logical_not(odd_col))):
        message[...] = jnp.where(up, to_right, to_left)


def folded(strip, spot):
    lane = lax.broadcasted_iota(jnp.int32, (1, LANES), 1)
    groups = strip.shape[0] // 8
    pieces = []
    for group in range(groups):
        target = 2 * group if group < groups - 1 else 0
        moved = rolled(strip[8 * group : 8 * (group + 1)], target - spot)
        pieces.append(jnp.where((lane % PITCH) // 2 == target // 2, moved, 0.0))
    return jnp.concatenate([functools.reduce(jnp.add, pieces[:-1]), pieces[-1]], axis=0)


def unfolded(message, spot, planes):
    lane = lax.broadcasted_iota(jnp.int32, (1, LANES), 1)
    pieces = [rolled(message[:8], spot - 2 * group) for group in range(planes // 8)] + [rolled(message[8:], spot)]
    return jnp.where((lane % PITCH) // 2 == spot // 2, jnp.concatenate(pieces, axis=0), 0.0)


def rolled(value, shift):
    return pltpu.roll(value, shift % LANES, 1) if shift % LANES else value


def apply_operator(rows3, weight_rows):
    width = rows3[1].shape[1]
    total = jnp.sum(weight_rows, axis=0, keepdims=True) * rows3[1]
    for across in (0, -1, 1):
        moved = pltpu.roll(weight_rows, across % width, 1) if across else weight_rows
        terms = [
            moved[position : position + 1] * rows3[up + 1]
            for position, (up, side) in enumerate(NEIGHBOURS)
            if side == across
        ]
        part = functools.reduce(jnp.add, terms)
        total = total + (pltpu.roll(part, -across % width, 1) if across else part)
    return total


def gram_of(value, other):
    return lax.dot_general(
        value, other, (((1,), (1,)), ((), ())), precision=HIGHEST, preferred_element_type=jnp.float32
    )


def split(value):
    high = value.astype(jnp.bfloat16)
    rest = value - high.astype(jnp.float32)
    middle = rest.astype(jnp.bfloat16)
    low = (rest - middle.astype(jnp.float32)).astype(jnp.bfloat16)
    return high, middle, low


def inner_parts(image):
    width = image.shape[1]
    lane = lax.broadcasted_iota(jnp.int32, (1, LANES), 1)
    kept = [
        jnp.where(lane >= 2, image[:, :LANES], 0.0),
        image[:, LANES : width - LANES],
        jnp.where(lane < LANES - 2, image[:, width - LANES :], 0.0),
    ]
    return jnp.concatenate(split(jnp.concatenate(kept, axis=1)), axis=0)


def products_of(parts):
    return lax.dot_general(parts, parts, (((1,), (1,)), ((), ())), preferred_element_type=jnp.float32)


def images_of(middle, weights, wanted, second, products):
    for at, row in enumerate(wanted):
        parts = inner_parts(apply_operator([middle(row - 1), middle(row), middle(row + 1)], weights(row)))
        second[at] = parts
        products = products + products_of(parts)
    return products


def inner_rows_kernel(by_row, weights_by_row, middle, second, first_products, second_products):
    rows = by_row.shape[0]
    products = jnp.zeros(first_products.shape, jnp.float32)
    for row in range(1, rows - 1):
        image = apply_operator([by_row[row - 1], by_row[row], by_row[row + 1]], weights_by_row[row])
        middle[row - 1] = image
        products = products + products_of(inner_parts(image))
    first_products[...] = products
    second_products[...] = images_of(
        lambda row: middle[row - 1],
        lambda row: weights_by_row[row],
        range(2, rows - 2),
        second,
        jnp.zeros(second_products.shape, jnp.float32),
    )


def outer_rows_kernel(
    by_row,
    weights_by_row,
    first_message,
    second_message,
    middle,
    first_products,
    second_products,
    second,
    grams,
    left_halo,
    right_halo,
    outer,
):
    rows, planes, width = by_row.shape
    odd_row, has_below, has_above = sides_of("row")
    one, other = first_message[: 2 * planes + 8], second_message[...]
    below = jnp.where(has_below, jnp.where(odd_row, other, one), 0.0)
    above = jnp.where(has_above, jnp.where(odd_row, one, other), 0.0)
    halos = [None, None]
    for side, (halo, present) in enumerate(
        ((below, jnp.logical_not(odd_row)), (above, odd_row))
    ):
        for slot in range(2):
            index = slot if side == 0 else rows + 2 + slot
            blank = jnp.zeros((8, width), jnp.float32)
            weight = halo[2 * planes :] if slot != side else blank
            row_values = jnp.concatenate([halo[slot * planes : (slot + 1) * planes], weight], axis=0)
            parts = edge_columns(row_values[:, :LANES], row_values[:, width - LANES :], PITCH * index)
            parts = [jnp.where(present, part, 0.0) for part in parts]
            halos = [part if total is None else total + part for total, part in zip(halos, parts)]
    left_halo[...], right_halo[...] = halos

    def field(row):
        if 0 <= row < rows:
            return by_row[row]
        at = (row + 2 if row < 0 else row - rows) * planes
        return (below if row < 0 else above)[at : at + planes]

    def weights(row):
        if 0 <= row < rows:
            return weights_by_row[row]
        return (below if row < 0 else above)[2 * planes :]

    products = first_products[...]
    places = (-1, 0, rows - 1, rows)
    for at, row in enumerate(places):
        image = apply_operator([field(row - 1), field(row), field(row + 1)], weights(row))
        outer[at] = image
        if 0 <= row < rows:
            products = products + products_of(inner_parts(image))
    both = [products]
    both.append(
        images_of(
            lambda row: outer[places.index(row)] if row in places else middle[row - 1],
            weights,
            (0, 1, rows - 2, rows - 1),
            second,
            second_products[...],
        )
    )
    for at, products in enumerate(both):
        some = products[:planes] + products[planes : 2 * planes] + products[2 * planes :]
        total = some[:, :planes] + some[:, planes : 2 * planes] + some[:, 2 * planes :]
        grams[:, at * planes : (at + 1) * planes] = total


def apply_on_strip(values, weights):
    total = jnp.sum(weights, axis=0, keepdims=True) * values
    for position, (up, across) in enumerate(NEIGHBOURS):
        moved = pltpu.roll(values, (-PITCH * up - across) % LANES, 1)
        total = total + weights[position : position + 1] * moved
    return total


def late_kernel(rows, left, right, left_halo, right_halo, *rest):
    diagonal_messages, col_messages, (early_grams, grams, edges) = rest[:2], rest[2:4], rest[4:]
    planes = early_grams.shape[0]
    odd_row, has_below, has_above = sides_of("row")
    odd_col, has_left, has_right = sides_of("col")
    beyond = jnp.where(odd_row, has_above, has_below)
    one, other = (
        col[...] + jnp.where(beyond, diagonal[...], 0.0)
        for col, diagonal in zip(col_messages, diagonal_messages)
    )
    lane = lax.broadcasted_iota(jnp.int32, (1, LANES), 1)
    spot, row = lane % PITCH, lane // PITCH
    strips, masks = [], []
    for side, (strip, present, halo) in enumerate(
        (
            (left[...] + left_halo[...], has_left, jnp.where(odd_col, other, one)),
            (right[...] + right_halo[...], has_right, jnp.where(odd_col, one, other)),
        )
    ):
        strips.append(strip + jnp.where(present, unfolded(halo, side * (PITCH - 2), planes), 0.0))
        low = 2 if side == 0 else PITCH - 4
        masks.append((spot >= low) & (spot < low + 2) & (row >= 2) & (row < rows + 2))
    values = [strip[:planes] for strip in strips]
    gram = []
    for at in range(2):
        values = [apply_on_strip(value, strip[planes:]) for value, strip in zip(values, strips)]
        kept = jnp.concatenate([jnp.where(mask, value, 0.0) for mask, value in zip(masks, values)], axis=1)
        both = jnp.concatenate(values, axis=1)
        gram.append(early_grams[:, at * planes : (at + 1) * planes] + gram_of(kept, both))
    edges[...] = both
    at_row = lax.broadcasted_iota(jnp.int32, (planes, planes), 0)
    at_col = lax.broadcasted_iota(jnp.int32, (planes, planes), 1)
    mixed = jnp.where(at_row >= at_col, gram[0], gram[1])
    diagonal = jnp.sum(jnp.where(at_row == at_col, gram[1], 0.0), axis=0, keepdims=True)
    block = jnp.concatenate([mixed[8 * g : 8 * (g + 1)] for g in range(planes // 8)], axis=1)
    last = jnp.concatenate([diagonal] * (LANES // planes), axis=1)
    for target in range(grams.shape[0]):
        for at in range(8):
            grams[target, :, at * LANES : (at + 1) * LANES] = block[at : at + 1]
        grams[target, :, 8 * LANES :] = last


def eliminate(grams, planes, half_way):
    lane = lax.broadcasted_iota(jnp.int32, (8, LANES), 1)
    sub = lax.broadcasted_iota(jnp.int32, (8, LANES), 0)
    first_half = lane < 2 * planes
    groups = planes // 8
    sources = [[gram[8 * g : 8 * (g + 1)] for g in range(groups)] for gram in grams]
    state = []
    for g in range(groups):
        unit = jnp.where(sub + 8 * g == lane % (2 * planes) - planes, 1.0, 0.0)
        unit = unit[:, planes : 2 * planes]
        state.append(jnp.concatenate([sources[0][g], unit, sources[1][g], unit], axis=1))
    columns = []
    for j in range(planes):
        columns.append(
            {
                g: jnp.where(
                    first_half,
                    jnp.broadcast_to(sources[0][g][:, j : j + 1], (8, LANES)),
                    jnp.broadcast_to(sources[1][g][:, j : j + 1], (8, LANES)),
                )
                for g in range(j // 8, groups)
            }
        )
    scale = [jnp.ones((8, LANES), jnp.float32)] * groups
    for step in range(planes):
        own, at = step // 8, step % 8
        column = columns[step]
        root = lax.rsqrt(jnp.broadcast_to(column[own][at : at + 1], (8, LANES)))
        inverse = root * root
        scale[own] = jnp.where(sub == at, root, scale[own])
        left = {g: jnp.where(sub > at, value, 0.0) if g == own else value for g, value in column.items()}
        factors = {g: value * inverse for g, value in left.items()}
        for j in range(step + 1, planes):
            entry = jnp.broadcast_to(column[j // 8][j % 8 : j % 8 + 1], (8, LANES))
            for g in columns[j]:
                change = (left[g] * entry) * inverse if j == step + 1 else factors[g] * entry
                columns[j][g] = columns[j][g] - change
        pivot_row = jnp.broadcast_to(state[own][at : at + 1], (8, LANES))
        for g in range(own, groups):
            state[g] = state[g] - factors[g] * pivot_row
        if step + 1 == planes // 2:
            half_way(jnp.concatenate([state[g] * scale[g] for g in range(groups // 2)], axis=0))
    return jnp.concatenate([state[g] * scale[g] for g in range(groups)], axis=0)


def finish_kernel(
    pixel_count, inner_second, outer_second, edges, parts, basis_out, factor_out, basis, factor, written
):
    planes, rows, width = basis.shape
    half = planes // 2
    at_row = lax.broadcasted_iota(jnp.int32, (planes, planes), 0)
    at_col = lax.broadcasted_iota(jnp.int32, (planes, planes), 1)
    lane = lax.broadcasted_iota(jnp.int32, (1, LANES), 1)
    outer_parts = split(edges[...])
    copies = []

    def solve(inverse, start):
        stop = start + inverse.shape[0]
        high, middle, low = split(inverse)
        left_side = jnp.concatenate([high, high, middle, high, low, middle], axis=1)

        def solved(high, middle, low):
            right_side = jnp.concatenate([high, middle, high, low, high, middle], axis=0)
            return jnp.dot(left_side, right_side, preferred_element_type=jnp.float32)

        outer = solved(*(part[:stop] for part in outer_parts))
        for row in range(rows):
            if 2 <= row < rows - 2:
                held, spot = inner_second, row - 2
            else:
                held, spot = outer_second, row if row < 2 else row - rows + 4
            value = solved(*(held[spot, at * planes : at * planes + stop] for at in range(3)))
            place = PITCH * (row + 2)
            first = rolled(outer[:, :LANES], -(place + 2))
            last = rolled(outer[:, LANES:], LANES - 2 - (place + PITCH - 4))
            basis[start:stop, row, :LANES] = jnp.where(lane < 2, first, value[:, :LANES])
            basis[start:stop, row, LANES : width - LANES] = value[:, LANES : width - LANES]
            basis[start:stop, row, width - LANES :] = jnp.where(
                lane >= LANES - 2, last, value[:, width - LANES :]
            )
        some = pl.ds(start, stop - start)
        copies.append(pltpu.make_async_copy(basis.at[some], basis_out.at[some], written.at[len(copies)]))
        copies[-1].start()

    block = tree_sum([parts[at] for at in range(parts.shape[0])]) / pixel_count
    block = [block[:, at * LANES : (at + 1) * LANES] for at in range(9)]
    mixed, diagonal = jnp.concatenate(block[:8], axis=0), block[8][:, :planes]
    mixed = jnp.concatenate([mixed[:, at * planes : (at + 1) * planes] for at in range(LANES // planes)], axis=0)
    flipped = mixed.T
    first = jnp.where(at_row >= at_col, mixed, flipped)
    second = jnp.where(at_row < at_col, mixed, jnp.where(at_row > at_col, flipped, diagonal))
    low_half = (at_col <= at_row)[:half, :half]
    state = eliminate(
        [first, second],
        planes,
        lambda state: solve(jnp.where(low_half, state[:, 3 * planes : 3 * planes + half], 0.0), 0),
    )
    first_inverse = state[:, planes : 2 * planes]
    product_upper = jnp.where(at_col >= at_row, state[:, 2 * planes : 3 * planes], 0.0)
    solve(jnp.where(at_col <= at_row, state[:, 3 * planes :], 0.0)[half:], half)
    factor[...] = jnp.where(at_col >= at_row, gram_of(product_upper, first_inverse), 0.0)
    copies.append(pltpu.make_async_copy(factor, factor_out, written.at[2]))
    copies[-1].start()
    for copy in copies:
        copy.wait()


def tree_sum(parts):
    while len(parts) > 1:
        parts = [sum(parts[at + 1 : at + 2], parts[at]) for at in range(0, len(parts), 2)]
    return parts[0]


def swap(value, row_pairing=None, col_pairing=None):
    names = ("sec", "row", "col")
    shape = [lax.axis_size(name) for name in names]

    def partner(at, place, pairing):
        other = place if pairing is None else place + 1 if place % 2 != pairing else place - 1
        return other if 0 <= other < shape[at] else None

    pairs = []
    for sec, row, col in itertools.product(*(range(extent) for extent in shape)):
        other_row, other_col = partner(1, row, row_pairing), partner(2, col, col_pairing)
        if other_col is None:
            target = (sec, row ^ 1, col)
        elif other_row is None:
            target = (sec ^ 1, row, col)
        else:
            target = (sec, other_row, other_col)
        pairs.append(tuple((a * shape[1] + b) * shape[2] + c for a, b, c in ((sec, row, col), target)))
    return lax.ppermute(value, names, pairs)


def on_device(sketch, weights):
    planes, rows, width = sketch.shape
    group = lax.axis_size("row") * lax.axis_size("col")
    side = f32(planes + 8, LANES)
    by_row, weights_by_row, left, right, *messages = call(
        pack_rows_kernel,
        [f32(rows, planes, width), f32(rows, 8, width), side, side]
        + [f32(2 * planes + 16, width), f32(2 * planes + 8, width)]
        + [f32(16, LANES)] * 2,
        pltpu.with_memory_space_constraint(sketch, pltpu.HBM),
        pltpu.with_memory_space_constraint(weights, pltpu.HBM),
        memory=pltpu.HBM,
        scratch=[
            pltpu.VMEM(sketch.shape, jnp.float32),
            pltpu.VMEM(weights.shape, jnp.float32),
            pltpu.SemaphoreType.DMA((2,)),
        ],
    )
    from_rows = [swap(messages[at], row_pairing=at) for at in range(2)]
    from_diagonals = [swap(messages[2 + at], row_pairing=0, col_pairing=at) for at in range(2)]
    left, right, *messages = call(
        functools.partial(strips_kernel, rows), [side, side] + [f32(16, LANES)] * 2, left, right, from_rows[1]
    )
    from_cols = [swap(messages[at], col_pairing=at) for at in range(2)]
    parts_of = functools.partial(jax.ShapeDtypeStruct, dtype=jnp.bfloat16)
    products = f32(3 * planes, 3 * planes)
    middle, inner_second, *inner_products = call(
        inner_rows_kernel,
        [f32(rows - 2, planes, width), parts_of((rows - 4, 3 * planes, width)), products, products],
        by_row,
        weights_by_row,
    )
    outer_second, early_grams, *halos = call(
        outer_rows_kernel,
        [parts_of((4, 3 * planes, width)), f32(planes, 2 * planes), side, side],
        by_row,
        weights_by_row,
        *from_rows,
        middle,
        *inner_products,
        scratch=[pltpu.VMEM((4, planes, width), jnp.float32)],
    )
    grams, edges = call(
        functools.partial(late_kernel, rows),
        [f32(group, 1, 9 * LANES), f32(planes, 2 * LANES)],
        left,
        right,
        *halos,
        *from_diagonals,
        *from_cols,
        early_grams,
    )
    parts = lax.all_to_all(grams, ("row", "col"), 0, 0, tiled=True)
    return call(
        functools.partial(finish_kernel, float(rows * width * group)),
        [f32(planes, rows, width), f32(planes, planes)],
        inner_second,
        outer_second,
        edges,
        parts,
        out_memory=pl.ANY,
        scratch=[
            pltpu.VMEM(sketch.shape, jnp.float32),
            pltpu.VMEM((planes, planes), jnp.float32),
            pltpu.SemaphoreType.DMA((3,)),
        ],
    )


def solution(mesh):
    return jax.shard_map(
        on_device,
        mesh=mesh,
        in_specs=(P(None, ("sec", "row"), "col"), P(None, ("sec", "row"), "col")),
        out_specs=(P(None, ("sec", "row"), "col"), P("sec", None)),
        check_vma=False,
    )
```

```python
import functools
import itertools

import jax
import jax.numpy as jnp
from jax import lax
from jax.experimental import pallas as pl
from jax.experimental.pallas import tpu as pltpu
from jax.sharding import PartitionSpec as P

NEIGHBOURS = ((-1, -1), (-1, 0), (-1, 1), (0, -1), (0, 1), (1, -1), (1, 0), (1, 1))
LANES = 128
PITCH = 8
HIGHEST = lax.Precision.HIGHEST


def call(kernel, out_shapes, *operands, memory=pltpu.VMEM, out_memory=pltpu.VMEM, scratch=(), cost=None):
    return pl.pallas_call(
        kernel,
        out_shape=out_shapes,
        in_specs=[pl.BlockSpec(memory_space=memory)] * len(operands),
        out_specs=[pl.BlockSpec(memory_space=out_memory)] * len(out_shapes),
        scratch_shapes=scratch,
        cost_estimate=cost,
        compiler_params=pltpu.CompilerParams(vmem_limit_bytes=40 * 1024 * 1024),
    )(*operands)


def f32(*shape):
    return jax.ShapeDtypeStruct(shape, jnp.float32)


def sides_of(axis):
    place = lax.axis_index(axis)
    return place % 2 == 1, place > 0, place < lax.axis_size(axis) - 1


def edge_columns(first, last, place):
    lane = lax.broadcasted_iota(jnp.int32, (1, LANES), 1)
    own = PITCH - 2
    left = jnp.where((lane >= place + 2) & (lane < place + PITCH), pltpu.roll(first, place + 2, 1), 0.0)
    right = jnp.where((lane >= place) & (lane < place + own), pltpu.roll(last, place + own, 1), 0.0)
    return left, right


def pack_rows_kernel(sketch, weights, by_row, weights_by_row, left, right, *rest):
    bulk_messages, diagonal_messages = rest[:2], rest[2:4]
    tile, weight_tile, arrived = rest[4:]
    copies = [
        pltpu.make_async_copy(sketch, tile, arrived.at[0]),
        pltpu.make_async_copy(weights, weight_tile, arrived.at[1]),
    ]
    for copy in copies:
        copy.start()
    for copy in copies:
        copy.wait()
    rows, planes, width = by_row.shape
    odd_row, _, _ = sides_of("row")
    odd_col, _, _ = sides_of("col")
    lane = lax.broadcasted_iota(jnp.int32, (1, LANES), 1)
    for row in range(rows):
        weights_by_row[row] = weight_tile[:, row, :]
        by_row[row] = tile[:, row, :]
    for message, up in zip(bulk_messages, (odd_row, jnp.logical_not(odd_row))):
        start = jnp.where(up, rows - 2, 0)
        for slot in range(2):
            message[slot * planes : (slot + 1) * planes] = by_row[start + slot]
        message[2 * planes : 2 * planes + 8] = weights_by_row[jnp.where(up, rows - 1, 0)]
    strips = [None, None]
    for row in range(rows):
        first = jnp.concatenate([by_row[row, :, :LANES], weights_by_row[row, :, :LANES]], axis=0)
        last = jnp.concatenate([by_row[row, :, width - LANES :], weights_by_row[row, :, width - LANES :]], axis=0)
        parts = edge_columns(first, last, PITCH * (row + 2))
        strips = [part if strip is None else strip + part for strip, part in zip(strips, parts)]
    left[...], right[...] = strips
    bulk_messages[0][2 * planes + 8 :] = jnp.zeros((8, width), jnp.float32)
    pair = 2 * PITCH
    to_left, to_right = folded(strips[0], 2), folded(strips[1], PITCH - 4)
    for message, up in zip(diagonal_messages, (odd_col, jnp.logical_not(odd_col))):
        edge = jnp.where(up, to_right, to_left)
        below = jnp.where(lane < pair, rolled(edge, -PITCH * rows), 0.0)
        start = PITCH * (rows + 2)
        above = jnp.where((lane >= start) & (lane < start + pair), rolled(edge, PITCH * rows), 0.0)
        message[...] = jnp.where(odd_row, below, above)


def strips_kernel(rows, own_left, own_right, bulk_message, left, right, *col_messages):
    planes = own_left.shape[0] - 8
    odd_row, has_below, has_above = sides_of("row")
    odd_col, _, _ = sides_of("col")
    width = bulk_message.shape[1]
    totals = [own_left[...], own_right[...]]
    present = jnp.where(odd_row, has_below, has_above)
    for slot in range(2):
        place = PITCH * (slot + jnp.where(odd_row, 0, rows + 2))
        halo = [bulk_message[slot * planes : (slot + 1) * planes], bulk_message[2 * planes :]]
        first = jnp.concatenate([part[:, :LANES] for part in halo], axis=0)
        last = jnp.concatenate([part[:, width - LANES :] for part in halo], axis=0)
        parts = edge_columns(first, last, place)
        totals = [total + jnp.where(present, part, 0.0) for total, part in zip(totals, parts)]
    left[...], right[...] = totals
    to_left, to_right = folded(left[...], 2), folded(right[...], PITCH - 4)
    for message, up in zip(col_messages, (odd_col, jnp.logical_not(odd_col))):
        message[...] = jnp.where(up, to_right, to_left)


def folded(strip, spot):
    lane = lax.broadcasted_iota(jnp.int32, (1, LANES), 1)
    groups = strip.shape[0] // 8
    pieces = []
    for group in range(groups):
        target = 2 * group if group < groups - 1 else 0
        moved = rolled(strip[8 * group : 8 * (group + 1)], target - spot)
        pieces.append(jnp.where((lane % PITCH) // 2 == target // 2, moved, 0.0))
    return jnp.concatenate([functools.reduce(jnp.add, pieces[:-1]), pieces[-1]], axis=0)


def unfolded(message, spot, planes):
    lane = lax.broadcasted_iota(jnp.int32, (1, LANES), 1)
    pieces = [rolled(message[:8], spot - 2 * group) for group in range(planes // 8)] + [rolled(message[8:], spot)]
    return jnp.where((lane % PITCH) // 2 == spot // 2, jnp.concatenate(pieces, axis=0), 0.0)


def rolled(value, shift):
    return pltpu.roll(value, shift % LANES, 1) if shift % LANES else value


def apply_operator(rows3, weight_rows):
    width = rows3[1].shape[1]
    total = jnp.sum(weight_rows, axis=0, keepdims=True) * rows3[1]
    for across in (0, -1, 1):
        moved = pltpu.roll(weight_rows, across % width, 1) if across else weight_rows
        terms = [
            moved[position : position + 1] * rows3[up + 1]
            for position, (up, side) in enumerate(NEIGHBOURS)
            if side == across
        ]
        part = functools.reduce(jnp.add, terms)
        total = total + (pltpu.roll(part, -across % width, 1) if across else part)
    return total


def gram_of(value, other):
    return lax.dot_general(
        value, other, (((1,), (1,)), ((), ())), precision=HIGHEST, preferred_element_type=jnp.float32
    )


def split(value):
    high = value.astype(jnp.bfloat16)
    rest = value - high.astype(jnp.float32)
    middle = rest.astype(jnp.bfloat16)
    low = (rest - middle.astype(jnp.float32)).astype(jnp.bfloat16)
    return high, middle, low


def inner_parts(image):
    width = image.shape[1]
    lane = lax.broadcasted_iota(jnp.int32, (1, LANES), 1)
    kept = [
        jnp.where(lane >= 2, image[:, :LANES], 0.0),
        image[:, LANES : width - LANES],
        jnp.where(lane < LANES - 2, image[:, width - LANES :], 0.0),
    ]
    return jnp.concatenate(split(jnp.concatenate(kept, axis=1)), axis=0)


def products_of(parts):
    return lax.dot_general(parts, parts, (((1,), (1,)), ((), ())), preferred_element_type=jnp.float32)


def images_of(middle, weights, wanted, second, products):
    for at, row in enumerate(wanted):
        parts = inner_parts(apply_operator([middle(row - 1), middle(row), middle(row + 1)], weights(row)))
        second[at] = parts
        products = products + products_of(parts)
    return products


def inner_rows_kernel(by_row, weights_by_row, middle, second, first_products, second_products):
    rows = by_row.shape[0]
    products = jnp.zeros(first_products.shape, jnp.float32)
    for row in range(1, rows - 1):
        image = apply_operator([by_row[row - 1], by_row[row], by_row[row + 1]], weights_by_row[row])
        middle[row - 1] = image
        products = products + products_of(inner_parts(image))
    first_products[...] = products
    second_products[...] = images_of(
        lambda row: middle[row - 1],
        lambda row: weights_by_row[row],
        range(2, rows - 2),
        second,
        jnp.zeros(second_products.shape, jnp.float32),
    )


def outer_rows_kernel(
    by_row,
    weights_by_row,
    first_message,
    second_message,
    middle,
    first_products,
    second_products,
    second,
    grams,
    left_halo,
    right_halo,
    outer,
):
    rows, planes, width = by_row.shape
    odd_row, has_below, has_above = sides_of("row")
    one, other = first_message[: 2 * planes + 8], second_message[...]
    below = jnp.where(has_below, jnp.where(odd_row, other, one), 0.0)
    above = jnp.where(has_above, jnp.where(odd_row, one, other), 0.0)
    halos = [None, None]
    for side, (halo, present) in enumerate(
        ((below, jnp.logical_not(odd_row)), (above, odd_row))
    ):
        for slot in range(2):
            index = slot if side == 0 else rows + 2 + slot
            blank = jnp.zeros((8, width), jnp.float32)
            weight = halo[2 * planes :] if slot != side else blank
            row_values = jnp.concatenate([halo[slot * planes : (slot + 1) * planes], weight], axis=0)
            parts = edge_columns(row_values[:, :LANES], row_values[:, width - LANES :], PITCH * index)
            parts = [jnp.where(present, part, 0.0) for part in parts]
            halos = [part if total is None else total + part for total, part in zip(halos, parts)]
    left_halo[...], right_halo[...] = halos

    def field(row):
        if 0 <= row < rows:
            return by_row[row]
        at = (row + 2 if row < 0 else row - rows) * planes
        return (below if row < 0 else above)[at : at + planes]

    def weights(row):
        if 0 <= row < rows:
            return weights_by_row[row]
        return (below if row < 0 else above)[2 * planes :]

    products = first_products[...]
    places = (-1, 0, rows - 1, rows)
    for at, row in enumerate(places):
        image = apply_operator([field(row - 1), field(row), field(row + 1)], weights(row))
        outer[at] = image
        if 0 <= row < rows:
            products = products + products_of(inner_parts(image))
    both = [products]
    both.append(
        images_of(
            lambda row: outer[places.index(row)] if row in places else middle[row - 1],
            weights,
            (0, 1, rows - 2, rows - 1),
            second,
            second_products[...],
        )
    )
    for at, products in enumerate(both):
        some = products[:planes] + products[planes : 2 * planes] + products[2 * planes :]
        total = some[:, :planes] + some[:, planes : 2 * planes] + some[:, 2 * planes :]
        grams[:, at * planes : (at + 1) * planes] = total


def apply_on_strip(values, weights):
    total = jnp.sum(weights, axis=0, keepdims=True) * values
    for position, (up, across) in enumerate(NEIGHBOURS):
        moved = pltpu.roll(values, (-PITCH * up - across) % LANES, 1)
        total = total + weights[position : position + 1] * moved
    return total


def late_kernel(rows, left, right, left_halo, right_halo, *rest):
    diagonal_messages, col_messages, (early_grams, grams, edges) = rest[:2], rest[2:4], rest[4:]
    planes = early_grams.shape[0]
    odd_row, has_below, has_above = sides_of("row")
    odd_col, has_left, has_right = sides_of("col")
    beyond = jnp.where(odd_row, has_above, has_below)
    one, other = (
        col[...] + jnp.where(beyond, diagonal[...], 0.0)
        for col, diagonal in zip(col_messages, diagonal_messages)
    )
    lane = lax.broadcasted_iota(jnp.int32, (1, LANES), 1)
    spot, row = lane % PITCH, lane // PITCH
    strips, masks = [], []
    for side, (strip, present, halo) in enumerate(
        (
            (left[...] + left_halo[...], has_left, jnp.where(odd_col, other, one)),
            (right[...] + right_halo[...], has_right, jnp.where(odd_col, one, other)),
        )
    ):
        strips.append(strip + jnp.where(present, unfolded(halo, side * (PITCH - 2), planes), 0.0))
        low = 2 if side == 0 else PITCH - 4
        masks.append((spot >= low) & (spot < low + 2) & (row >= 2) & (row < rows + 2))
    values = [strip[:planes] for strip in strips]
    gram = []
    for at in range(2):
        values = [apply_on_strip(value, strip[planes:]) for value, strip in zip(values, strips)]
        kept = jnp.concatenate([jnp.where(mask, value, 0.0) for mask, value in zip(masks, values)], axis=1)
        both = jnp.concatenate(values, axis=1)
        gram.append(early_grams[:, at * planes : (at + 1) * planes] + gram_of(kept, both))
    edges[...] = both
    at_row = lax.broadcasted_iota(jnp.int32, (planes, planes), 0)
    at_col = lax.broadcasted_iota(jnp.int32, (planes, planes), 1)
    mixed = jnp.where(at_row >= at_col, gram[0], gram[1])
    diagonal = jnp.sum(jnp.where(at_row == at_col, gram[1], 0.0), axis=0, keepdims=True)
    block = jnp.concatenate([mixed[8 * g : 8 * (g + 1)] for g in range(planes // 8)], axis=1)
    last = jnp.concatenate([diagonal] * (LANES // planes), axis=1)
    for target in range(grams.shape[0]):
        for at in range(8):
            grams[target, :, at * LANES : (at + 1) * LANES] = block[at : at + 1]
        grams[target, :, 8 * LANES :] = last


def eliminate(grams, planes, half_way):
    lane = lax.broadcasted_iota(jnp.int32, (8, LANES), 1)
    sub = lax.broadcasted_iota(jnp.int32, (8, LANES), 0)
    first_half = lane < 2 * planes
    groups = planes // 8
    sources = [[gram[8 * g : 8 * (g + 1)] for g in range(groups)] for gram in grams]
    state = []
    for g in range(groups):
        unit = jnp.where(sub + 8 * g == lane % (2 * planes) - planes, 1.0, 0.0)
        unit = unit[:, planes : 2 * planes]
        state.append(jnp.concatenate([sources[0][g], unit, sources[1][g], unit], axis=1))
    columns = []
    for j in range(planes):
        columns.append(
            {
                g: jnp.where(
                    first_half,
                    jnp.broadcast_to(sources[0][g][:, j : j + 1], (8, LANES)),
                    jnp.broadcast_to(sources[1][g][:, j : j + 1], (8, LANES)),
                )
                for g in range(j // 8, groups)
            }
        )
    scale = [jnp.ones((8, LANES), jnp.float32)] * groups
    for step in range(planes):
        own, at = step // 8, step % 8
        column = columns[step]
        root = lax.rsqrt(jnp.broadcast_to(column[own][at : at + 1], (8, LANES)))
        inverse = root * root
        scale[own] = jnp.where(sub == at, root, scale[own])
        left = {g: jnp.where(sub > at, value, 0.0) if g == own else value for g, value in column.items()}
        factors = {g: value * inverse for g, value in left.items()}
        for j in range(step + 1, planes):
            entry = jnp.broadcast_to(column[j // 8][j % 8 : j % 8 + 1], (8, LANES))
            for g in columns[j]:
                change = (left[g] * entry) * inverse if j == step + 1 else factors[g] * entry
                columns[j][g] = columns[j][g] - change
        pivot_row = jnp.broadcast_to(state[own][at : at + 1], (8, LANES))
        for g in range(own, groups):
            state[g] = state[g] - factors[g] * pivot_row
        if step + 1 == planes // 2:
            half_way(jnp.concatenate([state[g] * scale[g] for g in range(groups // 2)], axis=0))
    return jnp.concatenate([state[g] * scale[g] for g in range(groups)], axis=0)


def finish_kernel(
    pixel_count, inner_second, outer_second, edges, parts, basis_out, factor_out, basis, factor, written
):
    planes, rows, width = basis.shape
    half = planes // 2
    at_row = lax.broadcasted_iota(jnp.int32, (planes, planes), 0)
    at_col = lax.broadcasted_iota(jnp.int32, (planes, planes), 1)
    lane = lax.broadcasted_iota(jnp.int32, (1, LANES), 1)
    outer_parts = split(edges[...])
    copies = []

    def solve(inverse, start):
        stop = start + inverse.shape[0]
        high, middle, low = split(inverse)
        left_side = jnp.concatenate([high, high, middle, high, low, middle], axis=1)

        def solved(high, middle, low):
            right_side = jnp.concatenate([high, middle, high, low, high, middle], axis=0)
            return jnp.dot(left_side, right_side, preferred_element_type=jnp.float32)

        outer = solved(*(part[:stop] for part in outer_parts))
        for row in range(rows):
            if 2 <= row < rows - 2:
                held, spot = inner_second, row - 2
            else:
                held, spot = outer_second, row if row < 2 else row - rows + 4
            value = solved(*(held[spot, at * planes : at * planes + stop] for at in range(3)))
            place = PITCH * (row + 2)
            first = rolled(outer[:, :LANES], -(place + 2))
            last = rolled(outer[:, LANES:], LANES - 2 - (place + PITCH - 4))
            basis[start:stop, row, :LANES] = jnp.where(lane < 2, first, value[:, :LANES])
            basis[start:stop, row, LANES : width - LANES] = value[:, LANES : width - LANES]
            basis[start:stop, row, width - LANES :] = jnp.where(
                lane >= LANES - 2, last, value[:, width - LANES :]
            )
        some = pl.ds(start, stop - start)
        copies.append(pltpu.make_async_copy(basis.at[some], basis_out.at[some], written.at[len(copies)]))
        copies[-1].start()

    block = tree_sum([parts[at] for at in range(parts.shape[0])]) / pixel_count
    block = [block[:, at * LANES : (at + 1) * LANES] for at in range(9)]
    mixed, diagonal = jnp.concatenate(block[:8], axis=0), block[8][:, :planes]
    mixed = jnp.concatenate([mixed[:, at * planes : (at + 1) * planes] for at in range(LANES // planes)], axis=0)
    flipped = mixed.T
    first = jnp.where(at_row >= at_col, mixed, flipped)
    second = jnp.where(at_row < at_col, mixed, jnp.where(at_row > at_col, flipped, diagonal))
    low_half = (at_col <= at_row)[:half, :half]
    state = eliminate(
        [first, second],
        planes,
        lambda state: solve(jnp.where(low_half, state[:, 3 * planes : 3 * planes + half], 0.0), 0),
    )
    first_inverse = state[:, planes : 2 * planes]
    product_upper = jnp.where(at_col >= at_row, state[:, 2 * planes : 3 * planes], 0.0)
    solve(jnp.where(at_col <= at_row, state[:, 3 * planes :], 0.0)[half:], half)
    factor[...] = jnp.where(at_col >= at_row, gram_of(product_upper, first_inverse), 0.0)
    copies.append(pltpu.make_async_copy(factor, factor_out, written.at[2]))
    copies[-1].start()
    for copy in copies:
        copy.wait()


def tree_sum(parts):
    while len(parts) > 1:
        parts = [sum(parts[at + 1 : at + 2], parts[at]) for at in range(0, len(parts), 2)]
    return parts[0]


def swap(value, row_pairing=None, col_pairing=None):
    names = ("sec", "row", "col")
    shape = [lax.axis_size(name) for name in names]

    def partner(at, place, pairing):
        other = place if pairing is None else place + 1 if place % 2 != pairing else place - 1
        return other if 0 <= other < shape[at] else None

    pairs = []
    for sec, row, col in itertools.product(*(range(extent) for extent in shape)):
        other_row, other_col = partner(1, row, row_pairing), partner(2, col, col_pairing)
        if other_col is None:
            target = (sec, row ^ 1, col)
        elif other_row is None:
            target = (sec ^ 1, row, col)
        else:
            target = (sec, other_row, other_col)
        pairs.append(tuple((a * shape[1] + b) * shape[2] + c for a, b, c in ((sec, row, col), target)))
    return lax.ppermute(value, names, pairs)


def on_device(sketch, weights):
    planes, rows, width = sketch.shape
    group = lax.axis_size("row") * lax.axis_size("col")
    side = f32(planes + 8, LANES)
    by_row, weights_by_row, left, right, *messages = call(
        pack_rows_kernel,
        [f32(rows, planes, width), f32(rows, 8, width), side, side]
        + [f32(2 * planes + 16, width), f32(2 * planes + 8, width)]
        + [f32(16, LANES)] * 2,
        pltpu.with_memory_space_constraint(sketch, pltpu.HBM),
        pltpu.with_memory_space_constraint(weights, pltpu.HBM),
        memory=pltpu.HBM,
        scratch=[
            pltpu.VMEM(sketch.shape, jnp.float32),
            pltpu.VMEM(weights.shape, jnp.float32),
            pltpu.SemaphoreType.DMA((2,)),
        ],
    )
    from_rows = [swap(messages[at], row_pairing=at) for at in range(2)]
    from_diagonals = [swap(messages[2 + at], row_pairing=0, col_pairing=at) for at in range(2)]
    left, right, *messages = call(
        functools.partial(strips_kernel, rows), [side, side] + [f32(16, LANES)] * 2, left, right, from_rows[1]
    )
    from_cols = [swap(messages[at], col_pairing=at) for at in range(2)]
    parts_of = functools.partial(jax.ShapeDtypeStruct, dtype=jnp.bfloat16)
    products = f32(3 * planes, 3 * planes)
    middle, inner_second, *inner_products = call(
        inner_rows_kernel,
        [f32(rows - 2, planes, width), parts_of((rows - 4, 3 * planes, width)), products, products],
        by_row,
        weights_by_row,
    )
    outer_second, early_grams, *halos = call(
        outer_rows_kernel,
        [parts_of((4, 3 * planes, width)), f32(planes, 2 * planes), side, side],
        by_row,
        weights_by_row,
        *from_rows,
        middle,
        *inner_products,
        scratch=[pltpu.VMEM((4, planes, width), jnp.float32)],
    )
    grams, edges = call(
        functools.partial(late_kernel, rows),
        [f32(group, 1, 9 * LANES), f32(planes, 2 * LANES)],
        left,
        right,
        *halos,
        *from_diagonals,
        *from_cols,
        early_grams,
    )
    first = lax.axis_size("col") + lax.axis_size("col") // 2
    order = [first] + [place for place in range(group) if place != first]
    parts = lax.all_to_all(grams, ("row", "col"), 0, 0, axis_index_groups=[order], tiled=True)
    return call(
        functools.partial(finish_kernel, float(rows * width * group)),
        [f32(planes, rows, width), f32(planes, planes)],
        inner_second,
        outer_second,
        edges,
        parts,
        out_memory=pl.ANY,
        scratch=[
            pltpu.VMEM(sketch.shape, jnp.float32),
            pltpu.VMEM((planes, planes), jnp.float32),
            pltpu.SemaphoreType.DMA((3,)),
        ],
    )


def solution(mesh):
    return jax.shard_map(
        on_device,
        mesh=mesh,
        in_specs=(P(None, ("sec", "row"), "col"), P(None, ("sec", "row"), "col")),
        out_specs=(P(None, ("sec", "row"), "col"), P("sec", None)),
        check_vma=False,
    )
```

```python
import functools
import itertools

import jax
import jax.numpy as jnp
from jax import lax
from jax.experimental import pallas as pl
from jax.experimental.pallas import tpu as pltpu
from jax.sharding import PartitionSpec as P

NEIGHBOURS = ((-1, -1), (-1, 0), (-1, 1), (0, -1), (0, 1), (1, -1), (1, 0), (1, 1))
LANES = 128
PITCH = 8
HIGHEST = lax.Precision.HIGHEST


def call(kernel, out_shapes, *operands, memory=pltpu.VMEM, out_memory=pltpu.VMEM, scratch=(), cost=None):
    return pl.pallas_call(
        kernel,
        out_shape=out_shapes,
        in_specs=[pl.BlockSpec(memory_space=memory)] * len(operands),
        out_specs=[pl.BlockSpec(memory_space=out_memory)] * len(out_shapes),
        scratch_shapes=scratch,
        cost_estimate=cost,
        compiler_params=pltpu.CompilerParams(vmem_limit_bytes=40 * 1024 * 1024),
    )(*operands)


def f32(*shape):
    return jax.ShapeDtypeStruct(shape, jnp.float32)


def sides_of(axis):
    place = lax.axis_index(axis)
    return place % 2 == 1, place > 0, place < lax.axis_size(axis) - 1


def edge_columns(first, last, place):
    lane = lax.broadcasted_iota(jnp.int32, (1, LANES), 1)
    own = PITCH - 2
    left = jnp.where((lane >= place + 2) & (lane < place + PITCH), pltpu.roll(first, place + 2, 1), 0.0)
    right = jnp.where((lane >= place) & (lane < place + own), pltpu.roll(last, place + own, 1), 0.0)
    return left, right


def pack_rows_kernel(sketch, weights, by_row, weights_by_row, left, right, *rest):
    bulk_messages, diagonal_messages = rest[:2], rest[2:4]
    tile, weight_tile, arrived = rest[4:]
    copies = [
        pltpu.make_async_copy(sketch, tile, arrived.at[0]),
        pltpu.make_async_copy(weights, weight_tile, arrived.at[1]),
    ]
    for copy in copies:
        copy.start()
    for copy in copies:
        copy.wait()
    rows, planes, width = by_row.shape
    odd_row, _, _ = sides_of("row")
    odd_col, _, _ = sides_of("col")
    lane = lax.broadcasted_iota(jnp.int32, (1, LANES), 1)
    for row in range(rows):
        weights_by_row[row] = weight_tile[:, row, :]
        by_row[row] = tile[:, row, :]
    for message, up in zip(bulk_messages, (odd_row, jnp.logical_not(odd_row))):
        start = jnp.where(up, rows - 2, 0)
        for slot in range(2):
            message[slot * planes : (slot + 1) * planes] = by_row[start + slot]
        message[2 * planes : 2 * planes + 8] = weights_by_row[jnp.where(up, rows - 1, 0)]
    strips = [None, None]
    for row in range(rows):
        first = jnp.concatenate([by_row[row, :, :LANES], weights_by_row[row, :, :LANES]], axis=0)
        last = jnp.concatenate([by_row[row, :, width - LANES :], weights_by_row[row, :, width - LANES :]], axis=0)
        parts = edge_columns(first, last, PITCH * (row + 2))
        strips = [part if strip is None else strip + part for strip, part in zip(strips, parts)]
    left[...], right[...] = strips
    bulk_messages[0][2 * planes + 8 :] = jnp.zeros((8, width), jnp.float32)
    pair = 2 * PITCH
    to_left, to_right = folded(strips[0], 2), folded(strips[1], PITCH - 4)
    for message, up in zip(diagonal_messages, (odd_col, jnp.logical_not(odd_col))):
        edge = jnp.where(up, to_right, to_left)
        below = jnp.where(lane < pair, rolled(edge, -PITCH * rows), 0.0)
        start = PITCH * (rows + 2)
        above = jnp.where((lane >= start) & (lane < start + pair), rolled(edge, PITCH * rows), 0.0)
        message[...] = jnp.where(odd_row, below, above)


def strips_kernel(rows, own_left, own_right, bulk_message, left, right, *col_messages):
    planes = own_left.shape[0] - 8
    odd_row, has_below, has_above = sides_of("row")
    odd_col, _, _ = sides_of("col")
    width = bulk_message.shape[1]
    totals = [own_left[...], own_right[...]]
    present = jnp.where(odd_row, has_below, has_above)
    for slot in range(2):
        place = PITCH * (slot + jnp.where(odd_row, 0, rows + 2))
        halo = [bulk_message[slot * planes : (slot + 1) * planes], bulk_message[2 * planes :]]
        first = jnp.concatenate([part[:, :LANES] for part in halo], axis=0)
        last = jnp.concatenate([part[:, width - LANES :] for part in halo], axis=0)
        parts = edge_columns(first, last, place)
        totals = [total + jnp.where(present, part, 0.0) for total, part in zip(totals, parts)]
    left[...], right[...] = totals
    to_left, to_right = folded(left[...], 2), folded(right[...], PITCH - 4)
    for message, up in zip(col_messages, (odd_col, jnp.logical_not(odd_col))):
        message[...] = jnp.where(up, to_right, to_left)


def folded(strip, spot):
    lane = lax.broadcasted_iota(jnp.int32, (1, LANES), 1)
    groups = strip.shape[0] // 8
    pieces = []
    for group in range(groups):
        target = 2 * group if group < groups - 1 else 0
        moved = rolled(strip[8 * group : 8 * (group + 1)], target - spot)
        pieces.append(jnp.where((lane % PITCH) // 2 == target // 2, moved, 0.0))
    return jnp.concatenate([functools.reduce(jnp.add, pieces[:-1]), pieces[-1]], axis=0)


def unfolded(message, spot, planes):
    lane = lax.broadcasted_iota(jnp.int32, (1, LANES), 1)
    pieces = [rolled(message[:8], spot - 2 * group) for group in range(planes // 8)] + [rolled(message[8:], spot)]
    return jnp.where((lane % PITCH) // 2 == spot // 2, jnp.concatenate(pieces, axis=0), 0.0)


def rolled(value, shift):
    return pltpu.roll(value, shift % LANES, 1) if shift % LANES else value


def apply_operator(rows3, weight_rows):
    width = rows3[1].shape[1]
    total = jnp.sum(weight_rows, axis=0, keepdims=True) * rows3[1]
    for across in (0, -1, 1):
        moved = pltpu.roll(weight_rows, across % width, 1) if across else weight_rows
        terms = [
            moved[position : position + 1] * rows3[up + 1]
            for position, (up, side) in enumerate(NEIGHBOURS)
            if side == across
        ]
        part = functools.reduce(jnp.add, terms)
        total = total + (pltpu.roll(part, -across % width, 1) if across else part)
    return total


def gram_of(value, other):
    return lax.dot_general(
        value, other, (((1,), (1,)), ((), ())), precision=HIGHEST, preferred_element_type=jnp.float32
    )


def split(value):
    high = value.astype(jnp.bfloat16)
    rest = value - high.astype(jnp.float32)
    middle = rest.astype(jnp.bfloat16)
    low = (rest - middle.astype(jnp.float32)).astype(jnp.bfloat16)
    return high, middle, low


def inner_parts(image):
    width = image.shape[1]
    lane = lax.broadcasted_iota(jnp.int32, (1, LANES), 1)
    kept = [
        jnp.where(lane >= 2, image[:, :LANES], 0.0),
        image[:, LANES : width - LANES],
        jnp.where(lane < LANES - 2, image[:, width - LANES :], 0.0),
    ]
    return jnp.concatenate(split(jnp.concatenate(kept, axis=1)), axis=0)


def products_of(parts):
    return lax.dot_general(parts, parts, (((1,), (1,)), ((), ())), preferred_element_type=jnp.float32)


def images_of(middle, weights, wanted, second, products):
    for at, row in enumerate(wanted):
        parts = inner_parts(apply_operator([middle(row - 1), middle(row), middle(row + 1)], weights(row)))
        second[at] = parts
        products = products + products_of(parts)
    return products


def inner_rows_kernel(by_row, weights_by_row, middle, second, first_products, second_products):
    rows = by_row.shape[0]
    products = jnp.zeros(first_products.shape, jnp.float32)
    for row in range(1, rows - 1):
        image = apply_operator([by_row[row - 1], by_row[row], by_row[row + 1]], weights_by_row[row])
        middle[row - 1] = image
        products = products + products_of(inner_parts(image))
    first_products[...] = products
    second_products[...] = images_of(
        lambda row: middle[row - 1],
        lambda row: weights_by_row[row],
        range(2, rows - 2),
        second,
        jnp.zeros(second_products.shape, jnp.float32),
    )


def outer_rows_kernel(
    by_row,
    weights_by_row,
    first_message,
    second_message,
    middle,
    first_products,
    second_products,
    second,
    grams,
    left_halo,
    right_halo,
    outer,
):
    rows, planes, width = by_row.shape
    odd_row, has_below, has_above = sides_of("row")
    one, other = first_message[: 2 * planes + 8], second_message[...]
    below = jnp.where(has_below, jnp.where(odd_row, other, one), 0.0)
    above = jnp.where(has_above, jnp.where(odd_row, one, other), 0.0)
    halos = [None, None]
    for side, (halo, present) in enumerate(
        ((below, jnp.logical_not(odd_row)), (above, odd_row))
    ):
        for slot in range(2):
            index = slot if side == 0 else rows + 2 + slot
            blank = jnp.zeros((8, width), jnp.float32)
            weight = halo[2 * planes :] if slot != side else blank
            row_values = jnp.concatenate([halo[slot * planes : (slot + 1) * planes], weight], axis=0)
            parts = edge_columns(row_values[:, :LANES], row_values[:, width - LANES :], PITCH * index)
            parts = [jnp.where(present, part, 0.0) for part in parts]
            halos = [part if total is None else total + part for total, part in zip(halos, parts)]
    left_halo[...], right_halo[...] = halos

    def field(row):
        if 0 <= row < rows:
            return by_row[row]
        at = (row + 2 if row < 0 else row - rows) * planes
        return (below if row < 0 else above)[at : at + planes]

    def weights(row):
        if 0 <= row < rows:
            return weights_by_row[row]
        return (below if row < 0 else above)[2 * planes :]

    products = first_products[...]
    places = (-1, 0, rows - 1, rows)
    for at, row in enumerate(places):
        image = apply_operator([field(row - 1), field(row), field(row + 1)], weights(row))
        outer[at] = image
        if 0 <= row < rows:
            products = products + products_of(inner_parts(image))
    both = [products]
    both.append(
        images_of(
            lambda row: outer[places.index(row)] if row in places else middle[row - 1],
            weights,
            (0, 1, rows - 2, rows - 1),
            second,
            second_products[...],
        )
    )
    for at, products in enumerate(both):
        some = products[:planes] + products[planes : 2 * planes] + products[2 * planes :]
        total = some[:, :planes] + some[:, planes : 2 * planes] + some[:, 2 * planes :]
        grams[:, at * planes : (at + 1) * planes] = total


def apply_on_strip(values, weights):
    total = jnp.sum(weights, axis=0, keepdims=True) * values
    for position, (up, across) in enumerate(NEIGHBOURS):
        moved = pltpu.roll(values, (-PITCH * up - across) % LANES, 1)
        total = total + weights[position : position + 1] * moved
    return total


def late_kernel(rows, left, right, left_halo, right_halo, *rest):
    diagonal_messages, col_messages, (early_grams, grams, edges) = rest[:2], rest[2:4], rest[4:]
    planes = early_grams.shape[0]
    odd_row, has_below, has_above = sides_of("row")
    odd_col, has_left, has_right = sides_of("col")
    beyond = jnp.where(odd_row, has_above, has_below)
    one, other = (
        col[...] + jnp.where(beyond, diagonal[...], 0.0)
        for col, diagonal in zip(col_messages, diagonal_messages)
    )
    lane = lax.broadcasted_iota(jnp.int32, (1, LANES), 1)
    spot, row = lane % PITCH, lane // PITCH
    strips, masks = [], []
    for side, (strip, present, halo) in enumerate(
        (
            (left[...] + left_halo[...], has_left, jnp.where(odd_col, other, one)),
            (right[...] + right_halo[...], has_right, jnp.where(odd_col, one, other)),
        )
    ):
        strips.append(strip + jnp.where(present, unfolded(halo, side * (PITCH - 2), planes), 0.0))
        low = 2 if side == 0 else PITCH - 4
        masks.append((spot >= low) & (spot < low + 2) & (row >= 2) & (row < rows + 2))
    values = [strip[:planes] for strip in strips]
    gram = []
    for at in range(2):
        values = [apply_on_strip(value, strip[planes:]) for value, strip in zip(values, strips)]
        kept = jnp.concatenate([jnp.where(mask, value, 0.0) for mask, value in zip(masks, values)], axis=1)
        both = jnp.concatenate(values, axis=1)
        gram.append(early_grams[:, at * planes : (at + 1) * planes] + gram_of(kept, both))
    edges[...] = both
    at_row = lax.broadcasted_iota(jnp.int32, (planes, planes), 0)
    at_col = lax.broadcasted_iota(jnp.int32, (planes, planes), 1)
    mixed = jnp.where(at_row >= at_col, gram[0], gram[1])
    diagonal = jnp.sum(jnp.where(at_row == at_col, gram[1], 0.0), axis=0, keepdims=True)
    block = jnp.concatenate([mixed[8 * g : 8 * (g + 1)] for g in range(planes // 8)], axis=1)
    last = jnp.concatenate([diagonal] * (LANES // planes), axis=1)
    for target in range(grams.shape[0]):
        for at in range(8):
            grams[target, :, at * LANES : (at + 1) * LANES] = block[at : at + 1]
        grams[target, :, 8 * LANES :] = last


def eliminate(grams, planes, half_way):
    lane = lax.broadcasted_iota(jnp.int32, (8, LANES), 1)
    sub = lax.broadcasted_iota(jnp.int32, (8, LANES), 0)
    first_half = lane < 2 * planes
    groups = planes // 8
    sources = [[gram[8 * g : 8 * (g + 1)] for g in range(groups)] for gram in grams]
    state = []
    for g in range(groups):
        unit = jnp.where(sub + 8 * g == lane % (2 * planes) - planes, 1.0, 0.0)
        unit = unit[:, planes : 2 * planes]
        state.append(jnp.concatenate([sources[0][g], unit, sources[1][g], unit], axis=1))
    columns = []
    for j in range(planes):
        columns.append(
            {
                g: jnp.where(
                    first_half,
                    jnp.broadcast_to(sources[0][g][:, j : j + 1], (8, LANES)),
                    jnp.broadcast_to(sources[1][g][:, j : j + 1], (8, LANES)),
                )
                for g in range(j // 8, groups)
            }
        )
    scale = [jnp.ones((8, LANES), jnp.float32)] * groups
    for step in range(planes):
        own, at = step // 8, step % 8
        column = columns[step]
        root = lax.rsqrt(jnp.broadcast_to(column[own][at : at + 1], (8, LANES)))
        inverse = root * root
        scale[own] = jnp.where(sub == at, root, scale[own])
        left = {g: jnp.where(sub > at, value, 0.0) if g == own else value for g, value in column.items()}
        factors = {g: value * inverse for g, value in left.items()}
        for j in range(step + 1, planes):
            entry = jnp.broadcast_to(column[j // 8][j % 8 : j % 8 + 1], (8, LANES))
            for g in columns[j]:
                change = (left[g] * entry) * inverse if j == step + 1 else factors[g] * entry
                columns[j][g] = columns[j][g] - change
        pivot_row = jnp.broadcast_to(state[own][at : at + 1], (8, LANES))
        for g in range(own, groups):
            state[g] = state[g] - factors[g] * pivot_row
        if step + 1 == planes // 2:
            half_way(jnp.concatenate([state[g] * scale[g] for g in range(groups // 2)], axis=0))
    return jnp.concatenate([state[g] * scale[g] for g in range(groups)], axis=0)


def finish_kernel(
    pixel_count, inner_second, outer_second, edges, parts, basis_out, factor_out, basis, factor, written
):
    planes, rows, width = basis.shape
    half = planes // 2
    at_row = lax.broadcasted_iota(jnp.int32, (planes, planes), 0)
    at_col = lax.broadcasted_iota(jnp.int32, (planes, planes), 1)
    lane = lax.broadcasted_iota(jnp.int32, (1, LANES), 1)
    outer_parts = split(edges[...])
    copies = []

    def solve(inverse, start):
        stop = start + inverse.shape[0]
        high, middle, low = split(inverse)
        left_side = jnp.concatenate([high, high, middle, high, low, middle], axis=1)

        def solved(high, middle, low):
            right_side = jnp.concatenate([high, middle, high, low, high, middle], axis=0)
            return jnp.dot(left_side, right_side, preferred_element_type=jnp.float32)

        outer = solved(*(part[:stop] for part in outer_parts))
        for row in range(rows):
            if 2 <= row < rows - 2:
                held, spot = inner_second, row - 2
            else:
                held, spot = outer_second, row if row < 2 else row - rows + 4
            value = solved(*(held[spot, at * planes : at * planes + stop] for at in range(3)))
            place = PITCH * (row + 2)
            first = rolled(outer[:, :LANES], -(place + 2))
            last = rolled(outer[:, LANES:], LANES - 2 - (place + PITCH - 4))
            basis[start:stop, row, :LANES] = jnp.where(lane < 2, first, value[:, :LANES])
            basis[start:stop, row, LANES : width - LANES] = value[:, LANES : width - LANES]
            basis[start:stop, row, width - LANES :] = jnp.where(
                lane >= LANES - 2, last, value[:, width - LANES :]
            )
        some = pl.ds(start, stop - start)
        copies.append(pltpu.make_async_copy(basis.at[some], basis_out.at[some], written.at[len(copies)]))
        copies[-1].start()

    block = tree_sum([parts[at] for at in range(parts.shape[0])]) / pixel_count
    block = [block[:, at * LANES : (at + 1) * LANES] for at in range(9)]
    mixed, diagonal = jnp.concatenate(block[:8], axis=0), block[8][:, :planes]
    mixed = jnp.concatenate([mixed[:, at * planes : (at + 1) * planes] for at in range(LANES // planes)], axis=0)
    flipped = mixed.T
    first = jnp.where(at_row >= at_col, mixed, flipped)
    second = jnp.where(at_row < at_col, mixed, jnp.where(at_row > at_col, flipped, diagonal))
    low_half = (at_col <= at_row)[:half, :half]
    state = eliminate(
        [first, second],
        planes,
        lambda state: solve(jnp.where(low_half, state[:, 3 * planes : 3 * planes + half], 0.0), 0),
    )
    first_inverse = state[:, planes : 2 * planes]
    product_upper = jnp.where(at_col >= at_row, state[:, 2 * planes : 3 * planes], 0.0)
    solve(jnp.where(at_col <= at_row, state[:, 3 * planes :], 0.0)[half:], half)
    factor[...] = jnp.where(at_col >= at_row, gram_of(product_upper, first_inverse), 0.0)
    copies.append(pltpu.make_async_copy(factor, factor_out, written.at[2]))
    copies[-1].start()
    for copy in copies:
        copy.wait()


def tree_sum(parts):
    while len(parts) > 1:
        parts = [sum(parts[at + 1 : at + 2], parts[at]) for at in range(0, len(parts), 2)]
    return parts[0]


def swap(value, row_pairing=None, col_pairing=None):
    names = ("sec", "row", "col")
    shape = [lax.axis_size(name) for name in names]

    def partner(at, place, pairing):
        other = place if pairing is None else place + 1 if place % 2 != pairing else place - 1
        return other if 0 <= other < shape[at] else None

    pairs = []
    for sec, row, col in itertools.product(*(range(extent) for extent in shape)):
        other_row, other_col = partner(1, row, row_pairing), partner(2, col, col_pairing)
        if other_col is None:
            target = (sec, row ^ 1, col)
        elif other_row is None:
            target = (sec ^ 1, row, col)
        else:
            target = (sec, other_row, other_col)
        pairs.append(tuple((a * shape[1] + b) * shape[2] + c for a, b, c in ((sec, row, col), target)))
    return lax.ppermute(value, names, pairs)


def on_device(sketch, weights):
    planes, rows, width = sketch.shape
    group = lax.axis_size("row") * lax.axis_size("col")
    side = f32(planes + 8, LANES)
    by_row, weights_by_row, left, right, *messages = call(
        pack_rows_kernel,
        [f32(rows, planes, width), f32(rows, 8, width), side, side]
        + [f32(2 * planes + 16, width), f32(2 * planes + 8, width)]
        + [f32(16, LANES)] * 2,
        pltpu.with_memory_space_constraint(sketch, pltpu.HBM),
        pltpu.with_memory_space_constraint(weights, pltpu.HBM),
        memory=pltpu.HBM,
        scratch=[
            pltpu.VMEM(sketch.shape, jnp.float32),
            pltpu.VMEM(weights.shape, jnp.float32),
            pltpu.SemaphoreType.DMA((2,)),
        ],
    )
    from_rows = [swap(messages[at], row_pairing=at) for at in range(2)]
    from_diagonals = [swap(messages[2 + at], row_pairing=0, col_pairing=at) for at in range(2)]
    left, right, *messages = call(
        functools.partial(strips_kernel, rows), [side, side] + [f32(16, LANES)] * 2, left, right, from_rows[1]
    )
    from_cols = [swap(messages[at], col_pairing=at) for at in range(2)]
    parts_of = functools.partial(jax.ShapeDtypeStruct, dtype=jnp.bfloat16)
    products = f32(3 * planes, 3 * planes)
    middle, inner_second, *inner_products = call(
        inner_rows_kernel,
        [f32(rows - 2, planes, width), parts_of((rows - 4, 3 * planes, width)), products, products],
        by_row,
        weights_by_row,
    )
    outer_second, early_grams, *halos = call(
        outer_rows_kernel,
        [parts_of((4, 3 * planes, width)), f32(planes, 2 * planes), side, side],
        by_row,
        weights_by_row,
        *from_rows,
        middle,
        *inner_products,
        scratch=[pltpu.VMEM((4, planes, width), jnp.float32)],
    )
    grams, edges = call(
        functools.partial(late_kernel, rows),
        [f32(group, 1, 9 * LANES), f32(planes, 2 * LANES)],
        left,
        right,
        *halos,
        *from_diagonals,
        *from_cols,
        early_grams,
    )
    rows_of, cols_of = lax.axis_size("row"), lax.axis_size("col")
    first = 2 * cols_of - 1
    order = [first] + [row * cols_of + col for col in range(cols_of) for row in range(rows_of)]
    order = list(dict.fromkeys(order))
    parts = lax.all_to_all(grams, ("row", "col"), 0, 0, axis_index_groups=[order], tiled=True)
    return call(
        functools.partial(finish_kernel, float(rows * width * group)),
        [f32(planes, rows, width), f32(planes, planes)],
        inner_second,
        outer_second,
        edges,
        parts,
        out_memory=pl.ANY,
        scratch=[
            pltpu.VMEM(sketch.shape, jnp.float32),
            pltpu.VMEM((planes, planes), jnp.float32),
            pltpu.SemaphoreType.DMA((3,)),
        ],
    )


def solution(mesh):
    return jax.shard_map(
        on_device,
        mesh=mesh,
        in_specs=(P(None, ("sec", "row"), "col"), P(None, ("sec", "row"), "col")),
        out_specs=(P(None, ("sec", "row"), "col"), P("sec", None)),
        check_vma=False,
    )
```

```python
import functools
import itertools

import jax
import jax.numpy as jnp
from jax import lax
from jax.experimental import pallas as pl
from jax.experimental.pallas import tpu as pltpu
from jax.sharding import PartitionSpec as P

NEIGHBOURS = ((-1, -1), (-1, 0), (-1, 1), (0, -1), (0, 1), (1, -1), (1, 0), (1, 1))
LANES = 128
PITCH = 8
HIGHEST = lax.Precision.HIGHEST


def call(kernel, out_shapes, *operands, memory=pltpu.VMEM, out_memory=pltpu.VMEM, scratch=(), cost=None):
    return pl.pallas_call(
        kernel,
        out_shape=out_shapes,
        in_specs=[pl.BlockSpec(memory_space=memory)] * len(operands),
        out_specs=[pl.BlockSpec(memory_space=out_memory)] * len(out_shapes),
        scratch_shapes=scratch,
        cost_estimate=cost,
        compiler_params=pltpu.CompilerParams(vmem_limit_bytes=40 * 1024 * 1024),
    )(*operands)


def f32(*shape):
    return jax.ShapeDtypeStruct(shape, jnp.float32)


def sides_of(axis):
    place = lax.axis_index(axis)
    return place % 2 == 1, place > 0, place < lax.axis_size(axis) - 1


def edge_columns(first, last, place):
    lane = lax.broadcasted_iota(jnp.int32, (1, LANES), 1)
    own = PITCH - 2
    left = jnp.where((lane >= place + 2) & (lane < place + PITCH), pltpu.roll(first, place + 2, 1), 0.0)
    right = jnp.where((lane >= place) & (lane < place + own), pltpu.roll(last, place + own, 1), 0.0)
    return left, right


def pack_rows_kernel(sketch, weights, by_row, weights_by_row, left, right, *rest):
    bulk_messages, diagonal_messages = rest[:2], rest[2:4]
    tile, weight_tile, arrived = rest[4:]
    copies = [
        pltpu.make_async_copy(sketch, tile, arrived.at[0]),
        pltpu.make_async_copy(weights, weight_tile, arrived.at[1]),
    ]
    for copy in copies:
        copy.start()
    for copy in copies:
        copy.wait()
    rows, planes, width = by_row.shape
    odd_row, _, _ = sides_of("row")
    odd_col, _, _ = sides_of("col")
    lane = lax.broadcasted_iota(jnp.int32, (1, LANES), 1)
    for row in range(rows):
        weights_by_row[row] = weight_tile[:, row, :]
        by_row[row] = tile[:, row, :]
    for message, up in zip(bulk_messages, (odd_row, jnp.logical_not(odd_row))):
        start = jnp.where(up, rows - 2, 0)
        for slot in range(2):
            message[slot * planes : (slot + 1) * planes] = by_row[start + slot]
        message[2 * planes : 2 * planes + 8] = weights_by_row[jnp.where(up, rows - 1, 0)]
    strips = [None, None]
    for row in range(rows):
        first = jnp.concatenate([by_row[row, :, :LANES], weights_by_row[row, :, :LANES]], axis=0)
        last = jnp.concatenate([by_row[row, :, width - LANES :], weights_by_row[row, :, width - LANES :]], axis=0)
        parts = edge_columns(first, last, PITCH * (row + 2))
        strips = [part if strip is None else strip + part for strip, part in zip(strips, parts)]
    left[...], right[...] = strips
    bulk_messages[0][2 * planes + 8 :] = jnp.zeros((8, width), jnp.float32)
    pair = 2 * PITCH
    to_left, to_right = folded(strips[0], 2), folded(strips[1], PITCH - 4)
    for message, up in zip(diagonal_messages, (odd_col, jnp.logical_not(odd_col))):
        edge = jnp.where(up, to_right, to_left)
        below = jnp.where(lane < pair, rolled(edge, -PITCH * rows), 0.0)
        start = PITCH * (rows + 2)
        above = jnp.where((lane >= start) & (lane < start + pair), rolled(edge, PITCH * rows), 0.0)
        message[...] = jnp.where(odd_row, below, above)


def strips_kernel(rows, own_left, own_right, bulk_message, left, right, *col_messages):
    planes = own_left.shape[0] - 8
    odd_row, has_below, has_above = sides_of("row")
    odd_col, _, _ = sides_of("col")
    width = bulk_message.shape[1]
    totals = [own_left[...], own_right[...]]
    present = jnp.where(odd_row, has_below, has_above)
    for slot in range(2):
        place = PITCH * (slot + jnp.where(odd_row, 0, rows + 2))
        halo = [bulk_message[slot * planes : (slot + 1) * planes], bulk_message[2 * planes :]]
        first = jnp.concatenate([part[:, :LANES] for part in halo], axis=0)
        last = jnp.concatenate([part[:, width - LANES :] for part in halo], axis=0)
        parts = edge_columns(first, last, place)
        totals = [total + jnp.where(present, part, 0.0) for total, part in zip(totals, parts)]
    left[...], right[...] = totals
    to_left, to_right = folded(left[...], 2), folded(right[...], PITCH - 4)
    for message, up in zip(col_messages, (odd_col, jnp.logical_not(odd_col))):
        message[...] = jnp.where(up, to_right, to_left)


def folded(strip, spot):
    lane = lax.broadcasted_iota(jnp.int32, (1, LANES), 1)
    groups = strip.shape[0] // 8
    pieces = []
    for group in range(groups):
        target = 2 * group if group < groups - 1 else 0
        moved = rolled(strip[8 * group : 8 * (group + 1)], target - spot)
        pieces.append(jnp.where((lane % PITCH) // 2 == target // 2, moved, 0.0))
    return jnp.concatenate([functools.reduce(jnp.add, pieces[:-1]), pieces[-1]], axis=0)


def unfolded(message, spot, planes):
    lane = lax.broadcasted_iota(jnp.int32, (1, LANES), 1)
    pieces = [rolled(message[:8], spot - 2 * group) for group in range(planes // 8)] + [rolled(message[8:], spot)]
    return jnp.where((lane % PITCH) // 2 == spot // 2, jnp.concatenate(pieces, axis=0), 0.0)


def rolled(value, shift):
    return pltpu.roll(value, shift % LANES, 1) if shift % LANES else value


def apply_operator(rows3, weight_rows):
    width = rows3[1].shape[1]
    total = jnp.sum(weight_rows, axis=0, keepdims=True) * rows3[1]
    for across in (0, -1, 1):
        moved = pltpu.roll(weight_rows, across % width, 1) if across else weight_rows
        terms = [
            moved[position : position + 1] * rows3[up + 1]
            for position, (up, side) in enumerate(NEIGHBOURS)
            if side == across
        ]
        part = functools.reduce(jnp.add, terms)
        total = total + (pltpu.roll(part, -across % width, 1) if across else part)
    return total


def gram_of(value, other):
    return lax.dot_general(
        value, other, (((1,), (1,)), ((), ())), precision=HIGHEST, preferred_element_type=jnp.float32
    )


def split(value):
    high = value.astype(jnp.bfloat16)
    rest = value - high.astype(jnp.float32)
    middle = rest.astype(jnp.bfloat16)
    low = (rest - middle.astype(jnp.float32)).astype(jnp.bfloat16)
    return high, middle, low


def inner_parts(image):
    width = image.shape[1]
    lane = lax.broadcasted_iota(jnp.int32, (1, LANES), 1)
    kept = [
        jnp.where(lane >= 2, image[:, :LANES], 0.0),
        image[:, LANES : width - LANES],
        jnp.where(lane < LANES - 2, image[:, width - LANES :], 0.0),
    ]
    return jnp.concatenate(split(jnp.concatenate(kept, axis=1)), axis=0)


def products_of(parts):
    return lax.dot_general(parts, parts, (((1,), (1,)), ((), ())), preferred_element_type=jnp.float32)


def images_of(middle, weights, wanted, second, products):
    for at, row in enumerate(wanted):
        parts = inner_parts(apply_operator([middle(row - 1), middle(row), middle(row + 1)], weights(row)))
        second[at] = parts
        products = products + products_of(parts)
    return products


def inner_rows_kernel(by_row, weights_by_row, middle, second, first_products, second_products):
    rows = by_row.shape[0]
    products = jnp.zeros(first_products.shape, jnp.float32)
    for row in range(1, rows - 1):
        image = apply_operator([by_row[row - 1], by_row[row], by_row[row + 1]], weights_by_row[row])
        middle[row - 1] = image
        products = products + products_of(inner_parts(image))
    first_products[...] = products
    second_products[...] = images_of(
        lambda row: middle[row - 1],
        lambda row: weights_by_row[row],
        range(2, rows - 2),
        second,
        jnp.zeros(second_products.shape, jnp.float32),
    )


def outer_rows_kernel(
    by_row,
    weights_by_row,
    first_message,
    second_message,
    middle,
    first_products,
    second_products,
    second,
    grams,
    left_halo,
    right_halo,
    outer,
):
    rows, planes, width = by_row.shape
    odd_row, has_below, has_above = sides_of("row")
    one, other = first_message[: 2 * planes + 8], second_message[...]
    below = jnp.where(has_below, jnp.where(odd_row, other, one), 0.0)
    above = jnp.where(has_above, jnp.where(odd_row, one, other), 0.0)
    halos = [None, None]
    for side, (halo, present) in enumerate(
        ((below, jnp.logical_not(odd_row)), (above, odd_row))
    ):
        for slot in range(2):
            index = slot if side == 0 else rows + 2 + slot
            blank = jnp.zeros((8, width), jnp.float32)
            weight = halo[2 * planes :] if slot != side else blank
            row_values = jnp.concatenate([halo[slot * planes : (slot + 1) * planes], weight], axis=0)
            parts = edge_columns(row_values[:, :LANES], row_values[:, width - LANES :], PITCH * index)
            parts = [jnp.where(present, part, 0.0) for part in parts]
            halos = [part if total is None else total + part for total, part in zip(halos, parts)]
    left_halo[...], right_halo[...] = halos

    def field(row):
        if 0 <= row < rows:
            return by_row[row]
        at = (row + 2 if row < 0 else row - rows) * planes
        return (below if row < 0 else above)[at : at + planes]

    def weights(row):
        if 0 <= row < rows:
            return weights_by_row[row]
        return (below if row < 0 else above)[2 * planes :]

    products = first_products[...]
    places = (-1, 0, rows - 1, rows)
    for at, row in enumerate(places):
        image = apply_operator([field(row - 1), field(row), field(row + 1)], weights(row))
        outer[at] = image
        if 0 <= row < rows:
            products = products + products_of(inner_parts(image))
    both = [products]
    both.append(
        images_of(
            lambda row: outer[places.index(row)] if row in places else middle[row - 1],
            weights,
            (0, 1, rows - 2, rows - 1),
            second,
            second_products[...],
        )
    )
    for at, products in enumerate(both):
        some = products[:planes] + products[planes : 2 * planes] + products[2 * planes :]
        total = some[:, :planes] + some[:, planes : 2 * planes] + some[:, 2 * planes :]
        grams[:, at * planes : (at + 1) * planes] = total


def apply_on_strip(values, weights):
    total = jnp.sum(weights, axis=0, keepdims=True) * values
    for position, (up, across) in enumerate(NEIGHBOURS):
        moved = pltpu.roll(values, (-PITCH * up - across) % LANES, 1)
        total = total + weights[position : position + 1] * moved
    return total


def late_kernel(rows, left, right, left_halo, right_halo, *rest):
    diagonal_messages, col_messages, (early_grams, grams, edges) = rest[:2], rest[2:4], rest[4:]
    planes = early_grams.shape[0]
    odd_row, has_below, has_above = sides_of("row")
    odd_col, has_left, has_right = sides_of("col")
    beyond = jnp.where(odd_row, has_above, has_below)
    one, other = (
        col[...] + jnp.where(beyond, diagonal[...], 0.0)
        for col, diagonal in zip(col_messages, diagonal_messages)
    )
    lane = lax.broadcasted_iota(jnp.int32, (1, LANES), 1)
    spot, row = lane % PITCH, lane // PITCH
    strips, masks = [], []
    for side, (strip, present, halo) in enumerate(
        (
            (left[...] + left_halo[...], has_left, jnp.where(odd_col, other, one)),
            (right[...] + right_halo[...], has_right, jnp.where(odd_col, one, other)),
        )
    ):
        strips.append(strip + jnp.where(present, unfolded(halo, side * (PITCH - 2), planes), 0.0))
        low = 2 if side == 0 else PITCH - 4
        masks.append((spot >= low) & (spot < low + 2) & (row >= 2) & (row < rows + 2))
    values = [strip[:planes] for strip in strips]
    gram = []
    for at in range(2):
        values = [apply_on_strip(value, strip[planes:]) for value, strip in zip(values, strips)]
        kept = jnp.concatenate([jnp.where(mask, value, 0.0) for mask, value in zip(masks, values)], axis=1)
        both = jnp.concatenate(values, axis=1)
        gram.append(early_grams[:, at * planes : (at + 1) * planes] + gram_of(kept, both))
    edges[...] = both
    at_row = lax.broadcasted_iota(jnp.int32, (planes, planes), 0)
    at_col = lax.broadcasted_iota(jnp.int32, (planes, planes), 1)
    mixed = jnp.where(at_row >= at_col, gram[0], gram[1])
    diagonal = jnp.sum(jnp.where(at_row == at_col, gram[1], 0.0), axis=0, keepdims=True)
    block = jnp.concatenate([mixed[8 * g : 8 * (g + 1)] for g in range(planes // 8)], axis=1)
    last = jnp.concatenate([diagonal] * (LANES // planes), axis=1)
    for target in range(grams.shape[0]):
        for at in range(8):
            grams[target, :, at * LANES : (at + 1) * LANES] = block[at : at + 1]
        grams[target, :, 8 * LANES :] = last


def eliminate(grams, planes, half_way):
    lane = lax.broadcasted_iota(jnp.int32, (8, LANES), 1)
    sub = lax.broadcasted_iota(jnp.int32, (8, LANES), 0)
    first_half = lane < 2 * planes
    groups = planes // 8
    sources = [[gram[8 * g : 8 * (g + 1)] for g in range(groups)] for gram in grams]
    state = []
    for g in range(groups):
        unit = jnp.where(sub + 8 * g == lane % (2 * planes) - planes, 1.0, 0.0)
        unit = unit[:, planes : 2 * planes]
        state.append(jnp.concatenate([sources[0][g], unit, sources[1][g], unit], axis=1))
    columns = []
    for j in range(planes):
        columns.append(
            {
                g: jnp.where(
                    first_half,
                    jnp.broadcast_to(sources[0][g][:, j : j + 1], (8, LANES)),
                    jnp.broadcast_to(sources[1][g][:, j : j + 1], (8, LANES)),
                )
                for g in range(j // 8, groups)
            }
        )
    scale = [jnp.ones((8, LANES), jnp.float32)] * groups
    for step in range(planes):
        own, at = step // 8, step % 8
        column = columns[step]
        root = lax.rsqrt(jnp.broadcast_to(column[own][at : at + 1], (8, LANES)))
        inverse = root * root
        scale[own] = jnp.where(sub == at, root, scale[own])
        left = {g: jnp.where(sub > at, value, 0.0) if g == own else value for g, value in column.items()}
        factors = {g: value * inverse for g, value in left.items()}
        for j in range(step + 1, planes):
            entry = jnp.broadcast_to(column[j // 8][j % 8 : j % 8 + 1], (8, LANES))
            for g in columns[j]:
                change = (left[g] * entry) * inverse if j == step + 1 else factors[g] * entry
                columns[j][g] = columns[j][g] - change
        pivot_row = jnp.broadcast_to(state[own][at : at + 1], (8, LANES))
        for g in range(own, groups):
            state[g] = state[g] - factors[g] * pivot_row
        if step + 1 == planes // 2:
            half_way(jnp.concatenate([state[g] * scale[g] for g in range(groups // 2)], axis=0))
    return jnp.concatenate([state[g] * scale[g] for g in range(groups)], axis=0)


def finish_kernel(
    pixel_count, inner_second, outer_second, edges, parts, basis_out, factor_out, basis, factor, written
):
    planes, rows, width = basis.shape
    half = planes // 2
    at_row = lax.broadcasted_iota(jnp.int32, (planes, planes), 0)
    at_col = lax.broadcasted_iota(jnp.int32, (planes, planes), 1)
    lane = lax.broadcasted_iota(jnp.int32, (1, LANES), 1)
    outer_parts = split(edges[...])
    copies = []

    def solve(inverse, start):
        stop = start + inverse.shape[0]
        high, middle, low = split(inverse)
        left_side = jnp.concatenate([high, high, middle, high, low, middle], axis=1)

        def solved(high, middle, low):
            right_side = jnp.concatenate([high, middle, high, low, high, middle], axis=0)
            return jnp.dot(left_side, right_side, preferred_element_type=jnp.float32)

        outer = solved(*(part[:stop] for part in outer_parts))
        for row in range(rows):
            if 2 <= row < rows - 2:
                held, spot = inner_second, row - 2
            else:
                held, spot = outer_second, row if row < 2 else row - rows + 4
            value = solved(*(held[spot, at * planes : at * planes + stop] for at in range(3)))
            place = PITCH * (row + 2)
            first = rolled(outer[:, :LANES], -(place + 2))
            last = rolled(outer[:, LANES:], LANES - 2 - (place + PITCH - 4))
            basis[start:stop, row, :LANES] = jnp.where(lane < 2, first, value[:, :LANES])
            basis[start:stop, row, LANES : width - LANES] = value[:, LANES : width - LANES]
            basis[start:stop, row, width - LANES :] = jnp.where(
                lane >= LANES - 2, last, value[:, width - LANES :]
            )
        some = pl.ds(start, stop - start)
        copies.append(pltpu.make_async_copy(basis.at[some], basis_out.at[some], written.at[len(copies)]))
        copies[-1].start()

    block = tree_sum([parts[at] for at in range(parts.shape[0])]) / pixel_count
    block = [block[:, at * LANES : (at + 1) * LANES] for at in range(9)]
    mixed, diagonal = jnp.concatenate(block[:8], axis=0), block[8][:, :planes]
    mixed = jnp.concatenate([mixed[:, at * planes : (at + 1) * planes] for at in range(LANES // planes)], axis=0)
    flipped = mixed.T
    first = jnp.where(at_row >= at_col, mixed, flipped)
    second = jnp.where(at_row < at_col, mixed, jnp.where(at_row > at_col, flipped, diagonal))
    low_half = (at_col <= at_row)[:half, :half]
    state = eliminate(
        [first, second],
        planes,
        lambda state: solve(jnp.where(low_half, state[:, 3 * planes : 3 * planes + half], 0.0), 0),
    )
    first_inverse = state[:, planes : 2 * planes]
    product_upper = jnp.where(at_col >= at_row, state[:, 2 * planes : 3 * planes], 0.0)
    solve(jnp.where(at_col <= at_row, state[:, 3 * planes :], 0.0)[half:], half)
    factor[...] = jnp.where(at_col >= at_row, gram_of(product_upper, first_inverse), 0.0)
    copies.append(pltpu.make_async_copy(factor, factor_out, written.at[2]))
    copies[-1].start()
    for copy in copies:
        copy.wait()


def tree_sum(parts):
    while len(parts) > 1:
        parts = [sum(parts[at + 1 : at + 2], parts[at]) for at in range(0, len(parts), 2)]
    return parts[0]


def swap(value, row_pairing=None, col_pairing=None):
    names = ("sec", "row", "col")
    shape = [lax.axis_size(name) for name in names]

    def partner(at, place, pairing):
        other = place if pairing is None else place + 1 if place % 2 != pairing else place - 1
        return other if 0 <= other < shape[at] else None

    pairs = []
    for sec, row, col in itertools.product(*(range(extent) for extent in shape)):
        other_row, other_col = partner(1, row, row_pairing), partner(2, col, col_pairing)
        if other_col is None:
            target = (sec, row ^ 1, col)
        elif other_row is None:
            target = (sec ^ 1, row, col)
        else:
            target = (sec, other_row, other_col)
        pairs.append(tuple((a * shape[1] + b) * shape[2] + c for a, b, c in ((sec, row, col), target)))
    return lax.ppermute(value, names, pairs)


def on_device(sketch, weights):
    planes, rows, width = sketch.shape
    group = lax.axis_size("row") * lax.axis_size("col")
    side = f32(planes + 8, LANES)
    by_row, weights_by_row, left, right, *messages = call(
        pack_rows_kernel,
        [f32(rows, planes, width), f32(rows, 8, width), side, side]
        + [f32(2 * planes + 16, width), f32(2 * planes + 8, width)]
        + [f32(16, LANES)] * 2,
        pltpu.with_memory_space_constraint(sketch, pltpu.HBM),
        pltpu.with_memory_space_constraint(weights, pltpu.HBM),
        memory=pltpu.HBM,
        scratch=[
            pltpu.VMEM(sketch.shape, jnp.float32),
            pltpu.VMEM(weights.shape, jnp.float32),
            pltpu.SemaphoreType.DMA((2,)),
        ],
    )
    from_rows = [swap(messages[at], row_pairing=at) for at in range(2)]
    from_diagonals = [swap(messages[2 + at], row_pairing=0, col_pairing=at) for at in range(2)]
    left, right, *messages = call(
        functools.partial(strips_kernel, rows), [side, side] + [f32(16, LANES)] * 2, left, right, from_rows[1]
    )
    from_cols = [swap(messages[at], col_pairing=at) for at in range(2)]
    parts_of = functools.partial(jax.ShapeDtypeStruct, dtype=jnp.bfloat16)
    products = f32(3 * planes, 3 * planes)
    middle, inner_second, *inner_products = call(
        inner_rows_kernel,
        [f32(rows - 2, planes, width), parts_of((rows - 4, 3 * planes, width)), products, products],
        by_row,
        weights_by_row,
    )
    outer_second, early_grams, *halos = call(
        outer_rows_kernel,
        [parts_of((4, 3 * planes, width)), f32(planes, 2 * planes), side, side],
        by_row,
        weights_by_row,
        *from_rows,
        middle,
        *inner_products,
        scratch=[pltpu.VMEM((4, planes, width), jnp.float32)],
    )
    grams, edges = call(
        functools.partial(late_kernel, rows),
        [f32(group, 1, 9 * LANES), f32(planes, 2 * LANES)],
        left,
        right,
        *halos,
        *from_diagonals,
        *from_cols,
        early_grams,
    )
    rows_of, cols_of = lax.axis_size("row"), lax.axis_size("col")
    first = cols_of + cols_of // 2
    order = [first] + [row * cols_of + col for col in range(cols_of) for row in range(rows_of)]
    order = list(dict.fromkeys(order))
    parts = lax.all_to_all(grams, ("row", "col"), 0, 0, axis_index_groups=[order], tiled=True)
    return call(
        functools.partial(finish_kernel, float(rows * width * group)),
        [f32(planes, rows, width), f32(planes, planes)],
        inner_second,
        outer_second,
        edges,
        parts,
        out_memory=pl.ANY,
        scratch=[
            pltpu.VMEM(sketch.shape, jnp.float32),
            pltpu.VMEM((planes, planes), jnp.float32),
            pltpu.SemaphoreType.DMA((3,)),
        ],
    )


def solution(mesh):
    return jax.shard_map(
        on_device,
        mesh=mesh,
        in_specs=(P(None, ("sec", "row"), "col"), P(None, ("sec", "row"), "col")),
        out_specs=(P(None, ("sec", "row"), "col"), P("sec", None)),
        check_vma=False,
    )
```

```python
import functools
import itertools

import jax
import jax.numpy as jnp
from jax import lax
from jax.experimental import pallas as pl
from jax.experimental.pallas import tpu as pltpu
from jax.sharding import PartitionSpec as P

NEIGHBOURS = ((-1, -1), (-1, 0), (-1, 1), (0, -1), (0, 1), (1, -1), (1, 0), (1, 1))
LANES = 128
PITCH = 8
HIGHEST = lax.Precision.HIGHEST


def call(kernel, out_shapes, *operands, memory=pltpu.VMEM, out_memory=pltpu.VMEM, scratch=(), cost=None):
    return pl.pallas_call(
        kernel,
        out_shape=out_shapes,
        in_specs=[pl.BlockSpec(memory_space=memory)] * len(operands),
        out_specs=[pl.BlockSpec(memory_space=out_memory)] * len(out_shapes),
        scratch_shapes=scratch,
        cost_estimate=cost,
        compiler_params=pltpu.CompilerParams(vmem_limit_bytes=40 * 1024 * 1024),
    )(*operands)


def f32(*shape):
    return jax.ShapeDtypeStruct(shape, jnp.float32)


def sides_of(axis):
    place = lax.axis_index(axis)
    return place % 2 == 1, place > 0, place < lax.axis_size(axis) - 1


def edge_columns(first, last, place):
    lane = lax.broadcasted_iota(jnp.int32, (1, LANES), 1)
    own = PITCH - 2
    left = jnp.where((lane >= place + 2) & (lane < place + PITCH), pltpu.roll(first, place + 2, 1), 0.0)
    right = jnp.where((lane >= place) & (lane < place + own), pltpu.roll(last, place + own, 1), 0.0)
    return left, right


def pack_rows_kernel(sketch, weights, by_row, weights_by_row, left, right, *rest):
    bulk_messages, diagonal_messages = rest[:2], rest[2:4]
    tile, weight_tile, arrived = rest[4:]
    copies = [
        pltpu.make_async_copy(sketch, tile, arrived.at[0]),
        pltpu.make_async_copy(weights, weight_tile, arrived.at[1]),
    ]
    for copy in copies:
        copy.start()
    for copy in copies:
        copy.wait()
    rows, planes, width = by_row.shape
    odd_row, _, _ = sides_of("row")
    odd_col, _, _ = sides_of("col")
    lane = lax.broadcasted_iota(jnp.int32, (1, LANES), 1)
    for row in range(rows):
        weights_by_row[row] = weight_tile[:, row, :]
        by_row[row] = tile[:, row, :]
    for message, up in zip(bulk_messages, (odd_row, jnp.logical_not(odd_row))):
        start = jnp.where(up, rows - 2, 0)
        for slot in range(2):
            message[slot * planes : (slot + 1) * planes] = by_row[start + slot]
        message[2 * planes : 2 * planes + 8] = weights_by_row[jnp.where(up, rows - 1, 0)]
    strips = [None, None]
    for row in range(rows):
        first = jnp.concatenate([by_row[row, :, :LANES], weights_by_row[row, :, :LANES]], axis=0)
        last = jnp.concatenate([by_row[row, :, width - LANES :], weights_by_row[row, :, width - LANES :]], axis=0)
        parts = edge_columns(first, last, PITCH * (row + 2))
        strips = [part if strip is None else strip + part for strip, part in zip(strips, parts)]
    left[...], right[...] = strips
    bulk_messages[0][2 * planes + 8 :] = jnp.zeros((8, width), jnp.float32)
    pair = 2 * PITCH
    to_left, to_right = folded(strips[0], 2), folded(strips[1], PITCH - 4)
    for message, up in zip(diagonal_messages, (odd_col, jnp.logical_not(odd_col))):
        edge = jnp.where(up, to_right, to_left)
        below = jnp.where(lane < pair, rolled(edge, -PITCH * rows), 0.0)
        start = PITCH * (rows + 2)
        above = jnp.where((lane >= start) & (lane < start + pair), rolled(edge, PITCH * rows), 0.0)
        message[...] = jnp.where(odd_row, below, above)


def strips_kernel(rows, own_left, own_right, bulk_message, left, right, *col_messages):
    planes = own_left.shape[0] - 8
    odd_row, has_below, has_above = sides_of("row")
    odd_col, _, _ = sides_of("col")
    width = bulk_message.shape[1]
    totals = [own_left[...], own_right[...]]
    present = jnp.where(odd_row, has_below, has_above)
    for slot in range(2):
        place = PITCH * (slot + jnp.where(odd_row, 0, rows + 2))
        halo = [bulk_message[slot * planes : (slot + 1) * planes], bulk_message[2 * planes :]]
        first = jnp.concatenate([part[:, :LANES] for part in halo], axis=0)
        last = jnp.concatenate([part[:, width - LANES :] for part in halo], axis=0)
        parts = edge_columns(first, last, place)
        totals = [total + jnp.where(present, part, 0.0) for total, part in zip(totals, parts)]
    left[...], right[...] = totals
    to_left, to_right = folded(left[...], 2), folded(right[...], PITCH - 4)
    for message, up in zip(col_messages, (odd_col, jnp.logical_not(odd_col))):
        message[...] = jnp.where(up, to_right, to_left)


def folded(strip, spot):
    lane = lax.broadcasted_iota(jnp.int32, (1, LANES), 1)
    groups = strip.shape[0] // 8
    pieces = []
    for group in range(groups):
        target = 2 * group if group < groups - 1 else 0
        moved = rolled(strip[8 * group : 8 * (group + 1)], target - spot)
        pieces.append(jnp.where((lane % PITCH) // 2 == target // 2, moved, 0.0))
    return jnp.concatenate([functools.reduce(jnp.add, pieces[:-1]), pieces[-1]], axis=0)


def unfolded(message, spot, planes):
    lane = lax.broadcasted_iota(jnp.int32, (1, LANES), 1)
    pieces = [rolled(message[:8], spot - 2 * group) for group in range(planes // 8)] + [rolled(message[8:], spot)]
    return jnp.where((lane % PITCH) // 2 == spot // 2, jnp.concatenate(pieces, axis=0), 0.0)


def rolled(value, shift):
    return pltpu.roll(value, shift % LANES, 1) if shift % LANES else value


def apply_operator(rows3, weight_rows):
    width = rows3[1].shape[1]
    total = jnp.sum(weight_rows, axis=0, keepdims=True) * rows3[1]
    for across in (0, -1, 1):
        moved = pltpu.roll(weight_rows, across % width, 1) if across else weight_rows
        terms = [
            moved[position : position + 1] * rows3[up + 1]
            for position, (up, side) in enumerate(NEIGHBOURS)
            if side == across
        ]
        part = functools.reduce(jnp.add, terms)
        total = total + (pltpu.roll(part, -across % width, 1) if across else part)
    return total


def gram_of(value, other):
    return lax.dot_general(
        value, other, (((1,), (1,)), ((), ())), precision=HIGHEST, preferred_element_type=jnp.float32
    )


def split(value):
    high = value.astype(jnp.bfloat16)
    rest = value - high.astype(jnp.float32)
    middle = rest.astype(jnp.bfloat16)
    low = (rest - middle.astype(jnp.float32)).astype(jnp.bfloat16)
    return high, middle, low


def inner_parts(image):
    width = image.shape[1]
    lane = lax.broadcasted_iota(jnp.int32, (1, LANES), 1)
    kept = [
        jnp.where(lane >= 2, image[:, :LANES], 0.0),
        image[:, LANES : width - LANES],
        jnp.where(lane < LANES - 2, image[:, width - LANES :], 0.0),
    ]
    return jnp.concatenate(split(jnp.concatenate(kept, axis=1)), axis=0)


def products_of(parts):
    return lax.dot_general(parts, parts, (((1,), (1,)), ((), ())), preferred_element_type=jnp.float32)


def images_of(middle, weights, wanted, second, products):
    for at, row in enumerate(wanted):
        parts = inner_parts(apply_operator([middle(row - 1), middle(row), middle(row + 1)], weights(row)))
        second[at] = parts
        products = products + products_of(parts)
    return products


def inner_rows_kernel(by_row, weights_by_row, middle, second, first_products, second_products):
    rows = by_row.shape[0]
    products = jnp.zeros(first_products.shape, jnp.float32)
    for row in range(1, rows - 1):
        image = apply_operator([by_row[row - 1], by_row[row], by_row[row + 1]], weights_by_row[row])
        middle[row - 1] = image
        products = products + products_of(inner_parts(image))
    first_products[...] = products
    second_products[...] = images_of(
        lambda row: middle[row - 1],
        lambda row: weights_by_row[row],
        range(2, rows - 2),
        second,
        jnp.zeros(second_products.shape, jnp.float32),
    )


def outer_rows_kernel(
    by_row,
    weights_by_row,
    first_message,
    second_message,
    middle,
    first_products,
    second_products,
    second,
    grams,
    left_halo,
    right_halo,
    outer,
):
    rows, planes, width = by_row.shape
    odd_row, has_below, has_above = sides_of("row")
    one, other = first_message[: 2 * planes + 8], second_message[...]
    below = jnp.where(has_below, jnp.where(odd_row, other, one), 0.0)
    above = jnp.where(has_above, jnp.where(odd_row, one, other), 0.0)
    halos = [None, None]
    for side, (halo, present) in enumerate(
        ((below, jnp.logical_not(odd_row)), (above, odd_row))
    ):
        for slot in range(2):
            index = slot if side == 0 else rows + 2 + slot
            blank = jnp.zeros((8, width), jnp.float32)
            weight = halo[2 * planes :] if slot != side else blank
            row_values = jnp.concatenate([halo[slot * planes : (slot + 1) * planes], weight], axis=0)
            parts = edge_columns(row_values[:, :LANES], row_values[:, width - LANES :], PITCH * index)
            parts = [jnp.where(present, part, 0.0) for part in parts]
            halos = [part if total is None else total + part for total, part in zip(halos, parts)]
    left_halo[...], right_halo[...] = halos

    def field(row):
        if 0 <= row < rows:
            return by_row[row]
        at = (row + 2 if row < 0 else row - rows) * planes
        return (below if row < 0 else above)[at : at + planes]

    def weights(row):
        if 0 <= row < rows:
            return weights_by_row[row]
        return (below if row < 0 else above)[2 * planes :]

    products = first_products[...]
    places = (-1, 0, rows - 1, rows)
    for at, row in enumerate(places):
        image = apply_operator([field(row - 1), field(row), field(row + 1)], weights(row))
        outer[at] = image
        if 0 <= row < rows:
            products = products + products_of(inner_parts(image))
    both = [products]
    both.append(
        images_of(
            lambda row: outer[places.index(row)] if row in places else middle[row - 1],
            weights,
            (0, 1, rows - 2, rows - 1),
            second,
            second_products[...],
        )
    )
    for at, products in enumerate(both):
        some = products[:planes] + products[planes : 2 * planes] + products[2 * planes :]
        total = some[:, :planes] + some[:, planes : 2 * planes] + some[:, 2 * planes :]
        grams[:, at * planes : (at + 1) * planes] = total


def apply_on_strip(values, weights):
    total = jnp.sum(weights, axis=0, keepdims=True) * values
    for position, (up, across) in enumerate(NEIGHBOURS):
        moved = pltpu.roll(values, (-PITCH * up - across) % LANES, 1)
        total = total + weights[position : position + 1] * moved
    return total


def late_kernel(rows, left, right, left_halo, right_halo, *rest):
    diagonal_messages, col_messages, (early_grams, grams, edges) = rest[:2], rest[2:4], rest[4:]
    planes = early_grams.shape[0]
    odd_row, has_below, has_above = sides_of("row")
    odd_col, has_left, has_right = sides_of("col")
    beyond = jnp.where(odd_row, has_above, has_below)
    one, other = (
        col[...] + jnp.where(beyond, diagonal[...], 0.0)
        for col, diagonal in zip(col_messages, diagonal_messages)
    )
    lane = lax.broadcasted_iota(jnp.int32, (1, LANES), 1)
    spot, row = lane % PITCH, lane // PITCH
    strips, masks = [], []
    for side, (strip, present, halo) in enumerate(
        (
            (left[...] + left_halo[...], has_left, jnp.where(odd_col, other, one)),
            (right[...] + right_halo[...], has_right, jnp.where(odd_col, one, other)),
        )
    ):
        strips.append(strip + jnp.where(present, unfolded(halo, side * (PITCH - 2), planes), 0.0))
        low = 2 if side == 0 else PITCH - 4
        masks.append((spot >= low) & (spot < low + 2) & (row >= 2) & (row < rows + 2))
    values = [strip[:planes] for strip in strips]
    gram = []
    for at in range(2):
        values = [apply_on_strip(value, strip[planes:]) for value, strip in zip(values, strips)]
        kept = jnp.concatenate([jnp.where(mask, value, 0.0) for mask, value in zip(masks, values)], axis=1)
        both = jnp.concatenate(values, axis=1)
        gram.append(early_grams[:, at * planes : (at + 1) * planes] + gram_of(kept, both))
    edges[...] = both
    at_row = lax.broadcasted_iota(jnp.int32, (planes, planes), 0)
    at_col = lax.broadcasted_iota(jnp.int32, (planes, planes), 1)
    mixed = jnp.where(at_row >= at_col, gram[0], gram[1])
    diagonal = jnp.sum(jnp.where(at_row == at_col, gram[1], 0.0), axis=0, keepdims=True)
    block = jnp.concatenate([mixed[8 * g : 8 * (g + 1)] for g in range(planes // 8)], axis=1)
    last = jnp.concatenate([diagonal] * (LANES // planes), axis=1)
    for target in range(grams.shape[0]):
        for at in range(8):
            grams[target, :, at * LANES : (at + 1) * LANES] = block[at : at + 1]
        grams[target, :, 8 * LANES :] = last


def eliminate(grams, planes, half_way):
    lane = lax.broadcasted_iota(jnp.int32, (8, LANES), 1)
    sub = lax.broadcasted_iota(jnp.int32, (8, LANES), 0)
    first_half = lane < 2 * planes
    groups = planes // 8
    sources = [[gram[8 * g : 8 * (g + 1)] for g in range(groups)] for gram in grams]
    state = []
    for g in range(groups):
        unit = jnp.where(sub + 8 * g == lane % (2 * planes) - planes, 1.0, 0.0)
        unit = unit[:, planes : 2 * planes]
        state.append(jnp.concatenate([sources[0][g], unit, sources[1][g], unit], axis=1))
    columns = []
    for j in range(planes):
        columns.append(
            {
                g: jnp.where(
                    first_half,
                    jnp.broadcast_to(sources[0][g][:, j : j + 1], (8, LANES)),
                    jnp.broadcast_to(sources[1][g][:, j : j + 1], (8, LANES)),
                )
                for g in range(j // 8, groups)
            }
        )
    scale = [jnp.ones((8, LANES), jnp.float32)] * groups
    for step in range(planes):
        own, at = step // 8, step % 8
        column = columns[step]
        root = lax.rsqrt(jnp.broadcast_to(column[own][at : at + 1], (8, LANES)))
        inverse = root * root
        scale[own] = jnp.where(sub == at, root, scale[own])
        left = {g: jnp.where(sub > at, value, 0.0) if g == own else value for g, value in column.items()}
        factors = {g: value * inverse for g, value in left.items()}
        for j in range(step + 1, planes):
            entry = jnp.broadcast_to(column[j // 8][j % 8 : j % 8 + 1], (8, LANES))
            for g in columns[j]:
                change = (left[g] * entry) * inverse if j == step + 1 else factors[g] * entry
                columns[j][g] = columns[j][g] - change
        pivot_row = jnp.broadcast_to(state[own][at : at + 1], (8, LANES))
        for g in range(own, groups):
            state[g] = state[g] - factors[g] * pivot_row
        if step + 1 == planes // 2:
            half_way(jnp.concatenate([state[g] * scale[g] for g in range(groups // 2)], axis=0))
    return jnp.concatenate([state[g] * scale[g] for g in range(groups)], axis=0)


def finish_kernel(
    pixel_count, inner_second, outer_second, edges, parts, basis_out, factor_out, basis, factor, written
):
    planes, rows, width = basis.shape
    half = planes // 2
    at_row = lax.broadcasted_iota(jnp.int32, (planes, planes), 0)
    at_col = lax.broadcasted_iota(jnp.int32, (planes, planes), 1)
    lane = lax.broadcasted_iota(jnp.int32, (1, LANES), 1)
    outer_parts = split(edges[...])
    copies = []

    def solve(inverse, start):
        stop = start + inverse.shape[0]
        high, middle, low = split(inverse)
        left_side = jnp.concatenate([high, high, middle, high, low, middle], axis=1)

        def solved(high, middle, low):
            right_side = jnp.concatenate([high, middle, high, low, high, middle], axis=0)
            return jnp.dot(left_side, right_side, preferred_element_type=jnp.float32)

        outer = solved(*(part[:stop] for part in outer_parts))
        for row in range(rows):
            if 2 <= row < rows - 2:
                held, spot = inner_second, row - 2
            else:
                held, spot = outer_second, row if row < 2 else row - rows + 4
            value = solved(*(held[spot, at * planes : at * planes + stop] for at in range(3)))
            place = PITCH * (row + 2)
            first = rolled(outer[:, :LANES], -(place + 2))
            last = rolled(outer[:, LANES:], LANES - 2 - (place + PITCH - 4))
            basis[start:stop, row, :LANES] = jnp.where(lane < 2, first, value[:, :LANES])
            basis[start:stop, row, LANES : width - LANES] = value[:, LANES : width - LANES]
            basis[start:stop, row, width - LANES :] = jnp.where(
                lane >= LANES - 2, last, value[:, width - LANES :]
            )
        some = pl.ds(start, stop - start)
        copies.append(pltpu.make_async_copy(basis.at[some], basis_out.at[some], written.at[len(copies)]))
        copies[-1].start()

    block = tree_sum([parts[at] for at in range(parts.shape[0])]) / pixel_count
    block = [block[:, at * LANES : (at + 1) * LANES] for at in range(9)]
    mixed, diagonal = jnp.concatenate(block[:8], axis=0), block[8][:, :planes]
    mixed = jnp.concatenate([mixed[:, at * planes : (at + 1) * planes] for at in range(LANES // planes)], axis=0)
    flipped = mixed.T
    first = jnp.where(at_row >= at_col, mixed, flipped)
    second = jnp.where(at_row < at_col, mixed, jnp.where(at_row > at_col, flipped, diagonal))
    low_half = (at_col <= at_row)[:half, :half]
    state = eliminate(
        [first, second],
        planes,
        lambda state: solve(jnp.where(low_half, state[:, 3 * planes : 3 * planes + half], 0.0), 0),
    )
    first_inverse = state[:, planes : 2 * planes]
    product_upper = jnp.where(at_col >= at_row, state[:, 2 * planes : 3 * planes], 0.0)
    solve(jnp.where(at_col <= at_row, state[:, 3 * planes :], 0.0)[half:], half)
    factor[...] = jnp.where(at_col >= at_row, gram_of(product_upper, first_inverse), 0.0)
    copies.append(pltpu.make_async_copy(factor, factor_out, written.at[2]))
    copies[-1].start()
    for copy in copies:
        copy.wait()


def tree_sum(parts):
    while len(parts) > 1:
        parts = [sum(parts[at + 1 : at + 2], parts[at]) for at in range(0, len(parts), 2)]
    return parts[0]


def swap(value, row_pairing=None, col_pairing=None):
    names = ("sec", "row", "col")
    shape = [lax.axis_size(name) for name in names]

    def partner(at, place, pairing):
        other = place if pairing is None else place + 1 if place % 2 != pairing else place - 1
        return other if 0 <= other < shape[at] else None

    pairs = []
    for sec, row, col in itertools.product(*(range(extent) for extent in shape)):
        other_row, other_col = partner(1, row, row_pairing), partner(2, col, col_pairing)
        if other_col is None:
            target = (sec, row ^ 1, col)
        elif other_row is None:
            target = (sec ^ 1, row, col)
        else:
            target = (sec, other_row, other_col)
        pairs.append(tuple((a * shape[1] + b) * shape[2] + c for a, b, c in ((sec, row, col), target)))
    return lax.ppermute(value, names, pairs)


def on_device(sketch, weights):
    planes, rows, width = sketch.shape
    group = lax.axis_size("row") * lax.axis_size("col")
    side = f32(planes + 8, LANES)
    by_row, weights_by_row, left, right, *messages = call(
        pack_rows_kernel,
        [f32(rows, planes, width), f32(rows, 8, width), side, side]
        + [f32(2 * planes + 16, width), f32(2 * planes + 8, width)]
        + [f32(16, LANES)] * 2,
        pltpu.with_memory_space_constraint(sketch, pltpu.HBM),
        pltpu.with_memory_space_constraint(weights, pltpu.HBM),
        memory=pltpu.HBM,
        scratch=[
            pltpu.VMEM(sketch.shape, jnp.float32),
            pltpu.VMEM(weights.shape, jnp.float32),
            pltpu.SemaphoreType.DMA((2,)),
        ],
    )
    from_rows = [swap(messages[at], row_pairing=at) for at in range(2)]
    from_diagonals = [swap(messages[2 + at], row_pairing=0, col_pairing=at) for at in range(2)]
    left, right, *messages = call(
        functools.partial(strips_kernel, rows), [side, side] + [f32(16, LANES)] * 2, left, right, from_rows[1]
    )
    from_cols = [swap(messages[at], col_pairing=at) for at in range(2)]
    parts_of = functools.partial(jax.ShapeDtypeStruct, dtype=jnp.bfloat16)
    products = f32(3 * planes, 3 * planes)
    middle, inner_second, *inner_products = call(
        inner_rows_kernel,
        [f32(rows - 2, planes, width), parts_of((rows - 4, 3 * planes, width)), products, products],
        by_row,
        weights_by_row,
    )
    outer_second, early_grams, *halos = call(
        outer_rows_kernel,
        [parts_of((4, 3 * planes, width)), f32(planes, 2 * planes), side, side],
        by_row,
        weights_by_row,
        *from_rows,
        middle,
        *inner_products,
        scratch=[pltpu.VMEM((4, planes, width), jnp.float32)],
    )
    grams, edges = call(
        functools.partial(late_kernel, rows),
        [f32(group, 1, 9 * LANES), f32(planes, 2 * LANES)],
        left,
        right,
        *halos,
        *from_diagonals,
        *from_cols,
        early_grams,
    )
    rows_of, cols_of = lax.axis_size("row"), lax.axis_size("col")
    places = [(col > 0, col > 0 and row % 2 == 0, col, row) for col in range(cols_of) for row in range(rows_of)]
    order = [row * cols_of + col for _, _, col, row in sorted(places)]
    order = list(dict.fromkeys([cols_of + cols_of // 2] + order))
    parts = lax.all_to_all(grams, ("row", "col"), 0, 0, axis_index_groups=[order], tiled=True)
    return call(
        functools.partial(finish_kernel, float(rows * width * group)),
        [f32(planes, rows, width), f32(planes, planes)],
        inner_second,
        outer_second,
        edges,
        parts,
        out_memory=pl.ANY,
        scratch=[
            pltpu.VMEM(sketch.shape, jnp.float32),
            pltpu.VMEM((planes, planes), jnp.float32),
            pltpu.SemaphoreType.DMA((3,)),
        ],
    )


def solution(mesh):
    return jax.shard_map(
        on_device,
        mesh=mesh,
        in_specs=(P(None, ("sec", "row"), "col"), P(None, ("sec", "row"), "col")),
        out_specs=(P(None, ("sec", "row"), "col"), P("sec", None)),
        check_vma=False,
    )
```

```python
import functools
import itertools

import jax
import jax.numpy as jnp
from jax import lax
from jax.experimental import pallas as pl
from jax.experimental.pallas import tpu as pltpu
from jax.sharding import PartitionSpec as P

NEIGHBOURS = ((-1, -1), (-1, 0), (-1, 1), (0, -1), (0, 1), (1, -1), (1, 0), (1, 1))
LANES = 128
PITCH = 8
HIGHEST = lax.Precision.HIGHEST


def call(kernel, out_shapes, *operands, memory=pltpu.VMEM, out_memory=pltpu.VMEM, scratch=(), cost=None):
    return pl.pallas_call(
        kernel,
        out_shape=out_shapes,
        in_specs=[pl.BlockSpec(memory_space=memory)] * len(operands),
        out_specs=[pl.BlockSpec(memory_space=out_memory)] * len(out_shapes),
        scratch_shapes=scratch,
        cost_estimate=cost,
        compiler_params=pltpu.CompilerParams(vmem_limit_bytes=40 * 1024 * 1024),
    )(*operands)


def f32(*shape):
    return jax.ShapeDtypeStruct(shape, jnp.float32)


def sides_of(axis):
    place = lax.axis_index(axis)
    return place % 2 == 1, place > 0, place < lax.axis_size(axis) - 1


def edge_columns(first, last, place):
    lane = lax.broadcasted_iota(jnp.int32, (1, LANES), 1)
    own = PITCH - 2
    left = jnp.where((lane >= place + 2) & (lane < place + PITCH), pltpu.roll(first, place + 2, 1), 0.0)
    right = jnp.where((lane >= place) & (lane < place + own), pltpu.roll(last, place + own, 1), 0.0)
    return left, right


def pack_rows_kernel(sketch, weights, by_row, weights_by_row, left, right, *rest):
    bulk_messages, diagonal_messages = rest[:2], rest[2:4]
    tile, weight_tile, arrived = rest[4:]
    copies = [
        pltpu.make_async_copy(sketch, tile, arrived.at[0]),
        pltpu.make_async_copy(weights, weight_tile, arrived.at[1]),
    ]
    for copy in copies:
        copy.start()
    for copy in copies:
        copy.wait()
    rows, planes, width = by_row.shape
    odd_row, _, _ = sides_of("row")
    odd_col, _, _ = sides_of("col")
    lane = lax.broadcasted_iota(jnp.int32, (1, LANES), 1)
    for row in range(rows):
        weights_by_row[row] = weight_tile[:, row, :]
        by_row[row] = tile[:, row, :]
    for message, up in zip(bulk_messages, (odd_row, jnp.logical_not(odd_row))):
        start = jnp.where(up, rows - 2, 0)
        for slot in range(2):
            message[slot * planes : (slot + 1) * planes] = by_row[start + slot]
        message[2 * planes : 2 * planes + 8] = weights_by_row[jnp.where(up, rows - 1, 0)]
    strips = [None, None]
    for row in range(rows):
        first = jnp.concatenate([by_row[row, :, :LANES], weights_by_row[row, :, :LANES]], axis=0)
        last = jnp.concatenate([by_row[row, :, width - LANES :], weights_by_row[row, :, width - LANES :]], axis=0)
        parts = edge_columns(first, last, PITCH * (row + 2))
        strips = [part if strip is None else strip + part for strip, part in zip(strips, parts)]
    left[...], right[...] = strips
    bulk_messages[0][2 * planes + 8 :] = jnp.zeros((8, width), jnp.float32)
    pair = 2 * PITCH
    to_left, to_right = folded(strips[0], 2), folded(strips[1], PITCH - 4)
    for message, up in zip(diagonal_messages, (odd_col, jnp.logical_not(odd_col))):
        edge = jnp.where(up, to_right, to_left)
        below = jnp.where(lane < pair, rolled(edge, -PITCH * rows), 0.0)
        start = PITCH * (rows + 2)
        above = jnp.where((lane >= start) & (lane < start + pair), rolled(edge, PITCH * rows), 0.0)
        message[...] = jnp.where(odd_row, below, above)


def strips_kernel(rows, own_left, own_right, bulk_message, left, right, *col_messages):
    planes = own_left.shape[0] - 8
    odd_row, has_below, has_above = sides_of("row")
    odd_col, _, _ = sides_of("col")
    width = bulk_message.shape[1]
    totals = [own_left[...], own_right[...]]
    present = jnp.where(odd_row, has_below, has_above)
    for slot in range(2):
        place = PITCH * (slot + jnp.where(odd_row, 0, rows + 2))
        halo = [bulk_message[slot * planes : (slot + 1) * planes], bulk_message[2 * planes :]]
        first = jnp.concatenate([part[:, :LANES] for part in halo], axis=0)
        last = jnp.concatenate([part[:, width - LANES :] for part in halo], axis=0)
        parts = edge_columns(first, last, place)
        totals = [total + jnp.where(present, part, 0.0) for total, part in zip(totals, parts)]
    left[...], right[...] = totals
    to_left, to_right = folded(left[...], 2), folded(right[...], PITCH - 4)
    for message, up in zip(col_messages, (jnp.logical_not(odd_col), odd_col)):
        message[...] = jnp.where(up, to_right, to_left)


def folded(strip, spot):
    lane = lax.broadcasted_iota(jnp.int32, (1, LANES), 1)
    groups = strip.shape[0] // 8
    pieces = []
    for group in range(groups):
        target = 2 * group if group < groups - 1 else 0
        moved = rolled(strip[8 * group : 8 * (group + 1)], target - spot)
        pieces.append(jnp.where((lane % PITCH) // 2 == target // 2, moved, 0.0))
    return jnp.concatenate([functools.reduce(jnp.add, pieces[:-1]), pieces[-1]], axis=0)


def unfolded(message, spot, planes):
    lane = lax.broadcasted_iota(jnp.int32, (1, LANES), 1)
    pieces = [rolled(message[:8], spot - 2 * group) for group in range(planes // 8)] + [rolled(message[8:], spot)]
    return jnp.where((lane % PITCH) // 2 == spot // 2, jnp.concatenate(pieces, axis=0), 0.0)


def rolled(value, shift):
    return pltpu.roll(value, shift % LANES, 1) if shift % LANES else value


def apply_operator(rows3, weight_rows):
    width = rows3[1].shape[1]
    total = jnp.sum(weight_rows, axis=0, keepdims=True) * rows3[1]
    for across in (0, -1, 1):
        moved = pltpu.roll(weight_rows, across % width, 1) if across else weight_rows
        terms = [
            moved[position : position + 1] * rows3[up + 1]
            for position, (up, side) in enumerate(NEIGHBOURS)
            if side == across
        ]
        part = functools.reduce(jnp.add, terms)
        total = total + (pltpu.roll(part, -across % width, 1) if across else part)
    return total


def gram_of(value, other):
    return lax.dot_general(
        value, other, (((1,), (1,)), ((), ())), precision=HIGHEST, preferred_element_type=jnp.float32
    )


def split(value):
    high = value.astype(jnp.bfloat16)
    rest = value - high.astype(jnp.float32)
    middle = rest.astype(jnp.bfloat16)
    low = (rest - middle.astype(jnp.float32)).astype(jnp.bfloat16)
    return high, middle, low


def inner_parts(image):
    width = image.shape[1]
    lane = lax.broadcasted_iota(jnp.int32, (1, LANES), 1)
    kept = [
        jnp.where(lane >= 2, image[:, :LANES], 0.0),
        image[:, LANES : width - LANES],
        jnp.where(lane < LANES - 2, image[:, width - LANES :], 0.0),
    ]
    return jnp.concatenate(split(jnp.concatenate(kept, axis=1)), axis=0)


def products_of(parts):
    return lax.dot_general(parts, parts, (((1,), (1,)), ((), ())), preferred_element_type=jnp.float32)


def images_of(middle, weights, wanted, second, products):
    for at, row in enumerate(wanted):
        parts = inner_parts(apply_operator([middle(row - 1), middle(row), middle(row + 1)], weights(row)))
        second[at] = parts
        products = products + products_of(parts)
    return products


def inner_rows_kernel(by_row, weights_by_row, middle, second, first_products, second_products):
    rows = by_row.shape[0]
    products = jnp.zeros(first_products.shape, jnp.float32)
    for row in range(1, rows - 1):
        image = apply_operator([by_row[row - 1], by_row[row], by_row[row + 1]], weights_by_row[row])
        middle[row - 1] = image
        products = products + products_of(inner_parts(image))
    first_products[...] = products
    second_products[...] = images_of(
        lambda row: middle[row - 1],
        lambda row: weights_by_row[row],
        range(2, rows - 2),
        second,
        jnp.zeros(second_products.shape, jnp.float32),
    )


def outer_rows_kernel(
    by_row,
    weights_by_row,
    first_message,
    second_message,
    middle,
    first_products,
    second_products,
    second,
    grams,
    left_halo,
    right_halo,
    outer,
):
    rows, planes, width = by_row.shape
    odd_row, has_below, has_above = sides_of("row")
    one, other = first_message[: 2 * planes + 8], second_message[...]
    below = jnp.where(has_below, jnp.where(odd_row, other, one), 0.0)
    above = jnp.where(has_above, jnp.where(odd_row, one, other), 0.0)
    halos = [None, None]
    for side, (halo, present) in enumerate(
        ((below, jnp.logical_not(odd_row)), (above, odd_row))
    ):
        for slot in range(2):
            index = slot if side == 0 else rows + 2 + slot
            blank = jnp.zeros((8, width), jnp.float32)
            weight = halo[2 * planes :] if slot != side else blank
            row_values = jnp.concatenate([halo[slot * planes : (slot + 1) * planes], weight], axis=0)
            parts = edge_columns(row_values[:, :LANES], row_values[:, width - LANES :], PITCH * index)
            parts = [jnp.where(present, part, 0.0) for part in parts]
            halos = [part if total is None else total + part for total, part in zip(halos, parts)]
    left_halo[...], right_halo[...] = halos

    def field(row):
        if 0 <= row < rows:
            return by_row[row]
        at = (row + 2 if row < 0 else row - rows) * planes
        return (below if row < 0 else above)[at : at + planes]

    def weights(row):
        if 0 <= row < rows:
            return weights_by_row[row]
        return (below if row < 0 else above)[2 * planes :]

    products = first_products[...]
    places = (-1, 0, rows - 1, rows)
    for at, row in enumerate(places):
        image = apply_operator([field(row - 1), field(row), field(row + 1)], weights(row))
        outer[at] = image
        if 0 <= row < rows:
            products = products + products_of(inner_parts(image))
    both = [products]
    both.append(
        images_of(
            lambda row: outer[places.index(row)] if row in places else middle[row - 1],
            weights,
            (0, 1, rows - 2, rows - 1),
            second,
            second_products[...],
        )
    )
    for at, products in enumerate(both):
        some = products[:planes] + products[planes : 2 * planes] + products[2 * planes :]
        total = some[:, :planes] + some[:, planes : 2 * planes] + some[:, 2 * planes :]
        grams[:, at * planes : (at + 1) * planes] = total


def apply_on_strip(values, weights):
    total = jnp.sum(weights, axis=0, keepdims=True) * values
    for position, (up, across) in enumerate(NEIGHBOURS):
        moved = pltpu.roll(values, (-PITCH * up - across) % LANES, 1)
        total = total + weights[position : position + 1] * moved
    return total


def late_kernel(rows, left, right, left_halo, right_halo, *rest):
    diagonal_messages, col_messages, (early_grams, grams, edges) = rest[:2], rest[3:1:-1], rest[4:]
    planes = early_grams.shape[0]
    odd_row, has_below, has_above = sides_of("row")
    odd_col, has_left, has_right = sides_of("col")
    beyond = jnp.where(odd_row, has_above, has_below)
    one, other = (
        col[...] + jnp.where(beyond, diagonal[...], 0.0)
        for col, diagonal in zip(col_messages, diagonal_messages)
    )
    lane = lax.broadcasted_iota(jnp.int32, (1, LANES), 1)
    spot, row = lane % PITCH, lane // PITCH
    strips, masks = [], []
    for side, (strip, present, halo) in enumerate(
        (
            (left[...] + left_halo[...], has_left, jnp.where(odd_col, other, one)),
            (right[...] + right_halo[...], has_right, jnp.where(odd_col, one, other)),
        )
    ):
        strips.append(strip + jnp.where(present, unfolded(halo, side * (PITCH - 2), planes), 0.0))
        low = 2 if side == 0 else PITCH - 4
        masks.append((spot >= low) & (spot < low + 2) & (row >= 2) & (row < rows + 2))
    values = [strip[:planes] for strip in strips]
    gram = []
    for at in range(2):
        values = [apply_on_strip(value, strip[planes:]) for value, strip in zip(values, strips)]
        kept = jnp.concatenate([jnp.where(mask, value, 0.0) for mask, value in zip(masks, values)], axis=1)
        both = jnp.concatenate(values, axis=1)
        gram.append(early_grams[:, at * planes : (at + 1) * planes] + gram_of(kept, both))
    edges[...] = both
    at_row = lax.broadcasted_iota(jnp.int32, (planes, planes), 0)
    at_col = lax.broadcasted_iota(jnp.int32, (planes, planes), 1)
    mixed = jnp.where(at_row >= at_col, gram[0], gram[1])
    diagonal = jnp.sum(jnp.where(at_row == at_col, gram[1], 0.0), axis=0, keepdims=True)
    block = jnp.concatenate([mixed[8 * g : 8 * (g + 1)] for g in range(planes // 8)], axis=1)
    last = jnp.concatenate([diagonal] * (LANES // planes), axis=1)
    for target in range(grams.shape[0]):
        for at in range(8):
            grams[target, :, at * LANES : (at + 1) * LANES] = block[at : at + 1]
        grams[target, :, 8 * LANES :] = last


def eliminate(grams, planes, half_way):
    lane = lax.broadcasted_iota(jnp.int32, (8, LANES), 1)
    sub = lax.broadcasted_iota(jnp.int32, (8, LANES), 0)
    first_half = lane < 2 * planes
    groups = planes // 8
    sources = [[gram[8 * g : 8 * (g + 1)] for g in range(groups)] for gram in grams]
    state = []
    for g in range(groups):
        unit = jnp.where(sub + 8 * g == lane % (2 * planes) - planes, 1.0, 0.0)
        unit = unit[:, planes : 2 * planes]
        state.append(jnp.concatenate([sources[0][g], unit, sources[1][g], unit], axis=1))
    columns = []
    for j in range(planes):
        columns.append(
            {
                g: jnp.where(
                    first_half,
                    jnp.broadcast_to(sources[0][g][:, j : j + 1], (8, LANES)),
                    jnp.broadcast_to(sources[1][g][:, j : j + 1], (8, LANES)),
                )
                for g in range(j // 8, groups)
            }
        )
    scale = [jnp.ones((8, LANES), jnp.float32)] * groups
    for step in range(planes):
        own, at = step // 8, step % 8
        column = columns[step]
        root = lax.rsqrt(jnp.broadcast_to(column[own][at : at + 1], (8, LANES)))
        inverse = root * root
        scale[own] = jnp.where(sub == at, root, scale[own])
        left = {g: jnp.where(sub > at, value, 0.0) if g == own else value for g, value in column.items()}
        factors = {g: value * inverse for g, value in left.items()}
        for j in range(step + 1, planes):
            entry = jnp.broadcast_to(column[j // 8][j % 8 : j % 8 + 1], (8, LANES))
            for g in columns[j]:
                change = (left[g] * entry) * inverse if j == step + 1 else factors[g] * entry
                columns[j][g] = columns[j][g] - change
        pivot_row = jnp.broadcast_to(state[own][at : at + 1], (8, LANES))
        for g in range(own, groups):
            state[g] = state[g] - factors[g] * pivot_row
        if step + 1 == planes // 2:
            half_way(jnp.concatenate([state[g] * scale[g] for g in range(groups // 2)], axis=0))
    return jnp.concatenate([state[g] * scale[g] for g in range(groups)], axis=0)


def finish_kernel(
    pixel_count, inner_second, outer_second, edges, parts, basis_out, factor_out, basis, factor, written
):
    planes, rows, width = basis.shape
    half = planes // 2
    at_row = lax.broadcasted_iota(jnp.int32, (planes, planes), 0)
    at_col = lax.broadcasted_iota(jnp.int32, (planes, planes), 1)
    lane = lax.broadcasted_iota(jnp.int32, (1, LANES), 1)
    outer_parts = split(edges[...])
    copies = []

    def solve(inverse, start):
        stop = start + inverse.shape[0]
        high, middle, low = split(inverse)
        left_side = jnp.concatenate([high, high, middle, high, low, middle], axis=1)

        def solved(high, middle, low):
            right_side = jnp.concatenate([high, middle, high, low, high, middle], axis=0)
            return jnp.dot(left_side, right_side, preferred_element_type=jnp.float32)

        outer = solved(*(part[:stop] for part in outer_parts))
        for row in range(rows):
            if 2 <= row < rows - 2:
                held, spot = inner_second, row - 2
            else:
                held, spot = outer_second, row if row < 2 else row - rows + 4
            value = solved(*(held[spot, at * planes : at * planes + stop] for at in range(3)))
            place = PITCH * (row + 2)
            first = rolled(outer[:, :LANES], -(place + 2))
            last = rolled(outer[:, LANES:], LANES - 2 - (place + PITCH - 4))
            basis[start:stop, row, :LANES] = jnp.where(lane < 2, first, value[:, :LANES])
            basis[start:stop, row, LANES : width - LANES] = value[:, LANES : width - LANES]
            basis[start:stop, row, width - LANES :] = jnp.where(
                lane >= LANES - 2, last, value[:, width - LANES :]
            )
        some = pl.ds(start, stop - start)
        copies.append(pltpu.make_async_copy(basis.at[some], basis_out.at[some], written.at[len(copies)]))
        copies[-1].start()

    block = tree_sum([parts[at] for at in range(parts.shape[0])]) / pixel_count
    block = [block[:, at * LANES : (at + 1) * LANES] for at in range(9)]
    mixed, diagonal = jnp.concatenate(block[:8], axis=0), block[8][:, :planes]
    mixed = jnp.concatenate([mixed[:, at * planes : (at + 1) * planes] for at in range(LANES // planes)], axis=0)
    flipped = mixed.T
    first = jnp.where(at_row >= at_col, mixed, flipped)
    second = jnp.where(at_row < at_col, mixed, jnp.where(at_row > at_col, flipped, diagonal))
    low_half = (at_col <= at_row)[:half, :half]
    state = eliminate(
        [first, second],
        planes,
        lambda state: solve(jnp.where(low_half, state[:, 3 * planes : 3 * planes + half], 0.0), 0),
    )
    first_inverse = state[:, planes : 2 * planes]
    product_upper = jnp.where(at_col >= at_row, state[:, 2 * planes : 3 * planes], 0.0)
    solve(jnp.where(at_col <= at_row, state[:, 3 * planes :], 0.0)[half:], half)
    factor[...] = jnp.where(at_col >= at_row, gram_of(product_upper, first_inverse), 0.0)
    copies.append(pltpu.make_async_copy(factor, factor_out, written.at[2]))
    copies[-1].start()
    for copy in copies:
        copy.wait()


def tree_sum(parts):
    while len(parts) > 1:
        parts = [sum(parts[at + 1 : at + 2], parts[at]) for at in range(0, len(parts), 2)]
    return parts[0]


def swap(value, row_pairing=None, col_pairing=None):
    names = ("sec", "row", "col")
    shape = [lax.axis_size(name) for name in names]

    def partner(at, place, pairing):
        other = place if pairing is None else place + 1 if place % 2 != pairing else place - 1
        return other if 0 <= other < shape[at] else None

    pairs = []
    for sec, row, col in itertools.product(*(range(extent) for extent in shape)):
        other_row, other_col = partner(1, row, row_pairing), partner(2, col, col_pairing)
        if other_col is None:
            target = (sec, row ^ 1, col)
        elif other_row is None:
            target = (sec ^ 1, row, col)
        else:
            target = (sec, other_row, other_col)
        pairs.append(tuple((a * shape[1] + b) * shape[2] + c for a, b, c in ((sec, row, col), target)))
    return lax.ppermute(value, names, pairs)


def on_device(sketch, weights):
    planes, rows, width = sketch.shape
    group = lax.axis_size("row") * lax.axis_size("col")
    side = f32(planes + 8, LANES)
    by_row, weights_by_row, left, right, *messages = call(
        pack_rows_kernel,
        [f32(rows, planes, width), f32(rows, 8, width), side, side]
        + [f32(2 * planes + 16, width), f32(2 * planes + 8, width)]
        + [f32(16, LANES)] * 2,
        pltpu.with_memory_space_constraint(sketch, pltpu.HBM),
        pltpu.with_memory_space_constraint(weights, pltpu.HBM),
        memory=pltpu.HBM,
        scratch=[
            pltpu.VMEM(sketch.shape, jnp.float32),
            pltpu.VMEM(weights.shape, jnp.float32),
            pltpu.SemaphoreType.DMA((2,)),
        ],
    )
    from_rows = [swap(messages[at], row_pairing=at) for at in range(2)]
    from_diagonals = [swap(messages[2 + at], row_pairing=0, col_pairing=at) for at in range(2)]
    left, right, *messages = call(
        functools.partial(strips_kernel, rows), [side, side] + [f32(16, LANES)] * 2, left, right, from_rows[1]
    )
    from_cols = [swap(messages[1 - at], col_pairing=at) for at in (1, 0)]
    parts_of = functools.partial(jax.ShapeDtypeStruct, dtype=jnp.bfloat16)
    products = f32(3 * planes, 3 * planes)
    middle, inner_second, *inner_products = call(
        inner_rows_kernel,
        [f32(rows - 2, planes, width), parts_of((rows - 4, 3 * planes, width)), products, products],
        by_row,
        weights_by_row,
    )
    outer_second, early_grams, *halos = call(
        outer_rows_kernel,
        [parts_of((4, 3 * planes, width)), f32(planes, 2 * planes), side, side],
        by_row,
        weights_by_row,
        *from_rows,
        middle,
        *inner_products,
        scratch=[pltpu.VMEM((4, planes, width), jnp.float32)],
    )
    grams, edges = call(
        functools.partial(late_kernel, rows),
        [f32(group, 1, 9 * LANES), f32(planes, 2 * LANES)],
        left,
        right,
        *halos,
        *from_diagonals,
        *from_cols,
        early_grams,
    )
    rows_of, cols_of = lax.axis_size("row"), lax.axis_size("col")
    first = cols_of + cols_of // 2
    order = [first] + [row * cols_of + col for col in range(cols_of) for row in range(rows_of)]
    order = list(dict.fromkeys(order))
    parts = lax.all_to_all(grams, ("row", "col"), 0, 0, axis_index_groups=[order], tiled=True)
    return call(
        functools.partial(finish_kernel, float(rows * width * group)),
        [f32(planes, rows, width), f32(planes, planes)],
        inner_second,
        outer_second,
        edges,
        parts,
        out_memory=pl.ANY,
        scratch=[
            pltpu.VMEM(sketch.shape, jnp.float32),
            pltpu.VMEM((planes, planes), jnp.float32),
            pltpu.SemaphoreType.DMA((3,)),
        ],
    )


def solution(mesh):
    return jax.shard_map(
        on_device,
        mesh=mesh,
        in_specs=(P(None, ("sec", "row"), "col"), P(None, ("sec", "row"), "col")),
        out_specs=(P(None, ("sec", "row"), "col"), P("sec", None)),
        check_vma=False,
    )
```

```python
import functools
import itertools

import jax
import jax.numpy as jnp
from jax import lax
from jax.experimental import pallas as pl
from jax.experimental.pallas import tpu as pltpu
from jax.sharding import PartitionSpec as P

NEIGHBOURS = ((-1, -1), (-1, 0), (-1, 1), (0, -1), (0, 1), (1, -1), (1, 0), (1, 1))
LANES = 128
PITCH = 8
HIGHEST = lax.Precision.HIGHEST


def call(kernel, out_shapes, *operands, memory=pltpu.VMEM, out_memory=pltpu.VMEM, scratch=(), cost=None):
    return pl.pallas_call(
        kernel,
        out_shape=out_shapes,
        in_specs=[pl.BlockSpec(memory_space=memory)] * len(operands),
        out_specs=[pl.BlockSpec(memory_space=out_memory)] * len(out_shapes),
        scratch_shapes=scratch,
        cost_estimate=cost,
        compiler_params=pltpu.CompilerParams(vmem_limit_bytes=40 * 1024 * 1024),
    )(*operands)


def f32(*shape):
    return jax.ShapeDtypeStruct(shape, jnp.float32)


def sides_of(axis):
    place = lax.axis_index(axis)
    return place % 2 == 1, place > 0, place < lax.axis_size(axis) - 1


def edge_columns(first, last, place):
    lane = lax.broadcasted_iota(jnp.int32, (1, LANES), 1)
    own = PITCH - 2
    left = jnp.where((lane >= place + 2) & (lane < place + PITCH), pltpu.roll(first, place + 2, 1), 0.0)
    right = jnp.where((lane >= place) & (lane < place + own), pltpu.roll(last, place + own, 1), 0.0)
    return left, right


def pack_rows_kernel(sketch, weights, by_row, weights_by_row, left, right, *rest):
    bulk_messages, diagonal_messages = rest[:2], rest[2:4]
    tile, weight_tile, arrived = rest[4:]
    copies = [
        pltpu.make_async_copy(sketch, tile, arrived.at[0]),
        pltpu.make_async_copy(weights, weight_tile, arrived.at[1]),
    ]
    for copy in copies:
        copy.start()
    for copy in copies:
        copy.wait()
    rows, planes, width = by_row.shape
    odd_row, _, _ = sides_of("row")
    odd_col, _, _ = sides_of("col")
    lane = lax.broadcasted_iota(jnp.int32, (1, LANES), 1)
    for row in range(rows):
        weights_by_row[row] = weight_tile[:, row, :]
        by_row[row] = tile[:, row, :]
    for message, up in zip(bulk_messages, (odd_row, jnp.logical_not(odd_row))):
        start = jnp.where(up, rows - 2, 0)
        for slot in range(2):
            message[slot * planes : (slot + 1) * planes] = by_row[start + slot]
        message[2 * planes : 2 * planes + 8] = weights_by_row[jnp.where(up, rows - 1, 0)]
    strips = [None, None]
    for row in range(rows):
        first = jnp.concatenate([by_row[row, :, :LANES], weights_by_row[row, :, :LANES]], axis=0)
        last = jnp.concatenate([by_row[row, :, width - LANES :], weights_by_row[row, :, width - LANES :]], axis=0)
        parts = edge_columns(first, last, PITCH * (row + 2))
        strips = [part if strip is None else strip + part for strip, part in zip(strips, parts)]
    left[...], right[...] = strips
    bulk_messages[0][2 * planes + 8 :] = jnp.zeros((8, width), jnp.float32)
    pair = 2 * PITCH
    to_left, to_right = folded(strips[0], 2), folded(strips[1], PITCH - 4)
    for message, up in zip(diagonal_messages, (jnp.logical_not(odd_col), odd_col)):
        edge = jnp.where(up, to_right, to_left)
        below = jnp.where(lane < pair, rolled(edge, -PITCH * rows), 0.0)
        start = PITCH * (rows + 2)
        above = jnp.where((lane >= start) & (lane < start + pair), rolled(edge, PITCH * rows), 0.0)
        message[...] = jnp.where(odd_row, below, above)


def strips_kernel(rows, own_left, own_right, bulk_message, left, right, *col_messages):
    planes = own_left.shape[0] - 8
    odd_row, has_below, has_above = sides_of("row")
    odd_col, _, _ = sides_of("col")
    width = bulk_message.shape[1]
    totals = [own_left[...], own_right[...]]
    present = jnp.where(odd_row, has_below, has_above)
    for slot in range(2):
        place = PITCH * (slot + jnp.where(odd_row, 0, rows + 2))
        halo = [bulk_message[slot * planes : (slot + 1) * planes], bulk_message[2 * planes :]]
        first = jnp.concatenate([part[:, :LANES] for part in halo], axis=0)
        last = jnp.concatenate([part[:, width - LANES :] for part in halo], axis=0)
        parts = edge_columns(first, last, place)
        totals = [total + jnp.where(present, part, 0.0) for total, part in zip(totals, parts)]
    left[...], right[...] = totals
    to_left, to_right = folded(left[...], 2), folded(right[...], PITCH - 4)
    for message, up in zip(col_messages, (jnp.logical_not(odd_col), odd_col)):
        message[...] = jnp.where(up, to_right, to_left)


def folded(strip, spot):
    lane = lax.broadcasted_iota(jnp.int32, (1, LANES), 1)
    groups = strip.shape[0] // 8
    pieces = []
    for group in range(groups):
        target = 2 * group if group < groups - 1 else 0
        moved = rolled(strip[8 * group : 8 * (group + 1)], target - spot)
        pieces.append(jnp.where((lane % PITCH) // 2 == target // 2, moved, 0.0))
    return jnp.concatenate([functools.reduce(jnp.add, pieces[:-1]), pieces[-1]], axis=0)


def unfolded(message, spot, planes):
    lane = lax.broadcasted_iota(jnp.int32, (1, LANES), 1)
    pieces = [rolled(message[:8], spot - 2 * group) for group in range(planes // 8)] + [rolled(message[8:], spot)]
    return jnp.where((lane % PITCH) // 2 == spot // 2, jnp.concatenate(pieces, axis=0), 0.0)


def rolled(value, shift):
    return pltpu.roll(value, shift % LANES, 1) if shift % LANES else value


def apply_operator(rows3, weight_rows):
    width = rows3[1].shape[1]
    total = jnp.sum(weight_rows, axis=0, keepdims=True) * rows3[1]
    for across in (0, -1, 1):
        moved = pltpu.roll(weight_rows, across % width, 1) if across else weight_rows
        terms = [
            moved[position : position + 1] * rows3[up + 1]
            for position, (up, side) in enumerate(NEIGHBOURS)
            if side == across
        ]
        part = functools.reduce(jnp.add, terms)
        total = total + (pltpu.roll(part, -across % width, 1) if across else part)
    return total


def gram_of(value, other):
    return lax.dot_general(
        value, other, (((1,), (1,)), ((), ())), precision=HIGHEST, preferred_element_type=jnp.float32
    )


def split(value):
    high = value.astype(jnp.bfloat16)
    rest = value - high.astype(jnp.float32)
    middle = rest.astype(jnp.bfloat16)
    low = (rest - middle.astype(jnp.float32)).astype(jnp.bfloat16)
    return high, middle, low


def inner_parts(image):
    width = image.shape[1]
    lane = lax.broadcasted_iota(jnp.int32, (1, LANES), 1)
    kept = [
        jnp.where(lane >= 2, image[:, :LANES], 0.0),
        image[:, LANES : width - LANES],
        jnp.where(lane < LANES - 2, image[:, width - LANES :], 0.0),
    ]
    return jnp.concatenate(split(jnp.concatenate(kept, axis=1)), axis=0)


def products_of(parts):
    return lax.dot_general(parts, parts, (((1,), (1,)), ((), ())), preferred_element_type=jnp.float32)


def images_of(middle, weights, wanted, second, products):
    for at, row in enumerate(wanted):
        parts = inner_parts(apply_operator([middle(row - 1), middle(row), middle(row + 1)], weights(row)))
        second[at] = parts
        products = products + products_of(parts)
    return products


def inner_rows_kernel(by_row, weights_by_row, middle, second, first_products, second_products):
    rows = by_row.shape[0]
    products = jnp.zeros(first_products.shape, jnp.float32)
    for row in range(1, rows - 1):
        image = apply_operator([by_row[row - 1], by_row[row], by_row[row + 1]], weights_by_row[row])
        middle[row - 1] = image
        products = products + products_of(inner_parts(image))
    first_products[...] = products
    second_products[...] = images_of(
        lambda row: middle[row - 1],
        lambda row: weights_by_row[row],
        range(2, rows - 2),
        second,
        jnp.zeros(second_products.shape, jnp.float32),
    )


def outer_rows_kernel(
    by_row,
    weights_by_row,
    first_message,
    second_message,
    middle,
    first_products,
    second_products,
    second,
    grams,
    left_halo,
    right_halo,
    outer,
):
    rows, planes, width = by_row.shape
    odd_row, has_below, has_above = sides_of("row")
    one, other = first_message[: 2 * planes + 8], second_message[...]
    below = jnp.where(has_below, jnp.where(odd_row, other, one), 0.0)
    above = jnp.where(has_above, jnp.where(odd_row, one, other), 0.0)
    halos = [None, None]
    for side, (halo, present) in enumerate(
        ((below, jnp.logical_not(odd_row)), (above, odd_row))
    ):
        for slot in range(2):
            index = slot if side == 0 else rows + 2 + slot
            blank = jnp.zeros((8, width), jnp.float32)
            weight = halo[2 * planes :] if slot != side else blank
            row_values = jnp.concatenate([halo[slot * planes : (slot + 1) * planes], weight], axis=0)
            parts = edge_columns(row_values[:, :LANES], row_values[:, width - LANES :], PITCH * index)
            parts = [jnp.where(present, part, 0.0) for part in parts]
            halos = [part if total is None else total + part for total, part in zip(halos, parts)]
    left_halo[...], right_halo[...] = halos

    def field(row):
        if 0 <= row < rows:
            return by_row[row]
        at = (row + 2 if row < 0 else row - rows) * planes
        return (below if row < 0 else above)[at : at + planes]

    def weights(row):
        if 0 <= row < rows:
            return weights_by_row[row]
        return (below if row < 0 else above)[2 * planes :]

    products = first_products[...]
    places = (-1, 0, rows - 1, rows)
    for at, row in enumerate(places):
        image = apply_operator([field(row - 1), field(row), field(row + 1)], weights(row))
        outer[at] = image
        if 0 <= row < rows:
            products = products + products_of(inner_parts(image))
    both = [products]
    both.append(
        images_of(
            lambda row: outer[places.index(row)] if row in places else middle[row - 1],
            weights,
            (0, 1, rows - 2, rows - 1),
            second,
            second_products[...],
        )
    )
    for at, products in enumerate(both):
        some = products[:planes] + products[planes : 2 * planes] + products[2 * planes :]
        total = some[:, :planes] + some[:, planes : 2 * planes] + some[:, 2 * planes :]
        grams[:, at * planes : (at + 1) * planes] = total


def apply_on_strip(values, weights):
    total = jnp.sum(weights, axis=0, keepdims=True) * values
    for position, (up, across) in enumerate(NEIGHBOURS):
        moved = pltpu.roll(values, (-PITCH * up - across) % LANES, 1)
        total = total + weights[position : position + 1] * moved
    return total


def late_kernel(rows, left, right, left_halo, right_halo, *rest):
    diagonal_messages, col_messages, (early_grams, grams, edges) = rest[1::-1], rest[3:1:-1], rest[4:]
    planes = early_grams.shape[0]
    odd_row, has_below, has_above = sides_of("row")
    odd_col, has_left, has_right = sides_of("col")
    beyond = jnp.where(odd_row, has_above, has_below)
    one, other = (
        col[...] + jnp.where(beyond, diagonal[...], 0.0)
        for col, diagonal in zip(col_messages, diagonal_messages)
    )
    lane = lax.broadcasted_iota(jnp.int32, (1, LANES), 1)
    spot, row = lane % PITCH, lane // PITCH
    strips, masks = [], []
    for side, (strip, present, halo) in enumerate(
        (
            (left[...] + left_halo[...], has_left, jnp.where(odd_col, other, one)),
            (right[...] + right_halo[...], has_right, jnp.where(odd_col, one, other)),
        )
    ):
        strips.append(strip + jnp.where(present, unfolded(halo, side * (PITCH - 2), planes), 0.0))
        low = 2 if side == 0 else PITCH - 4
        masks.append((spot >= low) & (spot < low + 2) & (row >= 2) & (row < rows + 2))
    values = [strip[:planes] for strip in strips]
    gram = []
    for at in range(2):
        values = [apply_on_strip(value, strip[planes:]) for value, strip in zip(values, strips)]
        kept = jnp.concatenate([jnp.where(mask, value, 0.0) for mask, value in zip(masks, values)], axis=1)
        both = jnp.concatenate(values, axis=1)
        gram.append(early_grams[:, at * planes : (at + 1) * planes] + gram_of(kept, both))
    edges[...] = both
    at_row = lax.broadcasted_iota(jnp.int32, (planes, planes), 0)
    at_col = lax.broadcasted_iota(jnp.int32, (planes, planes), 1)
    mixed = jnp.where(at_row >= at_col, gram[0], gram[1])
    diagonal = jnp.sum(jnp.where(at_row == at_col, gram[1], 0.0), axis=0, keepdims=True)
    block = jnp.concatenate([mixed[8 * g : 8 * (g + 1)] for g in range(planes // 8)], axis=1)
    last = jnp.concatenate([diagonal] * (LANES // planes), axis=1)
    for target in range(grams.shape[0]):
        for at in range(8):
            grams[target, :, at * LANES : (at + 1) * LANES] = block[at : at + 1]
        grams[target, :, 8 * LANES :] = last


def eliminate(grams, planes, half_way):
    lane = lax.broadcasted_iota(jnp.int32, (8, LANES), 1)
    sub = lax.broadcasted_iota(jnp.int32, (8, LANES), 0)
    first_half = lane < 2 * planes
    groups = planes // 8
    sources = [[gram[8 * g : 8 * (g + 1)] for g in range(groups)] for gram in grams]
    state = []
    for g in range(groups):
        unit = jnp.where(sub + 8 * g == lane % (2 * planes) - planes, 1.0, 0.0)
        unit = unit[:, planes : 2 * planes]
        state.append(jnp.concatenate([sources[0][g], unit, sources[1][g], unit], axis=1))
    columns = []
    for j in range(planes):
        columns.append(
            {
                g: jnp.where(
                    first_half,
                    jnp.broadcast_to(sources[0][g][:, j : j + 1], (8, LANES)),
                    jnp.broadcast_to(sources[1][g][:, j : j + 1], (8, LANES)),
                )
                for g in range(j // 8, groups)
            }
        )
    scale = [jnp.ones((8, LANES), jnp.float32)] * groups
    for step in range(planes):
        own, at = step // 8, step % 8
        column = columns[step]
        root = lax.rsqrt(jnp.broadcast_to(column[own][at : at + 1], (8, LANES)))
        inverse = root * root
        scale[own] = jnp.where(sub == at, root, scale[own])
        left = {g: jnp.where(sub > at, value, 0.0) if g == own else value for g, value in column.items()}
        factors = {g: value * inverse for g, value in left.items()}
        for j in range(step + 1, planes):
            entry = jnp.broadcast_to(column[j // 8][j % 8 : j % 8 + 1], (8, LANES))
            for g in columns[j]:
                change = (left[g] * entry) * inverse if j == step + 1 else factors[g] * entry
                columns[j][g] = columns[j][g] - change
        pivot_row = jnp.broadcast_to(state[own][at : at + 1], (8, LANES))
        for g in range(own, groups):
            state[g] = state[g] - factors[g] * pivot_row
        if step + 1 == planes // 2:
            half_way(jnp.concatenate([state[g] * scale[g] for g in range(groups // 2)], axis=0))
    return jnp.concatenate([state[g] * scale[g] for g in range(groups)], axis=0)


def finish_kernel(
    pixel_count, inner_second, outer_second, edges, parts, basis_out, factor_out, basis, factor, written
):
    planes, rows, width = basis.shape
    half = planes // 2
    at_row = lax.broadcasted_iota(jnp.int32, (planes, planes), 0)
    at_col = lax.broadcasted_iota(jnp.int32, (planes, planes), 1)
    lane = lax.broadcasted_iota(jnp.int32, (1, LANES), 1)
    outer_parts = split(edges[...])
    copies = []

    def solve(inverse, start):
        stop = start + inverse.shape[0]
        high, middle, low = split(inverse)
        left_side = jnp.concatenate([high, high, middle, high, low, middle], axis=1)

        def solved(high, middle, low):
            right_side = jnp.concatenate([high, middle, high, low, high, middle], axis=0)
            return jnp.dot(left_side, right_side, preferred_element_type=jnp.float32)

        outer = solved(*(part[:stop] for part in outer_parts))
        for row in range(rows):
            if 2 <= row < rows - 2:
                held, spot = inner_second, row - 2
            else:
                held, spot = outer_second, row if row < 2 else row - rows + 4
            value = solved(*(held[spot, at * planes : at * planes + stop] for at in range(3)))
            place = PITCH * (row + 2)
            first = rolled(outer[:, :LANES], -(place + 2))
            last = rolled(outer[:, LANES:], LANES - 2 - (place + PITCH - 4))
            basis[start:stop, row, :LANES] = jnp.where(lane < 2, first, value[:, :LANES])
            basis[start:stop, row, LANES : width - LANES] = value[:, LANES : width - LANES]
            basis[start:stop, row, width - LANES :] = jnp.where(
                lane >= LANES - 2, last, value[:, width - LANES :]
            )
        some = pl.ds(start, stop - start)
        copies.append(pltpu.make_async_copy(basis.at[some], basis_out.at[some], written.at[len(copies)]))
        copies[-1].start()

    block = tree_sum([parts[at] for at in range(parts.shape[0])]) / pixel_count
    block = [block[:, at * LANES : (at + 1) * LANES] for at in range(9)]
    mixed, diagonal = jnp.concatenate(block[:8], axis=0), block[8][:, :planes]
    mixed = jnp.concatenate([mixed[:, at * planes : (at + 1) * planes] for at in range(LANES // planes)], axis=0)
    flipped = mixed.T
    first = jnp.where(at_row >= at_col, mixed, flipped)
    second = jnp.where(at_row < at_col, mixed, jnp.where(at_row > at_col, flipped, diagonal))
    low_half = (at_col <= at_row)[:half, :half]
    state = eliminate(
        [first, second],
        planes,
        lambda state: solve(jnp.where(low_half, state[:, 3 * planes : 3 * planes + half], 0.0), 0),
    )
    first_inverse = state[:, planes : 2 * planes]
    product_upper = jnp.where(at_col >= at_row, state[:, 2 * planes : 3 * planes], 0.0)
    solve(jnp.where(at_col <= at_row, state[:, 3 * planes :], 0.0)[half:], half)
    factor[...] = jnp.where(at_col >= at_row, gram_of(product_upper, first_inverse), 0.0)
    copies.append(pltpu.make_async_copy(factor, factor_out, written.at[2]))
    copies[-1].start()
    for copy in copies:
        copy.wait()


def tree_sum(parts):
    while len(parts) > 1:
        parts = [sum(parts[at + 1 : at + 2], parts[at]) for at in range(0, len(parts), 2)]
    return parts[0]


def swap(value, row_pairing=None, col_pairing=None):
    names = ("sec", "row", "col")
    shape = [lax.axis_size(name) for name in names]

    def partner(at, place, pairing):
        other = place if pairing is None else place + 1 if place % 2 != pairing else place - 1
        return other if 0 <= other < shape[at] else None

    pairs = []
    for sec, row, col in itertools.product(*(range(extent) for extent in shape)):
        other_row, other_col = partner(1, row, row_pairing), partner(2, col, col_pairing)
        if other_col is None:
            target = (sec, row ^ 1, col)
        elif other_row is None:
            target = (sec ^ 1, row, col)
        else:
            target = (sec, other_row, other_col)
        pairs.append(tuple((a * shape[1] + b) * shape[2] + c for a, b, c in ((sec, row, col), target)))
    return lax.ppermute(value, names, pairs)


def on_device(sketch, weights):
    planes, rows, width = sketch.shape
    group = lax.axis_size("row") * lax.axis_size("col")
    side = f32(planes + 8, LANES)
    by_row, weights_by_row, left, right, *messages = call(
        pack_rows_kernel,
        [f32(rows, planes, width), f32(rows, 8, width), side, side]
        + [f32(2 * planes + 16, width), f32(2 * planes + 8, width)]
        + [f32(16, LANES)] * 2,
        pltpu.with_memory_space_constraint(sketch, pltpu.HBM),
        pltpu.with_memory_space_constraint(weights, pltpu.HBM),
        memory=pltpu.HBM,
        scratch=[
            pltpu.VMEM(sketch.shape, jnp.float32),
            pltpu.VMEM(weights.shape, jnp.float32),
            pltpu.SemaphoreType.DMA((2,)),
        ],
    )
    from_rows = [swap(messages[at], row_pairing=at) for at in range(2)]
    from_diagonals = [swap(messages[3 - at], row_pairing=0, col_pairing=at) for at in (1, 0)]
    left, right, *messages = call(
        functools.partial(strips_kernel, rows), [side, side] + [f32(16, LANES)] * 2, left, right, from_rows[1]
    )
    from_cols = [swap(messages[1 - at], col_pairing=at) for at in (1, 0)]
    parts_of = functools.partial(jax.ShapeDtypeStruct, dtype=jnp.bfloat16)
    products = f32(3 * planes, 3 * planes)
    middle, inner_second, *inner_products = call(
        inner_rows_kernel,
        [f32(rows - 2, planes, width), parts_of((rows - 4, 3 * planes, width)), products, products],
        by_row,
        weights_by_row,
    )
    outer_second, early_grams, *halos = call(
        outer_rows_kernel,
        [parts_of((4, 3 * planes, width)), f32(planes, 2 * planes), side, side],
        by_row,
        weights_by_row,
        *from_rows,
        middle,
        *inner_products,
        scratch=[pltpu.VMEM((4, planes, width), jnp.float32)],
    )
    grams, edges = call(
        functools.partial(late_kernel, rows),
        [f32(group, 1, 9 * LANES), f32(planes, 2 * LANES)],
        left,
        right,
        *halos,
        *from_diagonals,
        *from_cols,
        early_grams,
    )
    rows_of, cols_of = lax.axis_size("row"), lax.axis_size("col")
    first = cols_of + cols_of // 2
    order = [first] + [row * cols_of + col for col in range(cols_of) for row in range(rows_of)]
    order = list(dict.fromkeys(order))
    parts = lax.all_to_all(grams, ("row", "col"), 0, 0, axis_index_groups=[order], tiled=True)
    return call(
        functools.partial(finish_kernel, float(rows * width * group)),
        [f32(planes, rows, width), f32(planes, planes)],
        inner_second,
        outer_second,
        edges,
        parts,
        out_memory=pl.ANY,
        scratch=[
            pltpu.VMEM(sketch.shape, jnp.float32),
            pltpu.VMEM((planes, planes), jnp.float32),
            pltpu.SemaphoreType.DMA((3,)),
        ],
    )


def solution(mesh):
    return jax.shard_map(
        on_device,
        mesh=mesh,
        in_specs=(P(None, ("sec", "row"), "col"), P(None, ("sec", "row"), "col")),
        out_specs=(P(None, ("sec", "row"), "col"), P("sec", None)),
        check_vma=False,
    )
```

```python
import functools
import itertools

import jax
import jax.numpy as jnp
from jax import lax
from jax.experimental import pallas as pl
from jax.experimental.pallas import tpu as pltpu
from jax.sharding import PartitionSpec as P

NEIGHBOURS = ((-1, -1), (-1, 0), (-1, 1), (0, -1), (0, 1), (1, -1), (1, 0), (1, 1))
LANES = 128
PITCH = 8
HIGHEST = lax.Precision.HIGHEST


def call(kernel, out_shapes, *operands, memory=pltpu.VMEM, out_memory=pltpu.VMEM, scratch=(), cost=None):
    return pl.pallas_call(
        kernel,
        out_shape=out_shapes,
        in_specs=[pl.BlockSpec(memory_space=memory)] * len(operands),
        out_specs=[pl.BlockSpec(memory_space=out_memory)] * len(out_shapes),
        scratch_shapes=scratch,
        cost_estimate=cost,
        compiler_params=pltpu.CompilerParams(vmem_limit_bytes=40 * 1024 * 1024),
    )(*operands)


def f32(*shape):
    return jax.ShapeDtypeStruct(shape, jnp.float32)


def sides_of(axis):
    place = lax.axis_index(axis)
    return place % 2 == 1, place > 0, place < lax.axis_size(axis) - 1


def edge_columns(first, last, place):
    lane = lax.broadcasted_iota(jnp.int32, (1, LANES), 1)
    own = PITCH - 2
    left = jnp.where((lane >= place + 2) & (lane < place + PITCH), pltpu.roll(first, place + 2, 1), 0.0)
    right = jnp.where((lane >= place) & (lane < place + own), pltpu.roll(last, place + own, 1), 0.0)
    return left, right


def pack_rows_kernel(sketch, weights, by_row, weights_by_row, left, right, *rest):
    bulk_messages, diagonal_messages = rest[:2], rest[2:4]
    tile, weight_tile, arrived = rest[4:]
    copies = [
        pltpu.make_async_copy(sketch, tile, arrived.at[0]),
        pltpu.make_async_copy(weights, weight_tile, arrived.at[1]),
    ]
    for copy in copies:
        copy.start()
    for copy in copies:
        copy.wait()
    rows, planes, width = by_row.shape
    odd_row, _, _ = sides_of("row")
    odd_col, _, _ = sides_of("col")
    lane = lax.broadcasted_iota(jnp.int32, (1, LANES), 1)
    for row in range(rows):
        weights_by_row[row] = weight_tile[:, row, :]
        by_row[row] = tile[:, row, :]
    for message, up in zip(bulk_messages, (odd_row, jnp.logical_not(odd_row))):
        start = jnp.where(up, rows - 2, 0)
        for slot in range(2):
            message[slot * planes : (slot + 1) * planes] = by_row[start + slot]
        message[2 * planes : 2 * planes + 8] = weights_by_row[jnp.where(up, rows - 1, 0)]
    strips = [None, None]
    for row in range(rows):
        first = jnp.concatenate([by_row[row, :, :LANES], weights_by_row[row, :, :LANES]], axis=0)
        last = jnp.concatenate([by_row[row, :, width - LANES :], weights_by_row[row, :, width - LANES :]], axis=0)
        parts = edge_columns(first, last, PITCH * (row + 2))
        strips = [part if strip is None else strip + part for strip, part in zip(strips, parts)]
    left[...], right[...] = strips
    bulk_messages[0][2 * planes + 8 :] = jnp.zeros((8, width), jnp.float32)
    pair = 2 * PITCH
    to_left, to_right = folded(strips[0], 2), folded(strips[1], PITCH - 4)
    for message, up in zip(diagonal_messages, (odd_col, jnp.logical_not(odd_col))):
        edge = jnp.where(up, to_right, to_left)
        below = jnp.where(lane < pair, rolled(edge, -PITCH * rows), 0.0)
        start = PITCH * (rows + 2)
        above = jnp.where((lane >= start) & (lane < start + pair), rolled(edge, PITCH * rows), 0.0)
        message[...] = jnp.where(odd_row, below, above)


def strips_kernel(rows, own_left, own_right, bulk_message, left, right, *col_messages):
    planes = own_left.shape[0] - 8
    odd_row, has_below, has_above = sides_of("row")
    odd_col, _, _ = sides_of("col")
    width = bulk_message.shape[1]
    totals = [own_left[...], own_right[...]]
    present = jnp.where(odd_row, has_below, has_above)
    for slot in range(2):
        place = PITCH * (slot + jnp.where(odd_row, 0, rows + 2))
        halo = [bulk_message[slot * planes : (slot + 1) * planes], bulk_message[2 * planes :]]
        first = jnp.concatenate([part[:, :LANES] for part in halo], axis=0)
        last = jnp.concatenate([part[:, width - LANES :] for part in halo], axis=0)
        parts = edge_columns(first, last, place)
        totals = [total + jnp.where(present, part, 0.0) for total, part in zip(totals, parts)]
    left[...], right[...] = totals
    to_left, to_right = folded(left[...], 2), folded(right[...], PITCH - 4)
    for message, up in zip(col_messages, (odd_col, jnp.logical_not(odd_col))):
        message[...] = jnp.where(up, to_right, to_left)


def folded(strip, spot):
    lane = lax.broadcasted_iota(jnp.int32, (1, LANES), 1)
    groups = strip.shape[0] // 8
    pieces = []
    for group in range(groups):
        target = 2 * group if group < groups - 1 else 0
        moved = rolled(strip[8 * group : 8 * (group + 1)], target - spot)
        pieces.append(jnp.where((lane % PITCH) // 2 == target // 2, moved, 0.0))
    return jnp.concatenate([functools.reduce(jnp.add, pieces[:-1]), pieces[-1]], axis=0)


def unfolded(message, spot, planes):
    lane = lax.broadcasted_iota(jnp.int32, (1, LANES), 1)
    pieces = [rolled(message[:8], spot - 2 * group) for group in range(planes // 8)] + [rolled(message[8:], spot)]
    return jnp.where((lane % PITCH) // 2 == spot // 2, jnp.concatenate(pieces, axis=0), 0.0)


def rolled(value, shift):
    return pltpu.roll(value, shift % LANES, 1) if shift % LANES else value


def apply_operator(rows3, weight_rows):
    width = rows3[1].shape[1]
    total = jnp.sum(weight_rows, axis=0, keepdims=True) * rows3[1]
    for across in (0, -1, 1):
        moved = pltpu.roll(weight_rows, across % width, 1) if across else weight_rows
        terms = [
            moved[position : position + 1] * rows3[up + 1]
            for position, (up, side) in enumerate(NEIGHBOURS)
            if side == across
        ]
        part = functools.reduce(jnp.add, terms)
        total = total + (pltpu.roll(part, -across % width, 1) if across else part)
    return total


def gram_of(value, other):
    return lax.dot_general(
        value, other, (((1,), (1,)), ((), ())), precision=HIGHEST, preferred_element_type=jnp.float32
    )


def split(value):
    high = value.astype(jnp.bfloat16)
    rest = value - high.astype(jnp.float32)
    middle = rest.astype(jnp.bfloat16)
    low = (rest - middle.astype(jnp.float32)).astype(jnp.bfloat16)
    return high, middle, low


def inner_parts(image):
    width = image.shape[1]
    lane = lax.broadcasted_iota(jnp.int32, (1, LANES), 1)
    kept = [
        jnp.where(lane >= 2, image[:, :LANES], 0.0),
        image[:, LANES : width - LANES],
        jnp.where(lane < LANES - 2, image[:, width - LANES :], 0.0),
    ]
    return jnp.concatenate(split(jnp.concatenate(kept, axis=1)), axis=0)


def products_of(parts):
    return lax.dot_general(parts, parts, (((1,), (1,)), ((), ())), preferred_element_type=jnp.float32)


def images_of(middle, weights, wanted, second, products):
    for at, row in enumerate(wanted):
        parts = inner_parts(apply_operator([middle(row - 1), middle(row), middle(row + 1)], weights(row)))
        second[at] = parts
        products = products + products_of(parts)
    return products


def inner_rows_kernel(by_row, weights_by_row, middle, second, first_products, second_products):
    rows = by_row.shape[0]
    products = jnp.zeros(first_products.shape, jnp.float32)
    for row in range(1, rows - 1):
        image = apply_operator([by_row[row - 1], by_row[row], by_row[row + 1]], weights_by_row[row])
        middle[row - 1] = image
        products = products + products_of(inner_parts(image))
    first_products[...] = products
    second_products[...] = images_of(
        lambda row: middle[row - 1],
        lambda row: weights_by_row[row],
        range(2, rows - 2),
        second,
        jnp.zeros(second_products.shape, jnp.float32),
    )


def outer_rows_kernel(
    by_row,
    weights_by_row,
    first_message,
    second_message,
    middle,
    first_products,
    second_products,
    second,
    grams,
    left_halo,
    right_halo,
    outer,
):
    rows, planes, width = by_row.shape
    odd_row, has_below, has_above = sides_of("row")
    one, other = first_message[: 2 * planes + 8], second_message[...]
    below = jnp.where(has_below, jnp.where(odd_row, other, one), 0.0)
    above = jnp.where(has_above, jnp.where(odd_row, one, other), 0.0)
    halos = [None, None]
    for side, (halo, present) in enumerate(
        ((below, jnp.logical_not(odd_row)), (above, odd_row))
    ):
        for slot in range(2):
            index = slot if side == 0 else rows + 2 + slot
            blank = jnp.zeros((8, width), jnp.float32)
            weight = halo[2 * planes :] if slot != side else blank
            row_values = jnp.concatenate([halo[slot * planes : (slot + 1) * planes], weight], axis=0)
            parts = edge_columns(row_values[:, :LANES], row_values[:, width - LANES :], PITCH * index)
            parts = [jnp.where(present, part, 0.0) for part in parts]
            halos = [part if total is None else total + part for total, part in zip(halos, parts)]
    left_halo[...], right_halo[...] = halos

    def field(row):
        if 0 <= row < rows:
            return by_row[row]
        at = (row + 2 if row < 0 else row - rows) * planes
        return (below if row < 0 else above)[at : at + planes]

    def weights(row):
        if 0 <= row < rows:
            return weights_by_row[row]
        return (below if row < 0 else above)[2 * planes :]

    products = first_products[...]
    places = (-1, 0, rows - 1, rows)
    for at, row in enumerate(places):
        image = apply_operator([field(row - 1), field(row), field(row + 1)], weights(row))
        outer[at] = image
        if 0 <= row < rows:
            products = products + products_of(inner_parts(image))
    both = [products]
    both.append(
        images_of(
            lambda row: outer[places.index(row)] if row in places else middle[row - 1],
            weights,
            (0, 1, rows - 2, rows - 1),
            second,
            second_products[...],
        )
    )
    for at, products in enumerate(both):
        some = products[:planes] + products[planes : 2 * planes] + products[2 * planes :]
        total = some[:, :planes] + some[:, planes : 2 * planes] + some[:, 2 * planes :]
        grams[:, at * planes : (at + 1) * planes] = total


def apply_on_strip(values, weights):
    total = jnp.sum(weights, axis=0, keepdims=True) * values
    for position, (up, across) in enumerate(NEIGHBOURS):
        moved = pltpu.roll(values, (-PITCH * up - across) % LANES, 1)
        total = total + weights[position : position + 1] * moved
    return total


def late_kernel(rows, left, right, left_halo, right_halo, *rest):
    diagonal_messages, col_messages, (early_grams, grams, edges) = rest[:2], rest[2:4], rest[4:]
    planes = early_grams.shape[0]
    odd_row, has_below, has_above = sides_of("row")
    odd_col, has_left, has_right = sides_of("col")
    beyond = jnp.where(odd_row, has_above, has_below)
    one, other = (
        col[...] + jnp.where(beyond, diagonal[...], 0.0)
        for col, diagonal in zip(col_messages, diagonal_messages)
    )
    lane = lax.broadcasted_iota(jnp.int32, (1, LANES), 1)
    spot, row = lane % PITCH, lane // PITCH
    strips, masks = [], []
    for side, (strip, present, halo) in enumerate(
        (
            (left[...] + left_halo[...], has_left, jnp.where(odd_col, other, one)),
            (right[...] + right_halo[...], has_right, jnp.where(odd_col, one, other)),
        )
    ):
        strips.append(strip + jnp.where(present, unfolded(halo, side * (PITCH - 2), planes), 0.0))
        low = 2 if side == 0 else PITCH - 4
        masks.append((spot >= low) & (spot < low + 2) & (row >= 2) & (row < rows + 2))
    values = [strip[:planes] for strip in strips]
    gram = []
    for at in range(2):
        values = [apply_on_strip(value, strip[planes:]) for value, strip in zip(values, strips)]
        kept = jnp.concatenate([jnp.where(mask, value, 0.0) for mask, value in zip(masks, values)], axis=1)
        both = jnp.concatenate(values, axis=1)
        gram.append(early_grams[:, at * planes : (at + 1) * planes] + gram_of(kept, both))
    edges[...] = both
    at_row = lax.broadcasted_iota(jnp.int32, (planes, planes), 0)
    at_col = lax.broadcasted_iota(jnp.int32, (planes, planes), 1)
    mixed = jnp.where(at_row >= at_col, gram[0], gram[1])
    diagonal = jnp.sum(jnp.where(at_row == at_col, gram[1], 0.0), axis=0, keepdims=True)
    block = jnp.concatenate([mixed[8 * g : 8 * (g + 1)] for g in range(planes // 8)], axis=1)
    last = jnp.concatenate([diagonal] * (LANES // planes), axis=1)
    for target in range(grams.shape[0]):
        for at in range(8):
            grams[target, :, at * LANES : (at + 1) * LANES] = block[at : at + 1]
        grams[target, :, 8 * LANES :] = last


def eliminate(grams, planes, half_way):
    lane = lax.broadcasted_iota(jnp.int32, (8, LANES), 1)
    sub = lax.broadcasted_iota(jnp.int32, (8, LANES), 0)
    first_half = lane < 2 * planes
    groups = planes // 8
    sources = [[gram[8 * g : 8 * (g + 1)] for g in range(groups)] for gram in grams]
    state = []
    for g in range(groups):
        unit = jnp.where(sub + 8 * g == lane % (2 * planes) - planes, 1.0, 0.0)
        unit = unit[:, planes : 2 * planes]
        state.append(jnp.concatenate([sources[0][g], unit, sources[1][g], unit], axis=1))
    columns = []
    for j in range(planes):
        columns.append(
            {
                g: jnp.where(
                    first_half,
                    jnp.broadcast_to(sources[0][g][:, j : j + 1], (8, LANES)),
                    jnp.broadcast_to(sources[1][g][:, j : j + 1], (8, LANES)),
                )
                for g in range(j // 8, groups)
            }
        )
    scale = [jnp.ones((8, LANES), jnp.float32)] * groups
    for step in range(planes):
        own, at = step // 8, step % 8
        column = columns[step]
        root = lax.rsqrt(jnp.broadcast_to(column[own][at : at + 1], (8, LANES)))
        inverse = root * root
        scale[own] = jnp.where(sub == at, root, scale[own])
        left = {g: jnp.where(sub > at, value, 0.0) if g == own else value for g, value in column.items()}
        factors = {g: value * inverse for g, value in left.items()}
        for j in range(step + 1, planes):
            entry = jnp.broadcast_to(column[j // 8][j % 8 : j % 8 + 1], (8, LANES))
            for g in columns[j]:
                change = (left[g] * entry) * inverse if j == step + 1 else factors[g] * entry
                columns[j][g] = columns[j][g] - change
        pivot_row = jnp.broadcast_to(state[own][at : at + 1], (8, LANES))
        for g in range(own, groups):
            state[g] = state[g] - factors[g] * pivot_row
        if step + 1 == planes // 2:
            half_way(jnp.concatenate([state[g] * scale[g] for g in range(groups // 2)], axis=0))
    return jnp.concatenate([state[g] * scale[g] for g in range(groups)], axis=0)


def finish_kernel(
    pixel_count, inner_second, outer_second, edges, parts, basis_out, factor_out, basis, factor, written
):
    planes, rows, width = basis.shape
    half = planes // 2
    at_row = lax.broadcasted_iota(jnp.int32, (planes, planes), 0)
    at_col = lax.broadcasted_iota(jnp.int32, (planes, planes), 1)
    lane = lax.broadcasted_iota(jnp.int32, (1, LANES), 1)
    outer_parts = split(edges[...])
    copies = []

    def solve(inverse, start):
        stop = start + inverse.shape[0]
        high, middle, low = split(inverse)
        left_side = jnp.concatenate([high, high, middle, high, low, middle], axis=1)

        def solved(high, middle, low):
            right_side = jnp.concatenate([high, middle, high, low, high, middle], axis=0)
            return jnp.dot(left_side, right_side, preferred_element_type=jnp.float32)

        outer = solved(*(part[:stop] for part in outer_parts))
        for row in range(rows):
            if 2 <= row < rows - 2:
                held, spot = inner_second, row - 2
            else:
                held, spot = outer_second, row if row < 2 else row - rows + 4
            value = solved(*(held[spot, at * planes : at * planes + stop] for at in range(3)))
            place = PITCH * (row + 2)
            first = rolled(outer[:, :LANES], -(place + 2))
            last = rolled(outer[:, LANES:], LANES - 2 - (place + PITCH - 4))
            basis[start:stop, row, :LANES] = jnp.where(lane < 2, first, value[:, :LANES])
            basis[start:stop, row, LANES : width - LANES] = value[:, LANES : width - LANES]
            basis[start:stop, row, width - LANES :] = jnp.where(
                lane >= LANES - 2, last, value[:, width - LANES :]
            )
        some = pl.ds(start, stop - start)
        copies.append(pltpu.make_async_copy(basis.at[some], basis_out.at[some], written.at[len(copies)]))
        copies[-1].start()

    block = tree_sum([parts[at] for at in range(parts.shape[0])]) / pixel_count
    block = [block[:, at * LANES : (at + 1) * LANES] for at in range(9)]
    mixed, diagonal = jnp.concatenate(block[:8], axis=0), block[8][:, :planes]
    mixed = jnp.concatenate([mixed[:, at * planes : (at + 1) * planes] for at in range(LANES // planes)], axis=0)
    flipped = mixed.T
    first = jnp.where(at_row >= at_col, mixed, flipped)
    second = jnp.where(at_row < at_col, mixed, jnp.where(at_row > at_col, flipped, diagonal))
    low_half = (at_col <= at_row)[:half, :half]
    state = eliminate(
        [first, second],
        planes,
        lambda state: solve(jnp.where(low_half, state[:, 3 * planes : 3 * planes + half], 0.0), 0),
    )
    first_inverse = state[:, planes : 2 * planes]
    product_upper = jnp.where(at_col >= at_row, state[:, 2 * planes : 3 * planes], 0.0)
    solve(jnp.where(at_col <= at_row, state[:, 3 * planes :], 0.0)[half:], half)
    factor[...] = jnp.where(at_col >= at_row, gram_of(product_upper, first_inverse), 0.0)
    copies.append(pltpu.make_async_copy(factor, factor_out, written.at[2]))
    copies[-1].start()
    for copy in copies:
        copy.wait()


def tree_sum(parts):
    while len(parts) > 1:
        parts = [sum(parts[at + 1 : at + 2], parts[at]) for at in range(0, len(parts), 2)]
    return parts[0]


def swap(value, row_pairing=None, col_pairing=None):
    names = ("sec", "row", "col")
    shape = [lax.axis_size(name) for name in names]

    def partner(at, place, pairing):
        other = place if pairing is None else place + 1 if place % 2 != pairing else place - 1
        return other if 0 <= other < shape[at] else None

    pairs = []
    for sec, row, col in itertools.product(*(range(extent) for extent in shape)):
        other_row, other_col = partner(1, row, row_pairing), partner(2, col, col_pairing)
        if other_col is None:
            target = (sec, row ^ 1, col)
        elif other_row is None:
            target = (sec ^ 1, row, col)
        else:
            target = (sec, other_row, other_col)
        pairs.append(tuple((a * shape[1] + b) * shape[2] + c for a, b, c in ((sec, row, col), target)))
    return lax.ppermute(value, names, pairs)


def on_device(sketch, weights):
    planes, rows, width = sketch.shape
    group = lax.axis_size("row") * lax.axis_size("col")
    side = f32(planes + 8, LANES)
    by_row, weights_by_row, left, right, *messages = call(
        pack_rows_kernel,
        [f32(rows, planes, width), f32(rows, 8, width), side, side]
        + [f32(2 * planes + 16, width), f32(2 * planes + 8, width)]
        + [f32(16, LANES)] * 2,
        pltpu.with_memory_space_constraint(sketch, pltpu.HBM),
        pltpu.with_memory_space_constraint(weights, pltpu.HBM),
        memory=pltpu.HBM,
        scratch=[
            pltpu.VMEM(sketch.shape, jnp.float32),
            pltpu.VMEM(weights.shape, jnp.float32),
            pltpu.SemaphoreType.DMA((2,)),
        ],
    )
    from_rows = [swap(messages[at], row_pairing=at) for at in range(2)]
    from_diagonals = [swap(messages[2 + at], row_pairing=0, col_pairing=at) for at in range(2)]
    left, right, *messages = call(
        functools.partial(strips_kernel, rows), [side, side] + [f32(16, LANES)] * 2, left, right, from_rows[1]
    )
    from_cols = [swap(messages[at], col_pairing=at) for at in range(2)]
    parts_of = functools.partial(jax.ShapeDtypeStruct, dtype=jnp.bfloat16)
    products = f32(3 * planes, 3 * planes)
    middle, inner_second, *inner_products = call(
        inner_rows_kernel,
        [f32(rows - 2, planes, width), parts_of((rows - 4, 3 * planes, width)), products, products],
        by_row,
        weights_by_row,
    )
    outer_second, early_grams, *halos = call(
        outer_rows_kernel,
        [parts_of((4, 3 * planes, width)), f32(planes, 2 * planes), side, side],
        by_row,
        weights_by_row,
        *from_rows,
        middle,
        *inner_products,
        scratch=[pltpu.VMEM((4, planes, width), jnp.float32)],
    )
    grams, edges = call(
        functools.partial(late_kernel, rows),
        [f32(group, 1, 9 * LANES), f32(planes, 2 * LANES)],
        left,
        right,
        *halos,
        *from_diagonals,
        *from_cols,
        early_grams,
    )
    rows_of, cols_of = lax.axis_size("row"), lax.axis_size("col")
    first = cols_of + (cols_of - 1) // 2
    order = [first] + [row * cols_of + col for col in range(cols_of) for row in range(rows_of)]
    order = list(dict.fromkeys(order))
    parts = lax.all_to_all(grams, ("row", "col"), 0, 0, axis_index_groups=[order], tiled=True)
    return call(
        functools.partial(finish_kernel, float(rows * width * group)),
        [f32(planes, rows, width), f32(planes, planes)],
        inner_second,
        outer_second,
        edges,
        parts,
        out_memory=pl.ANY,
        scratch=[
            pltpu.VMEM(sketch.shape, jnp.float32),
            pltpu.VMEM((planes, planes), jnp.float32),
            pltpu.SemaphoreType.DMA((3,)),
        ],
    )


def solution(mesh):
    return jax.shard_map(
        on_device,
        mesh=mesh,
        in_specs=(P(None, ("sec", "row"), "col"), P(None, ("sec", "row"), "col")),
        out_specs=(P(None, ("sec", "row"), "col"), P("sec", None)),
        check_vma=False,
    )
```

```python
import functools
import itertools

import jax
import jax.numpy as jnp
from jax import lax
from jax.experimental import pallas as pl
from jax.experimental.pallas import tpu as pltpu
from jax.sharding import PartitionSpec as P

NEIGHBOURS = ((-1, -1), (-1, 0), (-1, 1), (0, -1), (0, 1), (1, -1), (1, 0), (1, 1))
LANES = 128
PITCH = 8
HIGHEST = lax.Precision.HIGHEST


def call(kernel, out_shapes, *operands, memory=pltpu.VMEM, out_memory=pltpu.VMEM, scratch=(), cost=None):
    return pl.pallas_call(
        kernel,
        out_shape=out_shapes,
        in_specs=[pl.BlockSpec(memory_space=memory)] * len(operands),
        out_specs=[pl.BlockSpec(memory_space=out_memory)] * len(out_shapes),
        scratch_shapes=scratch,
        cost_estimate=cost,
        compiler_params=pltpu.CompilerParams(vmem_limit_bytes=40 * 1024 * 1024),
    )(*operands)


def f32(*shape):
    return jax.ShapeDtypeStruct(shape, jnp.float32)


def sides_of(axis):
    place = lax.axis_index(axis)
    return place % 2 == 1, place > 0, place < lax.axis_size(axis) - 1


def edge_columns(first, last, place):
    lane = lax.broadcasted_iota(jnp.int32, (1, LANES), 1)
    own = PITCH - 2
    left = jnp.where((lane >= place + 2) & (lane < place + PITCH), pltpu.roll(first, place + 2, 1), 0.0)
    right = jnp.where((lane >= place) & (lane < place + own), pltpu.roll(last, place + own, 1), 0.0)
    return left, right


def pack_rows_kernel(sketch, weights, by_row, weights_by_row, left, right, *rest):
    bulk_messages, diagonal_messages = rest[:2], rest[2:4]
    tile, weight_tile, arrived = rest[4:]
    copies = [
        pltpu.make_async_copy(sketch, tile, arrived.at[0]),
        pltpu.make_async_copy(weights, weight_tile, arrived.at[1]),
    ]
    for copy in copies:
        copy.start()
    for copy in copies:
        copy.wait()
    rows, planes, width = by_row.shape
    odd_row, _, _ = sides_of("row")
    odd_col, _, _ = sides_of("col")
    lane = lax.broadcasted_iota(jnp.int32, (1, LANES), 1)
    for row in range(rows):
        weights_by_row[row] = weight_tile[:, row, :]
        by_row[row] = tile[:, row, :]
    for message, up in zip(bulk_messages, (odd_row, jnp.logical_not(odd_row))):
        start = jnp.where(up, rows - 2, 0)
        for slot in range(2):
            message[slot * planes : (slot + 1) * planes] = by_row[start + slot]
        message[2 * planes : 2 * planes + 8] = weights_by_row[jnp.where(up, rows - 1, 0)]
    strips = [None, None]
    for row in range(rows):
        first = jnp.concatenate([by_row[row, :, :LANES], weights_by_row[row, :, :LANES]], axis=0)
        last = jnp.concatenate([by_row[row, :, width - LANES :], weights_by_row[row, :, width - LANES :]], axis=0)
        parts = edge_columns(first, last, PITCH * (row + 2))
        strips = [part if strip is None else strip + part for strip, part in zip(strips, parts)]
    left[...], right[...] = strips
    bulk_messages[0][2 * planes + 8 :] = jnp.zeros((8, width), jnp.float32)
    pair = 2 * PITCH
    to_left, to_right = folded(strips[0], 2), folded(strips[1], PITCH - 4)
    for message, up in zip(diagonal_messages, (odd_col, jnp.logical_not(odd_col))):
        edge = jnp.where(up, to_right, to_left)
        below = jnp.where(lane < pair, rolled(edge, -PITCH * rows), 0.0)
        start = PITCH * (rows + 2)
        above = jnp.where((lane >= start) & (lane < start + pair), rolled(edge, PITCH * rows), 0.0)
        message[...] = jnp.where(odd_row, below, above)


def strips_kernel(rows, own_left, own_right, bulk_message, left, right, *col_messages):
    planes = own_left.shape[0] - 8
    odd_row, has_below, has_above = sides_of("row")
    odd_col, _, _ = sides_of("col")
    width = bulk_message.shape[1]
    totals = [own_left[...], own_right[...]]
    present = jnp.where(odd_row, has_below, has_above)
    for slot in range(2):
        place = PITCH * (slot + jnp.where(odd_row, 0, rows + 2))
        halo = [bulk_message[slot * planes : (slot + 1) * planes], bulk_message[2 * planes :]]
        first = jnp.concatenate([part[:, :LANES] for part in halo], axis=0)
        last = jnp.concatenate([part[:, width - LANES :] for part in halo], axis=0)
        parts = edge_columns(first, last, place)
        totals = [total + jnp.where(present, part, 0.0) for total, part in zip(totals, parts)]
    left[...], right[...] = totals
    to_left, to_right = folded(left[...], 2), folded(right[...], PITCH - 4)
    for message, up in zip(col_messages, (odd_col, jnp.logical_not(odd_col))):
        message[...] = jnp.where(up, to_right, to_left)


def folded(strip, spot):
    lane = lax.broadcasted_iota(jnp.int32, (1, LANES), 1)
    groups = strip.shape[0] // 8
    pieces = []
    for group in range(groups):
        target = 2 * group if group < groups - 1 else 0
        moved = rolled(strip[8 * group : 8 * (group + 1)], target - spot)
        pieces.append(jnp.where((lane % PITCH) // 2 == target // 2, moved, 0.0))
    return jnp.concatenate([functools.reduce(jnp.add, pieces[:-1]), pieces[-1]], axis=0)


def unfolded(message, spot, planes):
    lane = lax.broadcasted_iota(jnp.int32, (1, LANES), 1)
    pieces = [rolled(message[:8], spot - 2 * group) for group in range(planes // 8)] + [rolled(message[8:], spot)]
    return jnp.where((lane % PITCH) // 2 == spot // 2, jnp.concatenate(pieces, axis=0), 0.0)


def rolled(value, shift):
    return pltpu.roll(value, shift % LANES, 1) if shift % LANES else value


def apply_operator(rows3, weight_rows):
    width = rows3[1].shape[1]
    total = jnp.sum(weight_rows, axis=0, keepdims=True) * rows3[1]
    for across in (0, -1, 1):
        moved = pltpu.roll(weight_rows, across % width, 1) if across else weight_rows
        terms = [
            moved[position : position + 1] * rows3[up + 1]
            for position, (up, side) in enumerate(NEIGHBOURS)
            if side == across
        ]
        part = functools.reduce(jnp.add, terms)
        total = total + (pltpu.roll(part, -across % width, 1) if across else part)
    return total


def gram_of(value, other):
    return lax.dot_general(
        value, other, (((1,), (1,)), ((), ())), precision=HIGHEST, preferred_element_type=jnp.float32
    )


def split(value):
    high = value.astype(jnp.bfloat16)
    rest = value - high.astype(jnp.float32)
    middle = rest.astype(jnp.bfloat16)
    low = (rest - middle.astype(jnp.float32)).astype(jnp.bfloat16)
    return high, middle, low


def inner_parts(image):
    width = image.shape[1]
    lane = lax.broadcasted_iota(jnp.int32, (1, LANES), 1)
    kept = [
        jnp.where(lane >= 2, image[:, :LANES], 0.0),
        image[:, LANES : width - LANES],
        jnp.where(lane < LANES - 2, image[:, width - LANES :], 0.0),
    ]
    return jnp.concatenate(split(jnp.concatenate(kept, axis=1)), axis=0)


def products_of(parts, others=None):
    others = parts if others is None else others
    return lax.dot_general(parts, others, (((1,), (1,)), ((), ())), preferred_element_type=jnp.float32)


def images_of(middle, weights, wanted, second, products):
    for at, row in enumerate(wanted):
        parts = inner_parts(apply_operator([middle(row - 1), middle(row), middle(row + 1)], weights(row)))
        second[at] = parts
        products = products + products_of(parts)
    return products


def inner_rows_kernel(by_row, weights_by_row, middle, second, first_products, second_products):
    rows = by_row.shape[0]
    products = jnp.zeros(first_products.shape, jnp.float32)
    for row in range(1, rows - 1):
        image = apply_operator([by_row[row - 1], by_row[row], by_row[row + 1]], weights_by_row[row])
        middle[row - 1] = image
        products = products + products_of(inner_parts(image))
    first_products[...] = products
    second_products[...] = images_of(
        lambda row: middle[row - 1],
        lambda row: weights_by_row[row],
        range(2, rows - 2),
        second,
        jnp.zeros(second_products.shape, jnp.float32),
    )


def outer_rows_kernel(
    by_row,
    weights_by_row,
    first_message,
    second_message,
    middle,
    first_products,
    second_products,
    second,
    grams,
    left_halo,
    right_halo,
    outer,
):
    rows, planes, width = by_row.shape
    odd_row, has_below, has_above = sides_of("row")
    one, other = first_message[: 2 * planes + 8], second_message[...]
    below = jnp.where(has_below, jnp.where(odd_row, other, one), 0.0)
    above = jnp.where(has_above, jnp.where(odd_row, one, other), 0.0)
    halos = [None, None]
    for side, (halo, present) in enumerate(
        ((below, jnp.logical_not(odd_row)), (above, odd_row))
    ):
        for slot in range(2):
            index = slot if side == 0 else rows + 2 + slot
            blank = jnp.zeros((8, width), jnp.float32)
            weight = halo[2 * planes :] if slot != side else blank
            row_values = jnp.concatenate([halo[slot * planes : (slot + 1) * planes], weight], axis=0)
            parts = edge_columns(row_values[:, :LANES], row_values[:, width - LANES :], PITCH * index)
            parts = [jnp.where(present, part, 0.0) for part in parts]
            halos = [part if total is None else total + part for total, part in zip(halos, parts)]
    left_halo[...], right_halo[...] = halos

    def field(row):
        if 0 <= row < rows:
            return by_row[row]
        at = (row + 2 if row < 0 else row - rows) * planes
        return (below if row < 0 else above)[at : at + planes]

    def weights(row):
        if 0 <= row < rows:
            return weights_by_row[row]
        return (below if row < 0 else above)[2 * planes :]

    products = first_products[...]
    places = (-1, 0, rows - 1, rows)
    for at, row in enumerate(places):
        image = apply_operator([field(row - 1), field(row), field(row + 1)], weights(row))
        outer[at] = image
        if 0 <= row < rows:
            products = products + products_of(inner_parts(image))
    both = [products]
    both.append(
        images_of(
            lambda row: outer[places.index(row)] if row in places else middle[row - 1],
            weights,
            (0, 1, rows - 2, rows - 1),
            second,
            second_products[...],
        )
    )
    for at, products in enumerate(both):
        some = products[:planes] + products[planes : 2 * planes] + products[2 * planes :]
        total = some[:, :planes] + some[:, planes : 2 * planes] + some[:, 2 * planes :]
        grams[:, at * planes : (at + 1) * planes] = total


def apply_on_strip(values, weights):
    total = jnp.sum(weights, axis=0, keepdims=True) * values
    for position, (up, across) in enumerate(NEIGHBOURS):
        moved = pltpu.roll(values, (-PITCH * up - across) % LANES, 1)
        total = total + weights[position : position + 1] * moved
    return total


def late_kernel(rows, left, right, left_halo, right_halo, *rest):
    diagonal_messages, col_messages, (early_grams, grams, edges) = rest[:2], rest[2:4], rest[4:]
    planes = early_grams.shape[0]
    odd_row, has_below, has_above = sides_of("row")
    odd_col, has_left, has_right = sides_of("col")
    beyond = jnp.where(odd_row, has_above, has_below)
    one, other = (
        col[...] + jnp.where(beyond, diagonal[...], 0.0)
        for col, diagonal in zip(col_messages, diagonal_messages)
    )
    lane = lax.broadcasted_iota(jnp.int32, (1, LANES), 1)
    spot, row = lane % PITCH, lane // PITCH
    strips, masks = [], []
    for side, (strip, present, halo) in enumerate(
        (
            (left[...] + left_halo[...], has_left, jnp.where(odd_col, other, one)),
            (right[...] + right_halo[...], has_right, jnp.where(odd_col, one, other)),
        )
    ):
        strips.append(strip + jnp.where(present, unfolded(halo, side * (PITCH - 2), planes), 0.0))
        low = 2 if side == 0 else PITCH - 4
        masks.append((spot >= low) & (spot < low + 2) & (row >= 2) & (row < rows + 2))
    values = [strip[:planes] for strip in strips]
    gram = []
    for at in range(2):
        values = [apply_on_strip(value, strip[planes:]) for value, strip in zip(values, strips)]
        kept = jnp.concatenate([jnp.where(mask, value, 0.0) for mask, value in zip(masks, values)], axis=1)
        both = jnp.concatenate(values, axis=1)
        high, middle, low = split(kept)
        one_side = jnp.concatenate([high, high, middle, high, low, middle], axis=1)
        other_side = jnp.concatenate([high, middle, high, low, high, middle], axis=1)
        gram.append(early_grams[:, at * planes : (at + 1) * planes] + products_of(one_side, other_side))
    edges[...] = both
    at_row = lax.broadcasted_iota(jnp.int32, (planes, planes), 0)
    at_col = lax.broadcasted_iota(jnp.int32, (planes, planes), 1)
    mixed = jnp.where(at_row >= at_col, gram[0], gram[1])
    diagonal = jnp.sum(jnp.where(at_row == at_col, gram[1], 0.0), axis=0, keepdims=True)
    block = jnp.concatenate([mixed[8 * g : 8 * (g + 1)] for g in range(planes // 8)], axis=1)
    last = jnp.concatenate([diagonal] * (LANES // planes), axis=1)
    for at in range(8):
        grams[:, at * LANES : (at + 1) * LANES] = block[at : at + 1]
    grams[:, 8 * LANES :] = last


def eliminate(grams, planes, half_way):
    lane = lax.broadcasted_iota(jnp.int32, (8, LANES), 1)
    sub = lax.broadcasted_iota(jnp.int32, (8, LANES), 0)
    first_half = lane < 2 * planes
    groups = planes // 8
    sources = [[gram[8 * g : 8 * (g + 1)] for g in range(groups)] for gram in grams]
    state = []
    for g in range(groups):
        unit = jnp.where(sub + 8 * g == lane % (2 * planes) - planes, 1.0, 0.0)
        unit = unit[:, planes : 2 * planes]
        state.append(jnp.concatenate([sources[0][g], unit, sources[1][g], unit], axis=1))
    columns = []
    for j in range(planes):
        columns.append(
            {
                g: jnp.where(
                    first_half,
                    jnp.broadcast_to(sources[0][g][:, j : j + 1], (8, LANES)),
                    jnp.broadcast_to(sources[1][g][:, j : j + 1], (8, LANES)),
                )
                for g in range(j // 8, groups)
            }
        )
    scale = [jnp.ones((8, LANES), jnp.float32)] * groups
    for step in range(planes):
        own, at = step // 8, step % 8
        column = columns[step]
        root = lax.rsqrt(jnp.broadcast_to(column[own][at : at + 1], (8, LANES)))
        inverse = root * root
        scale[own] = jnp.where(sub == at, root, scale[own])
        left = {g: jnp.where(sub > at, value, 0.0) if g == own else value for g, value in column.items()}
        factors = {g: value * inverse for g, value in left.items()}
        for j in range(step + 1, planes):
            entry = jnp.broadcast_to(column[j // 8][j % 8 : j % 8 + 1], (8, LANES))
            for g in columns[j]:
                change = (left[g] * entry) * inverse if j == step + 1 else factors[g] * entry
                columns[j][g] = columns[j][g] - change
        pivot_row = jnp.broadcast_to(state[own][at : at + 1], (8, LANES))
        for g in range(own, groups):
            state[g] = state[g] - factors[g] * pivot_row
        if step + 1 == planes // 2:
            half_way(jnp.concatenate([state[g] * scale[g] for g in range(groups // 2)], axis=0))
    return jnp.concatenate([state[g] * scale[g] for g in range(groups)], axis=0)


def finish_kernel(
    pixel_count, inner_second, outer_second, edges, parts, basis_out, factor_out, basis, factor, written
):
    planes, rows, width = basis.shape
    half = planes // 2
    at_row = lax.broadcasted_iota(jnp.int32, (planes, planes), 0)
    at_col = lax.broadcasted_iota(jnp.int32, (planes, planes), 1)
    lane = lax.broadcasted_iota(jnp.int32, (1, LANES), 1)
    outer_parts = split(edges[...])
    copies = []

    def solve(inverse, start):
        stop = start + inverse.shape[0]
        high, middle, low = split(inverse)
        left_side = jnp.concatenate([high, high, middle, high, low, middle], axis=1)

        def solved(high, middle, low):
            right_side = jnp.concatenate([high, middle, high, low, high, middle], axis=0)
            return jnp.dot(left_side, right_side, preferred_element_type=jnp.float32)

        outer = solved(*(part[:stop] for part in outer_parts))
        for row in range(rows):
            if 2 <= row < rows - 2:
                held, spot = inner_second, row - 2
            else:
                held, spot = outer_second, row if row < 2 else row - rows + 4
            value = solved(*(held[spot, at * planes : at * planes + stop] for at in range(3)))
            place = PITCH * (row + 2)
            first = rolled(outer[:, :LANES], -(place + 2))
            last = rolled(outer[:, LANES:], LANES - 2 - (place + PITCH - 4))
            basis[start:stop, row, :LANES] = jnp.where(lane < 2, first, value[:, :LANES])
            basis[start:stop, row, LANES : width - LANES] = value[:, LANES : width - LANES]
            basis[start:stop, row, width - LANES :] = jnp.where(
                lane >= LANES - 2, last, value[:, width - LANES :]
            )
        some = pl.ds(start, stop - start)
        copies.append(pltpu.make_async_copy(basis.at[some], basis_out.at[some], written.at[len(copies)]))
        copies[-1].start()

    block = tree_sum([parts[at] for at in range(parts.shape[0])]) / pixel_count
    block = [block[:, at * LANES : (at + 1) * LANES] for at in range(9)]
    mixed, diagonal = jnp.concatenate(block[:8], axis=0), block[8][:, :planes]
    mixed = jnp.concatenate([mixed[:, at * planes : (at + 1) * planes] for at in range(LANES // planes)], axis=0)
    flipped = mixed.T
    first = jnp.where(at_row >= at_col, mixed, flipped)
    second = jnp.where(at_row < at_col, mixed, jnp.where(at_row > at_col, flipped, diagonal))
    low_half = (at_col <= at_row)[:half, :half]
    state = eliminate(
        [first, second],
        planes,
        lambda state: solve(jnp.where(low_half, state[:, 3 * planes : 3 * planes + half], 0.0), 0),
    )
    first_inverse = state[:, planes : 2 * planes]
    product_upper = jnp.where(at_col >= at_row, state[:, 2 * planes : 3 * planes], 0.0)
    solve(jnp.where(at_col <= at_row, state[:, 3 * planes :], 0.0)[half:], half)
    factor[...] = jnp.where(at_col >= at_row, gram_of(product_upper, first_inverse), 0.0)
    copies.append(pltpu.make_async_copy(factor, factor_out, written.at[2]))
    copies[-1].start()
    for copy in copies:
        copy.wait()


def tree_sum(parts):
    while len(parts) > 1:
        parts = [sum(parts[at + 1 : at + 2], parts[at]) for at in range(0, len(parts), 2)]
    return parts[0]


def swap(value, row_pairing=None, col_pairing=None):
    names = ("sec", "row", "col")
    shape = [lax.axis_size(name) for name in names]

    def partner(at, place, pairing):
        other = place if pairing is None else place + 1 if place % 2 != pairing else place - 1
        return other if 0 <= other < shape[at] else None

    pairs = []
    for sec, row, col in itertools.product(*(range(extent) for extent in shape)):
        other_row, other_col = partner(1, row, row_pairing), partner(2, col, col_pairing)
        if other_col is None:
            target = (sec, row ^ 1, col)
        elif other_row is None:
            target = (sec ^ 1, row, col)
        else:
            target = (sec, other_row, other_col)
        pairs.append(tuple((a * shape[1] + b) * shape[2] + c for a, b, c in ((sec, row, col), target)))
    return lax.ppermute(value, names, pairs)


def on_device(sketch, weights):
    planes, rows, width = sketch.shape
    group = lax.axis_size("row") * lax.axis_size("col")
    side = f32(planes + 8, LANES)
    by_row, weights_by_row, left, right, *messages = call(
        pack_rows_kernel,
        [f32(rows, planes, width), f32(rows, 8, width), side, side]
        + [f32(2 * planes + 16, width), f32(2 * planes + 8, width)]
        + [f32(16, LANES)] * 2,
        pltpu.with_memory_space_constraint(sketch, pltpu.HBM),
        pltpu.with_memory_space_constraint(weights, pltpu.HBM),
        memory=pltpu.HBM,
        scratch=[
            pltpu.VMEM(sketch.shape, jnp.float32),
            pltpu.VMEM(weights.shape, jnp.float32),
            pltpu.SemaphoreType.DMA((2,)),
        ],
    )
    from_rows = [swap(messages[at], row_pairing=at) for at in range(2)]
    from_diagonals = [swap(messages[2 + at], row_pairing=0, col_pairing=at) for at in range(2)]
    left, right, *messages = call(
        functools.partial(strips_kernel, rows), [side, side] + [f32(16, LANES)] * 2, left, right, from_rows[1]
    )
    from_cols = [swap(messages[at], col_pairing=at) for at in range(2)]
    parts_of = functools.partial(jax.ShapeDtypeStruct, dtype=jnp.bfloat16)
    products = f32(3 * planes, 3 * planes)
    middle, inner_second, *inner_products = call(
        inner_rows_kernel,
        [f32(rows - 2, planes, width), parts_of((rows - 4, 3 * planes, width)), products, products],
        by_row,
        weights_by_row,
    )
    outer_second, early_grams, *halos = call(
        outer_rows_kernel,
        [parts_of((4, 3 * planes, width)), f32(planes, 2 * planes), side, side],
        by_row,
        weights_by_row,
        *from_rows,
        middle,
        *inner_products,
        scratch=[pltpu.VMEM((4, planes, width), jnp.float32)],
    )
    grams, edges = call(
        functools.partial(late_kernel, rows),
        [f32(1, 9 * LANES), f32(planes, 2 * LANES)],
        left,
        right,
        *halos,
        *from_diagonals,
        *from_cols,
        early_grams,
    )
    rows_of, cols_of = lax.axis_size("row"), lax.axis_size("col")
    first = cols_of + cols_of // 2
    order = [first] + [row * cols_of + col for col in range(cols_of) for row in range(rows_of)]
    order = list(dict.fromkeys(order))
    grams = jnp.broadcast_to(grams, (group, *grams.shape))
    parts = lax.all_to_all(grams, ("row", "col"), 0, 0, axis_index_groups=[order], tiled=True)
    return call(
        functools.partial(finish_kernel, float(rows * width * group)),
        [f32(planes, rows, width), f32(planes, planes)],
        inner_second,
        outer_second,
        edges,
        parts,
        out_memory=pl.ANY,
        scratch=[
            pltpu.VMEM(sketch.shape, jnp.float32),
            pltpu.VMEM((planes, planes), jnp.float32),
            pltpu.SemaphoreType.DMA((3,)),
        ],
    )


def solution(mesh):
    return jax.shard_map(
        on_device,
        mesh=mesh,
        in_specs=(P(None, ("sec", "row"), "col"), P(None, ("sec", "row"), "col")),
        out_specs=(P(None, ("sec", "row"), "col"), P("sec", None)),
        check_vma=False,
    )
```

```python
import functools
import itertools

import jax
import jax.numpy as jnp
from jax import lax
from jax.experimental import pallas as pl
from jax.experimental.pallas import tpu as pltpu
from jax.sharding import PartitionSpec as P

NEIGHBOURS = ((-1, -1), (-1, 0), (-1, 1), (0, -1), (0, 1), (1, -1), (1, 0), (1, 1))
LANES = 128
PITCH = 8
HIGHEST = lax.Precision.HIGHEST


def call(kernel, out_shapes, *operands, memory=pltpu.VMEM, out_memory=pltpu.VMEM, scratch=(), cost=None):
    return pl.pallas_call(
        kernel,
        out_shape=out_shapes,
        in_specs=[pl.BlockSpec(memory_space=memory)] * len(operands),
        out_specs=[pl.BlockSpec(memory_space=out_memory)] * len(out_shapes),
        scratch_shapes=scratch,
        cost_estimate=cost,
        compiler_params=pltpu.CompilerParams(vmem_limit_bytes=40 * 1024 * 1024),
    )(*operands)


def f32(*shape):
    return jax.ShapeDtypeStruct(shape, jnp.float32)


def sides_of(axis):
    place = lax.axis_index(axis)
    return place % 2 == 1, place > 0, place < lax.axis_size(axis) - 1


def edge_columns(first, last, place):
    lane = lax.broadcasted_iota(jnp.int32, (1, LANES), 1)
    own = PITCH - 2
    left = jnp.where((lane >= place + 2) & (lane < place + PITCH), pltpu.roll(first, place + 2, 1), 0.0)
    right = jnp.where((lane >= place) & (lane < place + own), pltpu.roll(last, place + own, 1), 0.0)
    return left, right


def pack_rows_kernel(sketch, weights, by_row, weights_by_row, left, right, *rest):
    bulk_messages, diagonal_messages = rest[:2], rest[2:4]
    tile, weight_tile, arrived = rest[4:]
    copies = [
        pltpu.make_async_copy(sketch, tile, arrived.at[0]),
        pltpu.make_async_copy(weights, weight_tile, arrived.at[1]),
    ]
    for copy in copies:
        copy.start()
    for copy in copies:
        copy.wait()
    rows, planes, width = by_row.shape
    odd_row, _, _ = sides_of("row")
    odd_col, _, _ = sides_of("col")
    lane = lax.broadcasted_iota(jnp.int32, (1, LANES), 1)
    for row in range(rows):
        weights_by_row[row] = weight_tile[:, row, :]
        by_row[row] = tile[:, row, :]
    for message, up in zip(bulk_messages, (odd_row, jnp.logical_not(odd_row))):
        start = jnp.where(up, rows - 2, 0)
        for slot in range(2):
            message[slot * planes : (slot + 1) * planes] = by_row[start + slot]
        message[2 * planes : 2 * planes + 8] = weights_by_row[jnp.where(up, rows - 1, 0)]
    strips = [None, None]
    for row in range(rows):
        first = jnp.concatenate([by_row[row, :, :LANES], weights_by_row[row, :, :LANES]], axis=0)
        last = jnp.concatenate([by_row[row, :, width - LANES :], weights_by_row[row, :, width - LANES :]], axis=0)
        parts = edge_columns(first, last, PITCH * (row + 2))
        strips = [part if strip is None else strip + part for strip, part in zip(strips, parts)]
    left[...], right[...] = strips
    bulk_messages[0][2 * planes + 8 :] = jnp.zeros((8, width), jnp.float32)
    pair = 2 * PITCH
    to_left, to_right = folded(strips[0], 2), folded(strips[1], PITCH - 4)
    for message, up in zip(diagonal_messages, (odd_col, jnp.logical_not(odd_col))):
        edge = jnp.where(up, to_right, to_left)
        below = jnp.where(lane < pair, rolled(edge, -PITCH * rows), 0.0)
        start = PITCH * (rows + 2)
        above = jnp.where((lane >= start) & (lane < start + pair), rolled(edge, PITCH * rows), 0.0)
        message[...] = jnp.where(odd_row, below, above)


def strips_kernel(rows, own_left, own_right, bulk_message, left, right, *col_messages):
    planes = own_left.shape[0] - 8
    odd_row, has_below, has_above = sides_of("row")
    odd_col, _, _ = sides_of("col")
    width = bulk_message.shape[1]
    totals = [own_left[...], own_right[...]]
    present = jnp.where(odd_row, has_below, has_above)
    for slot in range(2):
        place = PITCH * (slot + jnp.where(odd_row, 0, rows + 2))
        halo = [bulk_message[slot * planes : (slot + 1) * planes], bulk_message[2 * planes :]]
        first = jnp.concatenate([part[:, :LANES] for part in halo], axis=0)
        last = jnp.concatenate([part[:, width - LANES :] for part in halo], axis=0)
        parts = edge_columns(first, last, place)
        totals = [total + jnp.where(present, part, 0.0) for total, part in zip(totals, parts)]
    left[...], right[...] = totals
    to_left, to_right = folded(left[...], 2), folded(right[...], PITCH - 4)
    for message, up in zip(col_messages, (odd_col, jnp.logical_not(odd_col))):
        message[...] = jnp.where(up, to_right, to_left)


def folded(strip, spot):
    lane = lax.broadcasted_iota(jnp.int32, (1, LANES), 1)
    groups = strip.shape[0] // 8
    pieces = []
    for group in range(groups):
        target = 2 * group if group < groups - 1 else 0
        moved = rolled(strip[8 * group : 8 * (group + 1)], target - spot)
        pieces.append(jnp.where((lane % PITCH) // 2 == target // 2, moved, 0.0))
    return jnp.concatenate([functools.reduce(jnp.add, pieces[:-1]), pieces[-1]], axis=0)


def unfolded(message, spot, planes):
    lane = lax.broadcasted_iota(jnp.int32, (1, LANES), 1)
    pieces = [rolled(message[:8], spot - 2 * group) for group in range(planes // 8)] + [rolled(message[8:], spot)]
    return jnp.where((lane % PITCH) // 2 == spot // 2, jnp.concatenate(pieces, axis=0), 0.0)


def rolled(value, shift):
    return pltpu.roll(value, shift % LANES, 1) if shift % LANES else value


def apply_operator(rows3, weight_rows):
    width = rows3[1].shape[1]
    total = jnp.sum(weight_rows, axis=0, keepdims=True) * rows3[1]
    for across in (0, -1, 1):
        moved = pltpu.roll(weight_rows, across % width, 1) if across else weight_rows
        terms = [
            moved[position : position + 1] * rows3[up + 1]
            for position, (up, side) in enumerate(NEIGHBOURS)
            if side == across
        ]
        part = functools.reduce(jnp.add, terms)
        total = total + (pltpu.roll(part, -across % width, 1) if across else part)
    return total


def gram_of(value, other):
    return lax.dot_general(
        value, other, (((1,), (1,)), ((), ())), precision=HIGHEST, preferred_element_type=jnp.float32
    )


def split(value):
    high = value.astype(jnp.bfloat16)
    rest = value - high.astype(jnp.float32)
    middle = rest.astype(jnp.bfloat16)
    low = (rest - middle.astype(jnp.float32)).astype(jnp.bfloat16)
    return high, middle, low


def inner_parts(image):
    width = image.shape[1]
    lane = lax.broadcasted_iota(jnp.int32, (1, LANES), 1)
    kept = [
        jnp.where(lane >= 2, image[:, :LANES], 0.0),
        image[:, LANES : width - LANES],
        jnp.where(lane < LANES - 2, image[:, width - LANES :], 0.0),
    ]
    return jnp.concatenate(split(jnp.concatenate(kept, axis=1)), axis=0)


def products_of(parts):
    return lax.dot_general(parts, parts, (((1,), (1,)), ((), ())), preferred_element_type=jnp.float32)


def images_of(middle, weights, wanted, second, products):
    for at, row in enumerate(wanted):
        parts = inner_parts(apply_operator([middle(row - 1), middle(row), middle(row + 1)], weights(row)))
        second[at] = parts
        products = products + products_of(parts)
    return products


def inner_rows_kernel(by_row, weights_by_row, middle, second, first_products, second_products):
    rows = by_row.shape[0]
    products = jnp.zeros(first_products.shape, jnp.float32)
    for row in range(1, rows - 1):
        image = apply_operator([by_row[row - 1], by_row[row], by_row[row + 1]], weights_by_row[row])
        middle[row - 1] = image
        products = products + products_of(inner_parts(image))
    first_products[...] = products
    second_products[...] = images_of(
        lambda row: middle[row - 1],
        lambda row: weights_by_row[row],
        range(2, rows - 2),
        second,
        jnp.zeros(second_products.shape, jnp.float32),
    )


def outer_rows_kernel(
    by_row,
    weights_by_row,
    first_message,
    second_message,
    middle,
    first_products,
    second_products,
    second,
    grams,
    left_halo,
    right_halo,
    outer,
):
    rows, planes, width = by_row.shape
    odd_row, has_below, has_above = sides_of("row")
    one, other = first_message[: 2 * planes + 8], second_message[...]
    below = jnp.where(has_below, jnp.where(odd_row, other, one), 0.0)
    above = jnp.where(has_above, jnp.where(odd_row, one, other), 0.0)
    halos = [None, None]
    for side, (halo, present) in enumerate(
        ((below, jnp.logical_not(odd_row)), (above, odd_row))
    ):
        for slot in range(2):
            index = slot if side == 0 else rows + 2 + slot
            blank = jnp.zeros((8, width), jnp.float32)
            weight = halo[2 * planes :] if slot != side else blank
            row_values = jnp.concatenate([halo[slot * planes : (slot + 1) * planes], weight], axis=0)
            parts = edge_columns(row_values[:, :LANES], row_values[:, width - LANES :], PITCH * index)
            parts = [jnp.where(present, part, 0.0) for part in parts]
            halos = [part if total is None else total + part for total, part in zip(halos, parts)]
    left_halo[...], right_halo[...] = halos

    def field(row):
        if 0 <= row < rows:
            return by_row[row]
        at = (row + 2 if row < 0 else row - rows) * planes
        return (below if row < 0 else above)[at : at + planes]

    def weights(row):
        if 0 <= row < rows:
            return weights_by_row[row]
        return (below if row < 0 else above)[2 * planes :]

    products = first_products[...]
    places = (-1, 0, rows - 1, rows)
    for at, row in enumerate(places):
        image = apply_operator([field(row - 1), field(row), field(row + 1)], weights(row))
        outer[at] = image
        if 0 <= row < rows:
            products = products + products_of(inner_parts(image))
    both = [products]
    both.append(
        images_of(
            lambda row: outer[places.index(row)] if row in places else middle[row - 1],
            weights,
            (0, 1, rows - 2, rows - 1),
            second,
            second_products[...],
        )
    )
    for at, products in enumerate(both):
        some = products[:planes] + products[planes : 2 * planes] + products[2 * planes :]
        total = some[:, :planes] + some[:, planes : 2 * planes] + some[:, 2 * planes :]
        grams[:, at * planes : (at + 1) * planes] = total


def apply_on_strip(values, weights):
    total = jnp.sum(weights, axis=0, keepdims=True) * values
    for position, (up, across) in enumerate(NEIGHBOURS):
        moved = pltpu.roll(values, (-PITCH * up - across) % LANES, 1)
        total = total + weights[position : position + 1] * moved
    return total


def late_kernel(rows, left, right, left_halo, right_halo, *rest):
    diagonal_messages, col_messages, (early_grams, grams, edges) = rest[:2], rest[2:4], rest[4:]
    planes = early_grams.shape[0]
    odd_row, has_below, has_above = sides_of("row")
    odd_col, has_left, has_right = sides_of("col")
    beyond = jnp.where(odd_row, has_above, has_below)
    one, other = (
        col[...] + jnp.where(beyond, diagonal[...], 0.0)
        for col, diagonal in zip(col_messages, diagonal_messages)
    )
    lane = lax.broadcasted_iota(jnp.int32, (1, LANES), 1)
    spot, row = lane % PITCH, lane // PITCH
    strips, masks = [], []
    for side, (strip, present, halo) in enumerate(
        (
            (left[...] + left_halo[...], has_left, jnp.where(odd_col, other, one)),
            (right[...] + right_halo[...], has_right, jnp.where(odd_col, one, other)),
        )
    ):
        strips.append(strip + jnp.where(present, unfolded(halo, side * (PITCH - 2), planes), 0.0))
        low = 2 if side == 0 else PITCH - 4
        masks.append((spot >= low) & (spot < low + 2) & (row >= 2) & (row < rows + 2))
    values = [strip[:planes] for strip in strips]
    gram = []
    for at in range(2):
        values = [apply_on_strip(value, strip[planes:]) for value, strip in zip(values, strips)]
        kept = jnp.concatenate([jnp.where(mask, value, 0.0) for mask, value in zip(masks, values)], axis=1)
        both = jnp.concatenate(values, axis=1)
        gram.append(early_grams[:, at * planes : (at + 1) * planes] + gram_of(kept, both))
    edges[...] = both
    at_row = lax.broadcasted_iota(jnp.int32, (planes, planes), 0)
    at_col = lax.broadcasted_iota(jnp.int32, (planes, planes), 1)
    mixed = jnp.where(at_row >= at_col, gram[0], gram[1])
    diagonal = jnp.sum(jnp.where(at_row == at_col, gram[1], 0.0), axis=0, keepdims=True)
    block = jnp.concatenate([mixed[8 * g : 8 * (g + 1)] for g in range(planes // 8)], axis=1)
    last = jnp.concatenate([diagonal] * (LANES // planes), axis=1)
    for target in range(grams.shape[0]):
        for at in range(8):
            grams[target, :, at * LANES : (at + 1) * LANES] = block[at : at + 1]
        grams[target, :, 8 * LANES :] = last


def eliminate(grams, planes, half_way):
    lane = lax.broadcasted_iota(jnp.int32, (8, LANES), 1)
    sub = lax.broadcasted_iota(jnp.int32, (8, LANES), 0)
    first_half = lane < 2 * planes
    groups = planes // 8
    sources = [[gram[8 * g : 8 * (g + 1)] for g in range(groups)] for gram in grams]
    state = []
    for g in range(groups):
        unit = jnp.where(sub + 8 * g == lane % (2 * planes) - planes, 1.0, 0.0)
        unit = unit[:, planes : 2 * planes]
        state.append(jnp.concatenate([sources[0][g], unit, sources[1][g], unit], axis=1))
    columns = []
    for j in range(planes):
        columns.append(
            {
                g: jnp.where(
                    first_half,
                    jnp.broadcast_to(sources[0][g][:, j : j + 1], (8, LANES)),
                    jnp.broadcast_to(sources[1][g][:, j : j + 1], (8, LANES)),
                )
                for g in range(j // 8, groups)
            }
        )
    scale = [jnp.ones((8, LANES), jnp.float32)] * groups
    for step in range(planes):
        own, at = step // 8, step % 8
        column = columns[step]
        pivot = jnp.broadcast_to(column[own][at : at + 1], (8, LANES))
        inverse, root = pl.reciprocal(pivot, approx=False), lax.rsqrt(pivot)
        scale[own] = jnp.where(sub == at, root, scale[own])
        left = {g: jnp.where(sub > at, value, 0.0) if g == own else value for g, value in column.items()}
        factors = {g: value * inverse for g, value in left.items()}
        for j in range(step + 1, planes):
            entry = jnp.broadcast_to(column[j // 8][j % 8 : j % 8 + 1], (8, LANES))
            for g in columns[j]:
                change = (left[g] * entry) * inverse if j == step + 1 else factors[g] * entry
                columns[j][g] = columns[j][g] - change
        pivot_row = jnp.broadcast_to(state[own][at : at + 1], (8, LANES))
        for g in range(own, groups):
            state[g] = state[g] - factors[g] * pivot_row
        if step + 1 == planes // 2:
            half_way(jnp.concatenate([state[g] * scale[g] for g in range(groups // 2)], axis=0))
    return jnp.concatenate([state[g] * scale[g] for g in range(groups)], axis=0)


def finish_kernel(
    pixel_count, inner_second, outer_second, edges, parts, basis_out, factor_out, basis, factor, written
):
    planes, rows, width = basis.shape
    half = planes // 2
    at_row = lax.broadcasted_iota(jnp.int32, (planes, planes), 0)
    at_col = lax.broadcasted_iota(jnp.int32, (planes, planes), 1)
    lane = lax.broadcasted_iota(jnp.int32, (1, LANES), 1)
    outer_parts = split(edges[...])
    copies = []

    def solve(inverse, start):
        stop = start + inverse.shape[0]
        high, middle, low = split(inverse)
        left_side = jnp.concatenate([high, high, middle, high, low, middle], axis=1)

        def solved(high, middle, low):
            right_side = jnp.concatenate([high, middle, high, low, high, middle], axis=0)
            return jnp.dot(left_side, right_side, preferred_element_type=jnp.float32)

        outer = solved(*(part[:stop] for part in outer_parts))
        for row in range(rows):
            if 2 <= row < rows - 2:
                held, spot = inner_second, row - 2
            else:
                held, spot = outer_second, row if row < 2 else row - rows + 4
            value = solved(*(held[spot, at * planes : at * planes + stop] for at in range(3)))
            place = PITCH * (row + 2)
            first = rolled(outer[:, :LANES], -(place + 2))
            last = rolled(outer[:, LANES:], LANES - 2 - (place + PITCH - 4))
            basis[start:stop, row, :LANES] = jnp.where(lane < 2, first, value[:, :LANES])
            basis[start:stop, row, LANES : width - LANES] = value[:, LANES : width - LANES]
            basis[start:stop, row, width - LANES :] = jnp.where(
                lane >= LANES - 2, last, value[:, width - LANES :]
            )
        some = pl.ds(start, stop - start)
        copies.append(pltpu.make_async_copy(basis.at[some], basis_out.at[some], written.at[len(copies)]))
        copies[-1].start()

    block = tree_sum([parts[at] for at in range(parts.shape[0])]) / pixel_count
    block = [block[:, at * LANES : (at + 1) * LANES] for at in range(9)]
    mixed, diagonal = jnp.concatenate(block[:8], axis=0), block[8][:, :planes]
    mixed = jnp.concatenate([mixed[:, at * planes : (at + 1) * planes] for at in range(LANES // planes)], axis=0)
    flipped = mixed.T
    first = jnp.where(at_row >= at_col, mixed, flipped)
    second = jnp.where(at_row < at_col, mixed, jnp.where(at_row > at_col, flipped, diagonal))
    low_half = (at_col <= at_row)[:half, :half]
    state = eliminate(
        [first, second],
        planes,
        lambda state: solve(jnp.where(low_half, state[:, 3 * planes : 3 * planes + half], 0.0), 0),
    )
    first_inverse = state[:, planes : 2 * planes]
    product_upper = jnp.where(at_col >= at_row, state[:, 2 * planes : 3 * planes], 0.0)
    solve(jnp.where(at_col <= at_row, state[:, 3 * planes :], 0.0)[half:], half)
    factor[...] = jnp.where(at_col >= at_row, gram_of(product_upper, first_inverse), 0.0)
    copies.append(pltpu.make_async_copy(factor, factor_out, written.at[2]))
    copies[-1].start()
    for copy in copies:
        copy.wait()


def tree_sum(parts):
    while len(parts) > 1:
        parts = [sum(parts[at + 1 : at + 2], parts[at]) for at in range(0, len(parts), 2)]
    return parts[0]


def swap(value, row_pairing=None, col_pairing=None):
    names = ("sec", "row", "col")
    shape = [lax.axis_size(name) for name in names]

    def partner(at, place, pairing):
        other = place if pairing is None else place + 1 if place % 2 != pairing else place - 1
        return other if 0 <= other < shape[at] else None

    pairs = []
    for sec, row, col in itertools.product(*(range(extent) for extent in shape)):
        other_row, other_col = partner(1, row, row_pairing), partner(2, col, col_pairing)
        if other_col is None:
            target = (sec, row ^ 1, col)
        elif other_row is None:
            target = (sec ^ 1, row, col)
        else:
            target = (sec, other_row, other_col)
        pairs.append(tuple((a * shape[1] + b) * shape[2] + c for a, b, c in ((sec, row, col), target)))
    return lax.ppermute(value, names, pairs)


def on_device(sketch, weights):
    planes, rows, width = sketch.shape
    group = lax.axis_size("row") * lax.axis_size("col")
    side = f32(planes + 8, LANES)
    by_row, weights_by_row, left, right, *messages = call(
        pack_rows_kernel,
        [f32(rows, planes, width), f32(rows, 8, width), side, side]
        + [f32(2 * planes + 16, width), f32(2 * planes + 8, width)]
        + [f32(16, LANES)] * 2,
        pltpu.with_memory_space_constraint(sketch, pltpu.HBM),
        pltpu.with_memory_space_constraint(weights, pltpu.HBM),
        memory=pltpu.HBM,
        scratch=[
            pltpu.VMEM(sketch.shape, jnp.float32),
            pltpu.VMEM(weights.shape, jnp.float32),
            pltpu.SemaphoreType.DMA((2,)),
        ],
    )
    from_rows = [swap(messages[at], row_pairing=at) for at in range(2)]
    from_diagonals = [swap(messages[2 + at], row_pairing=0, col_pairing=at) for at in range(2)]
    left, right, *messages = call(
        functools.partial(strips_kernel, rows), [side, side] + [f32(16, LANES)] * 2, left, right, from_rows[1]
    )
    from_cols = [swap(messages[at], col_pairing=at) for at in range(2)]
    parts_of = functools.partial(jax.ShapeDtypeStruct, dtype=jnp.bfloat16)
    products = f32(3 * planes, 3 * planes)
    middle, inner_second, *inner_products = call(
        inner_rows_kernel,
        [f32(rows - 2, planes, width), parts_of((rows - 4, 3 * planes, width)), products, products],
        by_row,
        weights_by_row,
    )
    outer_second, early_grams, *halos = call(
        outer_rows_kernel,
        [parts_of((4, 3 * planes, width)), f32(planes, 2 * planes), side, side],
        by_row,
        weights_by_row,
        *from_rows,
        middle,
        *inner_products,
        scratch=[pltpu.VMEM((4, planes, width), jnp.float32)],
    )
    grams, edges = call(
        functools.partial(late_kernel, rows),
        [f32(group, 1, 9 * LANES), f32(planes, 2 * LANES)],
        left,
        right,
        *halos,
        *from_diagonals,
        *from_cols,
        early_grams,
    )
    rows_of, cols_of = lax.axis_size("row"), lax.axis_size("col")
    first = cols_of + cols_of // 2
    order = [first] + [row * cols_of + col for col in range(cols_of) for row in range(rows_of)]
    order = list(dict.fromkeys(order))
    parts = lax.all_to_all(grams, ("row", "col"), 0, 0, axis_index_groups=[order], tiled=True)
    return call(
        functools.partial(finish_kernel, float(rows * width * group)),
        [f32(planes, rows, width), f32(planes, planes)],
        inner_second,
        outer_second,
        edges,
        parts,
        out_memory=pl.ANY,
        scratch=[
            pltpu.VMEM(sketch.shape, jnp.float32),
            pltpu.VMEM((planes, planes), jnp.float32),
            pltpu.SemaphoreType.DMA((3,)),
        ],
    )


def solution(mesh):
    return jax.shard_map(
        on_device,
        mesh=mesh,
        in_specs=(P(None, ("sec", "row"), "col"), P(None, ("sec", "row"), "col")),
        out_specs=(P(None, ("sec", "row"), "col"), P("sec", None)),
        check_vma=False,
    )
```

```python
import functools
import itertools

import jax
import jax.numpy as jnp
from jax import lax
from jax.experimental import pallas as pl
from jax.experimental.pallas import tpu as pltpu
from jax.sharding import PartitionSpec as P

NEIGHBOURS = ((-1, -1), (-1, 0), (-1, 1), (0, -1), (0, 1), (1, -1), (1, 0), (1, 1))
LANES = 128
PITCH = 8
HIGHEST = lax.Precision.HIGHEST


def call(kernel, out_shapes, *operands, memory=pltpu.VMEM, out_memory=pltpu.VMEM, scratch=(), cost=None):
    return pl.pallas_call(
        kernel,
        out_shape=out_shapes,
        in_specs=[pl.BlockSpec(memory_space=memory)] * len(operands),
        out_specs=[pl.BlockSpec(memory_space=out_memory)] * len(out_shapes),
        scratch_shapes=scratch,
        cost_estimate=cost,
        compiler_params=pltpu.CompilerParams(vmem_limit_bytes=40 * 1024 * 1024),
    )(*operands)


def f32(*shape):
    return jax.ShapeDtypeStruct(shape, jnp.float32)


def sides_of(axis):
    place = lax.axis_index(axis)
    return place % 2 == 1, place > 0, place < lax.axis_size(axis) - 1


def edge_columns(first, last, place):
    lane = lax.broadcasted_iota(jnp.int32, (1, LANES), 1)
    own = PITCH - 2
    left = jnp.where((lane >= place + 2) & (lane < place + PITCH), pltpu.roll(first, place + 2, 1), 0.0)
    right = jnp.where((lane >= place) & (lane < place + own), pltpu.roll(last, place + own, 1), 0.0)
    return left, right


def pack_rows_kernel(sketch, weights, by_row, weights_by_row, left, right, *rest):
    bulk_messages, diagonal_messages = rest[:2], rest[2:4]
    tile, weight_tile, arrived = rest[4:]
    copies = [
        pltpu.make_async_copy(sketch, tile, arrived.at[0]),
        pltpu.make_async_copy(weights, weight_tile, arrived.at[1]),
    ]
    for copy in copies:
        copy.start()
    for copy in copies:
        copy.wait()
    rows, planes, width = by_row.shape
    odd_row, _, _ = sides_of("row")
    odd_col, _, _ = sides_of("col")
    lane = lax.broadcasted_iota(jnp.int32, (1, LANES), 1)
    for row in range(rows):
        weights_by_row[row] = weight_tile[:, row, :]
        by_row[row] = tile[:, row, :]
    for message, up in zip(bulk_messages, (odd_row, jnp.logical_not(odd_row))):
        start = jnp.where(up, rows - 2, 0)
        for slot in range(2):
            message[slot * planes : (slot + 1) * planes] = by_row[start + slot]
        message[2 * planes : 2 * planes + 8] = weights_by_row[jnp.where(up, rows - 1, 0)]
    strips = [None, None]
    for row in range(rows):
        first = jnp.concatenate([by_row[row, :, :LANES], weights_by_row[row, :, :LANES]], axis=0)
        last = jnp.concatenate([by_row[row, :, width - LANES :], weights_by_row[row, :, width - LANES :]], axis=0)
        parts = edge_columns(first, last, PITCH * (row + 2))
        strips = [part if strip is None else strip + part for strip, part in zip(strips, parts)]
    left[...], right[...] = strips
    bulk_messages[0][2 * planes + 8 :] = jnp.zeros((8, width), jnp.float32)
    pair = 2 * PITCH
    to_left, to_right = folded(strips[0], 2), folded(strips[1], PITCH - 4)
    for message, up in zip(diagonal_messages, (odd_col, jnp.logical_not(odd_col))):
        edge = jnp.where(up, to_right, to_left)
        below = jnp.where(lane < pair, rolled(edge, -PITCH * rows), 0.0)
        start = PITCH * (rows + 2)
        above = jnp.where((lane >= start) & (lane < start + pair), rolled(edge, PITCH * rows), 0.0)
        message[...] = jnp.where(odd_row, below, above)


def strips_kernel(rows, own_left, own_right, bulk_message, left, right, *col_messages):
    planes = own_left.shape[0] - 8
    odd_row, has_below, has_above = sides_of("row")
    odd_col, _, _ = sides_of("col")
    width = bulk_message.shape[1]
    totals = [own_left[...], own_right[...]]
    present = jnp.where(odd_row, has_below, has_above)
    for slot in range(2):
        place = PITCH * (slot + jnp.where(odd_row, 0, rows + 2))
        halo = [bulk_message[slot * planes : (slot + 1) * planes], bulk_message[2 * planes :]]
        first = jnp.concatenate([part[:, :LANES] for part in halo], axis=0)
        last = jnp.concatenate([part[:, width - LANES :] for part in halo], axis=0)
        parts = edge_columns(first, last, place)
        totals = [total + jnp.where(present, part, 0.0) for total, part in zip(totals, parts)]
    left[...], right[...] = totals
    to_left, to_right = folded(left[...], 2), folded(right[...], PITCH - 4)
    for message, up in zip(col_messages, (odd_col, jnp.logical_not(odd_col))):
        message[...] = jnp.where(up, to_right, to_left)


def folded(strip, spot):
    lane = lax.broadcasted_iota(jnp.int32, (1, LANES), 1)
    groups = strip.shape[0] // 8
    pieces = []
    for group in range(groups):
        target = 2 * group if group < groups - 1 else 0
        moved = rolled(strip[8 * group : 8 * (group + 1)], target - spot)
        pieces.append(jnp.where((lane % PITCH) // 2 == target // 2, moved, 0.0))
    return jnp.concatenate([functools.reduce(jnp.add, pieces[:-1]), pieces[-1]], axis=0)


def unfolded(message, spot, planes):
    lane = lax.broadcasted_iota(jnp.int32, (1, LANES), 1)
    pieces = [rolled(message[:8], spot - 2 * group) for group in range(planes // 8)] + [rolled(message[8:], spot)]
    return jnp.where((lane % PITCH) // 2 == spot // 2, jnp.concatenate(pieces, axis=0), 0.0)


def rolled(value, shift):
    return pltpu.roll(value, shift % LANES, 1) if shift % LANES else value


def apply_operator(rows3, weight_rows):
    width = rows3[1].shape[1]
    total = jnp.sum(weight_rows, axis=0, keepdims=True) * rows3[1]
    for across in (0, -1, 1):
        moved = pltpu.roll(weight_rows, across % width, 1) if across else weight_rows
        terms = [
            moved[position : position + 1] * rows3[up + 1]
            for position, (up, side) in enumerate(NEIGHBOURS)
            if side == across
        ]
        part = functools.reduce(jnp.add, terms)
        total = total + (pltpu.roll(part, -across % width, 1) if across else part)
    return total


def gram_of(value, other):
    return lax.dot_general(
        value, other, (((1,), (1,)), ((), ())), precision=HIGHEST, preferred_element_type=jnp.float32
    )


def split(value):
    high = value.astype(jnp.bfloat16)
    rest = value - high.astype(jnp.float32)
    middle = rest.astype(jnp.bfloat16)
    low = (rest - middle.astype(jnp.float32)).astype(jnp.bfloat16)
    return high, middle, low


def inner_parts(image):
    width = image.shape[1]
    lane = lax.broadcasted_iota(jnp.int32, (1, LANES), 1)
    kept = [
        jnp.where(lane >= 2, image[:, :LANES], 0.0),
        image[:, LANES : width - LANES],
        jnp.where(lane < LANES - 2, image[:, width - LANES :], 0.0),
    ]
    return jnp.concatenate(split(jnp.concatenate(kept, axis=1)), axis=0)


def products_of(parts):
    return lax.dot_general(parts, parts, (((1,), (1,)), ((), ())), preferred_element_type=jnp.float32)


def images_of(middle, weights, wanted, second, products):
    for at, row in enumerate(wanted):
        parts = inner_parts(apply_operator([middle(row - 1), middle(row), middle(row + 1)], weights(row)))
        second[at] = parts
        products = products + products_of(parts)
    return products


def inner_rows_kernel(
    by_row, weights_by_row, diagonal_message, middle, second, first_products, second_products, diagonal
):
    rows = by_row.shape[0]
    odd_row, has_below, has_above = sides_of("row")
    diagonal[...] = jnp.where(jnp.where(odd_row, has_above, has_below), diagonal_message[...], 0.0)
    products = jnp.zeros(first_products.shape, jnp.float32)
    for row in range(1, rows - 1):
        image = apply_operator([by_row[row - 1], by_row[row], by_row[row + 1]], weights_by_row[row])
        middle[row - 1] = image
        products = products + products_of(inner_parts(image))
    first_products[...] = products
    second_products[...] = images_of(
        lambda row: middle[row - 1],
        lambda row: weights_by_row[row],
        range(2, rows - 2),
        second,
        jnp.zeros(second_products.shape, jnp.float32),
    )


def outer_rows_kernel(
    by_row,
    weights_by_row,
    first_message,
    second_message,
    middle,
    first_products,
    second_products,
    second,
    grams,
    left_halo,
    right_halo,
    outer,
):
    rows, planes, width = by_row.shape
    odd_row, has_below, has_above = sides_of("row")
    one, other = first_message[: 2 * planes + 8], second_message[...]
    below = jnp.where(has_below, jnp.where(odd_row, other, one), 0.0)
    above = jnp.where(has_above, jnp.where(odd_row, one, other), 0.0)
    halos = [None, None]
    for side, (halo, present) in enumerate(
        ((below, jnp.logical_not(odd_row)), (above, odd_row))
    ):
        for slot in range(2):
            index = slot if side == 0 else rows + 2 + slot
            blank = jnp.zeros((8, width), jnp.float32)
            weight = halo[2 * planes :] if slot != side else blank
            row_values = jnp.concatenate([halo[slot * planes : (slot + 1) * planes], weight], axis=0)
            parts = edge_columns(row_values[:, :LANES], row_values[:, width - LANES :], PITCH * index)
            parts = [jnp.where(present, part, 0.0) for part in parts]
            halos = [part if total is None else total + part for total, part in zip(halos, parts)]
    left_halo[...], right_halo[...] = halos

    def field(row):
        if 0 <= row < rows:
            return by_row[row]
        at = (row + 2 if row < 0 else row - rows) * planes
        return (below if row < 0 else above)[at : at + planes]

    def weights(row):
        if 0 <= row < rows:
            return weights_by_row[row]
        return (below if row < 0 else above)[2 * planes :]

    products = first_products[...]
    places = (-1, 0, rows - 1, rows)
    for at, row in enumerate(places):
        image = apply_operator([field(row - 1), field(row), field(row + 1)], weights(row))
        outer[at] = image
        if 0 <= row < rows:
            products = products + products_of(inner_parts(image))
    both = [products]
    both.append(
        images_of(
            lambda row: outer[places.index(row)] if row in places else middle[row - 1],
            weights,
            (0, 1, rows - 2, rows - 1),
            second,
            second_products[...],
        )
    )
    for at, products in enumerate(both):
        some = products[:planes] + products[planes : 2 * planes] + products[2 * planes :]
        total = some[:, :planes] + some[:, planes : 2 * planes] + some[:, 2 * planes :]
        grams[:, at * planes : (at + 1) * planes] = total


def apply_on_strip(values, weights):
    total = jnp.sum(weights, axis=0, keepdims=True) * values
    for position, (up, across) in enumerate(NEIGHBOURS):
        moved = pltpu.roll(values, (-PITCH * up - across) % LANES, 1)
        total = total + weights[position : position + 1] * moved
    return total


def late_kernel(rows, left, right, left_halo, right_halo, *rest):
    diagonal_messages, col_messages, (early_grams, grams, edges) = rest[:2], rest[2:4], rest[4:]
    planes = early_grams.shape[0]
    odd_row, has_below, has_above = sides_of("row")
    odd_col, has_left, has_right = sides_of("col")
    beyond = jnp.where(odd_row, has_above, has_below)
    one, other = (
        col[...] + jnp.where(beyond, diagonal[...], 0.0)
        for col, diagonal in zip(col_messages, diagonal_messages)
    )
    lane = lax.broadcasted_iota(jnp.int32, (1, LANES), 1)
    spot, row = lane % PITCH, lane // PITCH
    strips, masks = [], []
    for side, (strip, present, halo) in enumerate(
        (
            (left[...] + left_halo[...], has_left, jnp.where(odd_col, other, one)),
            (right[...] + right_halo[...], has_right, jnp.where(odd_col, one, other)),
        )
    ):
        strips.append(strip + jnp.where(present, unfolded(halo, side * (PITCH - 2), planes), 0.0))
        low = 2 if side == 0 else PITCH - 4
        masks.append((spot >= low) & (spot < low + 2) & (row >= 2) & (row < rows + 2))
    values = [strip[:planes] for strip in strips]
    gram = []
    for at in range(2):
        values = [apply_on_strip(value, strip[planes:]) for value, strip in zip(values, strips)]
        kept = jnp.concatenate([jnp.where(mask, value, 0.0) for mask, value in zip(masks, values)], axis=1)
        both = jnp.concatenate(values, axis=1)
        gram.append(early_grams[:, at * planes : (at + 1) * planes] + gram_of(kept, both))
    edges[...] = both
    at_row = lax.broadcasted_iota(jnp.int32, (planes, planes), 0)
    at_col = lax.broadcasted_iota(jnp.int32, (planes, planes), 1)
    mixed = jnp.where(at_row >= at_col, gram[0], gram[1])
    diagonal = jnp.sum(jnp.where(at_row == at_col, gram[1], 0.0), axis=0, keepdims=True)
    block = jnp.concatenate([mixed[8 * g : 8 * (g + 1)] for g in range(planes // 8)], axis=1)
    last = jnp.concatenate([diagonal] * (LANES // planes), axis=1)
    for target in range(grams.shape[0]):
        for at in range(8):
            grams[target, :, at * LANES : (at + 1) * LANES] = block[at : at + 1]
        grams[target, :, 8 * LANES :] = last


def eliminate(grams, planes, half_way):
    lane = lax.broadcasted_iota(jnp.int32, (8, LANES), 1)
    sub = lax.broadcasted_iota(jnp.int32, (8, LANES), 0)
    first_half = lane < 2 * planes
    groups = planes // 8
    sources = [[gram[8 * g : 8 * (g + 1)] for g in range(groups)] for gram in grams]
    state = []
    for g in range(groups):
        unit = jnp.where(sub + 8 * g == lane % (2 * planes) - planes, 1.0, 0.0)
        unit = unit[:, planes : 2 * planes]
        state.append(jnp.concatenate([sources[0][g], unit, sources[1][g], unit], axis=1))
    columns = []
    for j in range(planes):
        columns.append(
            {
                g: jnp.where(
                    first_half,
                    jnp.broadcast_to(sources[0][g][:, j : j + 1], (8, LANES)),
                    jnp.broadcast_to(sources[1][g][:, j : j + 1], (8, LANES)),
                )
                for g in range(j // 8, groups)
            }
        )
    scale = [jnp.ones((8, LANES), jnp.float32)] * groups
    for step in range(planes):
        own, at = step // 8, step % 8
        column = columns[step]
        pivot = jnp.broadcast_to(column[own][at : at + 1], (8, LANES))
        inverse, root = pl.reciprocal(pivot, approx=False), lax.rsqrt(pivot)
        scale[own] = jnp.where(sub == at, root, scale[own])
        left = {g: jnp.where(sub > at, value, 0.0) if g == own else value for g, value in column.items()}
        factors = {g: value * inverse for g, value in left.items()}
        for j in range(step + 1, planes):
            entry = jnp.broadcast_to(column[j // 8][j % 8 : j % 8 + 1], (8, LANES))
            for g in columns[j]:
                change = (left[g] * entry) * inverse if j == step + 1 else factors[g] * entry
                columns[j][g] = columns[j][g] - change
        pivot_row = jnp.broadcast_to(state[own][at : at + 1], (8, LANES))
        for g in range(own, groups):
            state[g] = state[g] - factors[g] * pivot_row
        if step + 1 == planes // 2:
            half_way(jnp.concatenate([state[g] * scale[g] for g in range(groups // 2)], axis=0))
    return jnp.concatenate([state[g] * scale[g] for g in range(groups)], axis=0)


def finish_kernel(
    pixel_count, inner_second, outer_second, edges, parts, basis_out, factor_out, basis, factor, written
):
    planes, rows, width = basis.shape
    half = planes // 2
    at_row = lax.broadcasted_iota(jnp.int32, (planes, planes), 0)
    at_col = lax.broadcasted_iota(jnp.int32, (planes, planes), 1)
    lane = lax.broadcasted_iota(jnp.int32, (1, LANES), 1)
    outer_parts = split(edges[...])
    copies = []

    def solve(inverse, start):
        stop = start + inverse.shape[0]
        high, middle, low = split(inverse)
        left_side = jnp.concatenate([high, high, middle, high, low, middle], axis=1)

        def solved(high, middle, low):
            right_side = jnp.concatenate([high, middle, high, low, high, middle], axis=0)
            return jnp.dot(left_side, right_side, preferred_element_type=jnp.float32)

        outer = solved(*(part[:stop] for part in outer_parts))
        for row in range(rows):
            if 2 <= row < rows - 2:
                held, spot = inner_second, row - 2
            else:
                held, spot = outer_second, row if row < 2 else row - rows + 4
            value = solved(*(held[spot, at * planes : at * planes + stop] for at in range(3)))
            place = PITCH * (row + 2)
            first = rolled(outer[:, :LANES], -(place + 2))
            last = rolled(outer[:, LANES:], LANES - 2 - (place + PITCH - 4))
            basis[start:stop, row, :LANES] = jnp.where(lane < 2, first, value[:, :LANES])
            basis[start:stop, row, LANES : width - LANES] = value[:, LANES : width - LANES]
            basis[start:stop, row, width - LANES :] = jnp.where(
                lane >= LANES - 2, last, value[:, width - LANES :]
            )
        some = pl.ds(start, stop - start)
        copies.append(pltpu.make_async_copy(basis.at[some], basis_out.at[some], written.at[len(copies)]))
        copies[-1].start()

    block = tree_sum([parts[at] for at in range(parts.shape[0])]) / pixel_count
    block = [block[:, at * LANES : (at + 1) * LANES] for at in range(9)]
    mixed, diagonal = jnp.concatenate(block[:8], axis=0), block[8][:, :planes]
    mixed = jnp.concatenate([mixed[:, at * planes : (at + 1) * planes] for at in range(LANES // planes)], axis=0)
    flipped = mixed.T
    first = jnp.where(at_row >= at_col, mixed, flipped)
    second = jnp.where(at_row < at_col, mixed, jnp.where(at_row > at_col, flipped, diagonal))
    low_half = (at_col <= at_row)[:half, :half]
    state = eliminate(
        [first, second],
        planes,
        lambda state: solve(jnp.where(low_half, state[:, 3 * planes : 3 * planes + half], 0.0), 0),
    )
    first_inverse = state[:, planes : 2 * planes]
    product_upper = jnp.where(at_col >= at_row, state[:, 2 * planes : 3 * planes], 0.0)
    solve(jnp.where(at_col <= at_row, state[:, 3 * planes :], 0.0)[half:], half)
    factor[...] = jnp.where(at_col >= at_row, gram_of(product_upper, first_inverse), 0.0)
    copies.append(pltpu.make_async_copy(factor, factor_out, written.at[2]))
    copies[-1].start()
    for copy in copies:
        copy.wait()


def tree_sum(parts):
    while len(parts) > 1:
        parts = [sum(parts[at + 1 : at + 2], parts[at]) for at in range(0, len(parts), 2)]
    return parts[0]


def swap(value, row_pairing=None, col_pairing=None):
    names = ("sec", "row", "col")
    shape = [lax.axis_size(name) for name in names]

    def partner(at, place, pairing):
        other = place if pairing is None else place + 1 if place % 2 != pairing else place - 1
        return other if 0 <= other < shape[at] else None

    pairs = []
    for sec, row, col in itertools.product(*(range(extent) for extent in shape)):
        other_row, other_col = partner(1, row, row_pairing), partner(2, col, col_pairing)
        if other_col is None:
            target = (sec, row ^ 1, col)
        elif other_row is None:
            target = (sec ^ 1, row, col)
        else:
            target = (sec, other_row, other_col)
        pairs.append(tuple((a * shape[1] + b) * shape[2] + c for a, b, c in ((sec, row, col), target)))
    return lax.ppermute(value, names, pairs)


def on_device(sketch, weights):
    planes, rows, width = sketch.shape
    group = lax.axis_size("row") * lax.axis_size("col")
    side = f32(planes + 8, LANES)
    by_row, weights_by_row, left, right, *messages = call(
        pack_rows_kernel,
        [f32(rows, planes, width), f32(rows, 8, width), side, side]
        + [f32(2 * planes + 16, width), f32(2 * planes + 8, width)]
        + [f32(16, LANES)] * 2,
        pltpu.with_memory_space_constraint(sketch, pltpu.HBM),
        pltpu.with_memory_space_constraint(weights, pltpu.HBM),
        memory=pltpu.HBM,
        scratch=[
            pltpu.VMEM(sketch.shape, jnp.float32),
            pltpu.VMEM(weights.shape, jnp.float32),
            pltpu.SemaphoreType.DMA((2,)),
        ],
    )
    from_rows = [swap(messages[at], row_pairing=at) for at in range(2)]
    from_diagonals = [swap(messages[2 + at], row_pairing=0, col_pairing=at) for at in range(2)]
    left, right, *messages = call(
        functools.partial(strips_kernel, rows), [side, side] + [f32(16, LANES)] * 2, left, right, from_rows[1]
    )
    from_cols = [swap(messages[at], col_pairing=at) for at in range(2)]
    parts_of = functools.partial(jax.ShapeDtypeStruct, dtype=jnp.bfloat16)
    products = f32(3 * planes, 3 * planes)
    middle, inner_second, *inner_products, from_diagonals[0] = call(
        inner_rows_kernel,
        [f32(rows - 2, planes, width), parts_of((rows - 4, 3 * planes, width)), products, products]
        + [f32(16, LANES)],
        by_row,
        weights_by_row,
        from_diagonals[0],
        cost=pl.CostEstimate(flops=2000000000, bytes_accessed=4000000, transcendentals=0),
    )
    outer_second, early_grams, *halos = call(
        outer_rows_kernel,
        [parts_of((4, 3 * planes, width)), f32(planes, 2 * planes), side, side],
        by_row,
        weights_by_row,
        *from_rows,
        middle,
        *inner_products,
        scratch=[pltpu.VMEM((4, planes, width), jnp.float32)],
    )
    grams, edges = call(
        functools.partial(late_kernel, rows),
        [f32(group, 1, 9 * LANES), f32(planes, 2 * LANES)],
        left,
        right,
        *halos,
        *from_diagonals,
        *from_cols,
        early_grams,
    )
    rows_of, cols_of = lax.axis_size("row"), lax.axis_size("col")
    first = cols_of + cols_of // 2
    order = [first] + [row * cols_of + col for col in range(cols_of) for row in range(rows_of)]
    order = list(dict.fromkeys(order))
    parts = lax.all_to_all(grams, ("row", "col"), 0, 0, axis_index_groups=[order], tiled=True)
    return call(
        functools.partial(finish_kernel, float(rows * width * group)),
        [f32(planes, rows, width), f32(planes, planes)],
        inner_second,
        outer_second,
        edges,
        parts,
        out_memory=pl.ANY,
        scratch=[
            pltpu.VMEM(sketch.shape, jnp.float32),
            pltpu.VMEM((planes, planes), jnp.float32),
            pltpu.SemaphoreType.DMA((3,)),
        ],
    )


def solution(mesh):
    return jax.shard_map(
        on_device,
        mesh=mesh,
        in_specs=(P(None, ("sec", "row"), "col"), P(None, ("sec", "row"), "col")),
        out_specs=(P(None, ("sec", "row"), "col"), P("sec", None)),
        check_vma=False,
    )
```

```python
import functools
import itertools

import jax
import jax.numpy as jnp
from jax import lax
from jax.experimental import pallas as pl
from jax.experimental.pallas import tpu as pltpu
from jax.sharding import PartitionSpec as P

NEIGHBOURS = ((-1, -1), (-1, 0), (-1, 1), (0, -1), (0, 1), (1, -1), (1, 0), (1, 1))
LANES = 128
PITCH = 8
HIGHEST = lax.Precision.HIGHEST


def call(kernel, out_shapes, *operands, memory=pltpu.VMEM, out_memory=pltpu.VMEM, scratch=(), cost=None):
    return pl.pallas_call(
        kernel,
        out_shape=out_shapes,
        in_specs=[pl.BlockSpec(memory_space=memory)] * len(operands),
        out_specs=[pl.BlockSpec(memory_space=out_memory)] * len(out_shapes),
        scratch_shapes=scratch,
        cost_estimate=cost,
        compiler_params=pltpu.CompilerParams(vmem_limit_bytes=40 * 1024 * 1024),
    )(*operands)


def f32(*shape):
    return jax.ShapeDtypeStruct(shape, jnp.float32)


def sides_of(axis):
    place = lax.axis_index(axis)
    return place % 2 == 1, place > 0, place < lax.axis_size(axis) - 1


def edge_columns(first, last, place):
    lane = lax.broadcasted_iota(jnp.int32, (1, LANES), 1)
    own = PITCH - 2
    left = jnp.where((lane >= place + 2) & (lane < place + PITCH), pltpu.roll(first, place + 2, 1), 0.0)
    right = jnp.where((lane >= place) & (lane < place + own), pltpu.roll(last, place + own, 1), 0.0)
    return left, right


def pack_rows_kernel(sketch, weights, by_row, weights_by_row, left, right, *rest):
    bulk_messages, diagonal_messages = rest[:2], rest[2:4]
    tile, weight_tile, arrived = rest[4:]
    copies = [
        pltpu.make_async_copy(sketch, tile, arrived.at[0]),
        pltpu.make_async_copy(weights, weight_tile, arrived.at[1]),
    ]
    for copy in copies:
        copy.start()
    for copy in copies:
        copy.wait()
    rows, planes, width = by_row.shape
    odd_row, _, _ = sides_of("row")
    odd_col, _, _ = sides_of("col")
    lane = lax.broadcasted_iota(jnp.int32, (1, LANES), 1)
    for row in range(rows):
        weights_by_row[row] = weight_tile[:, row, :]
        by_row[row] = tile[:, row, :]
    for message, up in zip(bulk_messages, (odd_row, jnp.logical_not(odd_row))):
        start = jnp.where(up, rows - 2, 0)
        for slot in range(2):
            message[slot * planes : (slot + 1) * planes] = by_row[start + slot]
        message[2 * planes : 2 * planes + 8] = weights_by_row[jnp.where(up, rows - 1, 0)]
    strips = [None, None]
    for row in range(rows):
        first = jnp.concatenate([by_row[row, :, :LANES], weights_by_row[row, :, :LANES]], axis=0)
        last = jnp.concatenate([by_row[row, :, width - LANES :], weights_by_row[row, :, width - LANES :]], axis=0)
        parts = edge_columns(first, last, PITCH * (row + 2))
        strips = [part if strip is None else strip + part for strip, part in zip(strips, parts)]
    left[...], right[...] = strips
    bulk_messages[0][2 * planes + 8 :] = jnp.zeros((8, width), jnp.float32)
    pair = 2 * PITCH
    to_left, to_right = folded(strips[0], 2), folded(strips[1], PITCH - 4)
    for message, up in zip(diagonal_messages, (odd_col, jnp.logical_not(odd_col))):
        edge = jnp.where(up, to_right, to_left)
        below = jnp.where(lane < pair, rolled(edge, -PITCH * rows), 0.0)
        start = PITCH * (rows + 2)
        above = jnp.where((lane >= start) & (lane < start + pair), rolled(edge, PITCH * rows), 0.0)
        message[...] = jnp.where(odd_row, below, above)


def strips_kernel(rows, own_left, own_right, bulk_message, left, right, *col_messages):
    planes = own_left.shape[0] - 8
    odd_row, has_below, has_above = sides_of("row")
    odd_col, _, _ = sides_of("col")
    width = bulk_message.shape[1]
    totals = [own_left[...], own_right[...]]
    present = jnp.where(odd_row, has_below, has_above)
    for slot in range(2):
        place = PITCH * (slot + jnp.where(odd_row, 0, rows + 2))
        halo = [bulk_message[slot * planes : (slot + 1) * planes], bulk_message[2 * planes :]]
        first = jnp.concatenate([part[:, :LANES] for part in halo], axis=0)
        last = jnp.concatenate([part[:, width - LANES :] for part in halo], axis=0)
        parts = edge_columns(first, last, place)
        totals = [total + jnp.where(present, part, 0.0) for total, part in zip(totals, parts)]
    left[...], right[...] = totals
    to_left, to_right = folded(left[...], 2), folded(right[...], PITCH - 4)
    for message, up in zip(col_messages, (jnp.logical_not(odd_col), odd_col)):
        message[...] = jnp.where(up, to_right, to_left)


def folded(strip, spot):
    lane = lax.broadcasted_iota(jnp.int32, (1, LANES), 1)
    groups = strip.shape[0] // 8
    pieces = []
    for group in range(groups):
        target = 2 * group if group < groups - 1 else 0
        moved = rolled(strip[8 * group : 8 * (group + 1)], target - spot)
        pieces.append(jnp.where((lane % PITCH) // 2 == target // 2, moved, 0.0))
    return jnp.concatenate([functools.reduce(jnp.add, pieces[:-1]), pieces[-1]], axis=0)


def unfolded(message, spot, planes):
    lane = lax.broadcasted_iota(jnp.int32, (1, LANES), 1)
    pieces = [rolled(message[:8], spot - 2 * group) for group in range(planes // 8)] + [rolled(message[8:], spot)]
    return jnp.where((lane % PITCH) // 2 == spot // 2, jnp.concatenate(pieces, axis=0), 0.0)


def rolled(value, shift):
    return pltpu.roll(value, shift % LANES, 1) if shift % LANES else value


def apply_operator(rows3, weight_rows):
    width = rows3[1].shape[1]
    total = jnp.sum(weight_rows, axis=0, keepdims=True) * rows3[1]
    for across in (0, -1, 1):
        moved = pltpu.roll(weight_rows, across % width, 1) if across else weight_rows
        terms = [
            moved[position : position + 1] * rows3[up + 1]
            for position, (up, side) in enumerate(NEIGHBOURS)
            if side == across
        ]
        part = functools.reduce(jnp.add, terms)
        total = total + (pltpu.roll(part, -across % width, 1) if across else part)
    return total


def gram_of(value, other):
    return lax.dot_general(
        value, other, (((1,), (1,)), ((), ())), precision=HIGHEST, preferred_element_type=jnp.float32
    )


def split(value):
    high = value.astype(jnp.bfloat16)
    rest = value - high.astype(jnp.float32)
    middle = rest.astype(jnp.bfloat16)
    low = (rest - middle.astype(jnp.float32)).astype(jnp.bfloat16)
    return high, middle, low


def inner_parts(image):
    width = image.shape[1]
    lane = lax.broadcasted_iota(jnp.int32, (1, LANES), 1)
    kept = [
        jnp.where(lane >= 2, image[:, :LANES], 0.0),
        image[:, LANES : width - LANES],
        jnp.where(lane < LANES - 2, image[:, width - LANES :], 0.0),
    ]
    return jnp.concatenate(split(jnp.concatenate(kept, axis=1)), axis=0)


def products_of(parts):
    return lax.dot_general(parts, parts, (((1,), (1,)), ((), ())), preferred_element_type=jnp.float32)


def images_of(middle, weights, wanted, second, products):
    for at, row in enumerate(wanted):
        parts = inner_parts(apply_operator([middle(row - 1), middle(row), middle(row + 1)], weights(row)))
        second[at] = parts
        products = products + products_of(parts)
    return products


def inner_rows_kernel(
    by_row, weights_by_row, diagonal_message, middle, second, first_products, second_products, diagonal
):
    rows = by_row.shape[0]
    odd_row, has_below, has_above = sides_of("row")
    diagonal[...] = jnp.where(jnp.where(odd_row, has_above, has_below), diagonal_message[...], 0.0)
    products = jnp.zeros(first_products.shape, jnp.float32)
    for row in range(1, rows - 1):
        image = apply_operator([by_row[row - 1], by_row[row], by_row[row + 1]], weights_by_row[row])
        middle[row - 1] = image
        products = products + products_of(inner_parts(image))
    first_products[...] = products
    second_products[...] = images_of(
        lambda row: middle[row - 1],
        lambda row: weights_by_row[row],
        range(2, rows - 2),
        second,
        jnp.zeros(second_products.shape, jnp.float32),
    )


def outer_rows_kernel(
    by_row,
    weights_by_row,
    first_message,
    second_message,
    middle,
    first_products,
    second_products,
    second,
    grams,
    left_halo,
    right_halo,
    outer,
):
    rows, planes, width = by_row.shape
    odd_row, has_below, has_above = sides_of("row")
    one, other = first_message[: 2 * planes + 8], second_message[...]
    below = jnp.where(has_below, jnp.where(odd_row, other, one), 0.0)
    above = jnp.where(has_above, jnp.where(odd_row, one, other), 0.0)
    halos = [None, None]
    for side, (halo, present) in enumerate(
        ((below, jnp.logical_not(odd_row)), (above, odd_row))
    ):
        for slot in range(2):
            index = slot if side == 0 else rows + 2 + slot
            blank = jnp.zeros((8, width), jnp.float32)
            weight = halo[2 * planes :] if slot != side else blank
            row_values = jnp.concatenate([halo[slot * planes : (slot + 1) * planes], weight], axis=0)
            parts = edge_columns(row_values[:, :LANES], row_values[:, width - LANES :], PITCH * index)
            parts = [jnp.where(present, part, 0.0) for part in parts]
            halos = [part if total is None else total + part for total, part in zip(halos, parts)]
    left_halo[...], right_halo[...] = halos

    def field(row):
        if 0 <= row < rows:
            return by_row[row]
        at = (row + 2 if row < 0 else row - rows) * planes
        return (below if row < 0 else above)[at : at + planes]

    def weights(row):
        if 0 <= row < rows:
            return weights_by_row[row]
        return (below if row < 0 else above)[2 * planes :]

    products = first_products[...]
    places = (-1, 0, rows - 1, rows)
    for at, row in enumerate(places):
        image = apply_operator([field(row - 1), field(row), field(row + 1)], weights(row))
        outer[at] = image
        if 0 <= row < rows:
            products = products + products_of(inner_parts(image))
    both = [products]
    both.append(
        images_of(
            lambda row: outer[places.index(row)] if row in places else middle[row - 1],
            weights,
            (0, 1, rows - 2, rows - 1),
            second,
            second_products[...],
        )
    )
    for at, products in enumerate(both):
        some = products[:planes] + products[planes : 2 * planes] + products[2 * planes :]
        total = some[:, :planes] + some[:, planes : 2 * planes] + some[:, 2 * planes :]
        grams[:, at * planes : (at + 1) * planes] = total


def apply_on_strip(values, weights):
    total = jnp.sum(weights, axis=0, keepdims=True) * values
    for position, (up, across) in enumerate(NEIGHBOURS):
        moved = pltpu.roll(values, (-PITCH * up - across) % LANES, 1)
        total = total + weights[position : position + 1] * moved
    return total


def late_kernel(rows, left, right, left_halo, right_halo, *rest):
    diagonal_messages, col_messages, (early_grams, grams, edges) = rest[:2], rest[3:1:-1], rest[4:]
    planes = early_grams.shape[0]
    odd_row, has_below, has_above = sides_of("row")
    odd_col, has_left, has_right = sides_of("col")
    beyond = jnp.where(odd_row, has_above, has_below)
    one, other = (
        col[...] + jnp.where(beyond, diagonal[...], 0.0)
        for col, diagonal in zip(col_messages, diagonal_messages)
    )
    lane = lax.broadcasted_iota(jnp.int32, (1, LANES), 1)
    spot, row = lane % PITCH, lane // PITCH
    strips, masks = [], []
    for side, (strip, present, halo) in enumerate(
        (
            (left[...] + left_halo[...], has_left, jnp.where(odd_col, other, one)),
            (right[...] + right_halo[...], has_right, jnp.where(odd_col, one, other)),
        )
    ):
        strips.append(strip + jnp.where(present, unfolded(halo, side * (PITCH - 2), planes), 0.0))
        low = 2 if side == 0 else PITCH - 4
        masks.append((spot >= low) & (spot < low + 2) & (row >= 2) & (row < rows + 2))
    values = [strip[:planes] for strip in strips]
    gram = []
    for at in range(2):
        values = [apply_on_strip(value, strip[planes:]) for value, strip in zip(values, strips)]
        kept = jnp.concatenate([jnp.where(mask, value, 0.0) for mask, value in zip(masks, values)], axis=1)
        both = jnp.concatenate(values, axis=1)
        gram.append(early_grams[:, at * planes : (at + 1) * planes] + gram_of(kept, both))
    edges[...] = both
    at_row = lax.broadcasted_iota(jnp.int32, (planes, planes), 0)
    at_col = lax.broadcasted_iota(jnp.int32, (planes, planes), 1)
    mixed = jnp.where(at_row >= at_col, gram[0], gram[1])
    diagonal = jnp.sum(jnp.where(at_row == at_col, gram[1], 0.0), axis=0, keepdims=True)
    block = jnp.concatenate([mixed[8 * g : 8 * (g + 1)] for g in range(planes // 8)], axis=1)
    last = jnp.concatenate([diagonal] * (LANES // planes), axis=1)
    for target in range(grams.shape[0]):
        for at in range(8):
            grams[target, :, at * LANES : (at + 1) * LANES] = block[at : at + 1]
        grams[target, :, 8 * LANES :] = last


def eliminate(grams, planes, half_way):
    lane = lax.broadcasted_iota(jnp.int32, (8, LANES), 1)
    sub = lax.broadcasted_iota(jnp.int32, (8, LANES), 0)
    first_half = lane < 2 * planes
    groups = planes // 8
    sources = [[gram[8 * g : 8 * (g + 1)] for g in range(groups)] for gram in grams]
    state = []
    for g in range(groups):
        unit = jnp.where(sub + 8 * g == lane % (2 * planes) - planes, 1.0, 0.0)
        unit = unit[:, planes : 2 * planes]
        state.append(jnp.concatenate([sources[0][g], unit, sources[1][g], unit], axis=1))
    columns = []
    for j in range(planes):
        columns.append(
            {
                g: jnp.where(
                    first_half,
                    jnp.broadcast_to(sources[0][g][:, j : j + 1], (8, LANES)),
                    jnp.broadcast_to(sources[1][g][:, j : j + 1], (8, LANES)),
                )
                for g in range(j // 8, groups)
            }
        )
    scale = [jnp.ones((8, LANES), jnp.float32)] * groups
    for step in range(planes):
        own, at = step // 8, step % 8
        column = columns[step]
        pivot = jnp.broadcast_to(column[own][at : at + 1], (8, LANES))
        inverse, root = pl.reciprocal(pivot, approx=False), lax.rsqrt(pivot)
        scale[own] = jnp.where(sub == at, root, scale[own])
        left = {g: jnp.where(sub > at, value, 0.0) if g == own else value for g, value in column.items()}
        factors = {g: value * inverse for g, value in left.items()}
        for j in range(step + 1, planes):
            entry = jnp.broadcast_to(column[j // 8][j % 8 : j % 8 + 1], (8, LANES))
            for g in columns[j]:
                change = (left[g] * entry) * inverse if j == step + 1 else factors[g] * entry
                columns[j][g] = columns[j][g] - change
        pivot_row = jnp.broadcast_to(state[own][at : at + 1], (8, LANES))
        for g in range(own, groups):
            state[g] = state[g] - factors[g] * pivot_row
        if step + 1 == planes // 2:
            half_way(jnp.concatenate([state[g] * scale[g] for g in range(groups // 2)], axis=0))
    return jnp.concatenate([state[g] * scale[g] for g in range(groups)], axis=0)


def finish_kernel(
    pixel_count, inner_second, outer_second, edges, parts, basis_out, factor_out, basis, factor, written
):
    planes, rows, width = basis.shape
    half = planes // 2
    at_row = lax.broadcasted_iota(jnp.int32, (planes, planes), 0)
    at_col = lax.broadcasted_iota(jnp.int32, (planes, planes), 1)
    lane = lax.broadcasted_iota(jnp.int32, (1, LANES), 1)
    outer_parts = split(edges[...])
    copies = []

    def solve(inverse, start):
        stop = start + inverse.shape[0]
        high, middle, low = split(inverse)
        left_side = jnp.concatenate([high, high, middle, high, low, middle], axis=1)

        def solved(high, middle, low):
            right_side = jnp.concatenate([high, middle, high, low, high, middle], axis=0)
            return jnp.dot(left_side, right_side, preferred_element_type=jnp.float32)

        outer = solved(*(part[:stop] for part in outer_parts))
        for row in range(rows):
            if 2 <= row < rows - 2:
                held, spot = inner_second, row - 2
            else:
                held, spot = outer_second, row if row < 2 else row - rows + 4
            value = solved(*(held[spot, at * planes : at * planes + stop] for at in range(3)))
            place = PITCH * (row + 2)
            first = rolled(outer[:, :LANES], -(place + 2))
            last = rolled(outer[:, LANES:], LANES - 2 - (place + PITCH - 4))
            basis[start:stop, row, :LANES] = jnp.where(lane < 2, first, value[:, :LANES])
            basis[start:stop, row, LANES : width - LANES] = value[:, LANES : width - LANES]
            basis[start:stop, row, width - LANES :] = jnp.where(
                lane >= LANES - 2, last, value[:, width - LANES :]
            )
        some = pl.ds(start, stop - start)
        copies.append(pltpu.make_async_copy(basis.at[some], basis_out.at[some], written.at[len(copies)]))
        copies[-1].start()

    block = tree_sum([parts[at] for at in range(parts.shape[0])]) / pixel_count
    block = [block[:, at * LANES : (at + 1) * LANES] for at in range(9)]
    mixed, diagonal = jnp.concatenate(block[:8], axis=0), block[8][:, :planes]
    mixed = jnp.concatenate([mixed[:, at * planes : (at + 1) * planes] for at in range(LANES // planes)], axis=0)
    flipped = mixed.T
    first = jnp.where(at_row >= at_col, mixed, flipped)
    second = jnp.where(at_row < at_col, mixed, jnp.where(at_row > at_col, flipped, diagonal))
    low_half = (at_col <= at_row)[:half, :half]
    state = eliminate(
        [first, second],
        planes,
        lambda state: solve(jnp.where(low_half, state[:, 3 * planes : 3 * planes + half], 0.0), 0),
    )
    first_inverse = state[:, planes : 2 * planes]
    product_upper = jnp.where(at_col >= at_row, state[:, 2 * planes : 3 * planes], 0.0)
    solve(jnp.where(at_col <= at_row, state[:, 3 * planes :], 0.0)[half:], half)
    factor[...] = jnp.where(at_col >= at_row, gram_of(product_upper, first_inverse), 0.0)
    copies.append(pltpu.make_async_copy(factor, factor_out, written.at[2]))
    copies[-1].start()
    for copy in copies:
        copy.wait()


def tree_sum(parts):
    while len(parts) > 1:
        parts = [sum(parts[at + 1 : at + 2], parts[at]) for at in range(0, len(parts), 2)]
    return parts[0]


def swap(value, row_pairing=None, col_pairing=None):
    names = ("sec", "row", "col")
    shape = [lax.axis_size(name) for name in names]

    def partner(at, place, pairing):
        other = place if pairing is None else place + 1 if place % 2 != pairing else place - 1
        return other if 0 <= other < shape[at] else None

    pairs = []
    for sec, row, col in itertools.product(*(range(extent) for extent in shape)):
        other_row, other_col = partner(1, row, row_pairing), partner(2, col, col_pairing)
        if other_col is None:
            target = (sec, row ^ 1, col)
        elif other_row is None:
            target = (sec ^ 1, row, col)
        else:
            target = (sec, other_row, other_col)
        pairs.append(tuple((a * shape[1] + b) * shape[2] + c for a, b, c in ((sec, row, col), target)))
    return lax.ppermute(value, names, pairs)


def on_device(sketch, weights):
    planes, rows, width = sketch.shape
    group = lax.axis_size("row") * lax.axis_size("col")
    side = f32(planes + 8, LANES)
    by_row, weights_by_row, left, right, *messages = call(
        pack_rows_kernel,
        [f32(rows, planes, width), f32(rows, 8, width), side, side]
        + [f32(2 * planes + 16, width), f32(2 * planes + 8, width)]
        + [f32(16, LANES)] * 2,
        pltpu.with_memory_space_constraint(sketch, pltpu.HBM),
        pltpu.with_memory_space_constraint(weights, pltpu.HBM),
        memory=pltpu.HBM,
        scratch=[
            pltpu.VMEM(sketch.shape, jnp.float32),
            pltpu.VMEM(weights.shape, jnp.float32),
            pltpu.SemaphoreType.DMA((2,)),
        ],
    )
    from_rows = [swap(messages[at], row_pairing=at) for at in range(2)]
    from_diagonals = [swap(messages[2 + at], row_pairing=0, col_pairing=at) for at in range(2)]
    left, right, *messages = call(
        functools.partial(strips_kernel, rows), [side, side] + [f32(16, LANES)] * 2, left, right, from_rows[1]
    )
    from_cols = [swap(messages[1 - at], col_pairing=at) for at in (1, 0)]
    parts_of = functools.partial(jax.ShapeDtypeStruct, dtype=jnp.bfloat16)
    products = f32(3 * planes, 3 * planes)
    middle, inner_second, *inner_products, from_diagonals[1] = call(
        inner_rows_kernel,
        [f32(rows - 2, planes, width), parts_of((rows - 4, 3 * planes, width)), products, products]
        + [f32(16, LANES)],
        by_row,
        weights_by_row,
        from_diagonals[1],
        cost=pl.CostEstimate(flops=2000000000, bytes_accessed=4000000, transcendentals=0),
    )
    outer_second, early_grams, *halos = call(
        outer_rows_kernel,
        [parts_of((4, 3 * planes, width)), f32(planes, 2 * planes), side, side],
        by_row,
        weights_by_row,
        *from_rows,
        middle,
        *inner_products,
        scratch=[pltpu.VMEM((4, planes, width), jnp.float32)],
    )
    grams, edges = call(
        functools.partial(late_kernel, rows),
        [f32(group, 1, 9 * LANES), f32(planes, 2 * LANES)],
        left,
        right,
        *halos,
        *from_diagonals,
        *from_cols,
        early_grams,
    )
    rows_of, cols_of = lax.axis_size("row"), lax.axis_size("col")
    first = cols_of + cols_of // 2
    order = [first] + [row * cols_of + col for col in range(cols_of) for row in range(rows_of)]
    order = list(dict.fromkeys(order))
    parts = lax.all_to_all(grams, ("row", "col"), 0, 0, axis_index_groups=[order], tiled=True)
    return call(
        functools.partial(finish_kernel, float(rows * width * group)),
        [f32(planes, rows, width), f32(planes, planes)],
        inner_second,
        outer_second,
        edges,
        parts,
        out_memory=pl.ANY,
        scratch=[
            pltpu.VMEM(sketch.shape, jnp.float32),
            pltpu.VMEM((planes, planes), jnp.float32),
            pltpu.SemaphoreType.DMA((3,)),
        ],
    )


def solution(mesh):
    return jax.shard_map(
        on_device,
        mesh=mesh,
        in_specs=(P(None, ("sec", "row"), "col"), P(None, ("sec", "row"), "col")),
        out_specs=(P(None, ("sec", "row"), "col"), P("sec", None)),
        check_vma=False,
    )
```

```python
import functools
import itertools

import jax
import jax.numpy as jnp
from jax import lax
from jax.experimental import pallas as pl
from jax.experimental.pallas import tpu as pltpu
from jax.sharding import PartitionSpec as P

NEIGHBOURS = ((-1, -1), (-1, 0), (-1, 1), (0, -1), (0, 1), (1, -1), (1, 0), (1, 1))
LANES = 128
PITCH = 8
HIGHEST = lax.Precision.HIGHEST


def call(kernel, out_shapes, *operands, memory=pltpu.VMEM, out_memory=pltpu.VMEM, scratch=(), cost=None):
    return pl.pallas_call(
        kernel,
        out_shape=out_shapes,
        in_specs=[pl.BlockSpec(memory_space=memory)] * len(operands),
        out_specs=[pl.BlockSpec(memory_space=out_memory)] * len(out_shapes),
        scratch_shapes=scratch,
        cost_estimate=cost,
        compiler_params=pltpu.CompilerParams(vmem_limit_bytes=40 * 1024 * 1024),
    )(*operands)


def f32(*shape):
    return jax.ShapeDtypeStruct(shape, jnp.float32)


def sides_of(axis):
    place = lax.axis_index(axis)
    return place % 2 == 1, place > 0, place < lax.axis_size(axis) - 1


def edge_columns(first, last, place):
    lane = lax.broadcasted_iota(jnp.int32, (1, LANES), 1)
    own = PITCH - 2
    left = jnp.where((lane >= place + 2) & (lane < place + PITCH), pltpu.roll(first, place + 2, 1), 0.0)
    right = jnp.where((lane >= place) & (lane < place + own), pltpu.roll(last, place + own, 1), 0.0)
    return left, right


def pack_rows_kernel(sketch, weights, by_row, weights_by_row, left, right, *rest):
    bulk_messages, diagonal_messages = rest[:2], rest[2:4]
    tile, weight_tile, arrived = rest[4:]
    copies = [
        pltpu.make_async_copy(sketch, tile, arrived.at[0]),
        pltpu.make_async_copy(weights, weight_tile, arrived.at[1]),
    ]
    for copy in copies:
        copy.start()
    for copy in copies:
        copy.wait()
    rows, planes, width = by_row.shape
    odd_row, _, _ = sides_of("row")
    odd_col, _, _ = sides_of("col")
    lane = lax.broadcasted_iota(jnp.int32, (1, LANES), 1)
    for row in range(rows):
        weights_by_row[row] = weight_tile[:, row, :]
        by_row[row] = tile[:, row, :]
    for message, up in zip(bulk_messages, (odd_row, jnp.logical_not(odd_row))):
        start = jnp.where(up, rows - 2, 0)
        for slot in range(2):
            message[slot * planes : (slot + 1) * planes] = by_row[start + slot]
        message[2 * planes : 2 * planes + 8] = weights_by_row[jnp.where(up, rows - 1, 0)]
    strips = [None, None]
    for row in range(rows):
        first = jnp.concatenate([by_row[row, :, :LANES], weights_by_row[row, :, :LANES]], axis=0)
        last = jnp.concatenate([by_row[row, :, width - LANES :], weights_by_row[row, :, width - LANES :]], axis=0)
        parts = edge_columns(first, last, PITCH * (row + 2))
        strips = [part if strip is None else strip + part for strip, part in zip(strips, parts)]
    left[...], right[...] = strips
    bulk_messages[0][2 * planes + 8 :] = jnp.zeros((8, width), jnp.float32)
    pair = 2 * PITCH
    to_left, to_right = folded(strips[0], 2), folded(strips[1], PITCH - 4)
    for message, up in zip(diagonal_messages, (odd_col, jnp.logical_not(odd_col))):
        edge = jnp.where(up, to_right, to_left)
        below = jnp.where(lane < pair, rolled(edge, -PITCH * rows), 0.0)
        start = PITCH * (rows + 2)
        above = jnp.where((lane >= start) & (lane < start + pair), rolled(edge, PITCH * rows), 0.0)
        message[...] = jnp.where(odd_row, below, above)


def strips_kernel(rows, own_left, own_right, bulk_message, left, right, *col_messages):
    planes = own_left.shape[0] - 8
    odd_row, has_below, has_above = sides_of("row")
    odd_col, _, _ = sides_of("col")
    width = bulk_message.shape[1]
    totals = [own_left[...], own_right[...]]
    present = jnp.where(odd_row, has_below, has_above)
    for slot in range(2):
        place = PITCH * (slot + jnp.where(odd_row, 0, rows + 2))
        halo = [bulk_message[slot * planes : (slot + 1) * planes], bulk_message[2 * planes :]]
        first = jnp.concatenate([part[:, :LANES] for part in halo], axis=0)
        last = jnp.concatenate([part[:, width - LANES :] for part in halo], axis=0)
        parts = edge_columns(first, last, place)
        totals = [total + jnp.where(present, part, 0.0) for total, part in zip(totals, parts)]
    left[...], right[...] = totals
    to_left, to_right = folded(left[...], 2), folded(right[...], PITCH - 4)
    for message, up in zip(col_messages, (jnp.logical_not(odd_col), odd_col)):
        message[...] = jnp.where(up, to_right, to_left)


def folded(strip, spot):
    lane = lax.broadcasted_iota(jnp.int32, (1, LANES), 1)
    groups = strip.shape[0] // 8
    pieces = []
    for group in range(groups):
        target = 2 * group if group < groups - 1 else 0
        moved = rolled(strip[8 * group : 8 * (group + 1)], target - spot)
        pieces.append(jnp.where((lane % PITCH) // 2 == target // 2, moved, 0.0))
    return jnp.concatenate([functools.reduce(jnp.add, pieces[:-1]), pieces[-1]], axis=0)


def unfolded(message, spot, planes):
    lane = lax.broadcasted_iota(jnp.int32, (1, LANES), 1)
    pieces = [rolled(message[:8], spot - 2 * group) for group in range(planes // 8)] + [rolled(message[8:], spot)]
    return jnp.where((lane % PITCH) // 2 == spot // 2, jnp.concatenate(pieces, axis=0), 0.0)


def rolled(value, shift):
    return pltpu.roll(value, shift % LANES, 1) if shift % LANES else value


def apply_operator(rows3, weight_rows):
    width = rows3[1].shape[1]
    total = jnp.sum(weight_rows, axis=0, keepdims=True) * rows3[1]
    for across in (0, -1, 1):
        moved = pltpu.roll(weight_rows, across % width, 1) if across else weight_rows
        terms = [
            moved[position : position + 1] * rows3[up + 1]
            for position, (up, side) in enumerate(NEIGHBOURS)
            if side == across
        ]
        part = functools.reduce(jnp.add, terms)
        total = total + (pltpu.roll(part, -across % width, 1) if across else part)
    return total


def gram_of(value, other):
    return lax.dot_general(
        value, other, (((1,), (1,)), ((), ())), precision=HIGHEST, preferred_element_type=jnp.float32
    )


def split(value):
    high = value.astype(jnp.bfloat16)
    rest = value - high.astype(jnp.float32)
    middle = rest.astype(jnp.bfloat16)
    low = (rest - middle.astype(jnp.float32)).astype(jnp.bfloat16)
    return high, middle, low


def inner_parts(image):
    width = image.shape[1]
    lane = lax.broadcasted_iota(jnp.int32, (1, LANES), 1)
    kept = [
        jnp.where(lane >= 2, image[:, :LANES], 0.0),
        image[:, LANES : width - LANES],
        jnp.where(lane < LANES - 2, image[:, width - LANES :], 0.0),
    ]
    return jnp.concatenate(split(jnp.concatenate(kept, axis=1)), axis=0)


def products_of(parts):
    return lax.dot_general(parts, parts, (((1,), (1,)), ((), ())), preferred_element_type=jnp.float32)


def images_of(middle, weights, wanted, second, products):
    for at, row in enumerate(wanted):
        parts = inner_parts(apply_operator([middle(row - 1), middle(row), middle(row + 1)], weights(row)))
        second[at] = parts
        products = products + products_of(parts)
    return products


def side_rows(above, present, message, by_row, weights_by_row, middle, products):
    rows, planes, _ = by_row.shape

    def pick(high, low):
        return jnp.where(above, high, low)

    halo = jnp.where(present, message[: 2 * planes + 8], 0.0)
    one, other, halo_weights = halo[:planes], halo[planes : 2 * planes], halo[2 * planes :]
    near, far = pick(one, other), pick(other, one)
    edge, inside = pick(by_row[rows - 1], by_row[0]), pick(by_row[rows - 2], by_row[1])
    edge_weights = pick(weights_by_row[rows - 1], weights_by_row[0])
    inside_weights = pick(weights_by_row[rows - 2], weights_by_row[1])
    first_near = apply_operator([pick(edge, far), near, pick(far, edge)], halo_weights)
    first_edge = apply_operator([pick(inside, near), edge, pick(near, inside)], edge_weights)
    last = middle.shape[0] - 1
    first_inside, first_next = pick(middle[last], middle[0]), pick(middle[last - 1], middle[1])
    rows3 = [pick(first_inside, first_near), first_edge, pick(first_near, first_inside)]
    second_edge = inner_parts(apply_operator(rows3, edge_weights))
    rows3 = [pick(first_next, first_edge), first_inside, pick(first_edge, first_next)]
    second_inside = inner_parts(apply_operator(rows3, inside_weights))
    first, second = products
    first = first + products_of(inner_parts(first_edge))
    second = second + products_of(second_edge) + products_of(second_inside)
    return (second_edge, second_inside), (first, second)


def inner_rows_kernel(
    by_row, weights_by_row, diagonal_message, message, middle, second, side, first_products, second_products, diagonal
):
    rows = by_row.shape[0]
    odd_row, has_below, has_above = sides_of("row")
    diagonal[...] = jnp.where(jnp.where(odd_row, has_above, has_below), diagonal_message[...], 0.0)
    first = jnp.zeros(first_products.shape, jnp.float32)
    for row in range(1, rows - 1):
        image = apply_operator([by_row[row - 1], by_row[row], by_row[row + 1]], weights_by_row[row])
        middle[row - 1] = image
        first = first + products_of(inner_parts(image))
    products = first, images_of(
        lambda row: middle[row - 1],
        lambda row: weights_by_row[row],
        range(2, rows - 2),
        second,
        jnp.zeros(second_products.shape, jnp.float32),
    )
    above, present = jnp.logical_not(odd_row), jnp.where(odd_row, has_below, has_above)
    parts, products = side_rows(above, present, message, by_row, weights_by_row, middle, products)
    side[0], side[1] = parts
    first_products[...], second_products[...] = products


def outer_rows_kernel(
    by_row,
    weights_by_row,
    message,
    middle,
    side,
    first_products,
    second_products,
    second,
    grams,
    left_halo,
    right_halo,
):
    rows, planes, width = by_row.shape
    odd_row, has_below, has_above = sides_of("row")
    present = jnp.where(odd_row, has_above, has_below)
    halo = jnp.where(present, message[: 2 * planes + 8], 0.0)
    halos = [jnp.zeros(left_halo.shape, jnp.float32)] * 2
    for slot in range(2):
        place = PITCH * (slot + jnp.where(odd_row, rows + 2, 0))
        first = jnp.concatenate([halo[slot * planes : (slot + 1) * planes], halo[2 * planes :]], axis=0)
        parts = edge_columns(first[:, :LANES], first[:, width - LANES :], place)
        halos = [total + part for total, part in zip(halos, parts)]
    left_halo[...], right_halo[...] = halos
    products = first_products[...], second_products[...]
    parts, products = side_rows(odd_row, present, message, by_row, weights_by_row, middle, products)
    second[jnp.where(odd_row, 3, 0)], second[jnp.where(odd_row, 2, 1)] = parts
    second[jnp.where(odd_row, 0, 3)], second[jnp.where(odd_row, 1, 2)] = side[0], side[1]
    for at, both in enumerate(products):
        some = both[:planes] + both[planes : 2 * planes] + both[2 * planes :]
        total = some[:, :planes] + some[:, planes : 2 * planes] + some[:, 2 * planes :]
        grams[:, at * planes : (at + 1) * planes] = total


def apply_on_strip(values, weights):
    total = jnp.sum(weights, axis=0, keepdims=True) * values
    for position, (up, across) in enumerate(NEIGHBOURS):
        moved = pltpu.roll(values, (-PITCH * up - across) % LANES, 1)
        total = total + weights[position : position + 1] * moved
    return total


def late_kernel(rows, left, right, left_halo, right_halo, *rest):
    diagonal_messages, col_messages, (early_grams, grams, edges) = rest[:2], rest[3:1:-1], rest[4:]
    planes = early_grams.shape[0]
    odd_row, has_below, has_above = sides_of("row")
    odd_col, has_left, has_right = sides_of("col")
    beyond = jnp.where(odd_row, has_above, has_below)
    one, other = (
        col[...] + jnp.where(beyond, diagonal[...], 0.0)
        for col, diagonal in zip(col_messages, diagonal_messages)
    )
    lane = lax.broadcasted_iota(jnp.int32, (1, LANES), 1)
    spot, row = lane % PITCH, lane // PITCH
    strips, masks = [], []
    for side, (strip, present, halo) in enumerate(
        (
            (left[...] + left_halo[...], has_left, jnp.where(odd_col, other, one)),
            (right[...] + right_halo[...], has_right, jnp.where(odd_col, one, other)),
        )
    ):
        strips.append(strip + jnp.where(present, unfolded(halo, side * (PITCH - 2), planes), 0.0))
        low = 2 if side == 0 else PITCH - 4
        masks.append((spot >= low) & (spot < low + 2) & (row >= 2) & (row < rows + 2))
    values = [strip[:planes] for strip in strips]
    gram = []
    for at in range(2):
        values = [apply_on_strip(value, strip[planes:]) for value, strip in zip(values, strips)]
        kept = jnp.concatenate([jnp.where(mask, value, 0.0) for mask, value in zip(masks, values)], axis=1)
        both = jnp.concatenate(values, axis=1)
        gram.append(early_grams[:, at * planes : (at + 1) * planes] + gram_of(kept, both))
    edges[...] = both
    at_row = lax.broadcasted_iota(jnp.int32, (planes, planes), 0)
    at_col = lax.broadcasted_iota(jnp.int32, (planes, planes), 1)
    mixed = jnp.where(at_row >= at_col, gram[0], gram[1])
    diagonal = jnp.sum(jnp.where(at_row == at_col, gram[1], 0.0), axis=0, keepdims=True)
    block = jnp.concatenate([mixed[8 * g : 8 * (g + 1)] for g in range(planes // 8)], axis=1)
    last = jnp.concatenate([diagonal] * (LANES // planes), axis=1)
    for target in range(grams.shape[0]):
        for at in range(8):
            grams[target, :, at * LANES : (at + 1) * LANES] = block[at : at + 1]
        grams[target, :, 8 * LANES :] = last


def eliminate(grams, planes, half_way):
    lane = lax.broadcasted_iota(jnp.int32, (8, LANES), 1)
    sub = lax.broadcasted_iota(jnp.int32, (8, LANES), 0)
    first_half = lane < 2 * planes
    groups = planes // 8
    sources = [[gram[8 * g : 8 * (g + 1)] for g in range(groups)] for gram in grams]
    state = []
    for g in range(groups):
        unit = jnp.where(sub + 8 * g == lane % (2 * planes) - planes, 1.0, 0.0)
        unit = unit[:, planes : 2 * planes]
        state.append(jnp.concatenate([sources[0][g], unit, sources[1][g], unit], axis=1))
    columns = []
    for j in range(planes):
        columns.append(
            {
                g: jnp.where(
                    first_half,
                    jnp.broadcast_to(sources[0][g][:, j : j + 1], (8, LANES)),
                    jnp.broadcast_to(sources[1][g][:, j : j + 1], (8, LANES)),
                )
                for g in range(j // 8, groups)
            }
        )
    scale = [jnp.ones((8, LANES), jnp.float32)] * groups
    for step in range(planes):
        own, at = step // 8, step % 8
        column = columns[step]
        pivot = jnp.broadcast_to(column[own][at : at + 1], (8, LANES))
        inverse, root = pl.reciprocal(pivot, approx=False), lax.rsqrt(pivot)
        scale[own] = jnp.where(sub == at, root, scale[own])
        left = {g: jnp.where(sub > at, value, 0.0) if g == own else value for g, value in column.items()}
        factors = {g: value * inverse for g, value in left.items()}
        for j in range(step + 1, planes):
            entry = jnp.broadcast_to(column[j // 8][j % 8 : j % 8 + 1], (8, LANES))
            for g in columns[j]:
                change = (left[g] * entry) * inverse if j == step + 1 else factors[g] * entry
                columns[j][g] = columns[j][g] - change
        pivot_row = jnp.broadcast_to(state[own][at : at + 1], (8, LANES))
        for g in range(own, groups):
            state[g] = state[g] - factors[g] * pivot_row
        if step + 1 == planes // 2:
            half_way(jnp.concatenate([state[g] * scale[g] for g in range(groups // 2)], axis=0))
    return jnp.concatenate([state[g] * scale[g] for g in range(groups)], axis=0)


def finish_kernel(
    pixel_count, inner_second, outer_second, edges, parts, basis_out, factor_out, basis, factor, written
):
    planes, rows, width = basis.shape
    half = planes // 2
    at_row = lax.broadcasted_iota(jnp.int32, (planes, planes), 0)
    at_col = lax.broadcasted_iota(jnp.int32, (planes, planes), 1)
    lane = lax.broadcasted_iota(jnp.int32, (1, LANES), 1)
    outer_parts = split(edges[...])
    copies = []

    def solve(inverse, start):
        stop = start + inverse.shape[0]
        high, middle, low = split(inverse)
        left_side = jnp.concatenate([high, high, middle, high, low, middle], axis=1)

        def solved(high, middle, low):
            right_side = jnp.concatenate([high, middle, high, low, high, middle], axis=0)
            return jnp.dot(left_side, right_side, preferred_element_type=jnp.float32)

        outer = solved(*(part[:stop] for part in outer_parts))
        for row in range(rows):
            if 2 <= row < rows - 2:
                held, spot = inner_second, row - 2
            else:
                held, spot = outer_second, row if row < 2 else row - rows + 4
            value = solved(*(held[spot, at * planes : at * planes + stop] for at in range(3)))
            place = PITCH * (row + 2)
            first = rolled(outer[:, :LANES], -(place + 2))
            last = rolled(outer[:, LANES:], LANES - 2 - (place + PITCH - 4))
            basis[start:stop, row, :LANES] = jnp.where(lane < 2, first, value[:, :LANES])
            basis[start:stop, row, LANES : width - LANES] = value[:, LANES : width - LANES]
            basis[start:stop, row, width - LANES :] = jnp.where(
                lane >= LANES - 2, last, value[:, width - LANES :]
            )
        some = pl.ds(start, stop - start)
        copies.append(pltpu.make_async_copy(basis.at[some], basis_out.at[some], written.at[len(copies)]))
        copies[-1].start()

    block = tree_sum([parts[at] for at in range(parts.shape[0])]) / pixel_count
    block = [block[:, at * LANES : (at + 1) * LANES] for at in range(9)]
    mixed, diagonal = jnp.concatenate(block[:8], axis=0), block[8][:, :planes]
    mixed = jnp.concatenate([mixed[:, at * planes : (at + 1) * planes] for at in range(LANES // planes)], axis=0)
    flipped = mixed.T
    first = jnp.where(at_row >= at_col, mixed, flipped)
    second = jnp.where(at_row < at_col, mixed, jnp.where(at_row > at_col, flipped, diagonal))
    low_half = (at_col <= at_row)[:half, :half]
    state = eliminate(
        [first, second],
        planes,
        lambda state: solve(jnp.where(low_half, state[:, 3 * planes : 3 * planes + half], 0.0), 0),
    )
    first_inverse = state[:, planes : 2 * planes]
    product_upper = jnp.where(at_col >= at_row, state[:, 2 * planes : 3 * planes], 0.0)
    solve(jnp.where(at_col <= at_row, state[:, 3 * planes :], 0.0)[half:], half)
    factor[...] = jnp.where(at_col >= at_row, gram_of(product_upper, first_inverse), 0.0)
    copies.append(pltpu.make_async_copy(factor, factor_out, written.at[2]))
    copies[-1].start()
    for copy in copies:
        copy.wait()


def tree_sum(parts):
    while len(parts) > 1:
        parts = [sum(parts[at + 1 : at + 2], parts[at]) for at in range(0, len(parts), 2)]
    return parts[0]


def swap(value, row_pairing=None, col_pairing=None):
    names = ("sec", "row", "col")
    shape = [lax.axis_size(name) for name in names]

    def partner(at, place, pairing):
        other = place if pairing is None else place + 1 if place % 2 != pairing else place - 1
        return other if 0 <= other < shape[at] else None

    pairs = []
    for sec, row, col in itertools.product(*(range(extent) for extent in shape)):
        other_row, other_col = partner(1, row, row_pairing), partner(2, col, col_pairing)
        if other_col is None:
            target = (sec, row ^ 1, col)
        elif other_row is None:
            target = (sec ^ 1, row, col)
        else:
            target = (sec, other_row, other_col)
        pairs.append(tuple((a * shape[1] + b) * shape[2] + c for a, b, c in ((sec, row, col), target)))
    return lax.ppermute(value, names, pairs)


def on_device(sketch, weights):
    planes, rows, width = sketch.shape
    group = lax.axis_size("row") * lax.axis_size("col")
    side = f32(planes + 8, LANES)
    by_row, weights_by_row, left, right, *messages = call(
        pack_rows_kernel,
        [f32(rows, planes, width), f32(rows, 8, width), side, side]
        + [f32(2 * planes + 16, width), f32(2 * planes + 8, width)]
        + [f32(16, LANES)] * 2,
        pltpu.with_memory_space_constraint(sketch, pltpu.HBM),
        pltpu.with_memory_space_constraint(weights, pltpu.HBM),
        memory=pltpu.HBM,
        scratch=[
            pltpu.VMEM(sketch.shape, jnp.float32),
            pltpu.VMEM(weights.shape, jnp.float32),
            pltpu.SemaphoreType.DMA((2,)),
        ],
    )
    from_rows = [swap(messages[at], row_pairing=at) for at in range(2)]
    from_diagonals = [swap(messages[2 + at], row_pairing=0, col_pairing=at) for at in range(2)]
    left, right, *messages = call(
        functools.partial(strips_kernel, rows), [side, side] + [f32(16, LANES)] * 2, left, right, from_rows[1]
    )
    from_cols = [swap(messages[1 - at], col_pairing=at) for at in (1, 0)]
    parts_of = functools.partial(jax.ShapeDtypeStruct, dtype=jnp.bfloat16)
    products = f32(3 * planes, 3 * planes)
    middle, inner_second, side_second, *inner_products, from_diagonals[1] = call(
        inner_rows_kernel,
        [f32(rows - 2, planes, width), parts_of((rows - 4, 3 * planes, width)), parts_of((2, 3 * planes, width))]
        + [products, products, f32(16, LANES)],
        by_row,
        weights_by_row,
        from_diagonals[1],
        from_rows[1],
        cost=pl.CostEstimate(flops=400000000, bytes_accessed=800000, transcendentals=0),
    )
    outer_second, early_grams, *halos = call(
        outer_rows_kernel,
        [parts_of((4, 3 * planes, width)), f32(planes, 2 * planes), side, side],
        by_row,
        weights_by_row,
        from_rows[0],
        middle,
        side_second,
        *inner_products,
    )
    grams, edges = call(
        functools.partial(late_kernel, rows),
        [f32(group, 1, 9 * LANES), f32(planes, 2 * LANES)],
        left,
        right,
        *halos,
        *from_diagonals,
        *from_cols,
        early_grams,
    )
    rows_of, cols_of = lax.axis_size("row"), lax.axis_size("col")
    first = cols_of + cols_of // 2
    order = [first] + [row * cols_of + col for col in range(cols_of) for row in range(rows_of)]
    order = list(dict.fromkeys(order))
    parts = lax.all_to_all(grams, ("row", "col"), 0, 0, axis_index_groups=[order], tiled=True)
    return call(
        functools.partial(finish_kernel, float(rows * width * group)),
        [f32(planes, rows, width), f32(planes, planes)],
        inner_second,
        outer_second,
        edges,
        parts,
        out_memory=pl.ANY,
        scratch=[
            pltpu.VMEM(sketch.shape, jnp.float32),
            pltpu.VMEM((planes, planes), jnp.float32),
            pltpu.SemaphoreType.DMA((3,)),
        ],
    )


def solution(mesh):
    return jax.shard_map(
        on_device,
        mesh=mesh,
        in_specs=(P(None, ("sec", "row"), "col"), P(None, ("sec", "row"), "col")),
        out_specs=(P(None, ("sec", "row"), "col"), P("sec", None)),
        check_vma=False,
    )
```

```python
import functools
import itertools

import jax
import jax.numpy as jnp
from jax import lax
from jax.experimental import pallas as pl
from jax.experimental.pallas import tpu as pltpu
from jax.sharding import PartitionSpec as P

NEIGHBOURS = ((-1, -1), (-1, 0), (-1, 1), (0, -1), (0, 1), (1, -1), (1, 0), (1, 1))
LANES = 128
PITCH = 8
HIGHEST = lax.Precision.HIGHEST


def call(kernel, out_shapes, *operands, memory=pltpu.VMEM, out_memory=pltpu.VMEM, scratch=(), cost=None):
    return pl.pallas_call(
        kernel,
        out_shape=out_shapes,
        in_specs=[pl.BlockSpec(memory_space=memory)] * len(operands),
        out_specs=[pl.BlockSpec(memory_space=out_memory)] * len(out_shapes),
        scratch_shapes=scratch,
        cost_estimate=cost,
        compiler_params=pltpu.CompilerParams(vmem_limit_bytes=40 * 1024 * 1024),
    )(*operands)


def f32(*shape):
    return jax.ShapeDtypeStruct(shape, jnp.float32)


def sides_of(axis):
    place = lax.axis_index(axis)
    return place % 2 == 1, place > 0, place < lax.axis_size(axis) - 1


def edge_columns(first, last, place):
    lane = lax.broadcasted_iota(jnp.int32, (1, LANES), 1)
    own = PITCH - 2
    left = jnp.where((lane >= place + 2) & (lane < place + PITCH), pltpu.roll(first, place + 2, 1), 0.0)
    right = jnp.where((lane >= place) & (lane < place + own), pltpu.roll(last, place + own, 1), 0.0)
    return left, right


def pack_rows_kernel(sketch, weights, by_row, weights_by_row, left, right, *rest):
    bulk_messages, diagonal_messages = rest[:2], rest[2:4]
    tile, weight_tile, arrived = rest[4:]
    copies = [
        pltpu.make_async_copy(sketch, tile, arrived.at[0]),
        pltpu.make_async_copy(weights, weight_tile, arrived.at[1]),
    ]
    for copy in copies:
        copy.start()
    for copy in copies:
        copy.wait()
    rows, planes, width = by_row.shape
    odd_row, _, _ = sides_of("row")
    odd_col, _, _ = sides_of("col")
    lane = lax.broadcasted_iota(jnp.int32, (1, LANES), 1)
    for row in range(rows):
        weights_by_row[row] = weight_tile[:, row, :]
        by_row[row] = tile[:, row, :]
    for message, up in zip(bulk_messages, (odd_row, jnp.logical_not(odd_row))):
        start = jnp.where(up, rows - 2, 0)
        for slot in range(2):
            message[slot * planes : (slot + 1) * planes] = by_row[start + slot]
        message[2 * planes : 2 * planes + 8] = weights_by_row[jnp.where(up, rows - 1, 0)]
    strips = [None, None]
    for row in range(rows):
        first = jnp.concatenate([by_row[row, :, :LANES], weights_by_row[row, :, :LANES]], axis=0)
        last = jnp.concatenate([by_row[row, :, width - LANES :], weights_by_row[row, :, width - LANES :]], axis=0)
        parts = edge_columns(first, last, PITCH * (row + 2))
        strips = [part if strip is None else strip + part for strip, part in zip(strips, parts)]
    left[...], right[...] = strips
    bulk_messages[0][2 * planes + 8 :] = jnp.zeros((8, width), jnp.float32)
    pair = 2 * PITCH
    to_left, to_right = folded(strips[0], 2), folded(strips[1], PITCH - 4)
    for message, up in zip(diagonal_messages, (odd_col, jnp.logical_not(odd_col))):
        edge = jnp.where(up, to_right, to_left)
        below = jnp.where(lane < pair, rolled(edge, -PITCH * rows), 0.0)
        start = PITCH * (rows + 2)
        above = jnp.where((lane >= start) & (lane < start + pair), rolled(edge, PITCH * rows), 0.0)
        message[...] = jnp.where(odd_row, below, above)


def strips_kernel(rows, own_left, own_right, bulk_message, left, right, *col_messages):
    planes = own_left.shape[0] - 8
    odd_row, has_below, has_above = sides_of("row")
    odd_col, _, _ = sides_of("col")
    width = bulk_message.shape[1]
    totals = [own_left[...], own_right[...]]
    present = jnp.where(odd_row, has_below, has_above)
    for slot in range(2):
        place = PITCH * (slot + jnp.where(odd_row, 0, rows + 2))
        halo = [bulk_message[slot * planes : (slot + 1) * planes], bulk_message[2 * planes :]]
        first = jnp.concatenate([part[:, :LANES] for part in halo], axis=0)
        last = jnp.concatenate([part[:, width - LANES :] for part in halo], axis=0)
        parts = edge_columns(first, last, place)
        totals = [total + jnp.where(present, part, 0.0) for total, part in zip(totals, parts)]
    left[...], right[...] = totals
    to_left, to_right = folded(left[...], 2), folded(right[...], PITCH - 4)
    for message, up in zip(col_messages, (odd_col, jnp.logical_not(odd_col))):
        message[...] = jnp.where(up, to_right, to_left)


def folded(strip, spot):
    lane = lax.broadcasted_iota(jnp.int32, (1, LANES), 1)
    groups = strip.shape[0] // 8
    pieces = []
    for group in range(groups):
        target = 2 * group if group < groups - 1 else 0
        moved = rolled(strip[8 * group : 8 * (group + 1)], target - spot)
        pieces.append(jnp.where((lane % PITCH) // 2 == target // 2, moved, 0.0))
    return jnp.concatenate([functools.reduce(jnp.add, pieces[:-1]), pieces[-1]], axis=0)


def unfolded(message, spot, planes):
    lane = lax.broadcasted_iota(jnp.int32, (1, LANES), 1)
    pieces = [rolled(message[:8], spot - 2 * group) for group in range(planes // 8)] + [rolled(message[8:], spot)]
    return jnp.where((lane % PITCH) // 2 == spot // 2, jnp.concatenate(pieces, axis=0), 0.0)


def rolled(value, shift):
    return pltpu.roll(value, shift % LANES, 1) if shift % LANES else value


def apply_operator(rows3, weight_rows):
    width = rows3[1].shape[1]
    total = jnp.sum(weight_rows, axis=0, keepdims=True) * rows3[1]
    for across in (0, -1, 1):
        moved = pltpu.roll(weight_rows, across % width, 1) if across else weight_rows
        terms = [
            moved[position : position + 1] * rows3[up + 1]
            for position, (up, side) in enumerate(NEIGHBOURS)
            if side == across
        ]
        part = functools.reduce(jnp.add, terms)
        total = total + (pltpu.roll(part, -across % width, 1) if across else part)
    return total


def gram_of(value, other):
    return lax.dot_general(
        value, other, (((1,), (1,)), ((), ())), precision=HIGHEST, preferred_element_type=jnp.float32
    )


def split(value):
    high = value.astype(jnp.bfloat16)
    rest = value - high.astype(jnp.float32)
    middle = rest.astype(jnp.bfloat16)
    low = (rest - middle.astype(jnp.float32)).astype(jnp.bfloat16)
    return high, middle, low


def inner_parts(image):
    width = image.shape[1]
    lane = lax.broadcasted_iota(jnp.int32, (1, LANES), 1)
    kept = [
        jnp.where(lane >= 2, image[:, :LANES], 0.0),
        image[:, LANES : width - LANES],
        jnp.where(lane < LANES - 2, image[:, width - LANES :], 0.0),
    ]
    return jnp.concatenate(split(jnp.concatenate(kept, axis=1)), axis=0)


def products_of(parts):
    return lax.dot_general(parts, parts, (((1,), (1,)), ((), ())), preferred_element_type=jnp.float32)


def images_of(middle, weights, wanted, second, products):
    for at, row in enumerate(wanted):
        parts = inner_parts(apply_operator([middle(row - 1), middle(row), middle(row + 1)], weights(row)))
        second[at] = parts
        products = products + products_of(parts)
    return products


def side_rows(above, present, message, by_row, weights_by_row, middle, products):
    rows, planes, _ = by_row.shape

    def pick(high, low):
        return jnp.where(above, high, low)

    halo = jnp.where(present, message[: 2 * planes + 8], 0.0)
    one, other, halo_weights = halo[:planes], halo[planes : 2 * planes], halo[2 * planes :]
    near, far = pick(one, other), pick(other, one)
    edge, inside = pick(by_row[rows - 1], by_row[0]), pick(by_row[rows - 2], by_row[1])
    edge_weights = pick(weights_by_row[rows - 1], weights_by_row[0])
    inside_weights = pick(weights_by_row[rows - 2], weights_by_row[1])
    first_near = apply_operator([pick(edge, far), near, pick(far, edge)], halo_weights)
    first_edge = apply_operator([pick(inside, near), edge, pick(near, inside)], edge_weights)
    last = middle.shape[0] - 1
    first_inside, first_next = pick(middle[last], middle[0]), pick(middle[last - 1], middle[1])
    rows3 = [pick(first_inside, first_near), first_edge, pick(first_near, first_inside)]
    second_edge = inner_parts(apply_operator(rows3, edge_weights))
    rows3 = [pick(first_next, first_edge), first_inside, pick(first_edge, first_next)]
    second_inside = inner_parts(apply_operator(rows3, inside_weights))
    first, second = products
    first = first + products_of(inner_parts(first_edge))
    second = second + products_of(second_edge) + products_of(second_inside)
    return (second_edge, second_inside), (first, second)


def inner_rows_kernel(
    by_row, weights_by_row, diagonal_message, message, middle, second, side, first_products, second_products, diagonal
):
    rows = by_row.shape[0]
    odd_row, has_below, has_above = sides_of("row")
    diagonal[...] = jnp.where(jnp.where(odd_row, has_above, has_below), diagonal_message[...], 0.0)
    first = jnp.zeros(first_products.shape, jnp.float32)
    for row in range(1, rows - 1):
        image = apply_operator([by_row[row - 1], by_row[row], by_row[row + 1]], weights_by_row[row])
        middle[row - 1] = image
        first = first + products_of(inner_parts(image))
    products = first, images_of(
        lambda row: middle[row - 1],
        lambda row: weights_by_row[row],
        range(2, rows - 2),
        second,
        jnp.zeros(second_products.shape, jnp.float32),
    )
    above, present = jnp.logical_not(odd_row), jnp.where(odd_row, has_below, has_above)
    parts, products = side_rows(above, present, message, by_row, weights_by_row, middle, products)
    side[0], side[1] = parts
    first_products[...], second_products[...] = products


def outer_rows_kernel(
    by_row,
    weights_by_row,
    message,
    middle,
    side,
    first_products,
    second_products,
    second,
    grams,
    left_halo,
    right_halo,
):
    rows, planes, width = by_row.shape
    odd_row, has_below, has_above = sides_of("row")
    present = jnp.where(odd_row, has_above, has_below)
    halo = jnp.where(present, message[: 2 * planes + 8], 0.0)
    halos = [jnp.zeros(left_halo.shape, jnp.float32)] * 2
    for slot in range(2):
        place = PITCH * (slot + jnp.where(odd_row, rows + 2, 0))
        first = jnp.concatenate([halo[slot * planes : (slot + 1) * planes], halo[2 * planes :]], axis=0)
        parts = edge_columns(first[:, :LANES], first[:, width - LANES :], place)
        halos = [total + part for total, part in zip(halos, parts)]
    left_halo[...], right_halo[...] = halos
    products = first_products[...], second_products[...]
    parts, products = side_rows(odd_row, present, message, by_row, weights_by_row, middle, products)
    second[jnp.where(odd_row, 3, 0)], second[jnp.where(odd_row, 2, 1)] = parts
    second[jnp.where(odd_row, 0, 3)], second[jnp.where(odd_row, 1, 2)] = side[0], side[1]
    for at, both in enumerate(products):
        some = both[:planes] + both[planes : 2 * planes] + both[2 * planes :]
        total = some[:, :planes] + some[:, planes : 2 * planes] + some[:, 2 * planes :]
        grams[:, at * planes : (at + 1) * planes] = total


def apply_on_strip(values, weights):
    total = jnp.sum(weights, axis=0, keepdims=True) * values
    for position, (up, across) in enumerate(NEIGHBOURS):
        moved = pltpu.roll(values, (-PITCH * up - across) % LANES, 1)
        total = total + weights[position : position + 1] * moved
    return total


def late_kernel(rows, left, right, left_halo, right_halo, *rest):
    diagonal_messages, col_messages, (early_grams, grams, edges) = rest[:2], rest[2:4], rest[4:]
    planes = early_grams.shape[0]
    odd_row, has_below, has_above = sides_of("row")
    odd_col, has_left, has_right = sides_of("col")
    beyond = jnp.where(odd_row, has_above, has_below)
    one, other = (
        col[...] + jnp.where(beyond, diagonal[...], 0.0)
        for col, diagonal in zip(col_messages, diagonal_messages)
    )
    lane = lax.broadcasted_iota(jnp.int32, (1, LANES), 1)
    spot, row = lane % PITCH, lane // PITCH
    strips, masks = [], []
    for side, (strip, present, halo) in enumerate(
        (
            (left[...] + left_halo[...], has_left, jnp.where(odd_col, other, one)),
            (right[...] + right_halo[...], has_right, jnp.where(odd_col, one, other)),
        )
    ):
        strips.append(strip + jnp.where(present, unfolded(halo, side * (PITCH - 2), planes), 0.0))
        low = 2 if side == 0 else PITCH - 4
        masks.append((spot >= low) & (spot < low + 2) & (row >= 2) & (row < rows + 2))
    values = [strip[:planes] for strip in strips]
    gram = []
    for at in range(2):
        values = [apply_on_strip(value, strip[planes:]) for value, strip in zip(values, strips)]
        kept = jnp.concatenate([jnp.where(mask, value, 0.0) for mask, value in zip(masks, values)], axis=1)
        both = jnp.concatenate(values, axis=1)
        gram.append(early_grams[:, at * planes : (at + 1) * planes] + gram_of(kept, both))
    edges[...] = both
    at_row = lax.broadcasted_iota(jnp.int32, (planes, planes), 0)
    at_col = lax.broadcasted_iota(jnp.int32, (planes, planes), 1)
    mixed = jnp.where(at_row >= at_col, gram[0], gram[1])
    diagonal = jnp.sum(jnp.where(at_row == at_col, gram[1], 0.0), axis=0, keepdims=True)
    block = jnp.concatenate([mixed[8 * g : 8 * (g + 1)] for g in range(planes // 8)], axis=1)
    last = jnp.concatenate([diagonal] * (LANES // planes), axis=1)
    for target in range(grams.shape[0]):
        for at in range(8):
            grams[target, :, at * LANES : (at + 1) * LANES] = block[at : at + 1]
        grams[target, :, 8 * LANES :] = last


def eliminate(grams, planes, half_way):
    lane = lax.broadcasted_iota(jnp.int32, (8, LANES), 1)
    sub = lax.broadcasted_iota(jnp.int32, (8, LANES), 0)
    first_half = lane < 2 * planes
    groups = planes // 8
    sources = [[gram[8 * g : 8 * (g + 1)] for g in range(groups)] for gram in grams]
    state = []
    for g in range(groups):
        unit = jnp.where(sub + 8 * g == lane % (2 * planes) - planes, 1.0, 0.0)
        unit = unit[:, planes : 2 * planes]
        state.append(jnp.concatenate([sources[0][g], unit, sources[1][g], unit], axis=1))
    columns = []
    for j in range(planes):
        columns.append(
            {
                g: jnp.where(
                    first_half,
                    jnp.broadcast_to(sources[0][g][:, j : j + 1], (8, LANES)),
                    jnp.broadcast_to(sources[1][g][:, j : j + 1], (8, LANES)),
                )
                for g in range(j // 8, groups)
            }
        )
    scale = [jnp.ones((8, LANES), jnp.float32)] * groups
    for step in range(planes):
        own, at = step // 8, step % 8
        column = columns[step]
        pivot = jnp.broadcast_to(column[own][at : at + 1], (8, LANES))
        inverse, root = pl.reciprocal(pivot, approx=False), lax.rsqrt(pivot)
        scale[own] = jnp.where(sub == at, root, scale[own])
        left = {g: jnp.where(sub > at, value, 0.0) if g == own else value for g, value in column.items()}
        factors = {g: value * inverse for g, value in left.items()}
        for j in range(step + 1, planes):
            entry = jnp.broadcast_to(column[j // 8][j % 8 : j % 8 + 1], (8, LANES))
            for g in columns[j]:
                change = (left[g] * entry) * inverse if j == step + 1 else factors[g] * entry
                columns[j][g] = columns[j][g] - change
        pivot_row = jnp.broadcast_to(state[own][at : at + 1], (8, LANES))
        for g in range(own, groups):
            state[g] = state[g] - factors[g] * pivot_row
        if step + 1 == planes // 2:
            half_way(jnp.concatenate([state[g] * scale[g] for g in range(groups // 2)], axis=0))
    return jnp.concatenate([state[g] * scale[g] for g in range(groups)], axis=0)


def finish_kernel(
    pixel_count, inner_second, outer_second, edges, parts, basis_out, factor_out, basis, factor, written
):
    planes, rows, width = basis.shape
    half = planes // 2
    at_row = lax.broadcasted_iota(jnp.int32, (planes, planes), 0)
    at_col = lax.broadcasted_iota(jnp.int32, (planes, planes), 1)
    lane = lax.broadcasted_iota(jnp.int32, (1, LANES), 1)
    outer_parts = split(edges[...])
    copies = []

    def solve(inverse, start):
        stop = start + inverse.shape[0]
        high, middle, low = split(inverse)
        left_side = jnp.concatenate([high, high, middle, high, low, middle], axis=1)

        def solved(high, middle, low):
            right_side = jnp.concatenate([high, middle, high, low, high, middle], axis=0)
            return jnp.dot(left_side, right_side, preferred_element_type=jnp.float32)

        outer = solved(*(part[:stop] for part in outer_parts))
        for row in range(rows):
            if 2 <= row < rows - 2:
                held, spot = inner_second, row - 2
            else:
                held, spot = outer_second, row if row < 2 else row - rows + 4
            value = solved(*(held[spot, at * planes : at * planes + stop] for at in range(3)))
            place = PITCH * (row + 2)
            first = rolled(outer[:, :LANES], -(place + 2))
            last = rolled(outer[:, LANES:], LANES - 2 - (place + PITCH - 4))
            basis[start:stop, row, :LANES] = jnp.where(lane < 2, first, value[:, :LANES])
            basis[start:stop, row, LANES : width - LANES] = value[:, LANES : width - LANES]
            basis[start:stop, row, width - LANES :] = jnp.where(
                lane >= LANES - 2, last, value[:, width - LANES :]
            )
        some = pl.ds(start, stop - start)
        copies.append(pltpu.make_async_copy(basis.at[some], basis_out.at[some], written.at[len(copies)]))
        copies[-1].start()

    block = tree_sum([parts[at] for at in range(parts.shape[0])]) / pixel_count
    block = [block[:, at * LANES : (at + 1) * LANES] for at in range(9)]
    mixed, diagonal = jnp.concatenate(block[:8], axis=0), block[8][:, :planes]
    mixed = jnp.concatenate([mixed[:, at * planes : (at + 1) * planes] for at in range(LANES // planes)], axis=0)
    flipped = mixed.T
    first = jnp.where(at_row >= at_col, mixed, flipped)
    second = jnp.where(at_row < at_col, mixed, jnp.where(at_row > at_col, flipped, diagonal))
    low_half = (at_col <= at_row)[:half, :half]
    state = eliminate(
        [first, second],
        planes,
        lambda state: solve(jnp.where(low_half, state[:, 3 * planes : 3 * planes + half], 0.0), 0),
    )
    first_inverse = state[:, planes : 2 * planes]
    product_upper = jnp.where(at_col >= at_row, state[:, 2 * planes : 3 * planes], 0.0)
    solve(jnp.where(at_col <= at_row, state[:, 3 * planes :], 0.0)[half:], half)
    factor[...] = jnp.where(at_col >= at_row, gram_of(product_upper, first_inverse), 0.0)
    copies.append(pltpu.make_async_copy(factor, factor_out, written.at[2]))
    copies[-1].start()
    for copy in copies:
        copy.wait()


def tree_sum(parts):
    while len(parts) > 1:
        parts = [sum(parts[at + 1 : at + 2], parts[at]) for at in range(0, len(parts), 2)]
    return parts[0]


def swap(value, row_pairing=None, col_pairing=None):
    names = ("sec", "row", "col")
    shape = [lax.axis_size(name) for name in names]

    def partner(at, place, pairing):
        other = place if pairing is None else place + 1 if place % 2 != pairing else place - 1
        return other if 0 <= other < shape[at] else None

    pairs = []
    for sec, row, col in itertools.product(*(range(extent) for extent in shape)):
        other_row, other_col = partner(1, row, row_pairing), partner(2, col, col_pairing)
        if other_col is None:
            target = (sec, row ^ 1, col)
        elif other_row is None:
            target = (sec ^ 1, row, col)
        else:
            target = (sec, other_row, other_col)
        pairs.append(tuple((a * shape[1] + b) * shape[2] + c for a, b, c in ((sec, row, col), target)))
    return lax.ppermute(value, names, pairs)


def on_device(sketch, weights):
    planes, rows, width = sketch.shape
    group = lax.axis_size("row") * lax.axis_size("col")
    side = f32(planes + 8, LANES)
    by_row, weights_by_row, left, right, *messages = call(
        pack_rows_kernel,
        [f32(rows, planes, width), f32(rows, 8, width), side, side]
        + [f32(2 * planes + 16, width), f32(2 * planes + 8, width)]
        + [f32(16, LANES)] * 2,
        pltpu.with_memory_space_constraint(sketch, pltpu.HBM),
        pltpu.with_memory_space_constraint(weights, pltpu.HBM),
        memory=pltpu.HBM,
        scratch=[
            pltpu.VMEM(sketch.shape, jnp.float32),
            pltpu.VMEM(weights.shape, jnp.float32),
            pltpu.SemaphoreType.DMA((2,)),
        ],
    )
    from_rows = [swap(messages[at], row_pairing=at) for at in range(2)]
    from_diagonals = [swap(messages[2 + at], row_pairing=0, col_pairing=at) for at in range(2)]
    left, right, *messages = call(
        functools.partial(strips_kernel, rows), [side, side] + [f32(16, LANES)] * 2, left, right, from_rows[1]
    )
    from_cols = [swap(messages[at], col_pairing=at) for at in range(2)]
    parts_of = functools.partial(jax.ShapeDtypeStruct, dtype=jnp.bfloat16)
    products = f32(3 * planes, 3 * planes)
    middle, inner_second, side_second, *inner_products, from_diagonals[0] = call(
        inner_rows_kernel,
        [f32(rows - 2, planes, width), parts_of((rows - 4, 3 * planes, width)), parts_of((2, 3 * planes, width))]
        + [products, products, f32(16, LANES)],
        by_row,
        weights_by_row,
        from_diagonals[0],
        from_rows[1],
        cost=pl.CostEstimate(flops=20000000, bytes_accessed=40000, transcendentals=0),
    )
    outer_second, early_grams, *halos = call(
        outer_rows_kernel,
        [parts_of((4, 3 * planes, width)), f32(planes, 2 * planes), side, side],
        by_row,
        weights_by_row,
        from_rows[0],
        middle,
        side_second,
        *inner_products,
    )
    grams, edges = call(
        functools.partial(late_kernel, rows),
        [f32(group, 1, 9 * LANES), f32(planes, 2 * LANES)],
        left,
        right,
        *halos,
        *from_diagonals,
        *from_cols,
        early_grams,
    )
    rows_of, cols_of = lax.axis_size("row"), lax.axis_size("col")
    first = cols_of + cols_of // 2
    order = [first] + [row * cols_of + col for col in range(cols_of) for row in range(rows_of)]
    order = list(dict.fromkeys(order))
    parts = lax.all_to_all(grams, ("row", "col"), 0, 0, axis_index_groups=[order], tiled=True)
    return call(
        functools.partial(finish_kernel, float(rows * width * group)),
        [f32(planes, rows, width), f32(planes, planes)],
        inner_second,
        outer_second,
        edges,
        parts,
        out_memory=pl.ANY,
        scratch=[
            pltpu.VMEM(sketch.shape, jnp.float32),
            pltpu.VMEM((planes, planes), jnp.float32),
            pltpu.SemaphoreType.DMA((3,)),
        ],
    )


def solution(mesh):
    return jax.shard_map(
        on_device,
        mesh=mesh,
        in_specs=(P(None, ("sec", "row"), "col"), P(None, ("sec", "row"), "col")),
        out_specs=(P(None, ("sec", "row"), "col"), P("sec", None)),
        check_vma=False,
    )
```

```python
import functools
import itertools

import jax
import jax.numpy as jnp
from jax import lax
from jax.experimental import pallas as pl
from jax.experimental.pallas import tpu as pltpu
from jax.sharding import PartitionSpec as P

NEIGHBOURS = ((-1, -1), (-1, 0), (-1, 1), (0, -1), (0, 1), (1, -1), (1, 0), (1, 1))
LANES = 128
PITCH = 8
HIGHEST = lax.Precision.HIGHEST


def call(kernel, out_shapes, *operands, memory=pltpu.VMEM, out_memory=pltpu.VMEM, scratch=(), cost=None):
    return pl.pallas_call(
        kernel,
        out_shape=out_shapes,
        in_specs=[pl.BlockSpec(memory_space=memory)] * len(operands),
        out_specs=[pl.BlockSpec(memory_space=out_memory)] * len(out_shapes),
        scratch_shapes=scratch,
        cost_estimate=cost,
        compiler_params=pltpu.CompilerParams(vmem_limit_bytes=40 * 1024 * 1024),
    )(*operands)


def f32(*shape):
    return jax.ShapeDtypeStruct(shape, jnp.float32)


def sides_of(axis):
    place = lax.axis_index(axis)
    return place % 2 == 1, place > 0, place < lax.axis_size(axis) - 1


def edge_columns(first, last, place):
    lane = lax.broadcasted_iota(jnp.int32, (1, LANES), 1)
    own = PITCH - 2
    left = jnp.where((lane >= place + 2) & (lane < place + PITCH), pltpu.roll(first, place + 2, 1), 0.0)
    right = jnp.where((lane >= place) & (lane < place + own), pltpu.roll(last, place + own, 1), 0.0)
    return left, right


def pack_rows_kernel(sketch, weights, by_row, weights_by_row, left, right, *rest):
    bulk_messages, diagonal_messages = rest[:2], rest[2:4]
    tile, weight_tile, arrived = rest[4:]
    copies = [
        pltpu.make_async_copy(sketch, tile, arrived.at[0]),
        pltpu.make_async_copy(weights, weight_tile, arrived.at[1]),
    ]
    for copy in copies:
        copy.start()
    for copy in copies:
        copy.wait()
    rows, planes, width = by_row.shape
    odd_row, _, _ = sides_of("row")
    odd_col, _, _ = sides_of("col")
    lane = lax.broadcasted_iota(jnp.int32, (1, LANES), 1)
    for row in range(rows):
        weights_by_row[row] = weight_tile[:, row, :]
        by_row[row] = tile[:, row, :]
    for message, up in zip(bulk_messages, (odd_row, jnp.logical_not(odd_row))):
        start = jnp.where(up, rows - 2, 0)
        for slot in range(2):
            message[slot * planes : (slot + 1) * planes] = by_row[start + slot]
        message[2 * planes : 2 * planes + 8] = weights_by_row[jnp.where(up, rows - 1, 0)]
    strips = [None, None]
    for row in range(rows):
        first = jnp.concatenate([by_row[row, :, :LANES], weights_by_row[row, :, :LANES]], axis=0)
        last = jnp.concatenate([by_row[row, :, width - LANES :], weights_by_row[row, :, width - LANES :]], axis=0)
        parts = edge_columns(first, last, PITCH * (row + 2))
        strips = [part if strip is None else strip + part for strip, part in zip(strips, parts)]
    left[...], right[...] = strips
    bulk_messages[0][2 * planes + 8 :] = jnp.zeros((8, width), jnp.float32)
    pair = 2 * PITCH
    to_left, to_right = folded(strips[0], 2), folded(strips[1], PITCH - 4)
    for message, up in zip(diagonal_messages, (odd_col, jnp.logical_not(odd_col))):
        edge = jnp.where(up, to_right, to_left)
        below = jnp.where(lane < pair, rolled(edge, -PITCH * rows), 0.0)
        start = PITCH * (rows + 2)
        above = jnp.where((lane >= start) & (lane < start + pair), rolled(edge, PITCH * rows), 0.0)
        message[...] = jnp.where(odd_row, below, above)


def strips_kernel(rows, own_left, own_right, bulk_message, left, right, *col_messages):
    planes = own_left.shape[0] - 8
    odd_row, has_below, has_above = sides_of("row")
    odd_col, _, _ = sides_of("col")
    width = bulk_message.shape[1]
    totals = [own_left[...], own_right[...]]
    present = jnp.where(odd_row, has_below, has_above)
    for slot in range(2):
        place = PITCH * (slot + jnp.where(odd_row, 0, rows + 2))
        halo = [bulk_message[slot * planes : (slot + 1) * planes], bulk_message[2 * planes :]]
        first = jnp.concatenate([part[:, :LANES] for part in halo], axis=0)
        last = jnp.concatenate([part[:, width - LANES :] for part in halo], axis=0)
        parts = edge_columns(first, last, place)
        totals = [total + jnp.where(present, part, 0.0) for total, part in zip(totals, parts)]
    left[...], right[...] = totals
    to_left, to_right = folded(left[...], 2), folded(right[...], PITCH - 4)
    for message, up in zip(col_messages, (jnp.logical_not(odd_col), odd_col)):
        message[...] = jnp.where(up, to_right, to_left)


def folded(strip, spot):
    lane = lax.broadcasted_iota(jnp.int32, (1, LANES), 1)
    groups = strip.shape[0] // 8
    pieces = []
    for group in range(groups):
        target = 2 * group if group < groups - 1 else 0
        moved = rolled(strip[8 * group : 8 * (group + 1)], target - spot)
        pieces.append(jnp.where((lane % PITCH) // 2 == target // 2, moved, 0.0))
    return jnp.concatenate([functools.reduce(jnp.add, pieces[:-1]), pieces[-1]], axis=0)


def unfolded(message, spot, planes):
    lane = lax.broadcasted_iota(jnp.int32, (1, LANES), 1)
    pieces = [rolled(message[:8], spot - 2 * group) for group in range(planes // 8)] + [rolled(message[8:], spot)]
    return jnp.where((lane % PITCH) // 2 == spot // 2, jnp.concatenate(pieces, axis=0), 0.0)


def rolled(value, shift):
    return pltpu.roll(value, shift % LANES, 1) if shift % LANES else value


def apply_operator(rows3, weight_rows):
    width = rows3[1].shape[1]
    total = jnp.sum(weight_rows, axis=0, keepdims=True) * rows3[1]
    for across in (0, -1, 1):
        moved = pltpu.roll(weight_rows, across % width, 1) if across else weight_rows
        terms = [
            moved[position : position + 1] * rows3[up + 1]
            for position, (up, side) in enumerate(NEIGHBOURS)
            if side == across
        ]
        part = functools.reduce(jnp.add, terms)
        total = total + (pltpu.roll(part, -across % width, 1) if across else part)
    return total


def gram_of(value, other):
    return lax.dot_general(
        value, other, (((1,), (1,)), ((), ())), precision=HIGHEST, preferred_element_type=jnp.float32
    )


def split(value):
    high = value.astype(jnp.bfloat16)
    rest = value - high.astype(jnp.float32)
    middle = rest.astype(jnp.bfloat16)
    low = (rest - middle.astype(jnp.float32)).astype(jnp.bfloat16)
    return high, middle, low


def inner_parts(image):
    width = image.shape[1]
    lane = lax.broadcasted_iota(jnp.int32, (1, LANES), 1)
    kept = [
        jnp.where(lane >= 2, image[:, :LANES], 0.0),
        image[:, LANES : width - LANES],
        jnp.where(lane < LANES - 2, image[:, width - LANES :], 0.0),
    ]
    return jnp.concatenate(split(jnp.concatenate(kept, axis=1)), axis=0)


def products_of(parts):
    return lax.dot_general(parts, parts, (((1,), (1,)), ((), ())), preferred_element_type=jnp.float32)


def images_of(middle, weights, wanted, second, products):
    for at, row in enumerate(wanted):
        parts = inner_parts(apply_operator([middle(row - 1), middle(row), middle(row + 1)], weights(row)))
        second[at] = parts
        products = products + products_of(parts)
    return products


def side_rows(above, present, message, by_row, weights_by_row, middle, products):
    rows, planes, _ = by_row.shape

    def pick(high, low):
        return jnp.where(above, high, low)

    halo = jnp.where(present, message[: 2 * planes + 8], 0.0)
    one, other, halo_weights = halo[:planes], halo[planes : 2 * planes], halo[2 * planes :]
    near, far = pick(one, other), pick(other, one)
    edge, inside = pick(by_row[rows - 1], by_row[0]), pick(by_row[rows - 2], by_row[1])
    edge_weights = pick(weights_by_row[rows - 1], weights_by_row[0])
    inside_weights = pick(weights_by_row[rows - 2], weights_by_row[1])
    first_near = apply_operator([pick(edge, far), near, pick(far, edge)], halo_weights)
    first_edge = apply_operator([pick(inside, near), edge, pick(near, inside)], edge_weights)
    last = middle.shape[0] - 1
    first_inside, first_next = pick(middle[last], middle[0]), pick(middle[last - 1], middle[1])
    rows3 = [pick(first_inside, first_near), first_edge, pick(first_near, first_inside)]
    second_edge = inner_parts(apply_operator(rows3, edge_weights))
    rows3 = [pick(first_next, first_edge), first_inside, pick(first_edge, first_next)]
    second_inside = inner_parts(apply_operator(rows3, inside_weights))
    first, second = products
    first = first + products_of(inner_parts(first_edge))
    second = second + products_of(second_edge) + products_of(second_inside)
    return (second_edge, second_inside), (first, second)


def inner_rows_kernel(
    by_row, weights_by_row, diagonal_message, message, middle, second, side, first_products, second_products, diagonal
):
    rows = by_row.shape[0]
    odd_row, has_below, has_above = sides_of("row")
    diagonal[...] = jnp.where(jnp.where(odd_row, has_above, has_below), diagonal_message[...], 0.0)
    first = jnp.zeros(first_products.shape, jnp.float32)
    for row in range(1, rows - 1):
        image = apply_operator([by_row[row - 1], by_row[row], by_row[row + 1]], weights_by_row[row])
        middle[row - 1] = image
        first = first + products_of(inner_parts(image))
    products = first, images_of(
        lambda row: middle[row - 1],
        lambda row: weights_by_row[row],
        range(2, rows - 2),
        second,
        jnp.zeros(second_products.shape, jnp.float32),
    )
    above, present = jnp.logical_not(odd_row), jnp.where(odd_row, has_below, has_above)
    parts, products = side_rows(above, present, message, by_row, weights_by_row, middle, products)
    side[0], side[1] = parts
    first_products[...], second_products[...] = products


def outer_rows_kernel(
    by_row,
    weights_by_row,
    message,
    middle,
    side,
    first_products,
    second_products,
    second,
    grams,
    left_halo,
    right_halo,
):
    rows, planes, width = by_row.shape
    odd_row, has_below, has_above = sides_of("row")
    present = jnp.where(odd_row, has_above, has_below)
    halo = jnp.where(present, message[: 2 * planes + 8], 0.0)
    halos = [jnp.zeros(left_halo.shape, jnp.float32)] * 2
    for slot in range(2):
        place = PITCH * (slot + jnp.where(odd_row, rows + 2, 0))
        first = jnp.concatenate([halo[slot * planes : (slot + 1) * planes], halo[2 * planes :]], axis=0)
        parts = edge_columns(first[:, :LANES], first[:, width - LANES :], place)
        halos = [total + part for total, part in zip(halos, parts)]
    left_halo[...], right_halo[...] = halos
    products = first_products[...], second_products[...]
    parts, products = side_rows(odd_row, present, message, by_row, weights_by_row, middle, products)
    second[jnp.where(odd_row, 3, 0)], second[jnp.where(odd_row, 2, 1)] = parts
    second[jnp.where(odd_row, 0, 3)], second[jnp.where(odd_row, 1, 2)] = side[0], side[1]
    for at, both in enumerate(products):
        some = both[:planes] + both[planes : 2 * planes] + both[2 * planes :]
        total = some[:, :planes] + some[:, planes : 2 * planes] + some[:, 2 * planes :]
        grams[:, at * planes : (at + 1) * planes] = total


def apply_on_strip(values, weights):
    total = jnp.sum(weights, axis=0, keepdims=True) * values
    for position, (up, across) in enumerate(NEIGHBOURS):
        moved = pltpu.roll(values, (-PITCH * up - across) % LANES, 1)
        total = total + weights[position : position + 1] * moved
    return total


def late_kernel(rows, left, right, left_halo, right_halo, *rest):
    diagonal_messages, col_messages, (early_grams, grams, edges) = rest[:2], rest[3:1:-1], rest[4:]
    planes = early_grams.shape[0]
    odd_row, has_below, has_above = sides_of("row")
    odd_col, has_left, has_right = sides_of("col")
    beyond = jnp.where(odd_row, has_above, has_below)
    one, other = (
        col[...] + jnp.where(beyond, diagonal[...], 0.0)
        for col, diagonal in zip(col_messages, diagonal_messages)
    )
    lane = lax.broadcasted_iota(jnp.int32, (1, LANES), 1)
    spot, row = lane % PITCH, lane // PITCH
    strips, masks = [], []
    for side, (strip, present, halo) in enumerate(
        (
            (left[...] + left_halo[...], has_left, jnp.where(odd_col, other, one)),
            (right[...] + right_halo[...], has_right, jnp.where(odd_col, one, other)),
        )
    ):
        strips.append(strip + jnp.where(present, unfolded(halo, side * (PITCH - 2), planes), 0.0))
        low = 2 if side == 0 else PITCH - 4
        masks.append((spot >= low) & (spot < low + 2) & (row >= 2) & (row < rows + 2))
    values = [strip[:planes] for strip in strips]
    gram = []
    for at in range(2):
        values = [apply_on_strip(value, strip[planes:]) for value, strip in zip(values, strips)]
        kept = jnp.concatenate([jnp.where(mask, value, 0.0) for mask, value in zip(masks, values)], axis=1)
        both = jnp.concatenate(values, axis=1)
        gram.append(early_grams[:, at * planes : (at + 1) * planes] + gram_of(kept, both))
    edges[...] = both
    at_row = lax.broadcasted_iota(jnp.int32, (planes, planes), 0)
    at_col = lax.broadcasted_iota(jnp.int32, (planes, planes), 1)
    mixed = jnp.where(at_row >= at_col, gram[0], gram[1])
    diagonal = jnp.sum(jnp.where(at_row == at_col, gram[1], 0.0), axis=0, keepdims=True)
    block = jnp.concatenate([mixed[8 * g : 8 * (g + 1)] for g in range(planes // 8)], axis=1)
    last = jnp.concatenate([diagonal] * (LANES // planes), axis=1)
    for target in range(grams.shape[0]):
        for at in range(8):
            grams[target, :, at * LANES : (at + 1) * LANES] = block[at : at + 1]
        grams[target, :, 8 * LANES :] = last


def eliminate(grams, planes, half_way):
    lane = lax.broadcasted_iota(jnp.int32, (8, LANES), 1)
    sub = lax.broadcasted_iota(jnp.int32, (8, LANES), 0)
    first_half = lane < 2 * planes
    groups = planes // 8
    sources = [[gram[8 * g : 8 * (g + 1)] for g in range(groups)] for gram in grams]
    state = []
    for g in range(groups):
        unit = jnp.where(sub + 8 * g == lane % (2 * planes) - planes, 1.0, 0.0)
        unit = unit[:, planes : 2 * planes]
        state.append(jnp.concatenate([sources[0][g], unit, sources[1][g], unit], axis=1))
    columns = []
    for j in range(planes):
        columns.append(
            {
                g: jnp.where(
                    first_half,
                    jnp.broadcast_to(sources[0][g][:, j : j + 1], (8, LANES)),
                    jnp.broadcast_to(sources[1][g][:, j : j + 1], (8, LANES)),
                )
                for g in range(j // 8, groups)
            }
        )
    scale = [jnp.ones((8, LANES), jnp.float32)] * groups
    for step in range(planes):
        own, at = step // 8, step % 8
        column = columns[step]
        pivot = jnp.broadcast_to(column[own][at : at + 1], (8, LANES))
        inverse, root = pl.reciprocal(pivot, approx=False), lax.rsqrt(pivot)
        scale[own] = jnp.where(sub == at, root, scale[own])
        left = {g: jnp.where(sub > at, value, 0.0) if g == own else value for g, value in column.items()}
        factors = {g: value * inverse for g, value in left.items()}
        for j in range(step + 1, planes):
            entry = jnp.broadcast_to(column[j // 8][j % 8 : j % 8 + 1], (8, LANES))
            for g in columns[j]:
                change = (left[g] * entry) * inverse if j == step + 1 else factors[g] * entry
                columns[j][g] = columns[j][g] - change
        pivot_row = jnp.broadcast_to(state[own][at : at + 1], (8, LANES))
        for g in range(own, groups):
            state[g] = state[g] - factors[g] * pivot_row
        if step + 1 == planes // 2:
            half_way(jnp.concatenate([state[g] * scale[g] for g in range(groups // 2)], axis=0))
    return jnp.concatenate([state[g] * scale[g] for g in range(groups)], axis=0)


def finish_kernel(
    pixel_count, inner_second, outer_second, edges, parts, basis_out, factor_out, basis, factor, written
):
    planes, rows, width = basis.shape
    half = planes // 2
    at_row = lax.broadcasted_iota(jnp.int32, (planes, planes), 0)
    at_col = lax.broadcasted_iota(jnp.int32, (planes, planes), 1)
    lane = lax.broadcasted_iota(jnp.int32, (1, LANES), 1)
    outer_parts = split(edges[...])
    copies = []

    def solve(inverse, start):
        stop = start + inverse.shape[0]
        high, middle, low = split(inverse)
        left_side = jnp.concatenate([high, high, middle, high, low, middle], axis=1)

        def solved(high, middle, low):
            right_side = jnp.concatenate([high, middle, high, low, high, middle], axis=0)
            return jnp.dot(left_side, right_side, preferred_element_type=jnp.float32)

        outer = solved(*(part[:stop] for part in outer_parts))
        for row in range(rows):
            if 2 <= row < rows - 2:
                held, spot = inner_second, row - 2
            else:
                held, spot = outer_second, row if row < 2 else row - rows + 4
            value = solved(*(held[spot, at * planes : at * planes + stop] for at in range(3)))
            place = PITCH * (row + 2)
            first = rolled(outer[:, :LANES], -(place + 2))
            last = rolled(outer[:, LANES:], LANES - 2 - (place + PITCH - 4))
            basis[start:stop, row, :LANES] = jnp.where(lane < 2, first, value[:, :LANES])
            basis[start:stop, row, LANES : width - LANES] = value[:, LANES : width - LANES]
            basis[start:stop, row, width - LANES :] = jnp.where(
                lane >= LANES - 2, last, value[:, width - LANES :]
            )
        some = pl.ds(start, stop - start)
        copies.append(pltpu.make_async_copy(basis.at[some], basis_out.at[some], written.at[len(copies)]))
        copies[-1].start()

    block = tree_sum([parts[at] for at in range(parts.shape[0])]) / pixel_count
    block = [block[:, at * LANES : (at + 1) * LANES] for at in range(9)]
    mixed, diagonal = jnp.concatenate(block[:8], axis=0), block[8][:, :planes]
    mixed = jnp.concatenate([mixed[:, at * planes : (at + 1) * planes] for at in range(LANES // planes)], axis=0)
    flipped = mixed.T
    first = jnp.where(at_row >= at_col, mixed, flipped)
    second = jnp.where(at_row < at_col, mixed, jnp.where(at_row > at_col, flipped, diagonal))
    low_half = (at_col <= at_row)[:half, :half]
    state = eliminate(
        [first, second],
        planes,
        lambda state: solve(jnp.where(low_half, state[:, 3 * planes : 3 * planes + half], 0.0), 0),
    )
    first_inverse = state[:, planes : 2 * planes]
    product_upper = jnp.where(at_col >= at_row, state[:, 2 * planes : 3 * planes], 0.0)
    solve(jnp.where(at_col <= at_row, state[:, 3 * planes :], 0.0)[half:], half)
    factor[...] = jnp.where(at_col >= at_row, gram_of(product_upper, first_inverse), 0.0)
    copies.append(pltpu.make_async_copy(factor, factor_out, written.at[2]))
    copies[-1].start()
    for copy in copies:
        copy.wait()


def tree_sum(parts):
    while len(parts) > 1:
        parts = [sum(parts[at + 1 : at + 2], parts[at]) for at in range(0, len(parts), 2)]
    return parts[0]


def swap(value, row_pairing=None, col_pairing=None):
    names = ("sec", "row", "col")
    shape = [lax.axis_size(name) for name in names]

    def partner(at, place, pairing):
        other = place if pairing is None else place + 1 if place % 2 != pairing else place - 1
        return other if 0 <= other < shape[at] else None

    pairs = []
    for sec, row, col in itertools.product(*(range(extent) for extent in shape)):
        other_row, other_col = partner(1, row, row_pairing), partner(2, col, col_pairing)
        if other_col is None:
            target = (sec, row ^ 1, col)
        elif other_row is None:
            target = (sec ^ 1, row, col)
        else:
            target = (sec, other_row, other_col)
        pairs.append(tuple((a * shape[1] + b) * shape[2] + c for a, b, c in ((sec, row, col), target)))
    return lax.ppermute(value, names, pairs)


def on_device(sketch, weights):
    planes, rows, width = sketch.shape
    group = lax.axis_size("row") * lax.axis_size("col")
    side = f32(planes + 8, LANES)
    by_row, weights_by_row, left, right, *messages = call(
        pack_rows_kernel,
        [f32(rows, planes, width), f32(rows, 8, width), side, side]
        + [f32(2 * planes + 16, width), f32(2 * planes + 8, width)]
        + [f32(16, LANES)] * 2,
        pltpu.with_memory_space_constraint(sketch, pltpu.HBM),
        pltpu.with_memory_space_constraint(weights, pltpu.HBM),
        memory=pltpu.HBM,
        scratch=[
            pltpu.VMEM(sketch.shape, jnp.float32),
            pltpu.VMEM(weights.shape, jnp.float32),
            pltpu.SemaphoreType.DMA((2,)),
        ],
    )
    from_rows = [swap(messages[at], row_pairing=at) for at in range(2)]
    from_diagonals = [swap(messages[2 + at], row_pairing=0, col_pairing=at) for at in range(2)]
    left, right, *messages = call(
        functools.partial(strips_kernel, rows), [side, side] + [f32(16, LANES)] * 2, left, right, from_rows[1]
    )
    from_cols = [swap(messages[1 - at], col_pairing=at) for at in (1, 0)]
    parts_of = functools.partial(jax.ShapeDtypeStruct, dtype=jnp.bfloat16)
    products = f32(3 * planes, 3 * planes)
    middle, inner_second, side_second, *inner_products, from_diagonals[1] = call(
        inner_rows_kernel,
        [f32(rows - 2, planes, width), parts_of((rows - 4, 3 * planes, width)), parts_of((2, 3 * planes, width))]
        + [products, products, f32(16, LANES)],
        by_row,
        weights_by_row,
        from_diagonals[1],
        from_rows[1],
        cost=pl.CostEstimate(flops=20000000, bytes_accessed=40000, transcendentals=0),
    )
    outer_second, early_grams, *halos = call(
        outer_rows_kernel,
        [parts_of((4, 3 * planes, width)), f32(planes, 2 * planes), side, side],
        by_row,
        weights_by_row,
        from_rows[0],
        middle,
        side_second,
        *inner_products,
    )
    grams, edges = call(
        functools.partial(late_kernel, rows),
        [f32(group, 1, 9 * LANES), f32(planes, 2 * LANES)],
        left,
        right,
        *halos,
        *from_diagonals,
        *from_cols,
        early_grams,
    )
    rows_of, cols_of = lax.axis_size("row"), lax.axis_size("col")
    first = cols_of + cols_of // 2
    order = [first] + [row * cols_of + col for col in range(cols_of) for row in range(rows_of)]
    order = list(dict.fromkeys(order))
    parts = lax.all_to_all(grams, ("row", "col"), 0, 0, axis_index_groups=[order], tiled=True)
    return call(
        functools.partial(finish_kernel, float(rows * width * group)),
        [f32(planes, rows, width), f32(planes, planes)],
        inner_second,
        outer_second,
        edges,
        parts,
        out_memory=pl.ANY,
        scratch=[
            pltpu.VMEM(sketch.shape, jnp.float32),
            pltpu.VMEM((planes, planes), jnp.float32),
            pltpu.SemaphoreType.DMA((3,)),
        ],
    )


def solution(mesh):
    return jax.shard_map(
        on_device,
        mesh=mesh,
        in_specs=(P(None, ("sec", "row"), "col"), P(None, ("sec", "row"), "col")),
        out_specs=(P(None, ("sec", "row"), "col"), P("sec", None)),
        check_vma=False,
    )
```

```python
import functools
import itertools

import jax
import jax.numpy as jnp
from jax import lax
from jax.experimental import pallas as pl
from jax.experimental.pallas import tpu as pltpu
from jax.sharding import PartitionSpec as P

NEIGHBOURS = ((-1, -1), (-1, 0), (-1, 1), (0, -1), (0, 1), (1, -1), (1, 0), (1, 1))
LANES = 128
PITCH = 8
HIGHEST = lax.Precision.HIGHEST


def call(kernel, out_shapes, *operands, memory=pltpu.VMEM, out_memory=pltpu.VMEM, scratch=(), cost=None):
    return pl.pallas_call(
        kernel,
        out_shape=out_shapes,
        in_specs=[pl.BlockSpec(memory_space=memory)] * len(operands),
        out_specs=[pl.BlockSpec(memory_space=out_memory)] * len(out_shapes),
        scratch_shapes=scratch,
        cost_estimate=cost,
        compiler_params=pltpu.CompilerParams(vmem_limit_bytes=40 * 1024 * 1024),
    )(*operands)


def f32(*shape):
    return jax.ShapeDtypeStruct(shape, jnp.float32)


def sides_of(axis):
    place = lax.axis_index(axis)
    return place % 2 == 1, place > 0, place < lax.axis_size(axis) - 1


def edge_columns(first, last, place):
    lane = lax.broadcasted_iota(jnp.int32, (1, LANES), 1)
    own = PITCH - 2
    left = jnp.where((lane >= place + 2) & (lane < place + PITCH), pltpu.roll(first, place + 2, 1), 0.0)
    right = jnp.where((lane >= place) & (lane < place + own), pltpu.roll(last, place + own, 1), 0.0)
    return left, right


def pack_rows_kernel(sketch, weights, by_row, weights_by_row, left, right, *rest):
    bulk_messages, diagonal_messages = rest[:2], rest[2:4]
    tile, weight_tile, arrived = rest[4:]
    copies = [
        pltpu.make_async_copy(sketch, tile, arrived.at[0]),
        pltpu.make_async_copy(weights, weight_tile, arrived.at[1]),
    ]
    for copy in copies:
        copy.start()
    for copy in copies:
        copy.wait()
    rows, planes, width = by_row.shape
    odd_row, _, _ = sides_of("row")
    odd_col, _, _ = sides_of("col")
    lane = lax.broadcasted_iota(jnp.int32, (1, LANES), 1)
    for row in range(rows):
        weights_by_row[row] = weight_tile[:, row, :]
        by_row[row] = tile[:, row, :]
    for message, up in zip(bulk_messages, (odd_row, jnp.logical_not(odd_row))):
        start = jnp.where(up, rows - 2, 0)
        for slot in range(2):
            message[slot * planes : (slot + 1) * planes] = by_row[start + slot]
        message[2 * planes : 2 * planes + 8] = weights_by_row[jnp.where(up, rows - 1, 0)]
    strips = [None, None]
    for row in range(rows):
        first = jnp.concatenate([by_row[row, :, :LANES], weights_by_row[row, :, :LANES]], axis=0)
        last = jnp.concatenate([by_row[row, :, width - LANES :], weights_by_row[row, :, width - LANES :]], axis=0)
        parts = edge_columns(first, last, PITCH * (row + 2))
        strips = [part if strip is None else strip + part for strip, part in zip(strips, parts)]
    left[...], right[...] = strips
    bulk_messages[0][2 * planes + 8 :] = jnp.zeros((8, width), jnp.float32)
    pair = 2 * PITCH
    to_left, to_right = folded(strips[0], 2), folded(strips[1], PITCH - 4)
    for message, up in zip(diagonal_messages, (odd_col, jnp.logical_not(odd_col))):
        edge = jnp.where(up, to_right, to_left)
        below = jnp.where(lane < pair, rolled(edge, -PITCH * rows), 0.0)
        start = PITCH * (rows + 2)
        above = jnp.where((lane >= start) & (lane < start + pair), rolled(edge, PITCH * rows), 0.0)
        message[...] = jnp.where(odd_row, below, above)


def strips_kernel(rows, own_left, own_right, bulk_message, left, right, *col_messages):
    planes = own_left.shape[0] - 8
    odd_row, has_below, has_above = sides_of("row")
    odd_col, _, _ = sides_of("col")
    width = bulk_message.shape[1]
    totals = [own_left[...], own_right[...]]
    present = jnp.where(odd_row, has_below, has_above)
    for slot in range(2):
        place = PITCH * (slot + jnp.where(odd_row, 0, rows + 2))
        halo = [bulk_message[slot * planes : (slot + 1) * planes], bulk_message[2 * planes :]]
        first = jnp.concatenate([part[:, :LANES] for part in halo], axis=0)
        last = jnp.concatenate([part[:, width - LANES :] for part in halo], axis=0)
        parts = edge_columns(first, last, place)
        totals = [total + jnp.where(present, part, 0.0) for total, part in zip(totals, parts)]
    left[...], right[...] = totals
    to_left, to_right = folded(left[...], 2), folded(right[...], PITCH - 4)
    for message, up in zip(col_messages, (jnp.logical_not(odd_col), odd_col)):
        message[...] = jnp.where(up, to_right, to_left)


def folded(strip, spot):
    lane = lax.broadcasted_iota(jnp.int32, (1, LANES), 1)
    groups = strip.shape[0] // 8
    pieces = []
    for group in range(groups):
        target = 2 * group if group < groups - 1 else 0
        moved = rolled(strip[8 * group : 8 * (group + 1)], target - spot)
        pieces.append(jnp.where((lane % PITCH) // 2 == target // 2, moved, 0.0))
    return jnp.concatenate([functools.reduce(jnp.add, pieces[:-1]), pieces[-1]], axis=0)


def unfolded(message, spot, planes):
    lane = lax.broadcasted_iota(jnp.int32, (1, LANES), 1)
    pieces = [rolled(message[:8], spot - 2 * group) for group in range(planes // 8)] + [rolled(message[8:], spot)]
    return jnp.where((lane % PITCH) // 2 == spot // 2, jnp.concatenate(pieces, axis=0), 0.0)


def rolled(value, shift):
    return pltpu.roll(value, shift % LANES, 1) if shift % LANES else value


def apply_operator(rows3, weight_rows):
    width = rows3[1].shape[1]
    total = jnp.sum(weight_rows, axis=0, keepdims=True) * rows3[1]
    for across in (0, -1, 1):
        moved = pltpu.roll(weight_rows, across % width, 1) if across else weight_rows
        terms = [
            moved[position : position + 1] * rows3[up + 1]
            for position, (up, side) in enumerate(NEIGHBOURS)
            if side == across
        ]
        part = functools.reduce(jnp.add, terms)
        total = total + (pltpu.roll(part, -across % width, 1) if across else part)
    return total


def gram_of(value, other):
    return lax.dot_general(
        value, other, (((1,), (1,)), ((), ())), precision=HIGHEST, preferred_element_type=jnp.float32
    )


def split(value):
    high = value.astype(jnp.bfloat16)
    rest = value - high.astype(jnp.float32)
    middle = rest.astype(jnp.bfloat16)
    low = (rest - middle.astype(jnp.float32)).astype(jnp.bfloat16)
    return high, middle, low


def inner_parts(image):
    width = image.shape[1]
    lane = lax.broadcasted_iota(jnp.int32, (1, LANES), 1)
    kept = [
        jnp.where(lane >= 2, image[:, :LANES], 0.0),
        image[:, LANES : width - LANES],
        jnp.where(lane < LANES - 2, image[:, width - LANES :], 0.0),
    ]
    return jnp.concatenate(split(jnp.concatenate(kept, axis=1)), axis=0)


def products_of(parts):
    return lax.dot_general(parts, parts, (((1,), (1,)), ((), ())), preferred_element_type=jnp.float32)


def images_of(middle, weights, wanted, second, products):
    for at, row in enumerate(wanted):
        parts = inner_parts(apply_operator([middle(row - 1), middle(row), middle(row + 1)], weights(row)))
        second[at] = parts
        products = products + products_of(parts)
    return products


def side_rows(above, present, message, by_row, weights_by_row, middle, products):
    rows, planes, _ = by_row.shape

    def pick(high, low):
        return jnp.where(above, high, low)

    halo = jnp.where(present, message[: 2 * planes + 8], 0.0)
    one, other, halo_weights = halo[:planes], halo[planes : 2 * planes], halo[2 * planes :]
    near, far = pick(one, other), pick(other, one)
    edge, inside = pick(by_row[rows - 1], by_row[0]), pick(by_row[rows - 2], by_row[1])
    edge_weights = pick(weights_by_row[rows - 1], weights_by_row[0])
    inside_weights = pick(weights_by_row[rows - 2], weights_by_row[1])
    first_near = apply_operator([pick(edge, far), near, pick(far, edge)], halo_weights)
    first_edge = apply_operator([pick(inside, near), edge, pick(near, inside)], edge_weights)
    last = middle.shape[0] - 1
    first_inside, first_next = pick(middle[last], middle[0]), pick(middle[last - 1], middle[1])
    rows3 = [pick(first_inside, first_near), first_edge, pick(first_near, first_inside)]
    second_edge = inner_parts(apply_operator(rows3, edge_weights))
    rows3 = [pick(first_next, first_edge), first_inside, pick(first_edge, first_next)]
    second_inside = inner_parts(apply_operator(rows3, inside_weights))
    first, second = products
    first = first + products_of(inner_parts(first_edge))
    second = second + products_of(second_edge) + products_of(second_inside)
    return (second_edge, second_inside), (first, second)


def inner_rows_kernel(
    by_row, weights_by_row, diagonal_message, message, middle, second, side, first_products, second_products, diagonal
):
    rows = by_row.shape[0]
    odd_row, has_below, has_above = sides_of("row")
    diagonal[...] = jnp.where(jnp.where(odd_row, has_above, has_below), diagonal_message[...], 0.0)
    first = jnp.zeros(first_products.shape, jnp.float32)
    for row in range(1, rows - 1):
        image = apply_operator([by_row[row - 1], by_row[row], by_row[row + 1]], weights_by_row[row])
        middle[row - 1] = image
        first = first + products_of(inner_parts(image))
    products = first, images_of(
        lambda row: middle[row - 1],
        lambda row: weights_by_row[row],
        range(2, rows - 2),
        second,
        jnp.zeros(second_products.shape, jnp.float32),
    )
    above, present = jnp.logical_not(odd_row), jnp.where(odd_row, has_below, has_above)
    parts, products = side_rows(above, present, message, by_row, weights_by_row, middle, products)
    side[0], side[1] = parts
    first_products[...], second_products[...] = products


def outer_rows_kernel(
    by_row,
    weights_by_row,
    message,
    middle,
    side,
    first_products,
    second_products,
    second,
    grams,
    left_halo,
    right_halo,
):
    rows, planes, width = by_row.shape
    odd_row, has_below, has_above = sides_of("row")
    present = jnp.where(odd_row, has_above, has_below)
    halo = jnp.where(present, message[: 2 * planes + 8], 0.0)
    halos = [jnp.zeros(left_halo.shape, jnp.float32)] * 2
    for slot in range(2):
        place = PITCH * (slot + jnp.where(odd_row, rows + 2, 0))
        first = jnp.concatenate([halo[slot * planes : (slot + 1) * planes], halo[2 * planes :]], axis=0)
        parts = edge_columns(first[:, :LANES], first[:, width - LANES :], place)
        halos = [total + part for total, part in zip(halos, parts)]
    left_halo[...], right_halo[...] = halos
    products = first_products[...], second_products[...]
    parts, products = side_rows(odd_row, present, message, by_row, weights_by_row, middle, products)
    second[jnp.where(odd_row, 3, 0)], second[jnp.where(odd_row, 2, 1)] = parts
    second[jnp.where(odd_row, 0, 3)], second[jnp.where(odd_row, 1, 2)] = side[0], side[1]
    for at, both in enumerate(products):
        some = both[:planes] + both[planes : 2 * planes] + both[2 * planes :]
        total = some[:, :planes] + some[:, planes : 2 * planes] + some[:, 2 * planes :]
        grams[:, at * planes : (at + 1) * planes] = total


def apply_on_strip(values, weights):
    total = jnp.sum(weights, axis=0, keepdims=True) * values
    for position, (up, across) in enumerate(NEIGHBOURS):
        moved = pltpu.roll(values, (-PITCH * up - across) % LANES, 1)
        total = total + weights[position : position + 1] * moved
    return total


def late_kernel(rows, left, right, left_halo, right_halo, *rest):
    diagonal_messages, col_messages, (early_grams, grams, edges) = rest[:2], rest[3:1:-1], rest[4:]
    planes = early_grams.shape[0]
    odd_row, has_below, has_above = sides_of("row")
    odd_col, has_left, has_right = sides_of("col")
    beyond = jnp.where(odd_row, has_above, has_below)
    one, other = (
        col[...] + jnp.where(beyond, diagonal[...], 0.0)
        for col, diagonal in zip(col_messages, diagonal_messages)
    )
    lane = lax.broadcasted_iota(jnp.int32, (1, LANES), 1)
    spot, row = lane % PITCH, lane // PITCH
    strips, masks = [], []
    for side, (strip, present, halo) in enumerate(
        (
            (left[...] + left_halo[...], has_left, jnp.where(odd_col, other, one)),
            (right[...] + right_halo[...], has_right, jnp.where(odd_col, one, other)),
        )
    ):
        strips.append(strip + jnp.where(present, unfolded(halo, side * (PITCH - 2), planes), 0.0))
        low = 2 if side == 0 else PITCH - 4
        masks.append((spot >= low) & (spot < low + 2) & (row >= 2) & (row < rows + 2))
    values = [strip[:planes] for strip in strips]
    gram = []
    for at in range(2):
        values = [apply_on_strip(value, strip[planes:]) for value, strip in zip(values, strips)]
        kept = jnp.concatenate([jnp.where(mask, value, 0.0) for mask, value in zip(masks, values)], axis=1)
        both = jnp.concatenate(values, axis=1)
        gram.append(early_grams[:, at * planes : (at + 1) * planes] + gram_of(kept, both))
    edges[...] = both
    at_row = lax.broadcasted_iota(jnp.int32, (planes, planes), 0)
    at_col = lax.broadcasted_iota(jnp.int32, (planes, planes), 1)
    mixed = jnp.where(at_row >= at_col, gram[0], gram[1])
    diagonal = jnp.sum(jnp.where(at_row == at_col, gram[1], 0.0), axis=0, keepdims=True)
    block = jnp.concatenate([mixed[8 * g : 8 * (g + 1)] for g in range(planes // 8)], axis=1)
    last = jnp.concatenate([diagonal] * (LANES // planes), axis=1)
    for target in range(grams.shape[0]):
        for at in range(8):
            grams[target, :, at * LANES : (at + 1) * LANES] = block[at : at + 1]
        grams[target, :, 8 * LANES :] = last


def eliminate(grams, planes, half_way):
    lane = lax.broadcasted_iota(jnp.int32, (8, LANES), 1)
    sub = lax.broadcasted_iota(jnp.int32, (8, LANES), 0)
    first_half = lane < 2 * planes
    groups = planes // 8
    sources = [[gram[8 * g : 8 * (g + 1)] for g in range(groups)] for gram in grams]
    state = []
    for g in range(groups):
        unit = jnp.where(sub + 8 * g == lane % (2 * planes) - planes, 1.0, 0.0)
        unit = unit[:, planes : 2 * planes]
        state.append(jnp.concatenate([sources[0][g], unit, sources[1][g], unit], axis=1))
    columns = []
    for j in range(planes):
        columns.append(
            {
                g: jnp.where(
                    first_half,
                    jnp.broadcast_to(sources[0][g][:, j : j + 1], (8, LANES)),
                    jnp.broadcast_to(sources[1][g][:, j : j + 1], (8, LANES)),
                )
                for g in range(j // 8, groups)
            }
        )
    scale = [jnp.ones((8, LANES), jnp.float32)] * groups
    for step in range(planes):
        own, at = step // 8, step % 8
        column = columns[step]
        pivot = jnp.broadcast_to(column[own][at : at + 1], (8, LANES))
        inverse, root = pl.reciprocal(pivot, approx=False), lax.rsqrt(pivot)
        scale[own] = jnp.where(sub == at, root, scale[own])
        left = {g: jnp.where(sub > at, value, 0.0) if g == own else value for g, value in column.items()}
        factors = {g: value * inverse for g, value in left.items()}
        for j in range(step + 1, planes):
            entry = jnp.broadcast_to(column[j // 8][j % 8 : j % 8 + 1], (8, LANES))
            for g in columns[j]:
                change = (left[g] * entry) * inverse if j == step + 1 else factors[g] * entry
                columns[j][g] = columns[j][g] - change
        pivot_row = jnp.broadcast_to(state[own][at : at + 1], (8, LANES))
        for g in range(own, groups):
            state[g] = state[g] - factors[g] * pivot_row
        if step + 1 == planes // 2:
            half_way(jnp.concatenate([state[g] * scale[g] for g in range(groups // 2)], axis=0))
    return jnp.concatenate([state[g] * scale[g] for g in range(groups)], axis=0)


def finish_kernel(
    pixel_count, inner_second, outer_second, edges, parts, basis_out, factor_out, basis, factor, written
):
    planes, rows, width = basis.shape
    half = planes // 2
    at_row = lax.broadcasted_iota(jnp.int32, (planes, planes), 0)
    at_col = lax.broadcasted_iota(jnp.int32, (planes, planes), 1)
    lane = lax.broadcasted_iota(jnp.int32, (1, LANES), 1)
    outer_parts = split(edges[...])
    copies = []

    def solve(inverse, start):
        stop = start + inverse.shape[0]
        high, middle, low = split(inverse)
        left_side = jnp.concatenate([high, high, middle, high, low, middle], axis=1)

        def solved(high, middle, low):
            right_side = jnp.concatenate([high, middle, high, low, high, middle], axis=0)
            return jnp.dot(left_side, right_side, preferred_element_type=jnp.float32)

        outer = solved(*(part[:stop] for part in outer_parts))
        for row in range(rows):
            if 2 <= row < rows - 2:
                held, spot = inner_second, row - 2
            else:
                held, spot = outer_second, row if row < 2 else row - rows + 4
            value = solved(*(held[spot, at * planes : at * planes + stop] for at in range(3)))
            place = PITCH * (row + 2)
            first = rolled(outer[:, :LANES], -(place + 2))
            last = rolled(outer[:, LANES:], LANES - 2 - (place + PITCH - 4))
            basis[start:stop, row, :LANES] = jnp.where(lane < 2, first, value[:, :LANES])
            basis[start:stop, row, LANES : width - LANES] = value[:, LANES : width - LANES]
            basis[start:stop, row, width - LANES :] = jnp.where(
                lane >= LANES - 2, last, value[:, width - LANES :]
            )
        some = pl.ds(start, stop - start)
        copies.append(pltpu.make_async_copy(basis.at[some], basis_out.at[some], written.at[len(copies)]))
        copies[-1].start()

    block = tree_sum([parts[at] for at in range(parts.shape[0])]) / pixel_count
    block = [block[:, at * LANES : (at + 1) * LANES] for at in range(9)]
    mixed, diagonal = jnp.concatenate(block[:8], axis=0), block[8][:, :planes]
    mixed = jnp.concatenate([mixed[:, at * planes : (at + 1) * planes] for at in range(LANES // planes)], axis=0)
    flipped = mixed.T
    first = jnp.where(at_row >= at_col, mixed, flipped)
    second = jnp.where(at_row < at_col, mixed, jnp.where(at_row > at_col, flipped, diagonal))
    low_half = (at_col <= at_row)[:half, :half]
    state = eliminate(
        [first, second],
        planes,
        lambda state: solve(jnp.where(low_half, state[:, 3 * planes : 3 * planes + half], 0.0), 0),
    )
    first_inverse = state[:, planes : 2 * planes]
    product_upper = jnp.where(at_col >= at_row, state[:, 2 * planes : 3 * planes], 0.0)
    solve(jnp.where(at_col <= at_row, state[:, 3 * planes :], 0.0)[half:], half)
    factor[...] = jnp.where(at_col >= at_row, gram_of(product_upper, first_inverse), 0.0)
    copies.append(pltpu.make_async_copy(factor, factor_out, written.at[2]))
    copies[-1].start()
    for copy in copies:
        copy.wait()


def tree_sum(parts):
    while len(parts) > 1:
        parts = [sum(parts[at + 1 : at + 2], parts[at]) for at in range(0, len(parts), 2)]
    return parts[0]


def swap(value, row_pairing=None, col_pairing=None):
    names = ("sec", "row", "col")
    shape = [lax.axis_size(name) for name in names]

    def partner(at, place, pairing):
        other = place if pairing is None else place + 1 if place % 2 != pairing else place - 1
        return other if 0 <= other < shape[at] else None

    pairs = []
    for sec, row, col in itertools.product(*(range(extent) for extent in shape)):
        other_row, other_col = partner(1, row, row_pairing), partner(2, col, col_pairing)
        if other_col is None:
            target = (sec, row ^ 1, col)
        elif other_row is None:
            target = (sec ^ 1, row, col)
        else:
            target = (sec, other_row, other_col)
        pairs.append(tuple((a * shape[1] + b) * shape[2] + c for a, b, c in ((sec, row, col), target)))
    return lax.ppermute(value, names, pairs)


def on_device(sketch, weights):
    planes, rows, width = sketch.shape
    group = lax.axis_size("row") * lax.axis_size("col")
    side = f32(planes + 8, LANES)
    by_row, weights_by_row, left, right, *messages = call(
        pack_rows_kernel,
        [f32(rows, planes, width), f32(rows, 8, width), side, side]
        + [f32(2 * planes + 16, width), f32(2 * planes + 8, width)]
        + [f32(16, LANES)] * 2,
        pltpu.with_memory_space_constraint(sketch, pltpu.HBM),
        pltpu.with_memory_space_constraint(weights, pltpu.HBM),
        memory=pltpu.HBM,
        scratch=[
            pltpu.VMEM(sketch.shape, jnp.float32),
            pltpu.VMEM(weights.shape, jnp.float32),
            pltpu.SemaphoreType.DMA((2,)),
        ],
    )
    from_rows = [swap(messages[at], row_pairing=at) for at in range(2)]
    from_diagonals = [swap(messages[2 + at], row_pairing=0, col_pairing=at) for at in range(2)]
    left, right, *messages = call(
        functools.partial(strips_kernel, rows), [side, side] + [f32(16, LANES)] * 2, left, right, from_rows[1]
    )
    from_cols = [swap(messages[1 - at], col_pairing=at) for at in (1, 0)]
    parts_of = functools.partial(jax.ShapeDtypeStruct, dtype=jnp.bfloat16)
    products = f32(3 * planes, 3 * planes)
    middle, inner_second, side_second, *inner_products, from_diagonals[1] = call(
        inner_rows_kernel,
        [f32(rows - 2, planes, width), parts_of((rows - 4, 3 * planes, width)), parts_of((2, 3 * planes, width))]
        + [products, products, f32(16, LANES)],
        by_row,
        weights_by_row,
        from_diagonals[1],
        from_rows[1],
        cost=pl.CostEstimate(flops=400000000, bytes_accessed=800000, transcendentals=0),
    )
    outer_second, early_grams, *halos = call(
        outer_rows_kernel,
        [parts_of((4, 3 * planes, width)), f32(planes, 2 * planes), side, side],
        by_row,
        weights_by_row,
        from_rows[0],
        middle,
        side_second,
        *inner_products,
    )
    grams, edges = call(
        functools.partial(late_kernel, rows),
        [f32(group, 1, 9 * LANES), f32(planes, 2 * LANES)],
        left,
        right,
        *halos,
        *from_diagonals,
        *from_cols,
        early_grams,
    )
    rows_of, cols_of = lax.axis_size("row"), lax.axis_size("col")
    first = cols_of + (cols_of - 1) // 2
    order = [first] + [row * cols_of + col for col in range(cols_of) for row in range(rows_of)]
    order = list(dict.fromkeys(order))
    parts = lax.all_to_all(grams, ("row", "col"), 0, 0, axis_index_groups=[order], tiled=True)
    return call(
        functools.partial(finish_kernel, float(rows * width * group)),
        [f32(planes, rows, width), f32(planes, planes)],
        inner_second,
        outer_second,
        edges,
        parts,
        out_memory=pl.ANY,
        scratch=[
            pltpu.VMEM(sketch.shape, jnp.float32),
            pltpu.VMEM((planes, planes), jnp.float32),
            pltpu.SemaphoreType.DMA((3,)),
        ],
    )


def solution(mesh):
    return jax.shard_map(
        on_device,
        mesh=mesh,
        in_specs=(P(None, ("sec", "row"), "col"), P(None, ("sec", "row"), "col")),
        out_specs=(P(None, ("sec", "row"), "col"), P("sec", None)),
        check_vma=False,
    )
```
